128 devices in a mesh: dp: 16 (over x, z), ctx: 8 (over y, core).
Axes of the slice: x: 4, y: 4, z: 4, core: 2. Of those that a mesh axis runs over, the one named last changes fastest.
Arguments:
- tokens: bfloat16 [16, 1024, 896], P('dp', 'ctx'), may hold values from -6 to 6
- cotangent: bfloat16 [16, 1024, 896], P('dp', 'ctx'), may hold values from -6 to 6
- span_order: int32 [16], replicated, may hold values from 0 to 15, each once
- gain_one: bfloat16 [2, 896], P(None, ('dp', 'ctx')), may hold values from 0.5 to 1.5
- w_qkv: bfloat16 [2, 896, 1152], P(None, ('dp', 'ctx')), may hold values from -0.1875 to 0.1875
- b_qkv: bfloat16 [2, 1152], P(None, ('dp', 'ctx')), may hold values from -3 to 3
- w_out: bfloat16 [2, 896, 896], P(None, ('dp', 'ctx')), may hold values from -0.75 to 0.75
- gain_two: bfloat16 [2, 896], P(None, ('dp', 'ctx')), may hold values from 0.5 to 1.5
- w_gate: bfloat16 [2, 896, 4864], P(None, 'dp', 'ctx'), may hold values from -0.1875 to 0.1875
- w_up: bfloat16 [2, 896, 4864], P(None, 'dp', 'ctx'), may hold values from -0.1875 to 0.1875
- w_down: bfloat16 [2, 4864, 896], P(None, 'ctx', 'dp'), may hold values from -0.125 to 0.125
Outputs:
- result: bfloat16 [16, 1024, 896], P('dp', 'ctx')
- input_grad: float32 [16, 1024, 896], P('dp', 'ctx')
- grad_gain_one: float32 [2, 896], P(None, ('dp', 'ctx'))
- grad_w_qkv: float32 [2, 896, 1152], P(None, ('dp', 'ctx'))
- grad_b_qkv: float32 [2, 1024], P(None, ('dp', 'ctx'))
- grad_b_value: float32 [2, 128], P(None, ('dp', 'ctx'))
- grad_w_out: float32 [2, 896, 896], P(None, ('dp', 'ctx'))
- grad_gain_two: float32 [2, 896], P(None, ('dp', 'ctx'))
- grad_w_gate: float32 [2, 896, 4864], P(None, 'dp', 'ctx')
- grad_w_up: float32 [2, 896, 4864], P(None, 'dp', 'ctx')
- grad_w_down: float32 [2, 4864, 896], P(None, 'ctx', 'dp')
The draws below stay inside these ranges and needn't reach their ends.
Inputs may be any that keep to these rules, and one draw needn't show every extreme that they name: Storage block j of every sequence (its tokens j * 64 to j * 64 + 63) holds the positions from span_order[j] * 64 on; span_order is a permutation.
All inputs are finite; a program needn't handle non-finite values.
Results may differ from the reference program's by a relative error of at most 0.04.
Values may be sent and summed in bfloat16 or wider, within the bound.
A program may use at most 192 MiB of HBM per device.

```python
import jax
import jax.numpy as jnp
from jax import lax

D = 896
H = 14
KVH = 2
HD = 64
FF = 4864
LAYERS = 2
LEN = 1024
SEQUENCES = 16
QKV = 1152
SPAN = 64
N_CTX = 8


def block_scale(key, shape, shards, smallest, largest):
    def one(position, blocks):
        heights = jax.random.uniform(jax.random.fold_in(jax.random.fold_in(key, 6), position), (blocks,), jnp.float32, smallest / len(shards), largest / len(shards))
        return jnp.repeat(jnp.exp(heights), shape[position] // blocks).reshape((-1,) + (1,) * (len(shape) - position - 1))

    level = one(*shards[0])
    for cut in shards[1:]:
        level = level * one(*cut)
    return level


def bell_draw(own_key, shape, spread, limit, pieces=(), kind=jnp.bfloat16):
    array = jax.random.normal(own_key, shape, jnp.float32) * spread
    if len(pieces) > 0:
        array = block_scale(own_key, shape, pieces, -0.22, 0.18) * array
    return jnp.clip(array, min=-limit, max=limit).astype(kind)


def setup_inputs(seed: int = 0) -> dict:
    arg_keys = jax.random.split(jax.random.key(seed), 12)
    tokens = bell_draw(arg_keys[0], (SEQUENCES, LEN, D), 1.0, 6.0, ((0, 16), (1, 8)))
    cotangent = bell_draw(arg_keys[1], (SEQUENCES, LEN, D), 1.0, 6.0, ((0, 16), (1, 8)))
    span_order = jax.random.permutation(arg_keys[2], 2 * N_CTX).astype(jnp.int32)
    gain_one = jnp.clip(1.0 + 0.1 * jax.random.normal(arg_keys[3], (LAYERS, D), jnp.float32), 0.5, 1.5).astype(jnp.bfloat16)
    w_qkv = bell_draw(arg_keys[4], (LAYERS, D, QKV), D ** -0.5, 0.1875, ((1, 128),))
    b_qkv = bell_draw(arg_keys[5], (LAYERS, QKV), 0.5, 3.0, ((1, 128),))
    w_out = bell_draw(arg_keys[6], (LAYERS, D, D), (D // 16) ** -0.5, 0.75, ((1, 128),))
    gain_two = jnp.clip(1.0 + 0.1 * jax.random.normal(arg_keys[7], (LAYERS, D), jnp.float32), 0.5, 1.5).astype(jnp.bfloat16)
    w_gate = bell_draw(arg_keys[8], (LAYERS, D, FF), D ** -0.5, 0.1875, ((1, 16), (2, 8)))
    w_up = bell_draw(arg_keys[9], (LAYERS, D, FF), D ** -0.5, 0.1875, ((1, 16), (2, 8)))
    w_down = bell_draw(arg_keys[10], (LAYERS, FF, D), (FF // 2) ** -0.5, 0.125, ((1, 8), (2, 16)))
    return dict(tokens=tokens, cotangent=cotangent, span_order=span_order, gain_one=gain_one, w_qkv=w_qkv, b_qkv=b_qkv, w_out=w_out, gain_two=gain_two, w_gate=w_gate, w_up=w_up, w_down=w_down)


@jax.custom_vjp
def low(v):
    return lax.optimization_barrier(v.astype(jnp.bfloat16)).astype(jnp.float32)

@jax.custom_vjp
def low_back(v):
    return v

def low_keep(v):
    return (low(v), None)

def low_pass(kept, grad):
    return (grad,)

def back_keep(v):
    return (v, None)

def back_low(kept, grad):
    return (low(grad),)
low.defvjp(low_keep, low_pass)
low_back.defvjp(back_keep, back_low)
eps_norm = 1e-06
rope_base = 1000000.0
neg_fill = -1e+30
top_precision = lax.Precision.HIGHEST

def norm_scale(inputs, gain_vec):
    return inputs * lax.rsqrt(lax.optimization_barrier(jnp.mean(inputs * inputs, axis=-1, keepdims=True)) + eps_norm) * gain_vec

def rotate(inputs, positions):
    half_dim = inputs.shape[-1] // 2
    frequency = rope_base ** (-jnp.arange(half_dim, dtype=jnp.float32) * 2.0 / inputs.shape[-1])
    angles = positions.astype(jnp.float32)[:, None] * frequency[None, :]
    cosine_table = jnp.cos(angles)[:, None, :]
    sine_table = jnp.sin(angles)[:, None, :]
    lower_half = inputs[..., :half_dim]
    upper_half = inputs[..., half_dim:]
    return jnp.concatenate([lower_half * cosine_table - upper_half * sine_table, upper_half * cosine_table + lower_half * sine_table], axis=-1)

def matmul(left_side, right_side):
    return jnp.dot(left_side, right_side, precision=top_precision)

def layer_forward(inputs, positions, gain_first, qkv_weight, qkv_bias, out_weight, gain_second, gate_weight, up_weight, down_weight):
    width = inputs.shape[-1]
    kv_width = KVH * HD
    groups = H // KVH
    hidden = low(norm_scale(inputs, gain_first))
    packed = low_back(matmul(hidden, qkv_weight) + qkv_bias)
    queries = packed[:, :width].reshape(-1, H, HD)
    keys_rot = packed[:, width:width + kv_width].reshape(-1, KVH, HD)
    values = low(packed[:, width + kv_width:].reshape(-1, KVH, HD))
    queries = low(rotate(queries, positions)).reshape(-1, KVH, groups, HD)
    keys_rot = low(rotate(keys_rot, positions))
    scores = low_back(jnp.einsum('skgd,tkd->kgst', queries, keys_rot, precision=top_precision) * HD ** (-0.5))
    allowed = positions[None, :] <= positions[:, None]
    scores = jnp.where(allowed[None, None], scores, neg_fill)
    soft_weights = low(jax.nn.softmax(scores, axis=-1))
    attended = jnp.einsum('kgst,tkd->skgd', soft_weights, values, precision=top_precision).reshape(-1, width)
    attended = low(low_back(attended))
    after_attn = inputs + low_back(matmul(attended, out_weight))
    hidden_two = low(norm_scale(after_attn, gain_second))
    gate_pre = low_back(matmul(hidden_two, gate_weight))
    up_pre = low_back(matmul(hidden_two, up_weight))
    activated = low(jax.nn.silu(gate_pre) * up_pre)
    return after_attn + low_back(matmul(activated, down_weight))

def reference(tokens, cotangent, span_order, gain_one, w_qkv, b_qkv, w_out, gain_two, w_gate, w_up, w_down):
    offsets = jnp.arange(SPAN, dtype=jnp.int32)
    positions = (span_order.astype(jnp.int32)[:, None] * SPAN + offsets[None, :]).reshape(LEN).astype(jnp.int32)
    params = tuple((weight_arg.astype(jnp.float32) for weight_arg in (gain_one, w_qkv, b_qkv, w_out, gain_two, w_gate, w_up, w_down)))

    def forward(inputs, *weights):
        state = inputs
        for layer_index in range(LAYERS):
            state = layer_forward(state, positions, *[weight_arg[layer_index] for weight_arg in weights])
        return state

    def per_sequence(totals, pair):
        inputs = pair[0].astype(jnp.float32)
        upstream = pair[1].astype(jnp.float32)
        output, pullback = jax.vjp(forward, inputs, *params)
        gradients = pullback(upstream)
        totals = tuple((running + fresh for running, fresh in zip(totals, gradients[1:])))
        return (totals, (output.astype(jnp.bfloat16), gradients[0]))
    zeros_init = tuple((jnp.zeros(weight_arg.shape, jnp.float32) for weight_arg in params))
    totals, (outputs, input_grads) = lax.scan(per_sequence, zeros_init, (tokens, cotangent))
    split_at = D + KVH * HD
    return (outputs, input_grads, totals[0], totals[1], totals[2][:, :split_at], totals[2][:, split_at:], totals[3], totals[4], totals[5], totals[6], totals[7])
```

```python
import functools

import jax
import jax.numpy as jnp
import numpy as np
from jax import lax
from jax.experimental import pallas as pl
from jax.experimental.pallas import tpu as pltpu
from jax.sharding import PartitionSpec as P

H = 14
KVH = 2
HD = 64
LAYERS = 2
D = 896
QKV = 1152
FS = 608
MESH = pl.DeviceIdType.MESH
BF = jnp.bfloat16
F32 = jnp.float32

eps_norm = 1e-06
rope_base = 1000000.0
neg_fill = -1e30


def place():
    dp = lax.axis_index("dp")
    ctx = lax.axis_index("ctx")
    return lax.div(dp, 4), lax.rem(dp, 4), lax.div(ctx, 2), lax.rem(ctx, 2)


def up1(v):
    return lax.rem(v + 1, 4)


def up2(v):
    return lax.rem(v + 2, 4)


def down1(v):
    return lax.rem(v + 3, 4)


def device(x, z, y, c):
    return (x * 4 + z, y * 2 + c)


def greet(peers):
    barrier = pltpu.get_barrier_semaphore()
    for peer in peers:
        pl.semaphore_signal(barrier, inc=1, device_id=peer, device_id_type=MESH)
    pl.semaphore_wait(barrier, len(peers))


class Mail:
    def __init__(self, send_sem, recv_sem):
        self.send_sem = send_sem
        self.recv_sem = recv_sem
        self.sent = []

    def send(self, slot, src, dst, target):
        copy = pltpu.make_async_remote_copy(
            src_ref=src,
            dst_ref=dst,
            send_sem=self.send_sem.at[slot],
            recv_sem=self.recv_sem.at[slot],
            device_id=target,
            device_id_type=MESH,
        )
        copy.start()
        self.sent.append(copy)

    def take(self, slot, dst, source):
        pltpu.make_async_remote_copy(
            src_ref=dst,
            dst_ref=dst,
            send_sem=self.send_sem.at[slot],
            recv_sem=self.recv_sem.at[slot],
            device_id=source,
            device_id_type=MESH,
        ).wait_recv()

    def finish(self):
        for copy in self.sent:
            copy.wait_send()


def weights_kernel(m_ref, a_ref, mf, af, send_sem, recv_sem, local_sem):
    x, z, y, c = place()
    ctx = 2 * y + c
    mail = Mail(send_sem, recv_sem)
    xp, xm, zp, zm, yp, ym = up1(x), down1(x), up1(z), down1(z), up1(y), down1(y)
    to_xp, to_xm = device(xp, z, y, c), device(xm, z, y, c)
    to_zp, to_zm = device(x, zp, y, c), device(x, zm, y, c)
    to_yp, to_ym = device(x, z, yp, c), device(x, z, ym, c)
    other = device(x, z, y, 1 - c)
    own_m = pltpu.make_async_copy(m_ref, mf.at[:, x, z], local_sem.at[0])
    own_a = pltpu.make_async_copy(a_ref, af.at[:, x, z, ctx], local_sem.at[1])
    own_a.start()
    own_m.start()
    greet([to_xp, to_xm, to_zp, to_zm, to_yp, to_ym, other])

    lo, hi = pl.ds(0, 3), pl.ds(3, 3)
    mail.send(0, a_ref, af.at[:, x, z, ctx], to_xp)
    mail.send(1, a_ref, af.at[:, x, z, ctx], to_xm)
    mail.send(2, m_ref.at[lo], mf.at[lo, x, z], to_xp)
    mail.send(3, m_ref.at[lo], mf.at[lo, x, z], to_xm)
    mail.send(4, m_ref.at[hi], mf.at[hi, x, z], to_zp)
    mail.send(5, m_ref.at[hi], mf.at[hi, x, z], to_zm)
    mail.take(0, af.at[:, xm, z, ctx], to_xm)
    mail.send(6, af.at[0, xm, z, ctx], af.at[0, xm, z, ctx], to_xp)
    mail.take(1, af.at[:, xp, z, ctx], to_xp)
    mail.send(7, af.at[1, xp, z, ctx], af.at[1, xp, z, ctx], to_xm)
    x2, z2, y2 = up2(x), up2(z), up2(y)
    mail.take(6, af.at[0, x2, z, ctx], to_xm)
    mail.take(7, af.at[1, x2, z, ctx], to_xp)
    own_a.wait()
    mail.send(8, af.at[:, :, z, ctx], af.at[:, :, z, ctx], to_zp)
    mail.send(9, af.at[:, :, z, ctx], af.at[:, :, z, ctx], to_zm)
    mail.take(2, mf.at[lo, xm, z], to_xm)
    mail.send(10, mf.at[pl.ds(0, 2), xm, z], mf.at[pl.ds(0, 2), xm, z], to_xp)
    mail.take(3, mf.at[lo, xp, z], to_xp)
    mail.send(11, mf.at[pl.ds(2, 1), xp, z], mf.at[pl.ds(2, 1), xp, z], to_xm)
    mail.take(4, mf.at[hi, x, zm], to_zm)
    mail.send(12, mf.at[pl.ds(3, 1), x, zm], mf.at[pl.ds(3, 1), x, zm], to_zp)
    mail.take(5, mf.at[hi, x, zp], to_zp)
    mail.send(13, mf.at[pl.ds(4, 2), x, zp], mf.at[pl.ds(4, 2), x, zp], to_zm)
    mail.take(8, af.at[:, :, zm, ctx], to_zm)
    mail.send(14, af.at[0, :, zm, ctx], af.at[0, :, zm, ctx], to_zp)
    mail.take(9, af.at[:, :, zp, ctx], to_zp)
    mail.send(15, af.at[1, :, zp, ctx], af.at[1, :, zp, ctx], to_zm)
    mail.take(10, mf.at[pl.ds(0, 2), x2, z], to_xm)
    mail.take(11, mf.at[pl.ds(2, 1), x2, z], to_xp)
    own_m.wait()
    mail.send(16, mf.at[lo, :, z], mf.at[lo, :, z], to_zp)
    mail.send(17, mf.at[lo, :, z], mf.at[lo, :, z], to_zm)
    mail.take(12, mf.at[pl.ds(3, 1), x, z2], to_zm)
    mail.take(13, mf.at[pl.ds(4, 2), x, z2], to_zp)
    mail.send(18, mf.at[hi, x], mf.at[hi, x], to_xp)
    mail.send(19, mf.at[hi, x], mf.at[hi, x], to_xm)
    mail.take(14, af.at[0, :, z2, ctx], to_zm)
    mail.take(15, af.at[1, :, z2, ctx], to_zp)

    def kept(part, row):
        return af.at[part, :, :, 2 * row + c]

    def theirs(part, row):
        return af.at[part, :, :, 2 * row + (1 - c)]

    both = slice(None)
    mail.send(20, kept(both, y), kept(both, y), to_yp)
    mail.send(21, kept(both, y), kept(both, y), to_ym)
    mail.send(22, kept(both, y), kept(both, y), other)
    mail.take(16, mf.at[lo, :, zm], to_zm)
    mail.send(23, mf.at[pl.ds(0, 1), :, zm], mf.at[pl.ds(0, 1), :, zm], to_zp)
    mail.take(17, mf.at[lo, :, zp], to_zp)
    mail.send(24, mf.at[pl.ds(1, 2), :, zp], mf.at[pl.ds(1, 2), :, zp], to_zm)
    mail.take(18, mf.at[hi, xm], to_xm)
    mail.send(25, mf.at[pl.ds(3, 2), xm], mf.at[pl.ds(3, 2), xm], to_xp)
    mail.take(19, mf.at[hi, xp], to_xp)
    mail.send(26, mf.at[pl.ds(5, 1), xp], mf.at[pl.ds(5, 1), xp], to_xm)
    mail.take(20, kept(both, ym), to_ym)
    mail.send(27, kept(0, ym), kept(0, ym), to_yp)
    mail.send(28, kept(both, ym), kept(both, ym), other)
    mail.take(21, kept(both, yp), to_yp)
    mail.send(29, kept(1, yp), kept(1, yp), to_ym)
    mail.send(30, kept(both, yp), kept(both, yp), other)
    mail.take(27, kept(0, y2), to_ym)
    mail.send(31, kept(0, y2), kept(0, y2), other)
    mail.take(29, kept(1, y2), to_yp)
    mail.send(32, kept(1, y2), kept(1, y2), other)
    mail.take(23, mf.at[pl.ds(0, 1), :, z2], to_zm)
    mail.take(24, mf.at[pl.ds(1, 2), :, z2], to_zp)
    mail.take(25, mf.at[pl.ds(3, 2), x2], to_xm)
    mail.take(26, mf.at[pl.ds(5, 1), x2], to_xp)
    mail.take(22, theirs(both, y), other)
    mail.take(28, theirs(both, ym), other)
    mail.take(30, theirs(both, yp), other)
    mail.take(31, theirs(0, y2), other)
    mail.take(32, theirs(1, y2), other)
    mail.finish()


def gather_weights(m_block, a_block):
    return pl.pallas_call(
        weights_kernel,
        out_shape=(
            jax.ShapeDtypeStruct((6, 4, 4, 56, FS), BF),
            jax.ShapeDtypeStruct((2, 4, 4, 8, 16, 1024), BF),
        ),
        in_specs=[pl.BlockSpec(memory_space=pl.ANY)] * 2,
        out_specs=[pl.BlockSpec(memory_space=pl.ANY)] * 2,
        scratch_shapes=[
            pltpu.SemaphoreType.DMA((33,)),
            pltpu.SemaphoreType.DMA((33,)),
            pltpu.SemaphoreType.DMA((2,)),
        ],
        compiler_params=pltpu.CompilerParams(collective_id=1, has_side_effects=True),
        name="gather_weights",
    )(m_block, a_block)


def ctx_gather_kernel(rows, v_ref, o_ref, send_sem, recv_sem, local_sem):
    x, z, y, c = place()
    mail = Mail(send_sem, recv_sem)
    yp, ym, y2 = up1(y), down1(y), up2(y)
    to_yp, to_ym, other = device(x, z, yp, c), device(x, z, ym, c), device(x, z, y, 1 - c)
    own = pltpu.make_async_copy(v_ref, o_ref.at[y, c], local_sem.at[0])
    own.start()
    greet([to_yp, to_ym, other])
    half = rows // 2
    first, second = pl.ds(0, half), pl.ds(half, half)
    mail.send(0, v_ref, o_ref.at[y, c], to_yp)
    mail.send(1, v_ref, o_ref.at[y, c], to_ym)
    mail.send(2, v_ref, o_ref.at[y, c], other)
    mail.take(0, o_ref.at[ym, c], to_ym)
    mail.send(3, o_ref.at[ym, c, first], o_ref.at[ym, c, first], to_yp)
    mail.send(4, o_ref.at[ym, c], o_ref.at[ym, c], other)
    mail.take(1, o_ref.at[yp, c], to_yp)
    mail.send(5, o_ref.at[yp, c, second], o_ref.at[yp, c, second], to_ym)
    mail.send(6, o_ref.at[yp, c], o_ref.at[yp, c], other)
    mail.take(3, o_ref.at[y2, c, first], to_ym)
    mail.send(7, o_ref.at[y2, c, first], o_ref.at[y2, c, first], other)
    mail.take(5, o_ref.at[y2, c, second], to_yp)
    mail.send(8, o_ref.at[y2, c, second], o_ref.at[y2, c, second], other)
    own.wait()
    mail.take(2, o_ref.at[y, 1 - c], other)
    mail.take(4, o_ref.at[ym, 1 - c], other)
    mail.take(6, o_ref.at[yp, 1 - c], other)
    mail.take(7, o_ref.at[y2, 1 - c, first], other)
    mail.take(8, o_ref.at[y2, 1 - c, second], other)
    mail.finish()


def ctx_gather(value, collective_id):
    rows, columns = value.shape
    gathered = pl.pallas_call(
        functools.partial(ctx_gather_kernel, rows),
        out_shape=jax.ShapeDtypeStruct((4, 2, rows, columns), value.dtype),
        in_specs=[pl.BlockSpec(memory_space=pl.ANY)],
        out_specs=pl.BlockSpec(memory_space=pl.ANY),
        scratch_shapes=[
            pltpu.SemaphoreType.DMA((9,)),
            pltpu.SemaphoreType.DMA((9,)),
            pltpu.SemaphoreType.DMA((1,)),
        ],
        compiler_params=pltpu.CompilerParams(collective_id=collective_id, has_side_effects=True),
        name="ctx_gather_%d" % columns,
    )(value)
    return gathered.reshape(8 * rows, columns)


def ctx_scatter_kernel(rows, p_ref, o_ref, near, own, far_a, far_b, got_a, got_b, send_sem, recv_sem):
    x, z, y, c = place()
    mail = Mail(send_sem, recv_sem)
    yp, ym, y2 = up1(y), down1(y), up2(y)
    to_yp, to_ym, other = device(x, z, yp, c), device(x, z, ym, c), device(x, z, y, 1 - c)
    greet([to_yp, to_ym, other])
    half = rows // 2
    first, second = pl.ds(0, half), pl.ds(half, half)
    order = (y2, yp, ym, y)
    for slot, row in enumerate(order):
        mail.send(slot, p_ref.at[row, 1 - c], near.at[slot], other)
    mail.take(0, near.at[0], other)
    own[0] = (p_ref[y2, c].astype(F32) + near[0].astype(F32)).astype(BF)
    mail.send(4, own.at[0, first], far_a, to_yp)
    mail.send(5, own.at[0, second], far_b, to_ym)
    mail.take(1, near.at[1], other)
    mail.take(2, near.at[2], other)
    mail.take(4, far_a, to_ym)
    own[1, second] = (p_ref[yp, c, second].astype(F32) + near[1, second].astype(F32)).astype(BF)
    own[1, first] = (
        p_ref[yp, c, first].astype(F32) + near[1, first].astype(F32) + far_a[...].astype(F32)
    ).astype(BF)
    mail.send(6, own.at[1], got_a, to_yp)
    mail.take(5, far_b, to_yp)
    own[2, first] = (p_ref[ym, c, first].astype(F32) + near[2, first].astype(F32)).astype(BF)
    own[2, second] = (
        p_ref[ym, c, second].astype(F32) + near[2, second].astype(F32) + far_b[...].astype(F32)
    ).astype(BF)
    mail.send(7, own.at[2], got_b, to_ym)
    mail.take(3, near.at[3], other)
    o_ref[...] = p_ref[y, c].astype(F32) + near[3].astype(F32)
    mail.take(6, got_a, to_ym)
    mail.take(7, got_b, to_yp)
    o_ref[...] += got_a[...].astype(F32) + got_b[...].astype(F32)
    mail.finish()


def ctx_scatter(value, collective_id):
    rows, columns = value.shape[0] // 8, value.shape[1]
    return pl.pallas_call(
        functools.partial(ctx_scatter_kernel, rows),
        out_shape=jax.ShapeDtypeStruct((rows, columns), F32),
        in_specs=[pl.BlockSpec(memory_space=pltpu.VMEM)],
        out_specs=pl.BlockSpec(memory_space=pltpu.VMEM),
        scratch_shapes=[
            pltpu.VMEM((4, rows, columns), BF),
            pltpu.VMEM((3, rows, columns), BF),
            pltpu.VMEM((rows // 2, columns), BF),
            pltpu.VMEM((rows // 2, columns), BF),
            pltpu.VMEM((rows, columns), BF),
            pltpu.VMEM((rows, columns), BF),
            pltpu.SemaphoreType.DMA((8,)),
            pltpu.SemaphoreType.DMA((8,)),
        ],
        compiler_params=pltpu.CompilerParams(
            collective_id=collective_id, has_side_effects=True, vmem_limit_bytes=32 * 1024 * 1024
        ),
        name="ctx_scatter_%d" % columns,
    )(value.reshape(4, 2, rows, columns))


def grads_kernel(m_ref, a_ref, mo, ao, m_got, near, far_a, far_b, got_a, got_b, total, a_got, send_sem, recv_sem):
    x, z, y, c = place()
    ctx = 2 * y + c
    mail = Mail(send_sem, recv_sem)
    yp, ym, y2 = up1(y), down1(y), up2(y)
    to_yp, to_ym, other = device(x, z, yp, c), device(x, z, ym, c), device(x, z, y, 1 - c)
    shifts = [(i, j) for i in range(4) for j in range(4) if (i, j) != (0, 0)]

    def ahead(i, j):
        return lax.rem(x + i, 4), lax.rem(z + j, 4)

    def behind(i, j):
        return lax.rem(x + 4 - i, 4), lax.rem(z + 4 - j, 4)

    plane = [device(*ahead(i, j), y, c) for i, j in shifts]
    greet([to_yp, to_ym, other] + plane)
    for slot, row in enumerate((y2, yp, ym, y)):
        mail.send(slot, a_ref.at[:, :, 2 * row + (1 - c)], near.at[slot], other)
    for k, (i, j) in enumerate(shifts):
        tx, tz = ahead(i, j)
        mail.send(8 + k, m_ref.at[:, tx, tz], m_got.at[k], plane[k])

    def add_near(slot, row, part=None):
        def body(i, carry):
            near[slot, i] = (
                near[slot, i].astype(F32) + a_ref[i, :, 2 * row + c].astype(F32)
            ).astype(BF)
            return carry

        lax.fori_loop(0, 4, body, 0)

    first, second = pl.ds(0, 2), pl.ds(2, 2)
    mail.take(0, near.at[0], other)
    add_near(0, y2)
    mail.send(4, near.at[0, first], far_a, to_yp)
    mail.send(5, near.at[0, second], far_b, to_ym)
    mail.take(1, near.at[1], other)
    add_near(1, yp)
    mail.take(2, near.at[2], other)
    add_near(2, ym)
    mail.take(4, far_a, to_ym)
    near[1, first] = (near[1, first].astype(F32) + far_a[...].astype(F32)).astype(BF)
    mail.send(6, near.at[1], got_a, to_yp)
    mail.take(5, far_b, to_yp)
    near[2, second] = (near[2, second].astype(F32) + far_b[...].astype(F32)).astype(BF)
    mail.send(7, near.at[2], got_b, to_ym)
    mail.take(3, near.at[3], other)
    add_near(3, y)
    mail.take(6, got_a, to_ym)
    mail.take(7, got_b, to_yp)
    total[...] = (near[3].astype(F32) + got_a[...].astype(F32) + got_b[...].astype(F32)).astype(BF)
    for k, (i, j) in enumerate(shifts):
        tx, tz = ahead(i, j)
        mail.send(23 + k, total.at[tx, tz], a_got.at[k], plane[k])
    mo[...] = m_ref[:, x, z].astype(F32)
    for k, (i, j) in enumerate(shifts):
        sx, sz = behind(i, j)
        mail.take(8 + k, m_got.at[k], device(sx, sz, y, c))
        mo[...] += m_got[k].astype(F32)
    ao[...] = total[x, z].astype(F32)
    for k, (i, j) in enumerate(shifts):
        sx, sz = behind(i, j)
        mail.take(23 + k, a_got.at[k], device(sx, sz, y, c))
        ao[...] += a_got[k].astype(F32)
    mail.finish()


def scatter_grads(m_grads, a_grads):
    return pl.pallas_call(
        grads_kernel,
        out_shape=(
            jax.ShapeDtypeStruct((3, 56, FS), F32),
            jax.ShapeDtypeStruct((16, 1024), F32),
        ),
        in_specs=[pl.BlockSpec(memory_space=pltpu.VMEM)] * 2,
        out_specs=[pl.BlockSpec(memory_space=pltpu.VMEM)] * 2,
        scratch_shapes=[
            pltpu.VMEM((15, 3, 56, FS), BF),
            pltpu.VMEM((4, 4, 4, 16, 1024), BF),
            pltpu.VMEM((2, 4, 16, 1024), BF),
            pltpu.VMEM((2, 4, 16, 1024), BF),
            pltpu.VMEM((4, 4, 16, 1024), BF),
            pltpu.VMEM((4, 4, 16, 1024), BF),
            pltpu.VMEM((4, 4, 16, 1024), BF),
            pltpu.VMEM((15, 16, 1024), BF),
            pltpu.SemaphoreType.DMA((38,)),
            pltpu.SemaphoreType.DMA((38,)),
        ],
        compiler_params=pltpu.CompilerParams(
            collective_id=2, has_side_effects=True, vmem_limit_bytes=48 * 1024 * 1024
        ),
        name="scatter_grads",
    )(m_grads, a_grads)


def select_matrix():
    pick = np.zeros((226, 256), np.float32)
    for k in range(16):
        for r in range(7):
            pick[7 * k + r, 16 * k + r] = 1
            pick[112 + 7 * k + r, 16 * k + 8 + r] = 1
        pick[224, 16 * k + 7] = 1
        pick[225, 16 * k + 15] = 1
    return pick


def pack_attention(gain_one, w_qkv, b_qkv, w_out, gain_two):
    index = lax.axis_index("dp") * 8 + lax.axis_index("ctx")
    within = lax.rem(index, 16)
    zeros = jnp.zeros((LAYERS, D), BF)
    one = lax.dynamic_update_slice(zeros, gain_one, (0, 7 * index))
    two = lax.dynamic_update_slice(zeros, gain_two, (0, 7 * index))
    bias = lax.dynamic_update_slice(jnp.zeros((LAYERS, 256), BF), b_qkv, (0, 9 * within))
    row_seven = jnp.concatenate([one, bias[:, :128]], axis=1)[:, None]
    row_last = jnp.concatenate([two, bias[:, 128:]], axis=1)[:, None]
    joined = jnp.concatenate([w_qkv, w_out], axis=2)
    return jnp.concatenate([joined[:, :, :1024], row_seven, joined[:, :, 1024:], row_last], axis=1)


def unpack_attention(block, pick):
    groups = block.reshape(8, 256, 1024)
    out = jnp.einsum("ab,gbc->gac", pick, groups, preferred_element_type=F32).astype(BF)
    low = out[:, :112].reshape(D, 1024)
    high = out[:, 112:224].reshape(D, 1024)
    spare = out[:, 224:]
    gain_one = jnp.sum(spare[:, 0, :D].astype(F32), axis=0)
    gain_two = jnp.sum(spare[:, 1, :D].astype(F32), axis=0)
    bias = jnp.concatenate([spare[:, 0, D:], spare[:, 1, D : D + 16]], axis=1).reshape(QKV)
    qkv = jnp.concatenate([low, high[:, :128]], axis=1)
    return gain_one, qkv, bias, high[:, 128:], gain_two


def pack_attention_grads(gain_one, qkv, qk_bias, value_bias, out, gain_two, pick):
    low = qkv[:, :1024].astype(BF).reshape(8, 112, 1024)
    high = jnp.concatenate([qkv[:, 1024:], out], axis=1).astype(BF).reshape(8, 112, 1024)
    row_seven = jnp.concatenate(
        [jnp.broadcast_to(gain_one[None], (8, D)), qk_bias.reshape(8, 128)], axis=1
    )
    row_last = jnp.concatenate(
        [
            jnp.broadcast_to(gain_two[None], (8, D)),
            value_bias.reshape(8, 16),
            jnp.zeros((8, 112), F32),
        ],
        axis=1,
    )
    rows = jnp.concatenate(
        [low, high, row_seven.astype(BF)[:, None], row_last.astype(BF)[:, None]], axis=1
    )
    block = jnp.einsum("ab,gac->gbc", pick, rows, preferred_element_type=F32).astype(BF)
    return block.reshape(4, 4, 8, 16, 1024)


def unpack_attention_grads(block):
    index = lax.axis_index("dp") * 8 + lax.axis_index("ctx")
    within = lax.rem(index, 16)
    qkv = jnp.concatenate([block[:7], block[8:15, :128]], axis=1)
    out = block[8:15, 128:]
    gain_one = lax.dynamic_slice(block[7], (7 * index,), (7,))
    gain_two = lax.dynamic_slice(block[15], (7 * index,), (7,))
    qk_bias = lax.dynamic_slice(block[7], (D + 8 * within,), (8,))
    value_bias = lax.dynamic_slice(block[15], (D + within,), (1,))
    return gain_one, qkv, qk_bias, value_bias, out, gain_two


def norm_scale(inputs, gain_vec):
    return (
        inputs * lax.rsqrt(jnp.mean(inputs * inputs, axis=-1, keepdims=True) + eps_norm) * gain_vec
    )


def rotate(inputs, tables):
    cosine_table, sine_table = tables
    half_dim = inputs.shape[-1] // 2
    lower_half = inputs[..., :half_dim]
    upper_half = inputs[..., half_dim:]
    return jnp.concatenate(
        [
            lower_half * cosine_table - upper_half * sine_table,
            upper_half * cosine_table + lower_half * sine_table,
        ],
        axis=-1,
    )


def rotate_back(inputs, tables):
    return rotate(inputs, (tables[0], -tables[1]))


def swiglu(gate_pre, up_pre):
    return jax.nn.silu(gate_pre) * up_pre


def inner_rows(left_side, right_side):
    return lax.dot_general(
        left_side, right_side, (((0,), (0,)), ((), ())), preferred_element_type=F32
    )


def times_transposed(left_side, right_side):
    return lax.dot_general(
        left_side, right_side, (((1,), (1,)), ((), ())), preferred_element_type=F32
    )


def masked_scores(queries, keys_all, allowed):
    scores = jnp.einsum(
        "skgd,tkd->kgst", queries, keys_all, preferred_element_type=F32
    ) * queries.shape[-1] ** (-0.5)
    return jnp.where(allowed[None, None], scores, neg_fill)


def attend(queries, keys_all, values_all, allowed):
    scores = masked_scores(queries, keys_all, allowed)
    highest = jnp.max(scores, axis=-1, keepdims=True)
    log_total = highest + jnp.log(jnp.sum(jnp.exp(scores - highest), axis=-1, keepdims=True))
    soft_weights = jnp.exp(scores - log_total).astype(BF)
    output = jnp.einsum("kgst,tkd->skgd", soft_weights, values_all, preferred_element_type=F32)
    return (output, log_total)


def attend_back(queries, keys_all, values_all, log_total, grad_out, allowed):
    scale = queries.shape[-1] ** (-0.5)
    soft_weights = jnp.exp(masked_scores(queries, keys_all, allowed) - log_total)
    grad_soft = jnp.einsum("skgd,tkd->kgst", grad_out, values_all, preferred_element_type=F32)
    grad_values = jnp.einsum(
        "kgst,skgd->tkd", soft_weights.astype(BF), grad_out, preferred_element_type=F32
    )
    grad_scores = soft_weights * (
        grad_soft - jnp.sum(grad_soft * soft_weights, axis=-1, keepdims=True)
    )
    grad_scores = grad_scores.astype(BF)
    grad_queries = (
        jnp.einsum("kgst,tkd->skgd", grad_scores, keys_all, preferred_element_type=F32) * scale
    )
    grad_keys = (
        jnp.einsum("kgst,skgd->tkd", grad_scores, queries, preferred_element_type=F32) * scale
    )
    return (grad_queries, grad_keys, grad_values)


def layer_forward(inputs, weights, tables, allowed):
    gain_first, qkv_weight, qkv_bias, out_weight, gain_second, gate_weight, up_weight, down_weight = weights
    kv_width = KVH * HD
    groups = H // KVH
    tokens_here = inputs.shape[0]
    hidden = norm_scale(inputs, gain_first).astype(BF)
    packed = jnp.dot(hidden, qkv_weight, preferred_element_type=F32) + qkv_bias.astype(F32)
    queries = rotate(packed[:, :D].reshape(tokens_here, H, HD), tables).astype(BF)
    keys_here = rotate(packed[:, D : D + kv_width].reshape(tokens_here, KVH, HD), tables).astype(BF)
    values_here = packed[:, D + kv_width :].astype(BF)
    both = ctx_gather(
        jnp.concatenate([keys_here.reshape(tokens_here, kv_width), values_here], axis=1), 3
    )
    whole_len = both.shape[0]
    keys_all = both[:, :kv_width].reshape(whole_len, KVH, HD)
    values_all = both[:, kv_width:].reshape(whole_len, KVH, HD)
    queries_seq = queries.reshape(tokens_here, KVH, groups, HD)
    attended, log_total = attend(queries_seq, keys_all, values_all, allowed)
    attended = attended.reshape(tokens_here, D).astype(BF)
    after_attn = inputs + jnp.dot(attended, out_weight, preferred_element_type=F32)
    hidden_two = norm_scale(after_attn, gain_second).astype(BF)
    hidden_rows = ctx_gather(hidden_two, 4)
    gate_pre = jnp.dot(hidden_rows, gate_weight, preferred_element_type=F32)
    up_pre = jnp.dot(hidden_rows, up_weight, preferred_element_type=F32)
    activated = swiglu(gate_pre, up_pre).astype(BF)
    partial_out = times_transposed(activated, down_weight).astype(BF)
    output = after_attn + ctx_scatter(partial_out, 5)
    kept = (
        inputs,
        hidden,
        queries_seq,
        keys_all,
        values_all,
        log_total,
        attended,
        after_attn,
        hidden_rows,
        gate_pre,
        up_pre,
        activated,
    )
    return (output, kept)


def layer_backward(grad_output, kept, weights, tables, allowed, pick):
    gain_first, qkv_weight, qkv_bias, out_weight, gain_second, gate_weight, up_weight, down_weight = weights
    (
        inputs,
        hidden,
        queries_seq,
        keys_all,
        values_all,
        log_total,
        attended,
        after_attn,
        hidden_rows,
        gate_pre,
        up_pre,
        activated,
    ) = kept
    tokens_here = inputs.shape[0]
    kv_width = KVH * HD
    down_in = ctx_gather(grad_output.astype(BF), 4)
    grad_down = inner_rows(down_in, activated)
    grad_act = jnp.dot(down_in, down_weight, preferred_element_type=F32)
    unused_out, swiglu_back = jax.vjp(swiglu, gate_pre, up_pre)
    grad_gate, grad_up = swiglu_back(grad_act)
    grad_gate = grad_gate.astype(BF)
    grad_up = grad_up.astype(BF)
    grad_gate_w = inner_rows(hidden_rows, grad_gate)
    grad_up_w = inner_rows(hidden_rows, grad_up)
    partial_hidden = times_transposed(grad_gate, gate_weight) + times_transposed(grad_up, up_weight)
    grad_hidden_two = ctx_scatter(partial_hidden.astype(BF), 5)
    unused_out, norm_back_second = jax.vjp(norm_scale, after_attn, gain_second)
    grad_mid, grad_gain_second = norm_back_second(grad_hidden_two)
    grad_mid = grad_mid + grad_output
    attn_in = grad_mid.astype(BF)
    grad_out_w = inner_rows(attended, attn_in)
    grad_attended = times_transposed(attn_in, out_weight).astype(BF).reshape(queries_seq.shape)
    grad_queries, grad_keys, grad_values = attend_back(
        queries_seq, keys_all, values_all, log_total, grad_attended, allowed
    )
    whole_len = keys_all.shape[0]
    both = ctx_scatter(
        jnp.concatenate(
            [grad_keys.reshape(whole_len, kv_width), grad_values.reshape(whole_len, kv_width)],
            axis=1,
        ).astype(BF),
        6,
    )
    grad_keys = both[:, :kv_width]
    grad_values = both[:, kv_width:]
    grad_query_flat = rotate_back(grad_queries.reshape(tokens_here, H, HD), tables).reshape(
        tokens_here, D
    )
    grad_key_flat = rotate_back(grad_keys.reshape(tokens_here, KVH, HD), tables).reshape(
        tokens_here, kv_width
    )
    grad_packed = jnp.concatenate([grad_query_flat, grad_key_flat, grad_values], axis=1).astype(BF)
    grad_qkv_w = inner_rows(hidden, grad_packed)
    grad_qkv_b = jnp.sum(grad_packed.astype(F32), axis=0)
    grad_hidden = times_transposed(grad_packed, qkv_weight)
    unused_out, norm_back_first = jax.vjp(norm_scale, inputs, gain_first)
    grad_input, grad_gain_first = norm_back_first(grad_hidden)
    grad_input = grad_input + grad_mid
    a_grads = pack_attention_grads(
        grad_gain_first,
        grad_qkv_w,
        grad_qkv_b[: D + kv_width],
        grad_qkv_b[D + kv_width :],
        grad_out_w,
        grad_gain_second,
        pick,
    )
    m_grads = jnp.stack([grad_gate_w, grad_up_w, grad_down]).astype(BF).reshape(3, 4, 4, 56, FS)
    m_sum, a_sum = scatter_grads(m_grads, a_grads)
    sums = unpack_attention_grads(a_sum) + (m_sum[0], m_sum[1], m_sum[2].T)
    return (grad_input, sums)


def shards(
    tokens, cotangent, span_order, gain_one, w_qkv, b_qkv, w_out, gain_two, w_gate, w_up, w_down
):
    sequences, local_len, width = tokens.shape
    span_len = local_len // 2
    ctx_place = lax.axis_index("ctx")
    offsets = jnp.arange(span_len, dtype=jnp.int32)
    local_spans = lax.dynamic_slice_in_dim(span_order, 2 * ctx_place, 2)
    local_pos = (local_spans[:, None] * span_len + offsets[None, :]).reshape(local_len)
    all_pos = (span_order[:, None] * span_len + offsets[None, :]).reshape(-1)
    allowed = all_pos[None, :] <= local_pos[:, None]
    frequency = rope_base ** (-jnp.arange(HD // 2, dtype=F32) * 2.0 / HD)
    angles = local_pos.astype(F32)[:, None] * frequency[None, :]
    tables = (jnp.cos(angles)[:, None, :], jnp.sin(angles)[:, None, :])
    pick = jnp.asarray(select_matrix(), BF)

    m_block = jnp.stack([w_gate, w_up, w_down.transpose(0, 2, 1)], axis=1).reshape(6, 56, FS)
    a_block = pack_attention(gain_one, w_qkv, b_qkv, w_out, gain_two)
    m_full, a_full = gather_weights(m_block, a_block)
    m_full = m_full.reshape(2, 3, D, FS)
    weights = [
        unpack_attention(a_full[l], pick) + (m_full[l, 0], m_full[l, 1], m_full[l, 2])
        for l in range(LAYERS)
    ]
    state = tokens.reshape(local_len, width).astype(F32)
    kept_layers = []
    for l in range(LAYERS):
        state, kept = layer_forward(state, weights[l], tables, allowed)
        kept_layers.append(kept)
    grad_state = cotangent.reshape(local_len, width).astype(F32)
    grad_layers = []
    for l in reversed(range(LAYERS)):
        grad_state, sums = layer_backward(
            grad_state, kept_layers[l], weights[l], tables, allowed, pick
        )
        grad_layers.insert(0, sums)
    stacks = [jnp.stack([sums[member] for sums in grad_layers]) for member in range(9)]
    output = state.astype(BF).reshape(sequences, local_len, width)
    input_grad = grad_state.reshape(sequences, local_len, width)
    return (output, input_grad) + tuple(stacks)


def solution(mesh):
    return jax.shard_map(
        shards,
        mesh=mesh,
        in_specs=(
            P("dp", "ctx", None),
            P("dp", "ctx", None),
            P(),
            P(None, ("dp", "ctx")),
            P(None, ("dp", "ctx"), None),
            P(None, ("dp", "ctx")),
            P(None, ("dp", "ctx"), None),
            P(None, ("dp", "ctx")),
            P(None, "dp", "ctx"),
            P(None, "dp", "ctx"),
            P(None, "ctx", "dp"),
        ),
        out_specs=(
            P("dp", "ctx", None),
            P("dp", "ctx", None),
            P(None, ("dp", "ctx")),
            P(None, ("dp", "ctx"), None),
            P(None, ("dp", "ctx")),
            P(None, ("dp", "ctx")),
            P(None, ("dp", "ctx"), None),
            P(None, ("dp", "ctx")),
            P(None, "dp", "ctx"),
            P(None, "dp", "ctx"),
            P(None, "ctx", "dp"),
        ),
        check_vma=False,
    )
```

```python
import functools

import jax
import jax.numpy as jnp
import numpy as np
from jax import lax
from jax.experimental import pallas as pl
from jax.experimental.pallas import tpu as pltpu
from jax.sharding import PartitionSpec as P

H = 14
KVH = 2
HD = 64
LAYERS = 2
D = 896
QKV = 1152
FS = 608
MESH = pl.DeviceIdType.MESH
BF = jnp.bfloat16
F32 = jnp.float32

eps_norm = 1e-06
rope_base = 1000000.0
neg_fill = -1e30


def place():
    dp = lax.axis_index("dp")
    ctx = lax.axis_index("ctx")
    return lax.div(dp, 4), lax.rem(dp, 4), lax.div(ctx, 2), lax.rem(ctx, 2)


def up1(v):
    return lax.rem(v + 1, 4)


def up2(v):
    return lax.rem(v + 2, 4)


def down1(v):
    return lax.rem(v + 3, 4)


def device(x, z, y, c):
    return (x * 4 + z, y * 2 + c)


def greet(peers):
    barrier = pltpu.get_barrier_semaphore()
    for peer in peers:
        pl.semaphore_signal(barrier, inc=1, device_id=peer, device_id_type=MESH)
    pl.semaphore_wait(barrier, len(peers))


class Mail:
    def __init__(self, send_sem, recv_sem):
        self.send_sem = send_sem
        self.recv_sem = recv_sem
        self.sent = []

    def send(self, slot, src, dst, target):
        copy = pltpu.make_async_remote_copy(
            src_ref=src,
            dst_ref=dst,
            send_sem=self.send_sem.at[slot],
            recv_sem=self.recv_sem.at[slot],
            device_id=target,
            device_id_type=MESH,
        )
        copy.start()
        self.sent.append(copy)

    def take(self, slot, dst, source):
        pltpu.make_async_remote_copy(
            src_ref=dst,
            dst_ref=dst,
            send_sem=self.send_sem.at[slot],
            recv_sem=self.recv_sem.at[slot],
            device_id=source,
            device_id_type=MESH,
        ).wait_recv()

    def finish(self):
        for copy in self.sent:
            copy.wait_send()


def weights_kernel(m_ref, a_ref, mf, af, send_sem, recv_sem, local_sem):
    x, z, y, c = place()
    ctx = 2 * y + c
    mail = Mail(send_sem, recv_sem)
    xp, xm, zp, zm, yp, ym = up1(x), down1(x), up1(z), down1(z), up1(y), down1(y)
    to_xp, to_xm = device(xp, z, y, c), device(xm, z, y, c)
    to_zp, to_zm = device(x, zp, y, c), device(x, zm, y, c)
    to_yp, to_ym = device(x, z, yp, c), device(x, z, ym, c)
    other = device(x, z, y, 1 - c)
    own_m = pltpu.make_async_copy(m_ref, mf.at[:, x, z], local_sem.at[0])
    own_a = pltpu.make_async_copy(a_ref, af.at[:, x, z, ctx], local_sem.at[1])
    own_a.start()
    own_m.start()
    greet([to_xp, to_xm, to_zp, to_zm, to_yp, to_ym, other])

    lo, hi = pl.ds(0, 3), pl.ds(3, 3)
    mail.send(0, a_ref, af.at[:, x, z, ctx], to_xp)
    mail.send(1, a_ref, af.at[:, x, z, ctx], to_xm)
    mail.send(2, m_ref.at[lo], mf.at[lo, x, z], to_xp)
    mail.send(3, m_ref.at[lo], mf.at[lo, x, z], to_xm)
    mail.send(4, m_ref.at[hi], mf.at[hi, x, z], to_zp)
    mail.send(5, m_ref.at[hi], mf.at[hi, x, z], to_zm)
    mail.take(0, af.at[:, xm, z, ctx], to_xm)
    mail.send(6, af.at[0, xm, z, ctx], af.at[0, xm, z, ctx], to_xp)
    mail.take(1, af.at[:, xp, z, ctx], to_xp)
    mail.send(7, af.at[1, xp, z, ctx], af.at[1, xp, z, ctx], to_xm)
    x2, z2, y2 = up2(x), up2(z), up2(y)
    mail.take(6, af.at[0, x2, z, ctx], to_xm)
    mail.take(7, af.at[1, x2, z, ctx], to_xp)
    own_a.wait()
    mail.send(8, af.at[:, :, z, ctx], af.at[:, :, z, ctx], to_zp)
    mail.send(9, af.at[:, :, z, ctx], af.at[:, :, z, ctx], to_zm)
    mail.take(2, mf.at[lo, xm, z], to_xm)
    mail.send(10, mf.at[pl.ds(0, 2), xm, z], mf.at[pl.ds(0, 2), xm, z], to_xp)
    mail.take(3, mf.at[lo, xp, z], to_xp)
    mail.send(11, mf.at[pl.ds(2, 1), xp, z], mf.at[pl.ds(2, 1), xp, z], to_xm)
    mail.take(4, mf.at[hi, x, zm], to_zm)
    mail.send(12, mf.at[pl.ds(3, 1), x, zm], mf.at[pl.ds(3, 1), x, zm], to_zp)
    mail.take(5, mf.at[hi, x, zp], to_zp)
    mail.send(13, mf.at[pl.ds(4, 2), x, zp], mf.at[pl.ds(4, 2), x, zp], to_zm)
    mail.take(8, af.at[:, :, zm, ctx], to_zm)
    mail.send(14, af.at[0, :, zm, ctx], af.at[0, :, zm, ctx], to_zp)
    mail.take(9, af.at[:, :, zp, ctx], to_zp)
    mail.send(15, af.at[1, :, zp, ctx], af.at[1, :, zp, ctx], to_zm)
    mail.take(10, mf.at[pl.ds(0, 2), x2, z], to_xm)
    mail.take(11, mf.at[pl.ds(2, 1), x2, z], to_xp)
    own_m.wait()
    mail.send(16, mf.at[lo, :, z], mf.at[lo, :, z], to_zp)
    mail.send(17, mf.at[lo, :, z], mf.at[lo, :, z], to_zm)
    mail.take(12, mf.at[pl.ds(3, 1), x, z2], to_zm)
    mail.take(13, mf.at[pl.ds(4, 2), x, z2], to_zp)
    mail.send(18, mf.at[hi, x], mf.at[hi, x], to_xp)
    mail.send(19, mf.at[hi, x], mf.at[hi, x], to_xm)
    mail.take(14, af.at[0, :, z2, ctx], to_zm)
    mail.take(15, af.at[1, :, z2, ctx], to_zp)

    def kept(part, row):
        return af.at[part, :, :, 2 * row + c]

    def theirs(part, row):
        return af.at[part, :, :, 2 * row + (1 - c)]

    both = slice(None)
    mail.send(20, kept(both, y), kept(both, y), to_yp)
    mail.send(21, kept(both, y), kept(both, y), to_ym)
    mail.send(22, kept(both, y), kept(both, y), other)
    mail.take(16, mf.at[lo, :, zm], to_zm)
    mail.send(23, mf.at[pl.ds(0, 1), :, zm], mf.at[pl.ds(0, 1), :, zm], to_zp)
    mail.take(17, mf.at[lo, :, zp], to_zp)
    mail.send(24, mf.at[pl.ds(1, 2), :, zp], mf.at[pl.ds(1, 2), :, zp], to_zm)
    mail.take(18, mf.at[hi, xm], to_xm)
    mail.send(25, mf.at[pl.ds(3, 2), xm], mf.at[pl.ds(3, 2), xm], to_xp)
    mail.take(19, mf.at[hi, xp], to_xp)
    mail.send(26, mf.at[pl.ds(5, 1), xp], mf.at[pl.ds(5, 1), xp], to_xm)
    mail.take(20, kept(both, ym), to_ym)
    mail.send(27, kept(0, ym), kept(0, ym), to_yp)
    mail.send(28, kept(both, ym), kept(both, ym), other)
    mail.take(21, kept(both, yp), to_yp)
    mail.send(29, kept(1, yp), kept(1, yp), to_ym)
    mail.send(30, kept(both, yp), kept(both, yp), other)
    mail.take(27, kept(0, y2), to_ym)
    mail.send(31, kept(0, y2), kept(0, y2), other)
    mail.take(29, kept(1, y2), to_yp)
    mail.send(32, kept(1, y2), kept(1, y2), other)
    mail.take(23, mf.at[pl.ds(0, 1), :, z2], to_zm)
    mail.take(24, mf.at[pl.ds(1, 2), :, z2], to_zp)
    mail.take(25, mf.at[pl.ds(3, 2), x2], to_xm)
    mail.take(26, mf.at[pl.ds(5, 1), x2], to_xp)
    mail.take(22, theirs(both, y), other)
    mail.take(28, theirs(both, ym), other)
    mail.take(30, theirs(both, yp), other)
    mail.take(31, theirs(0, y2), other)
    mail.take(32, theirs(1, y2), other)
    mail.finish()


def gather_weights(m_block, a_block):
    return pl.pallas_call(
        weights_kernel,
        out_shape=(
            jax.ShapeDtypeStruct((6, 4, 4, 56, FS), BF),
            jax.ShapeDtypeStruct((2, 4, 4, 8, 16, 1024), BF),
        ),
        in_specs=[pl.BlockSpec(memory_space=pl.ANY)] * 2,
        out_specs=[pl.BlockSpec(memory_space=pl.ANY)] * 2,
        scratch_shapes=[
            pltpu.SemaphoreType.DMA((33,)),
            pltpu.SemaphoreType.DMA((33,)),
            pltpu.SemaphoreType.DMA((2,)),
        ],
        compiler_params=pltpu.CompilerParams(collective_id=1, has_side_effects=True),
        name="gather_weights",
    )(m_block, a_block)


def ctx_gather_kernel(rows, v_ref, o_ref, send_sem, recv_sem, local_sem):
    x, z, y, c = place()
    mail = Mail(send_sem, recv_sem)
    yp, ym, y2 = up1(y), down1(y), up2(y)
    to_yp, to_ym, other = device(x, z, yp, c), device(x, z, ym, c), device(x, z, y, 1 - c)
    own = pltpu.make_async_copy(v_ref, o_ref.at[y, c], local_sem.at[0])
    own.start()
    greet([to_yp, to_ym, other])
    half = rows // 2
    first, second = pl.ds(0, half), pl.ds(half, half)
    mail.send(0, v_ref, o_ref.at[y, c], to_yp)
    mail.send(1, v_ref, o_ref.at[y, c], to_ym)
    mail.send(2, v_ref, o_ref.at[y, c], other)
    mail.take(0, o_ref.at[ym, c], to_ym)
    mail.send(3, o_ref.at[ym, c, first], o_ref.at[ym, c, first], to_yp)
    mail.send(4, o_ref.at[ym, c], o_ref.at[ym, c], other)
    mail.take(1, o_ref.at[yp, c], to_yp)
    mail.send(5, o_ref.at[yp, c, second], o_ref.at[yp, c, second], to_ym)
    mail.send(6, o_ref.at[yp, c], o_ref.at[yp, c], other)
    mail.take(3, o_ref.at[y2, c, first], to_ym)
    mail.send(7, o_ref.at[y2, c, first], o_ref.at[y2, c, first], other)
    mail.take(5, o_ref.at[y2, c, second], to_yp)
    mail.send(8, o_ref.at[y2, c, second], o_ref.at[y2, c, second], other)
    own.wait()
    mail.take(2, o_ref.at[y, 1 - c], other)
    mail.take(4, o_ref.at[ym, 1 - c], other)
    mail.take(6, o_ref.at[yp, 1 - c], other)
    mail.take(7, o_ref.at[y2, 1 - c, first], other)
    mail.take(8, o_ref.at[y2, 1 - c, second], other)
    mail.finish()


def ctx_gather(value, collective_id):
    rows, columns = value.shape
    gathered = pl.pallas_call(
        functools.partial(ctx_gather_kernel, rows),
        out_shape=jax.ShapeDtypeStruct((4, 2, rows, columns), value.dtype),
        in_specs=[pl.BlockSpec(memory_space=pl.ANY)],
        out_specs=pl.BlockSpec(memory_space=pl.ANY),
        scratch_shapes=[
            pltpu.SemaphoreType.DMA((9,)),
            pltpu.SemaphoreType.DMA((9,)),
            pltpu.SemaphoreType.DMA((1,)),
        ],
        compiler_params=pltpu.CompilerParams(collective_id=collective_id, has_side_effects=True),
        name="ctx_gather_%d" % columns,
    )(value)
    return gathered.reshape(8 * rows, columns)


def ctx_scatter_kernel(rows, p_ref, o_ref, near, own, far_a, far_b, got_a, got_b, send_sem, recv_sem):
    x, z, y, c = place()
    mail = Mail(send_sem, recv_sem)
    yp, ym, y2 = up1(y), down1(y), up2(y)
    to_yp, to_ym, other = device(x, z, yp, c), device(x, z, ym, c), device(x, z, y, 1 - c)
    greet([to_yp, to_ym, other])
    half = rows // 2
    first, second = pl.ds(0, half), pl.ds(half, half)
    order = (y2, yp, ym, y)
    for slot, row in enumerate(order):
        mail.send(slot, p_ref.at[row, 1 - c], near.at[slot], other)
    mail.take(0, near.at[0], other)
    own[0] = (p_ref[y2, c].astype(F32) + near[0].astype(F32)).astype(BF)
    mail.send(4, own.at[0, first], far_a, to_yp)
    mail.send(5, own.at[0, second], far_b, to_ym)
    mail.take(1, near.at[1], other)
    mail.take(2, near.at[2], other)
    mail.take(4, far_a, to_ym)
    own[1, second] = (p_ref[yp, c, second].astype(F32) + near[1, second].astype(F32)).astype(BF)
    own[1, first] = (
        p_ref[yp, c, first].astype(F32) + near[1, first].astype(F32) + far_a[...].astype(F32)
    ).astype(BF)
    mail.send(6, own.at[1], got_a, to_yp)
    mail.take(5, far_b, to_yp)
    own[2, first] = (p_ref[ym, c, first].astype(F32) + near[2, first].astype(F32)).astype(BF)
    own[2, second] = (
        p_ref[ym, c, second].astype(F32) + near[2, second].astype(F32) + far_b[...].astype(F32)
    ).astype(BF)
    mail.send(7, own.at[2], got_b, to_ym)
    mail.take(3, near.at[3], other)
    o_ref[...] = p_ref[y, c].astype(F32) + near[3].astype(F32)
    mail.take(6, got_a, to_ym)
    mail.take(7, got_b, to_yp)
    o_ref[...] += got_a[...].astype(F32) + got_b[...].astype(F32)
    mail.finish()


def ctx_scatter(value, collective_id):
    rows, columns = value.shape[0] // 8, value.shape[1]
    return pl.pallas_call(
        functools.partial(ctx_scatter_kernel, rows),
        out_shape=jax.ShapeDtypeStruct((rows, columns), F32),
        in_specs=[pl.BlockSpec(memory_space=pltpu.VMEM)],
        out_specs=pl.BlockSpec(memory_space=pltpu.VMEM),
        scratch_shapes=[
            pltpu.VMEM((4, rows, columns), BF),
            pltpu.VMEM((3, rows, columns), BF),
            pltpu.VMEM((rows // 2, columns), BF),
            pltpu.VMEM((rows // 2, columns), BF),
            pltpu.VMEM((rows, columns), BF),
            pltpu.VMEM((rows, columns), BF),
            pltpu.SemaphoreType.DMA((8,)),
            pltpu.SemaphoreType.DMA((8,)),
        ],
        compiler_params=pltpu.CompilerParams(
            collective_id=collective_id, has_side_effects=True, vmem_limit_bytes=32 * 1024 * 1024
        ),
        name="ctx_scatter_%d" % columns,
    )(value.reshape(4, 2, rows, columns))


def nn(left, right):
    return jnp.dot(left, right, preferred_element_type=F32)


def nt(left, right):
    return lax.dot_general(left, right, (((1,), (1,)), ((), ())), preferred_element_type=F32)


def tn(left, right):
    return lax.dot_general(left, right, (((0,), (0,)), ((), ())), preferred_element_type=F32)


def mlp_scratch():
    return [
        pltpu.VMEM((4, 2, 128, D), BF),
        pltpu.VMEM((4, 2, 128, D), BF),
        pltpu.VMEM((4, 128, D), BF),
        pltpu.VMEM((3, 128, D), BF),
        pltpu.VMEM((2, 64, D), BF),
        pltpu.VMEM((2, 64, D), BF),
        pltpu.VMEM((2, 128, D), BF),
    ]


def mlp_exchange(mail, spot, src, buffers, chunk, fillers):
    rows, part, near, own, far, fin, got = buffers
    x, z, y, c = spot
    yp, ym, y2 = up1(y), down1(y), up2(y)
    to_yp, to_ym, other = device(x, z, yp, c), device(x, z, ym, c), device(x, z, y, 1 - c)
    first, second = pl.ds(0, 64), pl.ds(64, 64)
    mail.send(0, src, rows.at[y, c], to_yp)
    mail.send(1, src, rows.at[y, c], to_ym)
    mail.send(2, src, rows.at[y, c], other)
    rows[y, c] = src[...]
    mail.take(2, rows.at[y, 1 - c], other)
    chunk(y)
    mail.send(12, part.at[y, 1 - c], near.at[3], other)
    mail.take(0, rows.at[ym, c], to_ym)
    mail.send(3, rows.at[ym, c, first], rows.at[ym, c, first], to_yp)
    mail.send(4, rows.at[ym, c], rows.at[ym, c], other)
    mail.take(1, rows.at[yp, c], to_yp)
    mail.send(5, rows.at[yp, c, second], rows.at[yp, c, second], to_ym)
    mail.send(6, rows.at[yp, c], rows.at[yp, c], other)
    mail.take(4, rows.at[ym, 1 - c], other)
    chunk(ym)
    mail.send(11, part.at[ym, 1 - c], near.at[2], other)
    mail.take(6, rows.at[yp, 1 - c], other)
    chunk(yp)
    mail.send(10, part.at[yp, 1 - c], near.at[1], other)
    mail.take(3, rows.at[y2, c, first], to_ym)
    mail.send(7, rows.at[y2, c, first], rows.at[y2, c, first], other)
    mail.take(5, rows.at[y2, c, second], to_yp)
    mail.send(8, rows.at[y2, c, second], rows.at[y2, c, second], other)
    mail.take(11, near.at[2], other)
    own[2] = (part[ym, c].astype(F32) + near[2].astype(F32)).astype(BF)
    mail.send(16, own.at[2], got.at[1], to_ym)
    mail.take(10, near.at[1], other)
    own[1] = (part[yp, c].astype(F32) + near[1].astype(F32)).astype(BF)
    mail.send(15, own.at[1], got.at[0], to_yp)
    mail.take(7, rows.at[y2, 1 - c, first], other)
    mail.take(8, rows.at[y2, 1 - c, second], other)
    chunk(y2)
    mail.send(9, part.at[y2, 1 - c], near.at[0], other)
    fillers[0]()
    mail.take(9, near.at[0], other)
    own[0] = (part[y2, c].astype(F32) + near[0].astype(F32)).astype(BF)
    mail.send(13, own.at[0, first], far.at[0], to_yp)
    mail.send(14, own.at[0, second], far.at[1], to_ym)
    fillers[1]()
    mail.take(13, far.at[0], to_ym)
    mail.send(17, far.at[0], fin.at[0], to_yp)
    mail.take(14, far.at[1], to_yp)
    mail.send(18, far.at[1], fin.at[1], to_ym)
    fillers[2]()
    mail.take(12, near.at[3], other)
    mail.take(15, got.at[0], to_ym)
    mail.take(16, got.at[1], to_yp)
    mail.take(17, fin.at[0], to_ym)
    mail.take(18, fin.at[1], to_yp)
    total = (
        part[y, c].astype(F32)
        + near[3].astype(F32)
        + got[0].astype(F32)
        + got[1].astype(F32)
    )
    return total + fin[...].reshape(128, D).astype(F32)


def nothing():
    return None


def ctx_peers(spot):
    x, z, y, c = spot
    return [device(x, z, up1(y), c), device(x, z, down1(y), c), device(x, z, y, 1 - c)]


def mlp_forward_kernel(layer, h_ref, mid_ref, w_ref, out_ref, hr_ref, gate_ref, up_ref, *scratch):
    buffers = scratch[:7]
    w, gate, up, send_sem, recv_sem, local_sem = scratch[7:]
    rows, part = buffers[0], buffers[1]
    spot = place()
    mail = Mail(send_sem, recv_sem)
    load = pltpu.make_async_copy(w_ref.at[layer], w, local_sem.at[12])
    load.start()
    greet(ctx_peers(spot))
    stores = []
    loaded = []

    def chunk(row):
        if not loaded:
            load.wait()
            loaded.append(True)
        h = rows[row].reshape(256, D)
        g = nn(h, w[0])
        u = nn(h, w[1])
        gate[row] = g.astype(BF)
        up[row] = u.astype(BF)
        act = (g / (1.0 + jnp.exp(-g)) * u).astype(BF)
        part[row] = nt(act, w[2]).astype(BF).reshape(2, 128, D)
        k = len(stores)
        for i, (src, dst) in enumerate(((rows, hr_ref), (gate, gate_ref), (up, up_ref))):
            store = pltpu.make_async_copy(src.at[row], dst.at[row], local_sem.at[k + i])
            store.start()
            stores.append(store)

    total = mlp_exchange(mail, spot, h_ref, buffers, chunk, [nothing] * 3)
    out_ref[...] = mid_ref[...] + total
    for store in stores:
        store.wait()
    mail.finish()


def mlp_forward(layer, hidden_two, after_attn, m_full):
    anywhere = pl.BlockSpec(memory_space=pl.ANY)
    vmem = pl.BlockSpec(memory_space=pltpu.VMEM)
    return pl.pallas_call(
        functools.partial(mlp_forward_kernel, layer),
        out_shape=(
            jax.ShapeDtypeStruct((128, D), F32),
            jax.ShapeDtypeStruct((4, 2, 128, D), BF),
            jax.ShapeDtypeStruct((4, 256, FS), BF),
            jax.ShapeDtypeStruct((4, 256, FS), BF),
        ),
        in_specs=[vmem, vmem, anywhere],
        out_specs=[vmem, anywhere, anywhere, anywhere],
        scratch_shapes=mlp_scratch()
        + [
            pltpu.VMEM((3, D, FS), BF),
            pltpu.VMEM((4, 256, FS), BF),
            pltpu.VMEM((4, 256, FS), BF),
            pltpu.SemaphoreType.DMA((19,)),
            pltpu.SemaphoreType.DMA((19,)),
            pltpu.SemaphoreType.DMA((13,)),
        ],
        compiler_params=pltpu.CompilerParams(
            collective_id=8 + layer, has_side_effects=True, vmem_limit_bytes=48 * 1024 * 1024
        ),
        name="mlp_forward_%d" % layer,
    )(hidden_two, after_attn, m_full)


SHIFTS = [(i, j) for i in range(4) for j in range(4) if (i, j) != (0, 0)]


def ahead(spot, i, j):
    return lax.rem(spot[0] + i, 4), lax.rem(spot[1] + j, 4)


def behind(spot, i, j):
    return lax.rem(spot[0] + 4 - i, 4), lax.rem(spot[1] + 4 - j, 4)


def plane_peers(spot):
    x, z, y, c = spot
    return [device(*ahead(spot, i, j), y, c) for i, j in SHIFTS]


def plane_send(mail, base, spot, src, got):
    x, z, y, c = spot
    for k, (i, j) in enumerate(SHIFTS):
        tx, tz = ahead(spot, i, j)
        mail.send(base + k, src(tx, tz), got.at[k], device(tx, tz, y, c))


def plane_sum(mail, base, spot, mine, got, out):
    x, z, y, c = spot
    out[...] = mine(x, z).astype(F32)
    for k, (i, j) in enumerate(SHIFTS):
        sx, sz = behind(spot, i, j)
        mail.take(base + k, got.at[k], device(sx, sz, y, c))
        out[...] += got[k].astype(F32)


def mlp_backward_kernel(layer, carries, *refs):
    g_ref, w_ref, hr_ref, gate_ref, up_ref = refs[:5]
    refs = refs[5:]
    if carries:
        before, refs = refs[0], refs[1:]
    out_ref, grads = refs[:2]
    refs = refs[2:]
    if carries:
        summed, refs = refs[0], refs[1:]
    buffers, refs = refs[:7], refs[7:]
    w, hr, gate, up, act, src, send_sem, recv_sem, local_sem = refs[:9]
    rows, part = buffers[0], buffers[1]
    spot = place()
    x, z, y, c = spot
    mail = Mail(send_sem, recv_sem)
    loads = [
        pltpu.make_async_copy(a, b, local_sem.at[i])
        for i, (a, b) in enumerate(
            ((w_ref.at[layer], w), (gate_ref, gate), (up_ref, up), (hr_ref, hr))
        )
    ]
    if carries:
        got, mine = refs[9:]
        loads.append(pltpu.make_async_copy(before.at[:, x, z], mine, local_sem.at[4]))
    for load in loads:
        load.start()
    src[...] = g_ref[...].astype(BF)
    greet(ctx_peers(spot) + (plane_peers(spot) if carries else []))
    loaded = []

    def chunk(row):
        if not loaded:
            for load in loads[:3]:
                load.wait()
            loaded.append(True)
        gz = rows[row].reshape(256, D)
        gact = nn(gz, w[2])
        g = gate[row].astype(F32)
        u = up[row].astype(F32)
        s = 1.0 / (1.0 + jnp.exp(-g))
        silu = g * s
        act[row] = (silu * u).astype(BF)
        gg = (gact * u * (s + silu * (1.0 - s))).astype(BF)
        gu = (gact * silu).astype(BF)
        gate[row] = gg
        up[row] = gu
        part[row] = (nt(gg, w[0]) + nt(gu, w[1])).astype(BF).reshape(2, 128, D)

    def weight_grad(member, left, right):
        def run():
            r = right[...].reshape(1024, FS)
            for i in range(7):
                l = left[:, :, :, 128 * i : 128 * (i + 1)].reshape(1024, 128)
                grads[member, 128 * i : 128 * (i + 1)] = tn(l, r).astype(BF)

        return run

    def gates():
        loads[3].wait()
        weight_grad(0, hr, gate)()

    fillers = [weight_grad(2, rows, act), gates, weight_grad(1, hr, up)]
    if carries:
        plane_send(mail, 19, spot, lambda tx, tz: before.at[:, tx, tz], got)
    out_ref[...] = mlp_exchange(mail, spot, src, buffers, chunk, fillers)
    if carries:
        loads[4].wait()
        plane_sum(mail, 19, spot, lambda a, b: mine[...], got, summed)
    mail.finish()


def mlp_backward(layer, grad_output, m_full, hidden_rows, gate, up, before):
    anywhere = pl.BlockSpec(memory_space=pl.ANY)
    vmem = pl.BlockSpec(memory_space=pltpu.VMEM)
    carries = before is not None
    out_shape = [jax.ShapeDtypeStruct((128, D), F32), jax.ShapeDtypeStruct((3, D, FS), BF)]
    scratch = mlp_scratch() + [
        pltpu.VMEM((3, D, FS), BF),
        pltpu.VMEM((4, 2, 128, D), BF),
        pltpu.VMEM((4, 256, FS), BF),
        pltpu.VMEM((4, 256, FS), BF),
        pltpu.VMEM((4, 256, FS), BF),
        pltpu.VMEM((128, D), BF),
        pltpu.SemaphoreType.DMA((34,)),
        pltpu.SemaphoreType.DMA((34,)),
        pltpu.SemaphoreType.DMA((5,)),
    ]
    operands = [grad_output, m_full, hidden_rows, gate, up]
    if carries:
        out_shape.append(jax.ShapeDtypeStruct((3, 56, FS), F32))
        scratch += [pltpu.VMEM((15, 3, 56, FS), BF), pltpu.VMEM((3, 56, FS), BF)]
        operands.append(before.reshape(3, 4, 4, 56, FS))
    return pl.pallas_call(
        functools.partial(mlp_backward_kernel, layer, carries),
        out_shape=tuple(out_shape),
        in_specs=[vmem] + [anywhere] * (len(operands) - 1),
        out_specs=[vmem] * len(out_shape),
        scratch_shapes=scratch,
        compiler_params=pltpu.CompilerParams(
            collective_id=10 + layer, has_side_effects=True, vmem_limit_bytes=52 * 1024 * 1024
        ),
        name="mlp_backward_%d" % layer,
    )(*operands)


def grads_kernel(m_ref, a_ref, mo, ao, m_got, near, far_a, far_b, got_a, got_b, total, a_got, send_sem, recv_sem):
    spot = place()
    x, z, y, c = spot
    mail = Mail(send_sem, recv_sem)
    yp, ym, y2 = up1(y), down1(y), up2(y)
    to_yp, to_ym, other = device(x, z, yp, c), device(x, z, ym, c), device(x, z, y, 1 - c)
    greet([to_yp, to_ym, other] + plane_peers(spot))
    for slot, row in enumerate((y2, yp, ym, y)):
        mail.send(slot, a_ref.at[:, :, :, 2 * row + (1 - c)], near.at[slot], other)
    plane_send(mail, 8, spot, lambda tx, tz: m_ref.at[:, tx, tz], m_got)

    def add_near(slot, row):
        for l in range(2):

            def body(i, carry):
                near[slot, l, i] = (
                    near[slot, l, i].astype(F32) + a_ref[l, i, :, 2 * row + c].astype(F32)
                ).astype(BF)
                return carry

            lax.fori_loop(0, 4, body, 0)

    mail.take(0, near.at[0], other)
    add_near(0, y2)
    mail.send(4, near.at[0, 0], far_a, to_yp)
    mail.send(5, near.at[0, 1], far_b, to_ym)
    mail.take(1, near.at[1], other)
    add_near(1, yp)
    mail.take(2, near.at[2], other)
    add_near(2, ym)
    mail.take(4, far_a, to_ym)
    near[1, 0] = (near[1, 0].astype(F32) + far_a[...].astype(F32)).astype(BF)
    mail.send(6, near.at[1], got_a, to_yp)
    mail.take(5, far_b, to_yp)
    near[2, 1] = (near[2, 1].astype(F32) + far_b[...].astype(F32)).astype(BF)
    mail.send(7, near.at[2], got_b, to_ym)
    mail.take(3, near.at[3], other)
    add_near(3, y)
    mail.take(6, got_a, to_ym)
    mail.take(7, got_b, to_yp)
    total[...] = (near[3].astype(F32) + got_a[...].astype(F32) + got_b[...].astype(F32)).astype(BF)
    plane_send(mail, 23, spot, lambda tx, tz: total.at[:, tx, tz], a_got)
    plane_sum(mail, 8, spot, lambda a, b: m_ref[:, a, b], m_got, mo)
    plane_sum(mail, 23, spot, lambda a, b: total[:, a, b], a_got, ao)
    mail.finish()


def scatter_grads(m_grads, a_grads):
    return pl.pallas_call(
        grads_kernel,
        out_shape=(
            jax.ShapeDtypeStruct((3, 56, FS), F32),
            jax.ShapeDtypeStruct((2, 16, 1024), F32),
        ),
        in_specs=[pl.BlockSpec(memory_space=pltpu.VMEM)] * 2,
        out_specs=[pl.BlockSpec(memory_space=pltpu.VMEM)] * 2,
        scratch_shapes=[
            pltpu.VMEM((15, 3, 56, FS), BF),
            pltpu.VMEM((4, 2, 4, 4, 16, 1024), BF),
            pltpu.VMEM((4, 4, 16, 1024), BF),
            pltpu.VMEM((4, 4, 16, 1024), BF),
            pltpu.VMEM((2, 4, 4, 16, 1024), BF),
            pltpu.VMEM((2, 4, 4, 16, 1024), BF),
            pltpu.VMEM((2, 4, 4, 16, 1024), BF),
            pltpu.VMEM((15, 2, 16, 1024), BF),
            pltpu.SemaphoreType.DMA((38,)),
            pltpu.SemaphoreType.DMA((38,)),
        ],
        compiler_params=pltpu.CompilerParams(
            collective_id=2, has_side_effects=True, vmem_limit_bytes=52 * 1024 * 1024
        ),
        name="scatter_grads",
    )(m_grads.reshape(3, 4, 4, 56, FS), a_grads)


def select_matrix():
    pick = np.zeros((226, 256), np.float32)
    for k in range(16):
        for r in range(7):
            pick[7 * k + r, 16 * k + r] = 1
            pick[112 + 7 * k + r, 16 * k + 8 + r] = 1
        pick[224, 16 * k + 7] = 1
        pick[225, 16 * k + 15] = 1
    return pick


def pack_attention(gain_one, w_qkv, b_qkv, w_out, gain_two):
    index = lax.axis_index("dp") * 8 + lax.axis_index("ctx")
    within = lax.rem(index, 16)
    zeros = jnp.zeros((LAYERS, D), BF)
    one = lax.dynamic_update_slice(zeros, gain_one, (0, 7 * index))
    two = lax.dynamic_update_slice(zeros, gain_two, (0, 7 * index))
    bias = lax.dynamic_update_slice(jnp.zeros((LAYERS, 256), BF), b_qkv, (0, 9 * within))
    row_seven = jnp.concatenate([one, bias[:, :128]], axis=1)[:, None]
    row_last = jnp.concatenate([two, bias[:, 128:]], axis=1)[:, None]
    joined = jnp.concatenate([w_qkv, w_out], axis=2)
    return jnp.concatenate([joined[:, :, :1024], row_seven, joined[:, :, 1024:], row_last], axis=1)


def unpack_attention(block, pick):
    groups = block.reshape(8, 256, 1024)
    out = jnp.einsum("ab,gbc->gac", pick, groups, preferred_element_type=F32).astype(BF)
    low = out[:, :112].reshape(D, 1024)
    high = out[:, 112:224].reshape(D, 1024)
    spare = out[:, 224:]
    gain_one = jnp.sum(spare[:, 0, :D].astype(F32), axis=0)
    gain_two = jnp.sum(spare[:, 1, :D].astype(F32), axis=0)
    bias = jnp.concatenate([spare[:, 0, D:], spare[:, 1, D : D + 16]], axis=1).reshape(QKV)
    qkv = jnp.concatenate([low, high[:, :128]], axis=1)
    return gain_one, qkv, bias, high[:, 128:], gain_two


def pack_attention_grads(gain_one, qkv, qk_bias, value_bias, out, gain_two, pick):
    low = qkv[:, :1024].astype(BF).reshape(8, 112, 1024)
    high = jnp.concatenate([qkv[:, 1024:], out], axis=1).astype(BF).reshape(8, 112, 1024)
    row_seven = jnp.concatenate(
        [jnp.broadcast_to(gain_one[None], (8, D)), qk_bias.reshape(8, 128)], axis=1
    )
    row_last = jnp.concatenate(
        [
            jnp.broadcast_to(gain_two[None], (8, D)),
            value_bias.reshape(8, 16),
            jnp.zeros((8, 112), F32),
        ],
        axis=1,
    )
    rows = jnp.concatenate(
        [low, high, row_seven.astype(BF)[:, None], row_last.astype(BF)[:, None]], axis=1
    )
    block = jnp.einsum("ab,gac->gbc", pick, rows, preferred_element_type=F32).astype(BF)
    return block.reshape(4, 4, 8, 16, 1024)


def unpack_attention_grads(block):
    index = lax.axis_index("dp") * 8 + lax.axis_index("ctx")
    within = lax.rem(index, 16)
    qkv = jnp.concatenate([block[:7], block[8:15, :128]], axis=1)
    out = block[8:15, 128:]
    gain_one = lax.dynamic_slice(block[7], (7 * index,), (7,))
    gain_two = lax.dynamic_slice(block[15], (7 * index,), (7,))
    qk_bias = lax.dynamic_slice(block[7], (D + 8 * within,), (8,))
    value_bias = lax.dynamic_slice(block[15], (D + within,), (1,))
    return gain_one, qkv, qk_bias, value_bias, out, gain_two


def norm_scale(inputs, gain_vec):
    return (
        inputs * lax.rsqrt(jnp.mean(inputs * inputs, axis=-1, keepdims=True) + eps_norm) * gain_vec
    )


def rotate(inputs, tables):
    cosine_table, sine_table = tables
    half_dim = inputs.shape[-1] // 2
    lower_half = inputs[..., :half_dim]
    upper_half = inputs[..., half_dim:]
    return jnp.concatenate(
        [
            lower_half * cosine_table - upper_half * sine_table,
            upper_half * cosine_table + lower_half * sine_table,
        ],
        axis=-1,
    )


def rotate_back(inputs, tables):
    return rotate(inputs, (tables[0], -tables[1]))


def swiglu(gate_pre, up_pre):
    return jax.nn.silu(gate_pre) * up_pre


def inner_rows(left_side, right_side):
    return lax.dot_general(
        left_side, right_side, (((0,), (0,)), ((), ())), preferred_element_type=F32
    )


def times_transposed(left_side, right_side):
    return lax.dot_general(
        left_side, right_side, (((1,), (1,)), ((), ())), preferred_element_type=F32
    )


def masked_scores(queries, keys_all, allowed):
    scores = jnp.einsum(
        "skgd,tkd->kgst", queries, keys_all, preferred_element_type=F32
    ) * queries.shape[-1] ** (-0.5)
    return jnp.where(allowed[None, None], scores, neg_fill)


def attend(queries, keys_all, values_all, allowed):
    scores = masked_scores(queries, keys_all, allowed)
    highest = jnp.max(scores, axis=-1, keepdims=True)
    log_total = highest + jnp.log(jnp.sum(jnp.exp(scores - highest), axis=-1, keepdims=True))
    soft_weights = jnp.exp(scores - log_total).astype(BF)
    output = jnp.einsum("kgst,tkd->skgd", soft_weights, values_all, preferred_element_type=F32)
    return (output, log_total)


def attend_back(queries, keys_all, values_all, log_total, grad_out, allowed):
    scale = queries.shape[-1] ** (-0.5)
    soft_weights = jnp.exp(masked_scores(queries, keys_all, allowed) - log_total)
    grad_soft = jnp.einsum("skgd,tkd->kgst", grad_out, values_all, preferred_element_type=F32)
    grad_values = jnp.einsum(
        "kgst,skgd->tkd", soft_weights.astype(BF), grad_out, preferred_element_type=F32
    )
    grad_scores = soft_weights * (
        grad_soft - jnp.sum(grad_soft * soft_weights, axis=-1, keepdims=True)
    )
    grad_scores = grad_scores.astype(BF)
    grad_queries = (
        jnp.einsum("kgst,tkd->skgd", grad_scores, keys_all, preferred_element_type=F32) * scale
    )
    grad_keys = (
        jnp.einsum("kgst,skgd->tkd", grad_scores, queries, preferred_element_type=F32) * scale
    )
    return (grad_queries, grad_keys, grad_values)


def layer_forward(layer, inputs, weights, m_full, tables, allowed):
    gain_first, qkv_weight, qkv_bias, out_weight, gain_second = weights
    kv_width = KVH * HD
    groups = H // KVH
    tokens_here = inputs.shape[0]
    hidden = norm_scale(inputs, gain_first).astype(BF)
    packed = jnp.dot(hidden, qkv_weight, preferred_element_type=F32) + qkv_bias.astype(F32)
    queries = rotate(packed[:, :D].reshape(tokens_here, H, HD), tables).astype(BF)
    keys_here = rotate(packed[:, D : D + kv_width].reshape(tokens_here, KVH, HD), tables).astype(BF)
    values_here = packed[:, D + kv_width :].astype(BF)
    both = ctx_gather(
        jnp.concatenate([keys_here.reshape(tokens_here, kv_width), values_here], axis=1), 3
    )
    whole_len = both.shape[0]
    keys_all = both[:, :kv_width].reshape(whole_len, KVH, HD)
    values_all = both[:, kv_width:].reshape(whole_len, KVH, HD)
    queries_seq = queries.reshape(tokens_here, KVH, groups, HD)
    attended, log_total = attend(queries_seq, keys_all, values_all, allowed)
    attended = attended.reshape(tokens_here, D).astype(BF)
    after_attn = inputs + jnp.dot(attended, out_weight, preferred_element_type=F32)
    hidden_two = norm_scale(after_attn, gain_second).astype(BF)
    output, hidden_rows, gate_pre, up_pre = mlp_forward(layer, hidden_two, after_attn, m_full)
    kept = (
        inputs,
        hidden,
        queries_seq,
        keys_all,
        values_all,
        log_total,
        attended,
        after_attn,
        hidden_rows,
        gate_pre,
        up_pre,
    )
    return (output, kept)


def layer_backward(layer, grad_output, kept, weights, m_full, before, tables, allowed, pick):
    gain_first, qkv_weight, qkv_bias, out_weight, gain_second = weights
    (
        inputs,
        hidden,
        queries_seq,
        keys_all,
        values_all,
        log_total,
        attended,
        after_attn,
        hidden_rows,
        gate_pre,
        up_pre,
    ) = kept
    tokens_here = inputs.shape[0]
    kv_width = KVH * HD
    grad_hidden_two, m_grads, *m_sum = mlp_backward(
        layer, grad_output, m_full, hidden_rows, gate_pre, up_pre, before
    )
    unused_out, norm_back_second = jax.vjp(norm_scale, after_attn, gain_second)
    grad_mid, grad_gain_second = norm_back_second(grad_hidden_two)
    grad_mid = grad_mid + grad_output
    attn_in = grad_mid.astype(BF)
    grad_out_w = inner_rows(attended, attn_in)
    grad_attended = times_transposed(attn_in, out_weight).astype(BF).reshape(queries_seq.shape)
    grad_queries, grad_keys, grad_values = attend_back(
        queries_seq, keys_all, values_all, log_total, grad_attended, allowed
    )
    whole_len = keys_all.shape[0]
    both = ctx_scatter(
        jnp.concatenate(
            [grad_keys.reshape(whole_len, kv_width), grad_values.reshape(whole_len, kv_width)],
            axis=1,
        ).astype(BF),
        6,
    )
    grad_keys = both[:, :kv_width]
    grad_values = both[:, kv_width:]
    grad_query_flat = rotate_back(grad_queries.reshape(tokens_here, H, HD), tables).reshape(
        tokens_here, D
    )
    grad_key_flat = rotate_back(grad_keys.reshape(tokens_here, KVH, HD), tables).reshape(
        tokens_here, kv_width
    )
    grad_packed = jnp.concatenate([grad_query_flat, grad_key_flat, grad_values], axis=1).astype(BF)
    grad_qkv_w = inner_rows(hidden, grad_packed)
    grad_qkv_b = jnp.sum(grad_packed.astype(F32), axis=0)
    grad_hidden = times_transposed(grad_packed, qkv_weight)
    unused_out, norm_back_first = jax.vjp(norm_scale, inputs, gain_first)
    grad_input, grad_gain_first = norm_back_first(grad_hidden)
    grad_input = grad_input + grad_mid
    a_grads = pack_attention_grads(
        grad_gain_first,
        grad_qkv_w,
        grad_qkv_b[: D + kv_width],
        grad_qkv_b[D + kv_width :],
        grad_out_w,
        grad_gain_second,
        pick,
    )
    return (grad_input, a_grads, m_grads, m_sum)


def shards(
    tokens, cotangent, span_order, gain_one, w_qkv, b_qkv, w_out, gain_two, w_gate, w_up, w_down
):
    sequences, local_len, width = tokens.shape
    span_len = local_len // 2
    ctx_place = lax.axis_index("ctx")
    offsets = jnp.arange(span_len, dtype=jnp.int32)
    local_spans = lax.dynamic_slice_in_dim(span_order, 2 * ctx_place, 2)
    local_pos = (local_spans[:, None] * span_len + offsets[None, :]).reshape(local_len)
    all_pos = (span_order[:, None] * span_len + offsets[None, :]).reshape(-1)
    allowed = all_pos[None, :] <= local_pos[:, None]
    frequency = rope_base ** (-jnp.arange(HD // 2, dtype=F32) * 2.0 / HD)
    angles = local_pos.astype(F32)[:, None] * frequency[None, :]
    tables = (jnp.cos(angles)[:, None, :], jnp.sin(angles)[:, None, :])
    pick = jnp.asarray(select_matrix(), BF)

    m_block = jnp.stack([w_gate, w_up, w_down.transpose(0, 2, 1)], axis=1).reshape(6, 56, FS)
    a_block = pack_attention(gain_one, w_qkv, b_qkv, w_out, gain_two)
    m_full, a_full = gather_weights(m_block, a_block)
    m_full = m_full.reshape(2, 3, D, FS)
    weights = [unpack_attention(a_full[l], pick) for l in range(LAYERS)]
    state = tokens.reshape(local_len, width).astype(F32)
    kept_layers = []
    for l in range(LAYERS):
        state, kept = layer_forward(l, state, weights[l], m_full, tables, allowed)
        kept_layers.append(kept)
    grad_state = cotangent.reshape(local_len, width).astype(F32)
    grad_state, a_one, m_one, unused = layer_backward(
        1, grad_state, kept_layers[1], weights[1], m_full, None, tables, allowed, pick
    )
    grad_state, a_zero, m_zero, m_one_sum = layer_backward(
        0, grad_state, kept_layers[0], weights[0], m_full, m_one, tables, allowed, pick
    )
    m_zero_sum, a_sum = scatter_grads(m_zero, jnp.stack([a_zero, a_one]))
    m_sums = (m_zero_sum, m_one_sum[0])
    grad_layers = [
        unpack_attention_grads(a_sum[l]) + (m_sums[l][0], m_sums[l][1], m_sums[l][2].T)
        for l in range(LAYERS)
    ]
    stacks = [jnp.stack([sums[member] for sums in grad_layers]) for member in range(9)]
    output = state.astype(BF).reshape(sequences, local_len, width)
    input_grad = grad_state.reshape(sequences, local_len, width)
    return (output, input_grad) + tuple(stacks)


def solution(mesh):
    return jax.shard_map(
        shards,
        mesh=mesh,
        in_specs=(
            P("dp", "ctx", None),
            P("dp", "ctx", None),
            P(),
            P(None, ("dp", "ctx")),
            P(None, ("dp", "ctx"), None),
            P(None, ("dp", "ctx")),
            P(None, ("dp", "ctx"), None),
            P(None, ("dp", "ctx")),
            P(None, "dp", "ctx"),
            P(None, "dp", "ctx"),
            P(None, "ctx", "dp"),
        ),
        out_specs=(
            P("dp", "ctx", None),
            P("dp", "ctx", None),
            P(None, ("dp", "ctx")),
            P(None, ("dp", "ctx"), None),
            P(None, ("dp", "ctx")),
            P(None, ("dp", "ctx")),
            P(None, ("dp", "ctx"), None),
            P(None, ("dp", "ctx")),
            P(None, "dp", "ctx"),
            P(None, "dp", "ctx"),
            P(None, "ctx", "dp"),
        ),
        check_vma=False,
    )
```

```python
import functools

import jax
import jax.numpy as jnp
import numpy as np
from jax import lax
from jax.experimental import pallas as pl
from jax.experimental.pallas import tpu as pltpu
from jax.sharding import PartitionSpec as P

H = 14
KVH = 2
HD = 64
LAYERS = 2
D = 896
QKV = 1152
FS = 608
MESH = pl.DeviceIdType.MESH
BF = jnp.bfloat16
F32 = jnp.float32

eps_norm = 1e-06
rope_base = 1000000.0
neg_fill = -1e30


def place():
    dp = lax.axis_index("dp")
    ctx = lax.axis_index("ctx")
    return lax.div(dp, 4), lax.rem(dp, 4), lax.div(ctx, 2), lax.rem(ctx, 2)


def up1(v):
    return lax.rem(v + 1, 4)


def up2(v):
    return lax.rem(v + 2, 4)


def down1(v):
    return lax.rem(v + 3, 4)


def device(x, z, y, c):
    return (x * 4 + z, y * 2 + c)


def greet(peers):
    barrier = pltpu.get_barrier_semaphore()
    for peer in peers:
        pl.semaphore_signal(barrier, inc=1, device_id=peer, device_id_type=MESH)
    pl.semaphore_wait(barrier, len(peers))


class Mail:
    def __init__(self, send_sem, recv_sem):
        self.send_sem = send_sem
        self.recv_sem = recv_sem
        self.sent = []

    def send(self, slot, src, dst, target):
        copy = pltpu.make_async_remote_copy(
            src_ref=src,
            dst_ref=dst,
            send_sem=self.send_sem.at[slot],
            recv_sem=self.recv_sem.at[slot],
            device_id=target,
            device_id_type=MESH,
        )
        copy.start()
        self.sent.append(copy)

    def take(self, slot, dst, source):
        pltpu.make_async_remote_copy(
            src_ref=dst,
            dst_ref=dst,
            send_sem=self.send_sem.at[slot],
            recv_sem=self.recv_sem.at[slot],
            device_id=source,
            device_id_type=MESH,
        ).wait_recv()

    def finish(self):
        for copy in self.sent:
            copy.wait_send()


def weights_kernel(m_ref, a_ref, mf, af, send_sem, recv_sem, local_sem):
    x, z, y, c = place()
    ctx = 2 * y + c
    mail = Mail(send_sem, recv_sem)
    xp, xm, zp, zm, yp, ym = up1(x), down1(x), up1(z), down1(z), up1(y), down1(y)
    to_xp, to_xm = device(xp, z, y, c), device(xm, z, y, c)
    to_zp, to_zm = device(x, zp, y, c), device(x, zm, y, c)
    to_yp, to_ym = device(x, z, yp, c), device(x, z, ym, c)
    other = device(x, z, y, 1 - c)
    own_m = pltpu.make_async_copy(m_ref, mf.at[:, x, z], local_sem.at[0])
    own_a = pltpu.make_async_copy(a_ref, af.at[:, x, z, ctx], local_sem.at[1])
    own_a.start()
    own_m.start()
    greet([to_xp, to_xm, to_zp, to_zm, to_yp, to_ym, other])

    lo, hi = pl.ds(0, 3), pl.ds(3, 3)
    mail.send(0, a_ref, af.at[:, x, z, ctx], to_xp)
    mail.send(1, a_ref, af.at[:, x, z, ctx], to_xm)
    mail.send(2, m_ref.at[lo], mf.at[lo, x, z], to_xp)
    mail.send(3, m_ref.at[lo], mf.at[lo, x, z], to_xm)
    mail.send(4, m_ref.at[hi], mf.at[hi, x, z], to_zp)
    mail.send(5, m_ref.at[hi], mf.at[hi, x, z], to_zm)
    mail.take(0, af.at[:, xm, z, ctx], to_xm)
    mail.send(6, af.at[0, xm, z, ctx], af.at[0, xm, z, ctx], to_xp)
    mail.take(1, af.at[:, xp, z, ctx], to_xp)
    mail.send(7, af.at[1, xp, z, ctx], af.at[1, xp, z, ctx], to_xm)
    x2, z2, y2 = up2(x), up2(z), up2(y)
    mail.take(6, af.at[0, x2, z, ctx], to_xm)
    mail.take(7, af.at[1, x2, z, ctx], to_xp)
    own_a.wait()
    mail.send(8, af.at[:, :, z, ctx], af.at[:, :, z, ctx], to_zp)
    mail.send(9, af.at[:, :, z, ctx], af.at[:, :, z, ctx], to_zm)
    mail.take(2, mf.at[lo, xm, z], to_xm)
    mail.send(10, mf.at[pl.ds(0, 2), xm, z], mf.at[pl.ds(0, 2), xm, z], to_xp)
    mail.take(3, mf.at[lo, xp, z], to_xp)
    mail.send(11, mf.at[pl.ds(2, 1), xp, z], mf.at[pl.ds(2, 1), xp, z], to_xm)
    mail.take(4, mf.at[hi, x, zm], to_zm)
    mail.send(12, mf.at[pl.ds(3, 1), x, zm], mf.at[pl.ds(3, 1), x, zm], to_zp)
    mail.take(5, mf.at[hi, x, zp], to_zp)
    mail.send(13, mf.at[pl.ds(4, 2), x, zp], mf.at[pl.ds(4, 2), x, zp], to_zm)
    mail.take(8, af.at[:, :, zm, ctx], to_zm)
    mail.send(14, af.at[0, :, zm, ctx], af.at[0, :, zm, ctx], to_zp)
    mail.take(9, af.at[:, :, zp, ctx], to_zp)
    mail.send(15, af.at[1, :, zp, ctx], af.at[1, :, zp, ctx], to_zm)
    mail.take(10, mf.at[pl.ds(0, 2), x2, z], to_xm)
    mail.take(11, mf.at[pl.ds(2, 1), x2, z], to_xp)
    own_m.wait()
    mail.send(16, mf.at[lo, :, z], mf.at[lo, :, z], to_zp)
    mail.send(17, mf.at[lo, :, z], mf.at[lo, :, z], to_zm)
    mail.take(12, mf.at[pl.ds(3, 1), x, z2], to_zm)
    mail.take(13, mf.at[pl.ds(4, 2), x, z2], to_zp)
    mail.send(18, mf.at[hi, x], mf.at[hi, x], to_xp)
    mail.send(19, mf.at[hi, x], mf.at[hi, x], to_xm)
    mail.take(14, af.at[0, :, z2, ctx], to_zm)
    mail.take(15, af.at[1, :, z2, ctx], to_zp)

    def kept(part, row):
        return af.at[part, :, :, 2 * row + c]

    def theirs(part, row):
        return af.at[part, :, :, 2 * row + (1 - c)]

    both = slice(None)
    mail.send(20, kept(both, y), kept(both, y), to_yp)
    mail.send(21, kept(both, y), kept(both, y), to_ym)
    mail.send(22, kept(both, y), kept(both, y), other)
    mail.take(16, mf.at[lo, :, zm], to_zm)
    mail.send(23, mf.at[pl.ds(0, 1), :, zm], mf.at[pl.ds(0, 1), :, zm], to_zp)
    mail.take(17, mf.at[lo, :, zp], to_zp)
    mail.send(24, mf.at[pl.ds(1, 2), :, zp], mf.at[pl.ds(1, 2), :, zp], to_zm)
    mail.take(18, mf.at[hi, xm], to_xm)
    mail.send(25, mf.at[pl.ds(3, 2), xm], mf.at[pl.ds(3, 2), xm], to_xp)
    mail.take(19, mf.at[hi, xp], to_xp)
    mail.send(26, mf.at[pl.ds(5, 1), xp], mf.at[pl.ds(5, 1), xp], to_xm)
    mail.take(20, kept(both, ym), to_ym)
    mail.send(27, kept(0, ym), kept(0, ym), to_yp)
    mail.send(28, kept(both, ym), kept(both, ym), other)
    mail.take(21, kept(both, yp), to_yp)
    mail.send(29, kept(1, yp), kept(1, yp), to_ym)
    mail.send(30, kept(both, yp), kept(both, yp), other)
    mail.take(27, kept(0, y2), to_ym)
    mail.send(31, kept(0, y2), kept(0, y2), other)
    mail.take(29, kept(1, y2), to_yp)
    mail.send(32, kept(1, y2), kept(1, y2), other)
    mail.take(23, mf.at[pl.ds(0, 1), :, z2], to_zm)
    mail.take(24, mf.at[pl.ds(1, 2), :, z2], to_zp)
    mail.take(25, mf.at[pl.ds(3, 2), x2], to_xm)
    mail.take(26, mf.at[pl.ds(5, 1), x2], to_xp)
    mail.take(22, theirs(both, y), other)
    mail.take(28, theirs(both, ym), other)
    mail.take(30, theirs(both, yp), other)
    mail.take(31, theirs(0, y2), other)
    mail.take(32, theirs(1, y2), other)
    mail.finish()


def gather_weights(m_block, a_block):
    return pl.pallas_call(
        weights_kernel,
        out_shape=(
            jax.ShapeDtypeStruct((6, 4, 4, 56, FS), BF),
            jax.ShapeDtypeStruct((2, 4, 4, 8, 16, 1024), BF),
        ),
        in_specs=[pl.BlockSpec(memory_space=pl.ANY)] * 2,
        out_specs=[pl.BlockSpec(memory_space=pl.ANY)] * 2,
        scratch_shapes=[
            pltpu.SemaphoreType.DMA((33,)),
            pltpu.SemaphoreType.DMA((33,)),
            pltpu.SemaphoreType.DMA((2,)),
        ],
        compiler_params=pltpu.CompilerParams(collective_id=1, has_side_effects=True),
        name="gather_weights",
    )(m_block, a_block)


class PlaneSum:
    def __init__(self, mail, base, spot, g, cut, buffers):
        self.mail, self.base, self.spot, self.g, self.cut = mail, base, spot, g, cut
        self.count = g.shape[0]
        self.buffers = buffers

    @staticmethod
    def scratch(slabs, cut, rows, columns):
        rest = slabs - cut
        out = [
            pltpu.VMEM((2, cut, 2, rows, columns), BF),
            pltpu.VMEM((2, cut, 4, rows, columns), BF),
            pltpu.VMEM((2, rest, 2, rows, columns), BF),
            pltpu.VMEM((2, rest, 4, rows, columns), BF),
            pltpu.VMEM((2, cut // 2, rows, columns), BF),
            pltpu.VMEM((2, cut, rows, columns), BF),
            pltpu.VMEM((2, max(rest // 2, 1), rows, columns), BF),
            pltpu.VMEM((2, rest, rows, columns), BF),
        ]
        return out

    @staticmethod
    def peers(spot, slabs, cut):
        x, z, y, c = spot
        near = [device(up1(x), z, y, c), device(down1(x), z, y, c), device(x, up1(z), y, c), device(x, down1(z), y, c)]
        return near + ([device(x, up2(z), y, c)] if slabs - cut == 1 else [])

    def names(self):
        x, z, y, c = self.spot
        xp, xm, zp, zm = up1(x), down1(x), up1(z), down1(z)
        to = (device(xp, z, y, c), device(xm, z, y, c), device(x, zp, y, c), device(x, zm, y, c))
        return x, z, xp, xm, zp, zm, up2(x), up2(z), to

    def send(self, slot, src, dst, target):
        self.mail.send(self.base + slot, src, dst, target)

    def take(self, slot, dst, source):
        self.mail.take(self.base + slot, dst, source)

    def add(self, where, extra):
        self.g[where] = (self.g[where].astype(F32) + extra.astype(F32)).astype(BF)

    def step_one(self):
        x, z, xp, xm, zp, zm, x2, z2, (to_xp, to_xm, to_zp, to_zm) = self.names()
        fa, ga, fb, gb, pa, qa, pb, qb = self.buffers
        sa, sb = pl.ds(0, self.cut), pl.ds(self.cut, self.count - self.cut)
        lo, hi = pl.ds(0, 2), pl.ds(2, 2)
        self.send(0, self.g.at[sa, lo, z2], fa.at[0], to_zp)
        self.send(1, self.g.at[sa, hi, z2], fa.at[1], to_zm)
        self.send(2, self.g.at[sb, x2, lo], fb.at[0], to_xp)
        self.send(3, self.g.at[sb, x2, hi], fb.at[1], to_xm)

    def step_two(self):
        x, z, xp, xm, zp, zm, x2, z2, (to_xp, to_xm, to_zp, to_zm) = self.names()
        fa, ga, fb, gb, pa, qa, pb, qb = self.buffers
        sa, sb = pl.ds(0, self.cut), pl.ds(self.cut, self.count - self.cut)
        lo, hi, every = pl.ds(0, 2), pl.ds(2, 2), pl.ds(0, 4)
        self.take(0, fa.at[0], to_zm)
        self.add((sa, lo, zp), fa[0])
        self.send(4, self.g.at[sa, every, zp], ga.at[0], to_zp)
        self.take(2, fb.at[0], to_xm)
        self.add((sb, xp, lo), fb[0])
        self.send(6, self.g.at[sb, xp, every], gb.at[0], to_xp)
        self.take(1, fa.at[1], to_zp)
        self.add((sa, hi, zm), fa[1])
        self.send(5, self.g.at[sa, every, zm], ga.at[1], to_zm)
        self.take(3, fb.at[1], to_xp)
        self.add((sb, xm, hi), fb[1])
        self.send(7, self.g.at[sb, xm, every], gb.at[1], to_xm)

    def step_three(self):
        x, z, xp, xm, zp, zm, x2, z2, (to_xp, to_xm, to_zp, to_zm) = self.names()
        fa, ga, fb, gb, pa, qa, pb, qb = self.buffers
        y, c = self.spot[2:]
        cut, rest = self.cut, self.count - self.cut
        sa, sb = pl.ds(0, cut), pl.ds(cut, rest)
        every = pl.ds(0, 4)
        self.take(4, ga.at[0], to_zm)
        self.take(5, ga.at[1], to_zp)
        self.add((sa, every, z), ga[0].astype(F32) + ga[1].astype(F32))
        self.send(8, self.g.at[pl.ds(0, cut // 2), x2, z], pa.at[0], to_xp)
        self.send(9, self.g.at[pl.ds(cut // 2, cut // 2), x2, z], pa.at[1], to_xm)
        self.take(6, gb.at[0], to_xm)
        self.take(7, gb.at[1], to_xp)
        self.add((sb, x, every), gb[0].astype(F32) + gb[1].astype(F32))
        if rest == 1:
            self.send(10, self.g.at[sb, x, z2], pb.at[0], device(x, z2, y, c))
            self.send(14, self.g.at[sb, x, zp], qb.at[0], to_zp)
            self.send(15, self.g.at[sb, x, zm], qb.at[1], to_zm)
        else:
            self.send(10, self.g.at[pl.ds(cut, rest // 2), x, z2], pb.at[0], to_zp)
            self.send(11, self.g.at[pl.ds(cut + rest // 2, rest // 2), x, z2], pb.at[1], to_zm)

    def step_four(self):
        x, z, xp, xm, zp, zm, x2, z2, (to_xp, to_xm, to_zp, to_zm) = self.names()
        fa, ga, fb, gb, pa, qa, pb, qb = self.buffers
        cut, rest = self.cut, self.count - self.cut
        sa, sb = pl.ds(0, cut), pl.ds(cut, rest)
        self.take(8, pa.at[0], to_xm)
        self.add((pl.ds(0, cut // 2), xp, z), pa[0])
        self.send(12, self.g.at[sa, xp, z], qa.at[0], to_xp)
        self.take(9, pa.at[1], to_xp)
        self.add((pl.ds(cut // 2, cut // 2), xm, z), pa[1])
        self.send(13, self.g.at[sa, xm, z], qa.at[1], to_xm)
        if rest > 1:
            self.take(10, pb.at[0], to_zm)
            self.add((pl.ds(cut, rest // 2), x, zp), pb[0])
            self.send(14, self.g.at[sb, x, zp], qb.at[0], to_zp)
            self.take(11, pb.at[1], to_zp)
            self.add((pl.ds(cut + rest // 2, rest // 2), x, zm), pb[1])
            self.send(15, self.g.at[sb, x, zm], qb.at[1], to_zm)

    def step_five(self, out):
        x, z, xp, xm, zp, zm, x2, z2, (to_xp, to_xm, to_zp, to_zm) = self.names()
        fa, ga, fb, gb, pa, qa, pb, qb = self.buffers
        y, c = self.spot[2:]
        cut, rest = self.cut, self.count - self.cut
        sa, sb = pl.ds(0, cut), pl.ds(cut, rest)
        self.take(12, qa.at[0], to_xm)
        self.take(13, qa.at[1], to_xp)
        out[sa] = (
            self.g[sa, x, z].astype(F32) + qa[0].astype(F32) + qa[1].astype(F32)
        ).astype(out.dtype)
        self.take(14, qb.at[0], to_zm)
        self.take(15, qb.at[1], to_zp)
        total = self.g[sb, x, z].astype(F32) + qb[0].astype(F32) + qb[1].astype(F32)
        if rest == 1:
            self.take(10, pb.at[0], device(x, z2, y, c))
            total = total + pb[0].astype(F32)
        out[sb] = total.astype(out.dtype)


class AttentionSum:
    def __init__(self, mail, base, spot, a_ref, refs, load_sem):
        self.mail, self.base, self.spot, self.a_ref = mail, base, spot, a_ref
        self.mine, self.near, self.block, self.got = refs[:4]
        self.plane = PlaneSum(mail, base + 4, spot, self.mine, 2, refs[4:])
        self.load = pltpu.make_async_copy(a_ref.at[spot[3]], self.mine, load_sem)

    @staticmethod
    def scratch():
        return [
            pltpu.VMEM((4, 4, 4, 16, 1024), BF),
            pltpu.VMEM((4, 4, 4, 16, 1024), BF),
            pltpu.VMEM((4, 16, 1024), BF),
            pltpu.VMEM((3, 16, 1024), BF),
        ] + PlaneSum.scratch(4, 2, 16, 1024)

    slots = 20

    @staticmethod
    def peers(spot):
        x, z, y, c = spot
        return PlaneSum.peers(spot, 4, 2) + [
            device(x, z, up1(y), c),
            device(x, z, up2(y), c),
            device(x, z, down1(y), c),
            device(x, z, y, 1 - c),
        ]

    def start(self):
        x, z, y, c = self.spot
        self.mail.send(self.base, self.a_ref.at[1 - c], self.near, device(x, z, y, 1 - c))

    def cores(self):
        x, z, y, c = self.spot
        self.load.wait()
        self.mail.take(self.base, self.near, device(x, z, y, 1 - c))

        def body(i, carry):
            self.mine[i] = (self.mine[i].astype(F32) + self.near[i].astype(F32)).astype(BF)
            return carry

        lax.fori_loop(0, 4, body, 0)
        self.plane.step_one()

    def rows(self):
        x, z, y, c = self.spot
        self.plane.step_five(self.block)
        for k, step in enumerate((up1, up2, down1)):
            to = device(x, z, step(y), c)
            self.mail.send(self.base + 1 + k, self.block.at[step(y)], self.got.at[k], to)

    def last(self, out):
        x, z, y, c = self.spot
        total = self.block[y].astype(F32)
        for k, step in enumerate((down1, up2, up1)):
            self.mail.take(self.base + 1 + k, self.got.at[k], device(x, z, step(y), c))
            total = total + self.got[k].astype(F32)
        out[...] = total


def nn(left, right):
    return jnp.dot(left, right, preferred_element_type=F32)


def nt(left, right):
    return lax.dot_general(left, right, (((1,), (1,)), ((), ())), preferred_element_type=F32)


def tn(left, right):
    return lax.dot_general(left, right, (((0,), (0,)), ((), ())), preferred_element_type=F32)


def mlp_scratch():
    return [
        pltpu.VMEM((4, 2, 128, D), BF),
        pltpu.VMEM((4, 2, 128, D), BF),
        pltpu.VMEM((4, 128, D), BF),
        pltpu.VMEM((3, 128, D), BF),
        pltpu.VMEM((2, 64, D), BF),
        pltpu.VMEM((2, 64, D), BF),
        pltpu.VMEM((2, 128, D), BF),
    ]


def mlp_exchange(mail, spot, src, buffers, chunk, fillers, hook):
    rows, part, near, own, far, fin, got = buffers
    x, z, y, c = spot
    yp, ym, y2 = up1(y), down1(y), up2(y)
    to_yp, to_ym, other = device(x, z, yp, c), device(x, z, ym, c), device(x, z, y, 1 - c)
    first, second = pl.ds(0, 64), pl.ds(64, 64)
    mail.send(0, src, rows.at[y, c], to_yp)
    mail.send(1, src, rows.at[y, c], to_ym)
    mail.send(2, src, rows.at[y, c], other)
    rows[y, c] = src[...]
    mail.take(2, rows.at[y, 1 - c], other)
    chunk(y)
    mail.send(12, part.at[y, 1 - c], near.at[3], other)
    mail.take(0, rows.at[ym, c], to_ym)
    mail.send(3, rows.at[ym, c, first], rows.at[ym, c, first], to_yp)
    mail.send(4, rows.at[ym, c], rows.at[ym, c], other)
    mail.take(1, rows.at[yp, c], to_yp)
    mail.send(5, rows.at[yp, c, second], rows.at[yp, c, second], to_ym)
    mail.send(6, rows.at[yp, c], rows.at[yp, c], other)
    mail.take(4, rows.at[ym, 1 - c], other)
    chunk(ym)
    mail.send(11, part.at[ym, 1 - c], near.at[2], other)
    hook()
    mail.take(6, rows.at[yp, 1 - c], other)
    chunk(yp)
    mail.send(10, part.at[yp, 1 - c], near.at[1], other)
    mail.take(3, rows.at[y2, c, first], to_ym)
    mail.send(7, rows.at[y2, c, first], rows.at[y2, c, first], other)
    mail.take(5, rows.at[y2, c, second], to_yp)
    mail.send(8, rows.at[y2, c, second], rows.at[y2, c, second], other)
    mail.take(11, near.at[2], other)
    own[2] = (part[ym, c].astype(F32) + near[2].astype(F32)).astype(BF)
    mail.send(16, own.at[2], got.at[1], to_ym)
    mail.take(10, near.at[1], other)
    own[1] = (part[yp, c].astype(F32) + near[1].astype(F32)).astype(BF)
    mail.send(15, own.at[1], got.at[0], to_yp)
    mail.take(7, rows.at[y2, 1 - c, first], other)
    mail.take(8, rows.at[y2, 1 - c, second], other)
    chunk(y2)
    mail.send(9, part.at[y2, 1 - c], near.at[0], other)
    fillers[0]()
    mail.take(9, near.at[0], other)
    own[0] = (part[y2, c].astype(F32) + near[0].astype(F32)).astype(BF)
    mail.send(13, own.at[0, first], far.at[0], to_yp)
    mail.send(14, own.at[0, second], far.at[1], to_ym)
    fillers[1]()
    mail.take(13, far.at[0], to_ym)
    mail.send(17, far.at[0], fin.at[0], to_yp)
    mail.take(14, far.at[1], to_yp)
    mail.send(18, far.at[1], fin.at[1], to_ym)
    fillers[2]()
    mail.take(12, near.at[3], other)
    mail.take(15, got.at[0], to_ym)
    mail.take(16, got.at[1], to_yp)
    mail.take(17, fin.at[0], to_ym)
    mail.take(18, fin.at[1], to_yp)
    total = (
        part[y, c].astype(F32)
        + near[3].astype(F32)
        + got[0].astype(F32)
        + got[1].astype(F32)
    )
    return total + fin[...].reshape(128, D).astype(F32)


def nothing():
    return None


def ctx_peers(spot):
    x, z, y, c = spot
    return [device(x, z, up1(y), c), device(x, z, down1(y), c), device(x, z, y, 1 - c)]


def mlp_forward_kernel(layer, h_ref, mid_ref, w_ref, out_ref, hr_ref, gate_ref, up_ref, *scratch):
    buffers = scratch[:7]
    w, gate, up, send_sem, recv_sem, local_sem = scratch[7:]
    rows, part = buffers[0], buffers[1]
    spot = place()
    mail = Mail(send_sem, recv_sem)
    load = pltpu.make_async_copy(w_ref.at[layer], w, local_sem.at[12])
    load.start()
    greet(ctx_peers(spot))
    stores = []
    loaded = []

    def chunk(row):
        if not loaded:
            load.wait()
            loaded.append(True)
        h = rows[row].reshape(256, D)
        g = nn(h, w[0])
        u = nn(h, w[1])
        gate[row] = g.astype(BF)
        up[row] = u.astype(BF)
        act = (g / (1.0 + jnp.exp(-g)) * u).astype(BF)
        part[row] = nt(act, w[2]).astype(BF).reshape(2, 128, D)
        k = len(stores)
        for i, (src, dst) in enumerate(((rows, hr_ref), (gate, gate_ref), (up, up_ref))):
            store = pltpu.make_async_copy(src.at[row], dst.at[row], local_sem.at[k + i])
            store.start()
            stores.append(store)

    total = mlp_exchange(mail, spot, h_ref, buffers, chunk, [nothing] * 3, nothing)
    out_ref[...] = mid_ref[...] + total
    for store in stores:
        store.wait()
    mail.finish()


def mlp_forward(layer, hidden_two, after_attn, m_full):
    anywhere = pl.BlockSpec(memory_space=pl.ANY)
    vmem = pl.BlockSpec(memory_space=pltpu.VMEM)
    return pl.pallas_call(
        functools.partial(mlp_forward_kernel, layer),
        out_shape=(
            jax.ShapeDtypeStruct((128, D), F32),
            jax.ShapeDtypeStruct((4, 2, 128, D), BF),
            jax.ShapeDtypeStruct((4, 256, FS), BF),
            jax.ShapeDtypeStruct((4, 256, FS), BF),
        ),
        in_specs=[vmem, vmem, anywhere],
        out_specs=[vmem, anywhere, anywhere, anywhere],
        scratch_shapes=mlp_scratch()
        + [
            pltpu.VMEM((3, D, FS), BF),
            pltpu.VMEM((4, 256, FS), BF),
            pltpu.VMEM((4, 256, FS), BF),
            pltpu.SemaphoreType.DMA((19,)),
            pltpu.SemaphoreType.DMA((19,)),
            pltpu.SemaphoreType.DMA((13,)),
        ],
        compiler_params=pltpu.CompilerParams(
            collective_id=8 + layer, has_side_effects=True, vmem_limit_bytes=48 * 1024 * 1024
        ),
        name="mlp_forward_%d" % layer,
    )(hidden_two, after_attn, m_full)


def mlp_backward_kernel(layer, carries, *refs):
    g_ref, w_ref, hr_ref, gate_ref, up_ref = refs[:5]
    refs = refs[5:]
    if carries:
        before, refs = refs[0], refs[1:]
    out_ref, grads = refs[:2]
    refs = refs[2:]
    if carries:
        summed, refs = refs[0], refs[1:]
    buffers, refs = refs[:7], refs[7:]
    w, hr, gate, up, act, src, send_sem, recv_sem, local_sem = refs[:9]
    rows, part = buffers[0], buffers[1]
    spot = place()
    x, z, y, c = spot
    mail = Mail(send_sem, recv_sem)
    loads = [
        pltpu.make_async_copy(a, b, local_sem.at[i])
        for i, (a, b) in enumerate(
            ((w_ref.at[layer], w), (gate_ref, gate), (up_ref, up), (hr_ref, hr))
        )
    ]
    if carries:
        older = AttentionSum(mail, 19, spot, before, refs[9:], local_sem.at[4])
        loads.append(older.load)
    for load in loads:
        load.start()
    src[...] = g_ref[...].astype(BF)
    greet(AttentionSum.peers(spot) if carries else ctx_peers(spot))
    loaded = []

    def chunk(row):
        if not loaded:
            for load in loads[:3]:
                load.wait()
            loaded.append(True)
        gz = rows[row].reshape(256, D)
        gact = nn(gz, w[2])
        g = gate[row].astype(F32)
        u = up[row].astype(F32)
        s = 1.0 / (1.0 + jnp.exp(-g))
        silu = g * s
        act[row] = (silu * u).astype(BF)
        gg = (gact * u * (s + silu * (1.0 - s))).astype(BF)
        gu = (gact * silu).astype(BF)
        gate[row] = gg
        up[row] = gu
        part[row] = (nt(gg, w[0]) + nt(gu, w[1])).astype(BF).reshape(2, 128, D)

    def weight_grad(member, left, right):
        def run():
            r = right[...].reshape(1024, FS)
            for i in range(7):
                l = left[:, :, :, 128 * i : 128 * (i + 1)].reshape(1024, 128)
                grads[member, 128 * i : 128 * (i + 1)] = tn(l, r).astype(BF)

        return run

    def gates():
        loads[3].wait()
        weight_grad(0, hr, gate)()

    fillers = [weight_grad(2, rows, act), gates, weight_grad(1, hr, up)]
    hook = nothing
    if carries:
        older.start()
        hook = older.cores
        steps = [older.plane.step_two, older.plane.step_three, older.plane.step_four]

        def joined(step, filler):
            def run():
                step()
                filler()

            return run

        fillers = [joined(step, filler) for step, filler in zip(steps, fillers)]
    out_ref[...] = mlp_exchange(mail, spot, src, buffers, chunk, fillers, hook)
    if carries:
        older.rows()
        older.last(summed)
    mail.finish()


def mlp_backward(layer, grad_output, m_full, hidden_rows, gate, up, before):
    anywhere = pl.BlockSpec(memory_space=pl.ANY)
    vmem = pl.BlockSpec(memory_space=pltpu.VMEM)
    carries = before is not None
    out_shape = [jax.ShapeDtypeStruct((128, D), F32), jax.ShapeDtypeStruct((3, D, FS), BF)]
    scratch = mlp_scratch() + [
        pltpu.VMEM((3, D, FS), BF),
        pltpu.VMEM((4, 2, 128, D), BF),
        pltpu.VMEM((4, 256, FS), BF),
        pltpu.VMEM((4, 256, FS), BF),
        pltpu.VMEM((4, 256, FS), BF),
        pltpu.VMEM((128, D), BF),
        pltpu.SemaphoreType.DMA((39,)),
        pltpu.SemaphoreType.DMA((39,)),
        pltpu.SemaphoreType.DMA((5,)),
    ]
    operands = [grad_output, m_full, hidden_rows, gate, up]
    if carries:
        out_shape.append(jax.ShapeDtypeStruct((16, 1024), F32))
        scratch += AttentionSum.scratch()
        operands.append(before)
    return pl.pallas_call(
        functools.partial(mlp_backward_kernel, layer, carries),
        out_shape=tuple(out_shape),
        in_specs=[vmem] + [anywhere] * (len(operands) - 1),
        out_specs=[vmem] * len(out_shape),
        scratch_shapes=scratch,
        compiler_params=pltpu.CompilerParams(
            collective_id=10 + layer, has_side_effects=True, vmem_limit_bytes=52 * 1024 * 1024
        ),
        name="mlp_backward_%d" % layer,
    )(*operands)


def last_sum_kernel(a_ref, out_ref, *refs):
    send_sem, recv_sem, local_sem = refs[-3:]
    spot = place()
    mail = Mail(send_sem, recv_sem)
    older = AttentionSum(mail, 0, spot, a_ref, refs[:-3], local_sem.at[0])
    older.load.start()
    greet(AttentionSum.peers(spot))
    older.start()
    older.cores()
    older.plane.step_two()
    older.plane.step_three()
    older.plane.step_four()
    older.rows()
    older.last(out_ref)
    mail.finish()


def last_sum(a_grads):
    return pl.pallas_call(
        last_sum_kernel,
        out_shape=jax.ShapeDtypeStruct((16, 1024), F32),
        in_specs=[pl.BlockSpec(memory_space=pl.ANY)],
        out_specs=pl.BlockSpec(memory_space=pltpu.VMEM),
        scratch_shapes=AttentionSum.scratch()
        + [
            pltpu.SemaphoreType.DMA((20,)),
            pltpu.SemaphoreType.DMA((20,)),
            pltpu.SemaphoreType.DMA((1,)),
        ],
        compiler_params=pltpu.CompilerParams(
            collective_id=2, has_side_effects=True, vmem_limit_bytes=32 * 1024 * 1024
        ),
        name="last_sum",
    )(a_grads)


def swap_halves(u):
    width = u.shape[1]
    lane = lax.broadcasted_iota(jnp.int32, u.shape, 1)
    return jnp.where(
        lax.rem(lane, 64) < 32, pltpu.roll(u, width - 32, 1), pltpu.roll(u, 32, 1)
    )


def normal(v):
    r = lax.rsqrt(jnp.mean(v * v, axis=-1, keepdims=True) + eps_norm)
    return v * r, r


def attention_forward_kernel(
    layer,
    x_ref, a_ref, pick_ref, vec_ref, cos_ref, sin_ref, qpos_ref, kpos_ref,
    mid_ref, h2_ref, att_ref, qs_ref, kvs_ref, probs_ref, low_ref, high_ref,
    blocks, low, high, kv, kvs, probs, heads, mask, send_sem, recv_sem, local_sem,
):
    spot = place()
    x, z, y, c = spot
    mail = Mail(send_sem, recv_sem)
    load = pltpu.make_async_copy(a_ref.at[layer], blocks, local_sem.at[0])
    load.start()
    greet(ctx_peers(spot))
    inputs = x_ref[...]
    n, r = normal(inputs)
    hidden = (n * vec_ref[0:1, :D]).astype(BF)
    load.wait()
    for g in range(8):
        group = blocks[g // 2, 2 * (g % 2) : 2 * (g % 2) + 2].reshape(256, 1024)
        low[112 * g : 112 * (g + 1)] = nn(pick_ref[0:112, :], group).astype(BF)
        high[112 * g : 112 * (g + 1)] = nn(pick_ref[112:224, :], group).astype(BF)
    stores = [
        pltpu.make_async_copy(low, low_ref, local_sem.at[1]),
        pltpu.make_async_copy(high, high_ref, local_sem.at[2]),
    ]
    packed = nn(hidden, low[...]) + vec_ref[2:3, :1024]
    values = nn(hidden, high[:, :128]) + vec_ref[2:3, 1024:]
    turned = packed * cos_ref[...] + swap_halves(packed) * sin_ref[...]
    kv[y, c, :, 0:128] = turned[:, D:].astype(BF)
    kv[y, c, :, 128:256] = values.astype(BF)
    yp, ym, y2 = up1(y), down1(y), up2(y)
    to_yp, to_ym, other = ctx_peers(spot)
    first, second = pl.ds(0, 64), pl.ds(64, 64)
    mail.send(0, kv.at[y, c], kv.at[y, c], to_yp)
    mail.send(1, kv.at[y, c], kv.at[y, c], to_ym)
    mail.send(2, kv.at[y, c], kv.at[y, c], other)
    for store in stores:
        store.start()
    for h in range(H):
        qs_ref[h] = (turned[:, HD * h : HD * (h + 1)] * HD ** (-0.5)).astype(BF)
    mask[...] = jnp.where(kpos_ref[...] <= qpos_ref[...], 0.0, 1.0)
    mail.take(0, kv.at[ym, c], to_ym)
    mail.send(3, kv.at[ym, c, first], kv.at[ym, c, first], to_yp)
    mail.send(4, kv.at[ym, c], kv.at[ym, c], other)
    mail.take(1, kv.at[yp, c], to_yp)
    mail.send(5, kv.at[yp, c, second], kv.at[yp, c, second], to_ym)
    mail.send(6, kv.at[yp, c], kv.at[yp, c], other)
    mail.take(3, kv.at[y2, c, first], to_ym)
    mail.send(7, kv.at[y2, c, first], kv.at[y2, c, first], other)
    mail.take(5, kv.at[y2, c, second], to_yp)
    mail.send(8, kv.at[y2, c, second], kv.at[y2, c, second], other)
    mail.take(2, kv.at[y, 1 - c], other)
    mail.take(4, kv.at[ym, 1 - c], other)
    mail.take(6, kv.at[yp, 1 - c], other)
    mail.take(7, kv.at[y2, 1 - c, first], other)
    mail.take(8, kv.at[y2, 1 - c, second], other)
    for i in range(4):
        kvs[i] = kv[:, :, :, HD * i : HD * (i + 1)].reshape(1024, HD)
    stores.append(pltpu.make_async_copy(kvs, kvs_ref, local_sem.at[3]))
    stores[-1].start()

    def body(i, carry):
        for k in range(KVH):
            h = i + 7 * k
            scores = nt(qs_ref[h], kvs[k])
            scores = jnp.where(mask[...] > 0.5, neg_fill, scores)
            e = jnp.exp(scores - jnp.max(scores, axis=-1, keepdims=True))
            p = (e * (1.0 / jnp.sum(e, axis=-1, keepdims=True))).astype(BF)
            probs[h] = p
            heads[h] = nn(p, kvs[2 + k]).astype(BF)
        return carry

    lax.fori_loop(0, 7, body, 0)
    stores.append(pltpu.make_async_copy(probs, probs_ref, local_sem.at[4]))
    stores[-1].start()
    attended = jnp.concatenate([heads[h] for h in range(H)], axis=1)
    att_ref[...] = attended
    mid = inputs + nn(attended, high[:, 128:])
    mid_ref[...] = mid
    h2_ref[...] = (normal(mid)[0] * vec_ref[1:2, :D]).astype(BF)
    for store in stores:
        store.wait()
    mail.finish()


def attention_forward(layer, state, a_full, pick, vectors, tables, positions):
    anywhere = pl.BlockSpec(memory_space=pl.ANY)
    vmem = pl.BlockSpec(memory_space=pltpu.VMEM)
    return pl.pallas_call(
        functools.partial(attention_forward_kernel, layer),
        out_shape=(
            jax.ShapeDtypeStruct((128, D), F32),
            jax.ShapeDtypeStruct((128, D), BF),
            jax.ShapeDtypeStruct((128, D), BF),
            jax.ShapeDtypeStruct((H, 128, HD), BF),
            jax.ShapeDtypeStruct((4, 1024, HD), BF),
            jax.ShapeDtypeStruct((H, 128, 1024), BF),
            jax.ShapeDtypeStruct((D, 1024), BF),
            jax.ShapeDtypeStruct((D, 1024), BF),
        ),
        in_specs=[vmem, anywhere] + [vmem] * 6,
        out_specs=[vmem] * 4 + [anywhere] * 4,
        scratch_shapes=[
            pltpu.VMEM((4, 4, 8, 16, 1024), BF),
            pltpu.VMEM((D, 1024), BF),
            pltpu.VMEM((D, 1024), BF),
            pltpu.VMEM((4, 2, 128, 256), BF),
            pltpu.VMEM((4, 1024, HD), BF),
            pltpu.VMEM((H, 128, 1024), BF),
            pltpu.VMEM((H, 128, HD), BF),
            pltpu.VMEM((128, 1024), F32),
            pltpu.SemaphoreType.DMA((9,)),
            pltpu.SemaphoreType.DMA((9,)),
            pltpu.SemaphoreType.DMA((5,)),
        ],
        compiler_params=pltpu.CompilerParams(
            collective_id=12 + layer, has_side_effects=True, vmem_limit_bytes=48 * 1024 * 1024
        ),
        name="attention_forward_%d" % layer,
    )(state, a_full, pick, vectors, *tables, *positions)


def attention_backward_kernel(
    g_ref, ghid2_ref, mid_ref, x_ref, vec_ref, cos_ref, sin_ref, place_ref, att_ref, qs_ref,
    kvs_ref, probs_ref, low_ref, high_ref, m_ref,
    gin_ref, a_out, m_out,
    low, high, kvs, probs, m, gs, gatt, gqs, part, near, own, got, glow, ghigh, special,
    *refs,
):
    send_sem, recv_sem, local_sem = refs[-3:]
    spot = place()
    x, z, y, c = spot
    mail = Mail(send_sem, recv_sem)
    loads = [
        pltpu.make_async_copy(src, dst, local_sem.at[i])
        for i, (src, dst) in enumerate(
            ((m_ref, m), (high_ref, high), (probs_ref, probs), (kvs_ref, kvs), (low_ref, low))
        )
    ]
    for load in loads:
        load.start()
    plane = PlaneSum(mail, 7, spot, m, 2, refs[:-3])
    yp, ym, y2 = up1(y), down1(y), up2(y)
    to_yp, to_ym, other = ctx_peers(spot)
    to_y2 = device(x, z, y2, c)
    greet([to_yp, to_ym, other, to_y2] + PlaneSum.peers(spot, 3, 2))
    loads[0].wait()
    plane.step_one()
    mid = mid_ref[...]
    n, r = normal(mid)
    ghid2 = ghid2_ref[...]
    t = ghid2 * vec_ref[1:2, :D]
    gmid = g_ref[...] + r * (t - n * jnp.mean(t * n, axis=-1, keepdims=True))
    ggain_two = jnp.sum(ghid2 * n, axis=0, keepdims=True)
    gy = gmid.astype(BF)
    loads[1].wait()
    ga = nt(gy, high[:, 128:]).astype(BF)
    for h in range(H):
        gatt[h] = ga[:, HD * h : HD * (h + 1)]
    ghigh[:, 128:] = tn(att_ref[...], gy).astype(BF)
    loads[2].wait()
    loads[3].wait()

    def body(i, carry):
        for k in range(KVH):
            h = i + 7 * k
            p = probs[h].astype(F32)
            gp = nt(gatt[h], kvs[2 + k])
            s = (p * (gp - jnp.sum(gp * p, axis=-1, keepdims=True))).astype(BF)
            gs[h] = s
            gqs[h] = nn(s, kvs[k])
        return carry

    lax.fori_loop(0, 7, body, 0)
    plane.step_two()
    for k in range(KVH):
        heads = pl.ds(7 * k, 7)
        gk = tn(qs_ref[heads].reshape(D, HD), gs[heads].reshape(D, 1024)).astype(BF)
        gv = tn(gatt[heads].reshape(D, HD), probs[heads].reshape(D, 1024)).astype(BF)
        for j in range(8):
            part[j // 2, j % 2, HD * k : HD * (k + 1)] = gk[:, 128 * j : 128 * (j + 1)]
            part[j // 2, j % 2, 128 + HD * k : 128 + HD * (k + 1)] = gv[:, 128 * j : 128 * (j + 1)]
    mail.send(0, part.at[:, 1 - c], near, other)
    gq = jnp.concatenate([gqs[h] for h in range(H)], axis=1) * HD ** (-0.5)
    gq = (gq * cos_ref[:, :D] - swap_halves(gq) * sin_ref[:, :D]).astype(BF)
    inputs = x_ref[...]
    n, r = normal(inputs)
    hidden = (n * vec_ref[0:1, :D]).astype(BF)
    mail.take(0, near, other)
    own[...] = (part[:, c].astype(F32) + near[...].astype(F32)).astype(BF)
    mail.send(1, own.at[yp], got.at[0], to_yp)
    mail.send(2, own.at[ym], got.at[1], to_ym)
    mail.send(3, own.at[y2], got.at[2], to_y2)
    glow[:, :D] = tn(hidden, gq).astype(BF)
    loads[4].wait()
    ghid = nt(gq, low[:, :D])
    plane.step_three()
    mail.take(1, got.at[0], to_ym)
    mail.take(2, got.at[1], to_yp)
    mail.take(3, got.at[2], to_y2)
    total = own[y].astype(F32) + got[0].astype(F32) + got[1].astype(F32) + got[2].astype(F32)
    total = total.T
    gk = total[:, :128]
    gk = (gk * cos_ref[:, D:] - swap_halves(gk) * sin_ref[:, D:]).astype(BF)
    gv = total[:, 128:].astype(BF)
    ghid = ghid + nt(gk, low[:, D:]) + nt(gv, high[:, :128])
    glow[:, D:] = tn(hidden, gk).astype(BF)
    ghigh[:, :128] = tn(hidden, gv).astype(BF)
    t = ghid * vec_ref[0:1, :D]
    gin_ref[...] = gmid + r * (t - n * jnp.mean(t * n, axis=-1, keepdims=True))
    ggain_one = jnp.sum(ghid * n, axis=0, keepdims=True)
    plane.step_four()
    bias_q = jnp.sum(gq.astype(F32), axis=0, keepdims=True)
    bias_k = jnp.sum(gk.astype(F32), axis=0, keepdims=True)
    bias_v = jnp.sum(gv.astype(F32), axis=0, keepdims=True)
    bias = jnp.concatenate([bias_q, bias_k], axis=1)
    row = lax.broadcasted_iota(jnp.int32, (16, 1024), 0)
    row_last = jnp.concatenate([ggain_two, bias_v], axis=1)
    for g in range(8):
        row_seven = jnp.concatenate([ggain_one, bias[:, 128 * g : 128 * (g + 1)]], axis=1)
        extra = jnp.where(row == 0, row_seven, jnp.where(row == 1, row_last, 0.0))
        special[...] = extra.astype(BF)
        block = (
            nn(place_ref[0], glow[112 * g : 112 * (g + 1)])
            + nn(place_ref[1], ghigh[112 * g : 112 * (g + 1)])
            + nn(place_ref[2, :, 0:16], special[...])
        ).astype(BF)
        for k in range(16):
            ctx = k % 8
            a_out[ctx % 2, ctx // 2, g // 2, 2 * (g % 2) + k // 8] = block[16 * k : 16 * (k + 1)]
    plane.step_five(m_out)
    mail.finish()


def attention_backward(layer, grad_output, grad_hidden_two, kept, vectors, tables, place_rows, m_grads):
    x, mid, att, qs, kvs, probs, low, high = kept
    anywhere = pl.BlockSpec(memory_space=pl.ANY)
    vmem = pl.BlockSpec(memory_space=pltpu.VMEM)
    return pl.pallas_call(
        attention_backward_kernel,
        out_shape=(
            jax.ShapeDtypeStruct((128, D), F32),
            jax.ShapeDtypeStruct((2, 4, 4, 4, 16, 1024), BF),
            jax.ShapeDtypeStruct((3, 56, FS), F32),
        ),
        in_specs=[vmem] * 10 + [anywhere] * 5,
        out_specs=[vmem] * 3,
        scratch_shapes=[
            pltpu.VMEM((D, 1024), BF),
            pltpu.VMEM((D, 1024), BF),
            pltpu.VMEM((4, 1024, HD), BF),
            pltpu.VMEM((H, 128, 1024), BF),
            pltpu.VMEM((3, 4, 4, 56, FS), BF),
            pltpu.VMEM((H, 128, 1024), BF),
            pltpu.VMEM((H, 128, HD), BF),
            pltpu.VMEM((H, 128, HD), F32),
            pltpu.VMEM((4, 2, 256, 128), BF),
            pltpu.VMEM((4, 256, 128), BF),
            pltpu.VMEM((4, 256, 128), BF),
            pltpu.VMEM((3, 256, 128), BF),
            pltpu.VMEM((D, 1024), BF),
            pltpu.VMEM((D, 1024), BF),
            pltpu.VMEM((16, 1024), BF),
        ]
        + PlaneSum.scratch(3, 2, 56, FS)
        + [
            pltpu.SemaphoreType.DMA((23,)),
            pltpu.SemaphoreType.DMA((23,)),
            pltpu.SemaphoreType.DMA((5,)),
        ],
        compiler_params=pltpu.CompilerParams(
            collective_id=14 + layer, has_side_effects=True, vmem_limit_bytes=56 * 1024 * 1024
        ),
        name="attention_backward_%d" % layer,
    )(
        grad_output, grad_hidden_two, mid, x, vectors, *tables, place_rows, att, qs,
        kvs, probs, low, high, m_grads.reshape(3, 4, 4, 56, FS),
    )


def select_matrix():
    pick = np.zeros((226, 256), np.float32)
    for k in range(16):
        for r in range(7):
            pick[7 * k + r, 16 * k + r] = 1
            pick[112 + 7 * k + r, 16 * k + 8 + r] = 1
        pick[224, 16 * k + 7] = 1
        pick[225, 16 * k + 15] = 1
    return pick


def pack_attention(gain_one, w_qkv, b_qkv, w_out, gain_two):
    index = lax.axis_index("dp") * 8 + lax.axis_index("ctx")
    within = lax.rem(index, 16)
    zeros = jnp.zeros((LAYERS, D), BF)
    one = lax.dynamic_update_slice(zeros, gain_one, (0, 7 * index))
    two = lax.dynamic_update_slice(zeros, gain_two, (0, 7 * index))
    bias = lax.dynamic_update_slice(jnp.zeros((LAYERS, 256), BF), b_qkv, (0, 9 * within))
    row_seven = jnp.concatenate([one, bias[:, :128]], axis=1)[:, None]
    row_last = jnp.concatenate([two, bias[:, 128:]], axis=1)[:, None]
    joined = jnp.concatenate([w_qkv, w_out], axis=2)
    return jnp.concatenate([joined[:, :, :1024], row_seven, joined[:, :, 1024:], row_last], axis=1)


def small_vectors(block):
    spare = jnp.stack([block[:, :, :, 7], block[:, :, :, 15]]).astype(F32)
    spare = jnp.sum(spare.reshape(2, 8, 16, 1024), axis=2)
    gains = jnp.pad(jnp.sum(spare[:, :, :D], axis=1), ((0, 0), (0, QKV - D)))
    bias = jnp.concatenate([spare[0, :, D:], spare[1, :, D : D + 16]], axis=1).reshape(1, QKV)
    return jnp.concatenate([gains, bias], axis=0)


def unpack_attention_grads(block):
    index = lax.axis_index("dp") * 8 + lax.axis_index("ctx")
    within = lax.rem(index, 16)
    qkv = jnp.concatenate([block[:7], block[8:15, :128]], axis=1)
    out = block[8:15, 128:]
    gain_one = lax.dynamic_slice(block[7], (7 * index,), (7,))
    gain_two = lax.dynamic_slice(block[15], (7 * index,), (7,))
    qk_bias = lax.dynamic_slice(block[7], (D + 8 * within,), (8,))
    value_bias = lax.dynamic_slice(block[15], (D + index,), (1,))
    return gain_one, qkv, qk_bias, value_bias, out, gain_two


def shards(
    tokens, cotangent, span_order, gain_one, w_qkv, b_qkv, w_out, gain_two, w_gate, w_up, w_down
):
    sequences, local_len, width = tokens.shape
    span_len = local_len // 2
    ctx_place = lax.axis_index("ctx")
    offsets = jnp.arange(span_len, dtype=jnp.int32)
    local_spans = lax.dynamic_slice_in_dim(span_order, 2 * ctx_place, 2)
    local_pos = (local_spans[:, None] * span_len + offsets[None, :]).reshape(local_len)
    all_pos = (span_order[:, None] * span_len + offsets[None, :]).reshape(-1)
    positions = (local_pos[:, None], all_pos[None, :])
    frequency = rope_base ** (-jnp.arange(HD // 2, dtype=F32) * 2.0 / HD)
    angles = local_pos.astype(F32)[:, None] * frequency[None, :]
    cosine, sine = jnp.cos(angles), jnp.sin(angles)
    tables = (jnp.tile(cosine, (1, 32)), jnp.tile(jnp.concatenate([-sine, sine], axis=1), (1, 16)))
    chosen = select_matrix()
    pick = jnp.asarray(chosen[:224], BF)
    spread = np.zeros((3, 256, 112), np.float32)
    spread[0], spread[1], spread[2, :, :2] = chosen[:112].T, chosen[112:224].T, chosen[224:].T
    spread = jnp.asarray(spread, BF)

    m_block = jnp.stack([w_gate, w_up, w_down.transpose(0, 2, 1)], axis=1).reshape(6, 56, FS)
    a_block = pack_attention(gain_one, w_qkv, b_qkv, w_out, gain_two)
    m_full, a_full = gather_weights(m_block, a_block)
    m_full = m_full.reshape(2, 3, D, FS)
    vectors = [small_vectors(a_full[l]) for l in range(LAYERS)]
    state = tokens.reshape(local_len, width).astype(F32)
    kept_layers = []
    for l in range(LAYERS):
        mid, hidden_two, *kept = attention_forward(
            l, state, a_full, pick, vectors[l], tables, positions
        )
        output, *kept_mlp = mlp_forward(l, hidden_two, mid, m_full)
        kept_layers.append(((state, mid) + tuple(kept), kept_mlp))
        state = output
    grad_state = cotangent.reshape(local_len, width).astype(F32)
    a_grads = None
    sums = [None, None]
    a_sums = [None, None]
    for l in reversed(range(LAYERS)):
        kept, kept_mlp = kept_layers[l]
        grad_hidden_two, m_grads, *older = mlp_backward(l, grad_state, m_full, *kept_mlp, a_grads)
        if older:
            a_sums[l + 1] = older[0]
        grad_state, a_grads, sums[l] = attention_backward(
            l, grad_state, grad_hidden_two, kept, vectors[l], tables, spread, m_grads
        )
    a_sums[0] = last_sum(a_grads)
    grad_layers = [
        unpack_attention_grads(a_sums[l]) + (sums[l][0], sums[l][1], sums[l][2].T)
        for l in range(LAYERS)
    ]
    stacks = [jnp.stack([sums[member] for sums in grad_layers]) for member in range(9)]
    output = state.astype(BF).reshape(sequences, local_len, width)
    input_grad = grad_state.reshape(sequences, local_len, width)
    return (output, input_grad) + tuple(stacks)


def solution(mesh):
    return jax.shard_map(
        shards,
        mesh=mesh,
        in_specs=(
            P("dp", "ctx", None),
            P("dp", "ctx", None),
            P(),
            P(None, ("dp", "ctx")),
            P(None, ("dp", "ctx"), None),
            P(None, ("dp", "ctx")),
            P(None, ("dp", "ctx"), None),
            P(None, ("dp", "ctx")),
            P(None, "dp", "ctx"),
            P(None, "dp", "ctx"),
            P(None, "ctx", "dp"),
        ),
        out_specs=(
            P("dp", "ctx", None),
            P("dp", "ctx", None),
            P(None, ("dp", "ctx")),
            P(None, ("dp", "ctx"), None),
            P(None, ("dp", "ctx")),
            P(None, ("dp", "ctx")),
            P(None, ("dp", "ctx"), None),
            P(None, ("dp", "ctx")),
            P(None, "dp", "ctx"),
            P(None, "dp", "ctx"),
            P(None, "ctx", "dp"),
        ),
        check_vma=False,
    )
```

```python
import functools

import jax
import jax.numpy as jnp
import numpy as np
from jax import lax
from jax.experimental import pallas as pl
from jax.experimental.pallas import tpu as pltpu
from jax.sharding import PartitionSpec as P

H = 14
KVH = 2
HD = 64
LAYERS = 2
D = 896
QKV = 1152
FS = 608
MESH = pl.DeviceIdType.MESH
BF = jnp.bfloat16
F32 = jnp.float32

eps_norm = 1e-06
rope_base = 1000000.0
neg_fill = -1e30


def place():
    dp = lax.axis_index("dp")
    ctx = lax.axis_index("ctx")
    return lax.div(dp, 4), lax.rem(dp, 4), lax.div(ctx, 2), lax.rem(ctx, 2)


def up1(v):
    return lax.rem(v + 1, 4)


def up2(v):
    return lax.rem(v + 2, 4)


def down1(v):
    return lax.rem(v + 3, 4)


def device(x, z, y, c):
    return (x * 4 + z, y * 2 + c)


def greet(peers):
    barrier = pltpu.get_barrier_semaphore()
    for peer in peers:
        pl.semaphore_signal(barrier, inc=1, device_id=peer, device_id_type=MESH)
    pl.semaphore_wait(barrier, len(peers))


class Mail:
    def __init__(self, send_sem, recv_sem, base=0, sent=None):
        self.send_sem = send_sem
        self.recv_sem = recv_sem
        self.base = base
        self.sent = [] if sent is None else sent

    def shifted(self, base):
        return Mail(self.send_sem, self.recv_sem, self.base + base, self.sent)

    def send(self, slot, src, dst, target):
        copy = pltpu.make_async_remote_copy(
            src_ref=src,
            dst_ref=dst,
            send_sem=self.send_sem.at[self.base + slot],
            recv_sem=self.recv_sem.at[self.base + slot],
            device_id=target,
            device_id_type=MESH,
        )
        copy.start()
        self.sent.append(copy)

    def take(self, slot, dst, source):
        pltpu.make_async_remote_copy(
            src_ref=dst,
            dst_ref=dst,
            send_sem=self.send_sem.at[self.base + slot],
            recv_sem=self.recv_sem.at[self.base + slot],
            device_id=source,
            device_id_type=MESH,
        ).wait_recv()

    def finish(self):
        for copy in self.sent:
            copy.wait_send()


class LineGather:
    slots = 9

    def __init__(self, mail, base, spot, plane, full, local_sem):
        self.mail, self.base, self.spot, self.plane, self.full = mail, base, spot, plane, full
        y, c = spot[2:]
        self.own = pltpu.make_async_copy(plane, self.part(y, c), local_sem)

    def part(self, row, core, half=None):
        lead = pl.ds(0, 4) if half is None else pl.ds(2 * half, 2)
        return self.full.at[lead, pl.ds(0, 4), 2 * row + core]

    def send(self, slot, src, dst, target):
        self.mail.send(self.base + slot, src, dst, target)

    def take(self, slot, dst, source):
        self.mail.take(self.base + slot, dst, source)

    def names(self):
        y, c = self.spot[2:]
        return (y, c, up1(y), down1(y), up2(y)) + tuple(ctx_peers(self.spot))

    def step_one(self):
        y, c, yp, ym, y2, to_yp, to_ym, other = self.names()
        self.send(0, self.plane, self.part(y, c), to_yp)
        self.send(1, self.plane, self.part(y, c), to_ym)
        self.send(2, self.plane, self.part(y, c), other)
        self.own.start()

    def step_two(self):
        y, c, yp, ym, y2, to_yp, to_ym, other = self.names()
        self.take(0, self.part(ym, c), to_ym)
        self.send(3, self.part(ym, c, 0), self.part(ym, c, 0), to_yp)
        self.send(4, self.part(ym, c), self.part(ym, c), other)
        self.take(1, self.part(yp, c), to_yp)
        self.send(5, self.part(yp, c, 1), self.part(yp, c, 1), to_ym)
        self.send(6, self.part(yp, c), self.part(yp, c), other)

    def step_three(self):
        y, c, yp, ym, y2, to_yp, to_ym, other = self.names()
        self.take(3, self.part(y2, c, 0), to_ym)
        self.send(7, self.part(y2, c, 0), self.part(y2, c, 0), other)
        self.take(5, self.part(y2, c, 1), to_yp)
        self.send(8, self.part(y2, c, 1), self.part(y2, c, 1), other)

    def step_four(self):
        y, c, yp, ym, y2, to_yp, to_ym, other = self.names()
        self.own.wait()
        self.take(2, self.part(y, 1 - c), other)
        self.take(4, self.part(ym, 1 - c), other)
        self.take(6, self.part(yp, 1 - c), other)
        self.take(7, self.part(y2, 1 - c, 0), other)
        self.take(8, self.part(y2, 1 - c, 1), other)


class PlaneGather:
    slots = 15

    def __init__(self, mail, base, spot, own, full, local_sem):
        self.mail, self.base, self.spot, self.block, self.full = mail, base, spot, own, full
        x, z = spot[:2]
        self.own = pltpu.make_async_copy(own, full.at[:, x, z], local_sem)

    def names(self):
        x, z, y, c = self.spot
        xp, xm, zp, zm = up1(x), down1(x), up1(z), down1(z)
        to = (device(xp, z, y, c), device(xm, z, y, c), device(x, zp, y, c), device(x, zm, y, c))
        return x, z, xp, xm, zp, zm, up2(x), up2(z), to

    def pass_on(self, slot, where, target):
        region = self.full.at[where]
        self.mail.send(self.base + slot, region, region, target)

    def take(self, slot, where, source):
        self.mail.take(self.base + slot, self.full.at[where], source)

    pair, one, two, three = pl.ds(0, 2), pl.ds(0, 1), pl.ds(1, 1), pl.ds(2, 1)
    every, lo, hi = pl.ds(0, 4), pl.ds(0, 2), pl.ds(2, 2)

    def step_one(self):
        x, z, xp, xm, zp, zm, x2, z2, (to_xp, to_xm, to_zp, to_zm) = self.names()
        self.own.start()
        for slot, slabs, target in (
            (0, self.pair, to_xp),
            (1, self.pair, to_xm),
            (2, self.three, to_zp),
            (3, self.three, to_zm),
        ):
            self.mail.send(
                self.base + slot, self.block.at[slabs], self.full.at[slabs, x, z], target
            )

    def step_two(self):
        x, z, xp, xm, zp, zm, x2, z2, (to_xp, to_xm, to_zp, to_zm) = self.names()
        self.take(0, (self.pair, xm, z), to_xm)
        self.pass_on(4, (self.one, xm, z), to_xp)
        self.take(1, (self.pair, xp, z), to_xp)
        self.pass_on(5, (self.two, xp, z), to_xm)
        self.take(2, (self.three, x, zm), to_zm)
        self.pass_on(6, (self.three, x, zm), to_zp)
        self.take(3, (self.three, x, zp), to_zp)

    def step_three(self):
        x, z, xp, xm, zp, zm, x2, z2, (to_xp, to_xm, to_zp, to_zm) = self.names()
        self.take(4, (self.one, x2, z), to_xm)
        self.take(5, (self.two, x2, z), to_xp)
        self.own.wait()
        self.pass_on(7, (self.pair, self.every, z), to_zp)
        self.pass_on(8, (self.pair, self.every, z), to_zm)
        self.take(6, (self.three, x, z2), to_zm)
        self.pass_on(9, (self.three, x, self.every), to_xp)
        self.pass_on(10, (self.three, x, self.every), to_xm)

    def step_four(self):
        x, z, xp, xm, zp, zm, x2, z2, (to_xp, to_xm, to_zp, to_zm) = self.names()
        self.take(7, (self.pair, self.every, zm), to_zm)
        self.pass_on(11, (self.one, self.every, zm), to_zp)
        self.take(8, (self.pair, self.every, zp), to_zp)
        self.pass_on(12, (self.two, self.every, zp), to_zm)
        self.take(9, (self.three, xm, self.every), to_xm)
        self.pass_on(13, (self.three, xm, self.lo), to_xp)
        self.take(10, (self.three, xp, self.every), to_xp)
        self.pass_on(14, (self.three, xp, self.hi), to_xm)

    def step_five(self):
        x, z, xp, xm, zp, zm, x2, z2, (to_xp, to_xm, to_zp, to_zm) = self.names()
        self.take(11, (self.one, self.every, z2), to_zm)
        self.take(12, (self.two, self.every, z2), to_zp)
        self.take(13, (self.three, x2, self.lo), to_xm)
        self.take(14, (self.three, x2, self.hi), to_xp)


def ring_peers(spot):
    x, z, y, c = spot
    return [
        device(up1(x), z, y, c),
        device(down1(x), z, y, c),
        device(x, up1(z), y, c),
        device(x, down1(z), y, c),
    ]


def ctx_peers(spot):
    x, z, y, c = spot
    return [device(x, z, up1(y), c), device(x, z, down1(y), c), device(x, z, y, 1 - c)]


def first_gather_kernel(
    one_ref, qkv_ref, bias_ref, out_ref, two_ref,
    full, plane_out,
    rows, vectors, offsets, plane, send_sem, recv_sem, local_sem,
):
    spot = place()
    x, z, y, c = spot
    index = (x * 4 + z) * 8 + 2 * y + c
    mail = Mail(send_sem, recv_sem)
    vectors[...] = jnp.zeros_like(vectors)
    offsets[...] = jnp.zeros_like(offsets)
    vectors[0:2, 0:7] = one_ref[...].astype(F32)
    vectors[2:4, 0:7] = two_ref[...].astype(F32)
    offsets[0:2, 0:9] = bias_ref[...].astype(F32)
    gains = pltpu.roll(vectors[...], 7 * index, 1)
    bias = pltpu.roll(offsets[...], 9 * index - 128 * lax.div(index, 16), 1)
    for l in range(LAYERS):
        rows[l, 0:7, :] = qkv_ref[l, :, :1024].astype(F32)
        rows[l, 8:15, 0:128] = qkv_ref[l, :, 1024:].astype(F32)
        rows[l, 8:15, 128:1024] = out_ref[l].astype(F32)
        rows[l, 7:8, 0:D] = gains[l : l + 1, :D]
        rows[l, 15:16, 0:D] = gains[2 + l : 3 + l, :D]
        rows[l, 7:8, D:1024] = bias[l : l + 1, :128]
        rows[l, 15:16, D:1024] = bias[l : l + 1, 128:]
    plane[:, x, z] = rows[...].astype(BF)
    xp, xm, zp, zm, x2, z2 = up1(x), down1(x), up1(z), down1(z), up2(x), up2(z)
    to_xp, to_xm, to_zp, to_zm = ring_peers(spot)
    greet(ring_peers(spot) + ctx_peers(spot))

    def pass_on(slot, where, target):
        mail.send(slot, plane.at[where], plane.at[where], target)

    def take(slot, where, source):
        mail.take(slot, plane.at[where], source)

    both, every = pl.ds(0, 2), pl.ds(0, 4)
    pass_on(0, (both, x, z), to_xp)
    pass_on(1, (both, x, z), to_xm)
    take(0, (both, xm, z), to_xm)
    pass_on(2, (0, xm, z), to_xp)
    take(1, (both, xp, z), to_xp)
    pass_on(3, (1, xp, z), to_xm)
    take(2, (0, x2, z), to_xm)
    take(3, (1, x2, z), to_xp)
    pass_on(4, (both, every, z), to_zp)
    pass_on(5, (both, every, z), to_zm)
    take(4, (both, every, zm), to_zm)
    pass_on(6, (0, every, zm), to_zp)
    take(5, (both, every, zp), to_zp)
    pass_on(7, (1, every, zp), to_zm)
    take(6, (0, every, z2), to_zm)
    take(7, (1, every, z2), to_zp)
    line = LineGather(mail, 8, spot, plane.at[0], full, local_sem.at[0])
    line.step_one()
    kept = pltpu.make_async_copy(plane.at[1], plane_out, local_sem.at[1])
    kept.start()
    line.step_two()
    line.step_three()
    line.step_four()
    kept.wait()
    mail.finish()


def first_gather(gain_one, w_qkv, b_qkv, w_out, gain_two):
    return pl.pallas_call(
        first_gather_kernel,
        out_shape=(
            jax.ShapeDtypeStruct((4, 4, 8, 16, 1024), BF),
            jax.ShapeDtypeStruct((4, 4, 16, 1024), BF),
        ),
        in_specs=[pl.BlockSpec(memory_space=pltpu.VMEM)] * 5,
        out_specs=[pl.BlockSpec(memory_space=pl.ANY)] * 2,
        scratch_shapes=[
            pltpu.VMEM((2, 16, 1024), F32),
            pltpu.VMEM((8, 1024), F32),
            pltpu.VMEM((8, 256), F32),
            pltpu.VMEM((2, 4, 4, 16, 1024), BF),
            pltpu.SemaphoreType.DMA((17,)),
            pltpu.SemaphoreType.DMA((17,)),
            pltpu.SemaphoreType.DMA((2,)),
        ],
        compiler_params=pltpu.CompilerParams(
            collective_id=1, has_side_effects=True, vmem_limit_bytes=16 * 1024 * 1024
        ),
        name="first_gather",
    )(gain_one, w_qkv, b_qkv, w_out, gain_two)


class PlaneSum:
    def __init__(self, mail, base, spot, g, cut, buffers):
        self.mail, self.base, self.spot, self.g, self.cut = mail, base, spot, g, cut
        self.count = g.shape[0]
        self.buffers = buffers

    @staticmethod
    def scratch(slabs, cut, rows, columns):
        rest = slabs - cut
        out = [
            pltpu.VMEM((2, cut, 2, rows, columns), BF),
            pltpu.VMEM((2, cut, 4, rows, columns), BF),
            pltpu.VMEM((2, rest, 2, rows, columns), BF),
            pltpu.VMEM((2, rest, 4, rows, columns), BF),
            pltpu.VMEM((2, cut // 2, rows, columns), BF),
            pltpu.VMEM((2, cut, rows, columns), BF),
            pltpu.VMEM((2, max(rest // 2, 1), rows, columns), BF),
            pltpu.VMEM((2, rest, rows, columns), BF),
        ]
        return out

    @staticmethod
    def peers(spot, slabs, cut):
        x, z, y, c = spot
        near = [device(up1(x), z, y, c), device(down1(x), z, y, c), device(x, up1(z), y, c), device(x, down1(z), y, c)]
        return near + ([device(x, up2(z), y, c)] if slabs - cut == 1 else [])

    def names(self):
        x, z, y, c = self.spot
        xp, xm, zp, zm = up1(x), down1(x), up1(z), down1(z)
        to = (device(xp, z, y, c), device(xm, z, y, c), device(x, zp, y, c), device(x, zm, y, c))
        return x, z, xp, xm, zp, zm, up2(x), up2(z), to

    def send(self, slot, src, dst, target):
        self.mail.send(self.base + slot, src, dst, target)

    def take(self, slot, dst, source):
        self.mail.take(self.base + slot, dst, source)

    def add(self, where, extra):
        self.g[where] = (self.g[where].astype(F32) + extra.astype(F32)).astype(BF)

    def step_one(self):
        x, z, xp, xm, zp, zm, x2, z2, (to_xp, to_xm, to_zp, to_zm) = self.names()
        fa, ga, fb, gb, pa, qa, pb, qb = self.buffers
        sa, sb = pl.ds(0, self.cut), pl.ds(self.cut, self.count - self.cut)
        lo, hi = pl.ds(0, 2), pl.ds(2, 2)
        self.send(0, self.g.at[sa, lo, z2], fa.at[0], to_zp)
        self.send(1, self.g.at[sa, hi, z2], fa.at[1], to_zm)
        self.send(2, self.g.at[sb, x2, lo], fb.at[0], to_xp)
        self.send(3, self.g.at[sb, x2, hi], fb.at[1], to_xm)

    def step_two(self):
        x, z, xp, xm, zp, zm, x2, z2, (to_xp, to_xm, to_zp, to_zm) = self.names()
        fa, ga, fb, gb, pa, qa, pb, qb = self.buffers
        sa, sb = pl.ds(0, self.cut), pl.ds(self.cut, self.count - self.cut)
        lo, hi, every = pl.ds(0, 2), pl.ds(2, 2), pl.ds(0, 4)
        self.take(0, fa.at[0], to_zm)
        self.add((sa, lo, zp), fa[0])
        self.send(4, self.g.at[sa, every, zp], ga.at[0], to_zp)
        self.take(2, fb.at[0], to_xm)
        self.add((sb, xp, lo), fb[0])
        self.send(6, self.g.at[sb, xp, every], gb.at[0], to_xp)
        self.take(1, fa.at[1], to_zp)
        self.add((sa, hi, zm), fa[1])
        self.send(5, self.g.at[sa, every, zm], ga.at[1], to_zm)
        self.take(3, fb.at[1], to_xp)
        self.add((sb, xm, hi), fb[1])
        self.send(7, self.g.at[sb, xm, every], gb.at[1], to_xm)

    def step_three(self):
        x, z, xp, xm, zp, zm, x2, z2, (to_xp, to_xm, to_zp, to_zm) = self.names()
        fa, ga, fb, gb, pa, qa, pb, qb = self.buffers
        y, c = self.spot[2:]
        cut, rest = self.cut, self.count - self.cut
        sa, sb = pl.ds(0, cut), pl.ds(cut, rest)
        every = pl.ds(0, 4)
        self.take(4, ga.at[0], to_zm)
        self.take(5, ga.at[1], to_zp)
        self.add((sa, every, z), ga[0].astype(F32) + ga[1].astype(F32))
        self.send(8, self.g.at[pl.ds(0, cut // 2), x2, z], pa.at[0], to_xp)
        self.send(9, self.g.at[pl.ds(cut // 2, cut // 2), x2, z], pa.at[1], to_xm)
        self.take(6, gb.at[0], to_xm)
        self.take(7, gb.at[1], to_xp)
        self.add((sb, x, every), gb[0].astype(F32) + gb[1].astype(F32))
        if rest == 1:
            self.send(10, self.g.at[sb, x, z2], pb.at[0], device(x, z2, y, c))
            self.send(14, self.g.at[sb, x, zp], qb.at[0], to_zp)
            self.send(15, self.g.at[sb, x, zm], qb.at[1], to_zm)
        else:
            self.send(10, self.g.at[pl.ds(cut, rest // 2), x, z2], pb.at[0], to_zp)
            self.send(11, self.g.at[pl.ds(cut + rest // 2, rest // 2), x, z2], pb.at[1], to_zm)

    def step_four(self):
        x, z, xp, xm, zp, zm, x2, z2, (to_xp, to_xm, to_zp, to_zm) = self.names()
        fa, ga, fb, gb, pa, qa, pb, qb = self.buffers
        cut, rest = self.cut, self.count - self.cut
        sa, sb = pl.ds(0, cut), pl.ds(cut, rest)
        self.take(8, pa.at[0], to_xm)
        self.add((pl.ds(0, cut // 2), xp, z), pa[0])
        self.send(12, self.g.at[sa, xp, z], qa.at[0], to_xp)
        self.take(9, pa.at[1], to_xp)
        self.add((pl.ds(cut // 2, cut // 2), xm, z), pa[1])
        self.send(13, self.g.at[sa, xm, z], qa.at[1], to_xm)
        if rest > 1:
            self.take(10, pb.at[0], to_zm)
            self.add((pl.ds(cut, rest // 2), x, zp), pb[0])
            self.send(14, self.g.at[sb, x, zp], qb.at[0], to_zp)
            self.take(11, pb.at[1], to_zp)
            self.add((pl.ds(cut + rest // 2, rest // 2), x, zm), pb[1])
            self.send(15, self.g.at[sb, x, zm], qb.at[1], to_zm)

    def step_five(self, out):
        x, z, xp, xm, zp, zm, x2, z2, (to_xp, to_xm, to_zp, to_zm) = self.names()
        fa, ga, fb, gb, pa, qa, pb, qb = self.buffers
        y, c = self.spot[2:]
        cut, rest = self.cut, self.count - self.cut
        sa, sb = pl.ds(0, cut), pl.ds(cut, rest)
        self.take(12, qa.at[0], to_xm)
        self.take(13, qa.at[1], to_xp)
        out[sa] = (
            self.g[sa, x, z].astype(F32) + qa[0].astype(F32) + qa[1].astype(F32)
        ).astype(out.dtype)
        self.take(14, qb.at[0], to_zm)
        self.take(15, qb.at[1], to_zp)
        total = self.g[sb, x, z].astype(F32) + qb[0].astype(F32) + qb[1].astype(F32)
        if rest == 1:
            self.take(10, pb.at[0], device(x, z2, y, c))
            total = total + pb[0].astype(F32)
        out[sb] = total.astype(out.dtype)


class AttentionSum:
    def __init__(self, mail, base, spot, a_ref, refs, load_sem):
        self.mail, self.base, self.spot, self.a_ref = mail, base, spot, a_ref
        self.mine, self.near, self.block, self.got = refs[:4]
        self.plane = PlaneSum(mail, base + 4, spot, self.mine, 2, refs[4:])
        self.load = pltpu.make_async_copy(a_ref.at[spot[3]], self.mine, load_sem)

    @staticmethod
    def scratch():
        return [
            pltpu.VMEM((4, 4, 4, 16, 1024), BF),
            pltpu.VMEM((4, 4, 4, 16, 1024), BF),
            pltpu.VMEM((4, 16, 1024), BF),
            pltpu.VMEM((3, 16, 1024), BF),
        ] + PlaneSum.scratch(4, 2, 16, 1024)

    slots = 20

    @staticmethod
    def peers(spot):
        x, z, y, c = spot
        return PlaneSum.peers(spot, 4, 2) + [
            device(x, z, up1(y), c),
            device(x, z, up2(y), c),
            device(x, z, down1(y), c),
            device(x, z, y, 1 - c),
        ]

    def start(self):
        x, z, y, c = self.spot
        self.mail.send(self.base, self.a_ref.at[1 - c], self.near, device(x, z, y, 1 - c))

    def cores(self):
        x, z, y, c = self.spot
        self.load.wait()
        self.mail.take(self.base, self.near, device(x, z, y, 1 - c))

        def body(i, carry):
            self.mine[i] = (self.mine[i].astype(F32) + self.near[i].astype(F32)).astype(BF)
            return carry

        lax.fori_loop(0, 4, body, 0)
        self.plane.step_one()

    def rows(self):
        x, z, y, c = self.spot
        self.plane.step_five(self.block)
        for k, step in enumerate((up1, up2, down1)):
            to = device(x, z, step(y), c)
            self.mail.send(self.base + 1 + k, self.block.at[step(y)], self.got.at[k], to)

    def last(self, out):
        x, z, y, c = self.spot
        total = self.block[y].astype(F32)
        for k, step in enumerate((down1, up2, up1)):
            self.mail.take(self.base + 1 + k, self.got.at[k], device(x, z, step(y), c))
            total = total + self.got[k].astype(F32)
        out[...] = total


def nn(left, right):
    return jnp.dot(left, right, preferred_element_type=F32)


def nt(left, right):
    return lax.dot_general(left, right, (((1,), (1,)), ((), ())), preferred_element_type=F32)


def tn(left, right):
    return lax.dot_general(left, right, (((0,), (0,)), ((), ())), preferred_element_type=F32)


def mlp_scratch():
    return [
        pltpu.VMEM((4, 2, 128, D), BF),
        pltpu.VMEM((4, 2, 128, D), BF),
        pltpu.VMEM((4, 128, D), BF),
        pltpu.VMEM((3, 128, D), BF),
        pltpu.VMEM((2, 64, D), BF),
        pltpu.VMEM((2, 64, D), BF),
        pltpu.VMEM((2, 128, D), BF),
    ]


def mlp_exchange(mail, spot, src, buffers, chunk, fillers, hook):
    rows, part, near, own, far, fin, got = buffers
    x, z, y, c = spot
    yp, ym, y2 = up1(y), down1(y), up2(y)
    to_yp, to_ym, other = device(x, z, yp, c), device(x, z, ym, c), device(x, z, y, 1 - c)
    first, second = pl.ds(0, 64), pl.ds(64, 64)
    mail.send(0, src, rows.at[y, c], to_yp)
    mail.send(1, src, rows.at[y, c], to_ym)
    mail.send(2, src, rows.at[y, c], other)
    rows[y, c] = src[...]
    mail.take(2, rows.at[y, 1 - c], other)
    chunk(y)
    mail.send(12, part.at[y, 1 - c], near.at[3], other)
    mail.take(0, rows.at[ym, c], to_ym)
    mail.send(3, rows.at[ym, c, first], rows.at[ym, c, first], to_yp)
    mail.send(4, rows.at[ym, c], rows.at[ym, c], other)
    mail.take(1, rows.at[yp, c], to_yp)
    mail.send(5, rows.at[yp, c, second], rows.at[yp, c, second], to_ym)
    mail.send(6, rows.at[yp, c], rows.at[yp, c], other)
    mail.take(4, rows.at[ym, 1 - c], other)
    chunk(ym)
    mail.send(11, part.at[ym, 1 - c], near.at[2], other)
    hook()
    mail.take(6, rows.at[yp, 1 - c], other)
    chunk(yp)
    mail.send(10, part.at[yp, 1 - c], near.at[1], other)
    mail.take(3, rows.at[y2, c, first], to_ym)
    mail.send(7, rows.at[y2, c, first], rows.at[y2, c, first], other)
    mail.take(5, rows.at[y2, c, second], to_yp)
    mail.send(8, rows.at[y2, c, second], rows.at[y2, c, second], other)
    mail.take(11, near.at[2], other)
    own[2] = (part[ym, c].astype(F32) + near[2].astype(F32)).astype(BF)
    mail.send(16, own.at[2], got.at[1], to_ym)
    mail.take(10, near.at[1], other)
    own[1] = (part[yp, c].astype(F32) + near[1].astype(F32)).astype(BF)
    mail.send(15, own.at[1], got.at[0], to_yp)
    mail.take(7, rows.at[y2, 1 - c, first], other)
    mail.take(8, rows.at[y2, 1 - c, second], other)
    chunk(y2)
    mail.send(9, part.at[y2, 1 - c], near.at[0], other)
    fillers[0]()
    mail.take(9, near.at[0], other)
    own[0] = (part[y2, c].astype(F32) + near[0].astype(F32)).astype(BF)
    mail.send(13, own.at[0, first], far.at[0], to_yp)
    mail.send(14, own.at[0, second], far.at[1], to_ym)
    fillers[1]()
    mail.take(13, far.at[0], to_ym)
    mail.send(17, far.at[0], fin.at[0], to_yp)
    mail.take(14, far.at[1], to_yp)
    mail.send(18, far.at[1], fin.at[1], to_ym)
    fillers[2]()
    mail.take(12, near.at[3], other)
    mail.take(15, got.at[0], to_ym)
    mail.take(16, got.at[1], to_yp)
    mail.take(17, fin.at[0], to_ym)
    mail.take(18, fin.at[1], to_yp)
    total = (
        part[y, c].astype(F32)
        + near[3].astype(F32)
        + got[0].astype(F32)
        + got[1].astype(F32)
    )
    return total + fin[...].reshape(128, D).astype(F32)


def nothing():
    return None


def mlp_backward_kernel(layer, carries, *refs):
    g_ref, w_ref, hr_ref, gate_ref, up_ref = refs[:5]
    refs = refs[5:]
    if carries:
        before, refs = refs[0], refs[1:]
    out_ref, grads = refs[:2]
    refs = refs[2:]
    if carries:
        summed, refs = refs[0], refs[1:]
    buffers, refs = refs[:7], refs[7:]
    w, hr, gate, up, act, src, send_sem, recv_sem, local_sem = refs[:9]
    rows, part = buffers[0], buffers[1]
    spot = place()
    x, z, y, c = spot
    mail = Mail(send_sem, recv_sem)
    loads = [
        pltpu.make_async_copy(a, b, local_sem.at[i])
        for i, (a, b) in enumerate(
            ((w_ref, w), (gate_ref, gate), (up_ref, up), (hr_ref, hr))
        )
    ]
    if carries:
        older = AttentionSum(mail, 19, spot, before, refs[9:], local_sem.at[4])
        loads.append(older.load)
    for load in loads:
        load.start()
    src[...] = g_ref[...].astype(BF)
    greet(AttentionSum.peers(spot) if carries else ctx_peers(spot))
    loaded = []

    def chunk(row):
        if not loaded:
            for load in loads[:3]:
                load.wait()
            loaded.append(True)
        gz = rows[row].reshape(256, D)
        gact = nn(gz, w[2])
        g = gate[row].astype(F32)
        u = up[row].astype(F32)
        s = 1.0 / (1.0 + jnp.exp(-g))
        silu = g * s
        act[row] = (silu * u).astype(BF)
        gg = (gact * u * (s + silu * (1.0 - s))).astype(BF)
        gu = (gact * silu).astype(BF)
        gate[row] = gg
        up[row] = gu
        part[row] = (nt(gg, w[0]) + nt(gu, w[1])).astype(BF).reshape(2, 128, D)

    def weight_grad(member, left, right):
        def run():
            r = right[...].reshape(1024, FS)
            for i in range(7):
                l = left[:, :, :, 128 * i : 128 * (i + 1)].reshape(1024, 128)
                grads[member, 128 * i : 128 * (i + 1)] = tn(l, r).astype(BF)

        return run

    def gates():
        loads[3].wait()
        weight_grad(0, hr, gate)()

    fillers = [weight_grad(2, rows, act), gates, weight_grad(1, hr, up)]
    hook = nothing
    if carries:
        older.start()
        hook = older.cores
        steps = [older.plane.step_two, older.plane.step_three, older.plane.step_four]

        def joined(step, filler):
            def run():
                step()
                filler()

            return run

        fillers = [joined(step, filler) for step, filler in zip(steps, fillers)]
    out_ref[...] = mlp_exchange(mail, spot, src, buffers, chunk, fillers, hook)
    if carries:
        older.rows()
        older.last(summed)
    mail.finish()


def mlp_backward(layer, grad_output, m_full, hidden_rows, gate, up, before):
    anywhere = pl.BlockSpec(memory_space=pl.ANY)
    vmem = pl.BlockSpec(memory_space=pltpu.VMEM)
    carries = before is not None
    out_shape = [jax.ShapeDtypeStruct((128, D), F32), jax.ShapeDtypeStruct((3, D, FS), BF)]
    scratch = mlp_scratch() + [
        pltpu.VMEM((3, D, FS), BF),
        pltpu.VMEM((4, 2, 128, D), BF),
        pltpu.VMEM((4, 256, FS), BF),
        pltpu.VMEM((4, 256, FS), BF),
        pltpu.VMEM((4, 256, FS), BF),
        pltpu.VMEM((128, D), BF),
        pltpu.SemaphoreType.DMA((39,)),
        pltpu.SemaphoreType.DMA((39,)),
        pltpu.SemaphoreType.DMA((5,)),
    ]
    operands = [grad_output, m_full, hidden_rows, gate, up]
    if carries:
        out_shape.append(jax.ShapeDtypeStruct((16, 1024), F32))
        scratch += AttentionSum.scratch()
        operands.append(before)
    return pl.pallas_call(
        functools.partial(mlp_backward_kernel, layer, carries),
        out_shape=tuple(out_shape),
        in_specs=[vmem] + [anywhere] * (len(operands) - 1),
        out_specs=[vmem] * len(out_shape),
        scratch_shapes=scratch,
        compiler_params=pltpu.CompilerParams(
            collective_id=10 + layer, has_side_effects=True, vmem_limit_bytes=52 * 1024 * 1024
        ),
        name="mlp_backward_%d" % layer,
    )(*operands)


def last_sum_kernel(a_ref, out_ref, *refs):
    send_sem, recv_sem, local_sem = refs[-3:]
    spot = place()
    mail = Mail(send_sem, recv_sem)
    older = AttentionSum(mail, 0, spot, a_ref, refs[:-3], local_sem.at[0])
    older.load.start()
    greet(AttentionSum.peers(spot))
    older.start()
    older.cores()
    older.plane.step_two()
    older.plane.step_three()
    older.plane.step_four()
    older.rows()
    older.last(out_ref)
    mail.finish()


def last_sum(a_grads):
    return pl.pallas_call(
        last_sum_kernel,
        out_shape=jax.ShapeDtypeStruct((16, 1024), F32),
        in_specs=[pl.BlockSpec(memory_space=pl.ANY)],
        out_specs=pl.BlockSpec(memory_space=pltpu.VMEM),
        scratch_shapes=AttentionSum.scratch()
        + [
            pltpu.SemaphoreType.DMA((20,)),
            pltpu.SemaphoreType.DMA((20,)),
            pltpu.SemaphoreType.DMA((1,)),
        ],
        compiler_params=pltpu.CompilerParams(
            collective_id=2, has_side_effects=True, vmem_limit_bytes=32 * 1024 * 1024
        ),
        name="last_sum",
    )(a_grads)


def swap_halves(u):
    width = u.shape[1]
    lane = lax.broadcasted_iota(jnp.int32, u.shape, 1)
    return jnp.where(
        lax.rem(lane, 64) < 32, pltpu.roll(u, width - 32, 1), pltpu.roll(u, 32, 1)
    )


def normal(v):
    r = lax.rsqrt(jnp.mean(v * v, axis=-1, keepdims=True) + eps_norm)
    return v * r, r


def forward_kernel(layer, *refs):
    x_ref, a_ref, m_ref, pick_ref, cos_ref, sin_ref, qpos_ref, kpos_ref = refs[:8]
    refs = refs[8:]
    if layer == 0:
        plane_ref, refs = refs[0], refs[1:]
    out_ref, vec_ref, mid_ref, att_ref, qs_ref, kvs_ref, probs_ref, low_ref, high_ref = refs[:9]
    hr_ref, gate_ref, up_ref = refs[9:12]
    refs = refs[12:]
    if layer == 0:
        m_zero, m_one, a_one = refs[:3]
        refs = refs[3:]
    blocks, low, high, kv, kvs, probs, heads, mask, att, qs, mid, h2 = refs[:12]
    buffers, refs = refs[12:19], refs[19:]
    w, gate, up, send_sem, recv_sem, local_sem = refs[:6]
    rows, part = buffers[0], buffers[1]
    spot = place()
    x, z, y, c = spot
    mail = Mail(send_sem, recv_sem)
    load = pltpu.make_async_copy(a_ref, blocks, local_sem.at[0])
    load.start()
    if layer == 0:
        line = LineGather(mail, 28, spot, plane_ref, a_one, local_sem.at[21])
        now = PlaneGather(mail, 37, spot, m_ref.at[0], m_zero, local_sem.at[22])
        later = PlaneGather(mail, 52, spot, m_ref.at[1], m_one, local_sem.at[23])
        greet(ctx_peers(spot) + ring_peers(spot))
        now.step_one()
        line.step_one()
    else:
        load_w = pltpu.make_async_copy(m_ref, w, local_sem.at[1])
        load_w.start()
        greet(ctx_peers(spot))
    inputs = x_ref[...]
    n, r = normal(inputs)
    load.wait()
    spare = []
    for g in range(8):
        group = blocks[g // 2, 2 * (g % 2) : 2 * (g % 2) + 2].reshape(256, 1024)
        low[112 * g : 112 * (g + 1)] = nn(pick_ref[0:112, :], group).astype(BF)
        high[112 * g : 112 * (g + 1)] = nn(pick_ref[112:224, :], group).astype(BF)
        spare.append(nn(pick_ref[224:240, :], group))
    gains = functools.reduce(lambda u, v: u + v, [block[0:2, :D] for block in spare])
    vec_ref[0:2, 0:D] = gains
    for j in range(9):
        piece = jnp.zeros((1, 128), F32)
        if j < 8:
            piece = piece + spare[j][0:1, D:]
        if j > 0:
            piece = piece + spare[j - 1][1:2, D:]
        vec_ref[2:3, 128 * j : 128 * (j + 1)] = piece
    stores = [
        pltpu.make_async_copy(low, low_ref, local_sem.at[2]),
        pltpu.make_async_copy(high, high_ref, local_sem.at[3]),
    ]
    hidden = (n * gains[0:1]).astype(BF)
    packed = nn(hidden, low[...]) + vec_ref[2:3, :1024]
    values = nn(hidden, high[:, :128]) + vec_ref[2:3, 1024:]
    turned = packed * cos_ref[...] + swap_halves(packed) * sin_ref[...]
    kv[y, c, :, 0:128] = turned[:, D:].astype(BF)
    kv[y, c, :, 128:256] = values.astype(BF)
    yp, ym, y2 = up1(y), down1(y), up2(y)
    to_yp, to_ym, other = ctx_peers(spot)
    first, second = pl.ds(0, 64), pl.ds(64, 64)
    mail.send(0, kv.at[y, c], kv.at[y, c], to_yp)
    mail.send(1, kv.at[y, c], kv.at[y, c], to_ym)
    mail.send(2, kv.at[y, c], kv.at[y, c], other)
    for store in stores:
        store.start()
    if layer == 0:
        now.step_two()
    for h in range(H):
        qs[h] = (turned[:, HD * h : HD * (h + 1)] * HD ** (-0.5)).astype(BF)
    mask[...] = jnp.where(kpos_ref[...] <= qpos_ref[...], 0.0, 1.0)
    mail.take(0, kv.at[ym, c], to_ym)
    mail.send(3, kv.at[ym, c, first], kv.at[ym, c, first], to_yp)
    mail.send(4, kv.at[ym, c], kv.at[ym, c], other)
    mail.take(1, kv.at[yp, c], to_yp)
    mail.send(5, kv.at[yp, c, second], kv.at[yp, c, second], to_ym)
    mail.send(6, kv.at[yp, c], kv.at[yp, c], other)
    mail.take(3, kv.at[y2, c, first], to_ym)
    mail.send(7, kv.at[y2, c, first], kv.at[y2, c, first], other)
    mail.take(5, kv.at[y2, c, second], to_yp)
    mail.send(8, kv.at[y2, c, second], kv.at[y2, c, second], other)
    if layer == 0:
        now.step_three()
    mail.take(2, kv.at[y, 1 - c], other)
    mail.take(4, kv.at[ym, 1 - c], other)
    mail.take(6, kv.at[yp, 1 - c], other)
    mail.take(7, kv.at[y2, 1 - c, first], other)
    mail.take(8, kv.at[y2, 1 - c, second], other)
    for i in range(4):
        kvs[i] = kv[:, :, :, HD * i : HD * (i + 1)].reshape(1024, HD)

    def body(i, carry):
        for k in range(KVH):
            h = i + 7 * k
            scores = nt(qs[h], kvs[k])
            scores = jnp.where(mask[...] > 0.5, neg_fill, scores)
            e = jnp.exp(scores - jnp.max(scores, axis=-1, keepdims=True))
            p = (e * (1.0 / jnp.sum(e, axis=-1, keepdims=True))).astype(BF)
            probs[h] = p
            heads[h] = nn(p, kvs[2 + k]).astype(BF)
        return carry

    lax.fori_loop(0, 4, body, 0)
    if layer == 0:
        line.step_two()
    lax.fori_loop(4, 7, body, 0)
    if layer == 0:
        now.step_four()
    att[...] = jnp.concatenate([heads[h] for h in range(H)], axis=1)
    mid[...] = inputs + nn(att[...], high[:, 128:])
    h2[...] = (normal(mid[...])[0] * gains[1:2]).astype(BF)
    for i, (src, dst) in enumerate(
        ((kvs, kvs_ref), (probs, probs_ref), (att, att_ref), (qs, qs_ref), (mid, mid_ref))
    ):
        stores.append(pltpu.make_async_copy(src, dst, local_sem.at[4 + i]))
        stores[-1].start()
    if layer == 0:
        line.step_three()
        now.step_five()
        slabs = refs[6]
        load_w = pltpu.make_async_copy(m_zero, slabs, local_sem.at[1])
        load_w.start()
        later.step_one()

    loaded = []

    def chunk(row):
        if not loaded:
            load_w.wait()
            if layer == 0:
                for member in range(3):
                    for i in range(16):
                        w[member, 56 * i : 56 * (i + 1)] = slabs[member, i // 4, i % 4]
            loaded.append(True)
        h = rows[row].reshape(256, D)
        g = nn(h, w[0])
        u = nn(h, w[1])
        gate[row] = g.astype(BF)
        up[row] = u.astype(BF)
        act = (g / (1.0 + jnp.exp(-g)) * u).astype(BF)
        part[row] = nt(act, w[2]).astype(BF).reshape(2, 128, D)
        k = 9 + 3 * (len(loaded) - 1)
        loaded.append(True)
        for i, (src, dst) in enumerate(((rows, hr_ref), (gate, gate_ref), (up, up_ref))):
            stores.append(pltpu.make_async_copy(src.at[row], dst.at[row], local_sem.at[k + i]))
            stores[-1].start()

    steps = [nothing] * 4
    if layer == 0:
        steps = [later.step_two, later.step_three, later.step_four, nothing]
    total = mlp_exchange(mail.shifted(9), spot, h2, buffers, chunk, steps[1:], steps[0])
    out_ref[...] = mid[...] + total
    if layer == 0:
        later.step_five()
        line.step_four()
    for store in stores:
        store.wait()
    mail.finish()


def forward(layer, state, a_full, m_full, pick, tables, positions, plane):
    anywhere = pl.BlockSpec(memory_space=pl.ANY)
    vmem = pl.BlockSpec(memory_space=pltpu.VMEM)
    out_shape = [
        jax.ShapeDtypeStruct((128, D), F32),
        jax.ShapeDtypeStruct((8, QKV), F32),
        jax.ShapeDtypeStruct((128, D), F32),
        jax.ShapeDtypeStruct((128, D), BF),
        jax.ShapeDtypeStruct((H, 128, HD), BF),
        jax.ShapeDtypeStruct((4, 1024, HD), BF),
        jax.ShapeDtypeStruct((H, 128, 1024), BF),
        jax.ShapeDtypeStruct((D, 1024), BF),
        jax.ShapeDtypeStruct((D, 1024), BF),
        jax.ShapeDtypeStruct((4, 2, 128, D), BF),
        jax.ShapeDtypeStruct((4, 256, FS), BF),
        jax.ShapeDtypeStruct((4, 256, FS), BF),
    ]
    operands = [state, a_full, m_full, pick, *tables, *positions]
    in_specs = [vmem, anywhere, anywhere] + [vmem] * 5
    slots = 28
    if layer == 0:
        out_shape += [
            jax.ShapeDtypeStruct((3, 4, 4, 56, FS), BF),
            jax.ShapeDtypeStruct((3, 4, 4, 56, FS), BF),
            jax.ShapeDtypeStruct((4, 4, 8, 16, 1024), BF),
        ]
        operands.append(plane)
        in_specs.append(anywhere)
        slots = 67
    slabs = [pltpu.VMEM((3, 4, 4, 56, FS), BF)] if layer == 0 else []
    return pl.pallas_call(
        functools.partial(forward_kernel, layer),
        out_shape=tuple(out_shape),
        in_specs=in_specs,
        out_specs=[vmem] * 2 + [anywhere] * (len(out_shape) - 2),
        scratch_shapes=[
            pltpu.VMEM((4, 4, 8, 16, 1024), BF),
            pltpu.VMEM((D, 1024), BF),
            pltpu.VMEM((D, 1024), BF),
            pltpu.VMEM((4, 2, 128, 256), BF),
            pltpu.VMEM((4, 1024, HD), BF),
            pltpu.VMEM((H, 128, 1024), BF),
            pltpu.VMEM((H, 128, HD), BF),
            pltpu.VMEM((128, 1024), F32),
            pltpu.VMEM((128, D), BF),
            pltpu.VMEM((H, 128, HD), BF),
            pltpu.VMEM((128, D), F32),
            pltpu.VMEM((128, D), BF),
        ]
        + mlp_scratch()
        + [
            pltpu.VMEM((3, D, FS), BF),
            pltpu.VMEM((4, 256, FS), BF),
            pltpu.VMEM((4, 256, FS), BF),
            pltpu.SemaphoreType.DMA((slots,)),
            pltpu.SemaphoreType.DMA((slots,)),
            pltpu.SemaphoreType.DMA((24,)),
        ]
        + slabs,
        compiler_params=pltpu.CompilerParams(
            collective_id=12 + layer, has_side_effects=True, vmem_limit_bytes=56 * 1024 * 1024
        ),
        name="forward_layer_%d" % layer,
    )(*operands)


def attention_backward_kernel(
    g_ref, ghid2_ref, mid_ref, x_ref, vec_ref, cos_ref, sin_ref, place_ref, att_ref, qs_ref,
    kvs_ref, probs_ref, low_ref, high_ref, m_ref,
    gin_ref, a_out, m_out,
    low, high, kvs, probs, m, gs, gatt, gqs, part, near, own, got, glow, ghigh, special,
    *refs,
):
    send_sem, recv_sem, local_sem = refs[-3:]
    spot = place()
    x, z, y, c = spot
    mail = Mail(send_sem, recv_sem)
    loads = [
        pltpu.make_async_copy(src, dst, local_sem.at[i])
        for i, (src, dst) in enumerate(
            ((m_ref, m), (high_ref, high), (probs_ref, probs), (kvs_ref, kvs), (low_ref, low))
        )
    ]
    for load in loads:
        load.start()
    plane = PlaneSum(mail, 7, spot, m, 2, refs[:-3])
    yp, ym, y2 = up1(y), down1(y), up2(y)
    to_yp, to_ym, other = ctx_peers(spot)
    to_y2 = device(x, z, y2, c)
    greet([to_yp, to_ym, other, to_y2] + PlaneSum.peers(spot, 3, 2))
    loads[0].wait()
    plane.step_one()
    mid = mid_ref[...]
    n, r = normal(mid)
    ghid2 = ghid2_ref[...]
    t = ghid2 * vec_ref[1:2, :D]
    gmid = g_ref[...] + r * (t - n * jnp.mean(t * n, axis=-1, keepdims=True))
    ggain_two = jnp.sum(ghid2 * n, axis=0, keepdims=True)
    gy = gmid.astype(BF)
    loads[1].wait()
    ga = nt(gy, high[:, 128:]).astype(BF)
    for h in range(H):
        gatt[h] = ga[:, HD * h : HD * (h + 1)]
    ghigh[:, 128:] = tn(att_ref[...], gy).astype(BF)
    loads[2].wait()
    loads[3].wait()

    def body(i, carry):
        for k in range(KVH):
            h = i + 7 * k
            p = probs[h].astype(F32)
            gp = nt(gatt[h], kvs[2 + k])
            s = (p * (gp - jnp.sum(gp * p, axis=-1, keepdims=True))).astype(BF)
            gs[h] = s
            gqs[h] = nn(s, kvs[k])
        return carry

    lax.fori_loop(0, 7, body, 0)
    plane.step_two()
    for k in range(KVH):
        heads = pl.ds(7 * k, 7)
        gk = tn(qs_ref[heads].reshape(D, HD), gs[heads].reshape(D, 1024)).astype(BF)
        gv = tn(gatt[heads].reshape(D, HD), probs[heads].reshape(D, 1024)).astype(BF)
        for j in range(8):
            part[j // 2, j % 2, HD * k : HD * (k + 1)] = gk[:, 128 * j : 128 * (j + 1)]
            part[j // 2, j % 2, 128 + HD * k : 128 + HD * (k + 1)] = gv[:, 128 * j : 128 * (j + 1)]
    mail.send(0, part.at[:, 1 - c], near, other)
    gq = jnp.concatenate([gqs[h] for h in range(H)], axis=1) * HD ** (-0.5)
    gq = (gq * cos_ref[:, :D] - swap_halves(gq) * sin_ref[:, :D]).astype(BF)
    inputs = x_ref[...]
    n, r = normal(inputs)
    hidden = (n * vec_ref[0:1, :D]).astype(BF)
    mail.take(0, near, other)
    own[...] = (part[:, c].astype(F32) + near[...].astype(F32)).astype(BF)
    mail.send(1, own.at[yp], got.at[0], to_yp)
    mail.send(2, own.at[ym], got.at[1], to_ym)
    mail.send(3, own.at[y2], got.at[2], to_y2)
    glow[:, :D] = tn(hidden, gq).astype(BF)
    loads[4].wait()
    ghid = nt(gq, low[:, :D])
    plane.step_three()
    mail.take(1, got.at[0], to_ym)
    mail.take(2, got.at[1], to_yp)
    mail.take(3, got.at[2], to_y2)
    total = own[y].astype(F32) + got[0].astype(F32) + got[1].astype(F32) + got[2].astype(F32)
    total = total.T
    gk = total[:, :128]
    gk = (gk * cos_ref[:, D:] - swap_halves(gk) * sin_ref[:, D:]).astype(BF)
    gv = total[:, 128:].astype(BF)
    ghid = ghid + nt(gk, low[:, D:]) + nt(gv, high[:, :128])
    glow[:, D:] = tn(hidden, gk).astype(BF)
    ghigh[:, :128] = tn(hidden, gv).astype(BF)
    t = ghid * vec_ref[0:1, :D]
    gin_ref[...] = gmid + r * (t - n * jnp.mean(t * n, axis=-1, keepdims=True))
    ggain_one = jnp.sum(ghid * n, axis=0, keepdims=True)
    plane.step_four()
    bias_q = jnp.sum(gq.astype(F32), axis=0, keepdims=True)
    bias_k = jnp.sum(gk.astype(F32), axis=0, keepdims=True)
    bias_v = jnp.sum(gv.astype(F32), axis=0, keepdims=True)
    bias = jnp.concatenate([bias_q, bias_k], axis=1)
    row = lax.broadcasted_iota(jnp.int32, (16, 1024), 0)
    row_last = jnp.concatenate([ggain_two, bias_v], axis=1)
    for g in range(8):
        row_seven = jnp.concatenate([ggain_one, bias[:, 128 * g : 128 * (g + 1)]], axis=1)
        extra = jnp.where(row == 0, row_seven, jnp.where(row == 1, row_last, 0.0))
        special[...] = extra.astype(BF)
        block = (
            nn(place_ref[0], glow[112 * g : 112 * (g + 1)])
            + nn(place_ref[1], ghigh[112 * g : 112 * (g + 1)])
            + nn(place_ref[2, :, 0:16], special[...])
        ).astype(BF)
        for k in range(16):
            ctx = k % 8
            a_out[ctx % 2, ctx // 2, g // 2, 2 * (g % 2) + k // 8] = block[16 * k : 16 * (k + 1)]
    plane.step_five(m_out)
    mail.finish()


def attention_backward(layer, grad_output, grad_hidden_two, kept, vectors, tables, place_rows, m_grads):
    x, mid, att, qs, kvs, probs, low, high = kept
    anywhere = pl.BlockSpec(memory_space=pl.ANY)
    vmem = pl.BlockSpec(memory_space=pltpu.VMEM)
    return pl.pallas_call(
        attention_backward_kernel,
        out_shape=(
            jax.ShapeDtypeStruct((128, D), F32),
            jax.ShapeDtypeStruct((2, 4, 4, 4, 16, 1024), BF),
            jax.ShapeDtypeStruct((3, 56, FS), F32),
        ),
        in_specs=[vmem] * 10 + [anywhere] * 5,
        out_specs=[vmem] * 3,
        scratch_shapes=[
            pltpu.VMEM((D, 1024), BF),
            pltpu.VMEM((D, 1024), BF),
            pltpu.VMEM((4, 1024, HD), BF),
            pltpu.VMEM((H, 128, 1024), BF),
            pltpu.VMEM((3, 4, 4, 56, FS), BF),
            pltpu.VMEM((H, 128, 1024), BF),
            pltpu.VMEM((H, 128, HD), BF),
            pltpu.VMEM((H, 128, HD), F32),
            pltpu.VMEM((4, 2, 256, 128), BF),
            pltpu.VMEM((4, 256, 128), BF),
            pltpu.VMEM((4, 256, 128), BF),
            pltpu.VMEM((3, 256, 128), BF),
            pltpu.VMEM((D, 1024), BF),
            pltpu.VMEM((D, 1024), BF),
            pltpu.VMEM((16, 1024), BF),
        ]
        + PlaneSum.scratch(3, 2, 56, FS)
        + [
            pltpu.SemaphoreType.DMA((23,)),
            pltpu.SemaphoreType.DMA((23,)),
            pltpu.SemaphoreType.DMA((5,)),
        ],
        compiler_params=pltpu.CompilerParams(
            collective_id=14 + layer, has_side_effects=True, vmem_limit_bytes=56 * 1024 * 1024
        ),
        name="attention_backward_%d" % layer,
    )(
        grad_output, grad_hidden_two, mid, x, vectors, *tables, place_rows, att, qs,
        kvs, probs, low, high, m_grads.reshape(3, 4, 4, 56, FS),
    )


def select_matrix():
    pick = np.zeros((226, 256), np.float32)
    for k in range(16):
        for r in range(7):
            pick[7 * k + r, 16 * k + r] = 1
            pick[112 + 7 * k + r, 16 * k + 8 + r] = 1
        pick[224, 16 * k + 7] = 1
        pick[225, 16 * k + 15] = 1
    return pick


def assemble_kernel(a_zero, a_one, m_zero, m_one, g_one, g_qkv, g_qk, g_value, g_out, g_two, g_gate, g_up, rows):
    index = lax.axis_index("dp") * 8 + lax.axis_index("ctx")
    rows[...] = jnp.zeros_like(rows)
    for l, (a_ref, m_ref) in enumerate(((a_zero, m_zero), (a_one, m_one))):
        g_qkv[l, :, 0:1024] = a_ref[0:7, :]
        g_qkv[l, :, 1024:1152] = a_ref[8:15, 0:128]
        g_out[l] = a_ref[8:15, 128:1024]
        g_gate[l] = m_ref[0]
        g_up[l] = m_ref[1]
        rows[l : l + 1] = a_ref[7:8, :]
        rows[2 + l : 3 + l] = a_ref[15:16, :]
    gains = pltpu.roll(rows[...], lax.rem(1024 - 7 * index, 1024), 1)
    g_one[...] = gains[0:2, 0:7]
    g_two[...] = gains[2:4, 0:7]
    g_qk[...] = pltpu.roll(rows[...], 128 - 8 * lax.rem(index, 16), 1)[0:2, 0:8]
    g_value[...] = pltpu.roll(rows[...], 128 - index, 1)[2:4, 0:1]


def assemble(a_sums, m_sums):
    vmem = pl.BlockSpec(memory_space=pltpu.VMEM)
    shapes = ((2, 7), (2, 7, QKV), (2, 8), (2, 1), (2, 7, D), (2, 7), (2, 56, FS), (2, 56, FS))
    return pl.pallas_call(
        assemble_kernel,
        out_shape=tuple(jax.ShapeDtypeStruct(shape, F32) for shape in shapes),
        in_specs=[vmem] * 4,
        out_specs=[vmem] * len(shapes),
        scratch_shapes=[pltpu.VMEM((8, 1024), F32)],
        name="assemble",
    )(*a_sums, *m_sums)


def shards(
    tokens, cotangent, span_order, gain_one, w_qkv, b_qkv, w_out, gain_two, w_gate, w_up, w_down
):
    sequences, local_len, width = tokens.shape
    span_len = local_len // 2
    ctx_place = lax.axis_index("ctx")
    offsets = jnp.arange(span_len, dtype=jnp.int32)
    local_spans = lax.dynamic_slice_in_dim(span_order, 2 * ctx_place, 2)
    local_pos = (local_spans[:, None] * span_len + offsets[None, :]).reshape(local_len)
    all_pos = (span_order[:, None] * span_len + offsets[None, :]).reshape(-1)
    positions = (local_pos[:, None], all_pos[None, :])
    frequency = rope_base ** (-jnp.arange(HD // 2, dtype=F32) * 2.0 / HD)
    angles = local_pos.astype(F32)[:, None] * frequency[None, :]
    cosine, sine = jnp.cos(angles), jnp.sin(angles)
    tables = (jnp.tile(cosine, (1, 32)), jnp.tile(jnp.concatenate([-sine, sine], axis=1), (1, 16)))
    chosen = select_matrix()
    pick = jnp.asarray(np.concatenate([chosen, np.zeros((14, 256), np.float32)]), BF)
    spread = np.zeros((3, 256, 112), np.float32)
    spread[0], spread[1], spread[2, :, :2] = chosen[:112].T, chosen[112:224].T, chosen[224:].T
    spread = jnp.asarray(spread, BF)

    m_block = jnp.stack([w_gate, w_up, w_down.transpose(0, 2, 1)], axis=1)
    a_zero, plane_one = first_gather(gain_one, w_qkv, b_qkv, w_out, gain_two)
    state_zero = tokens.reshape(local_len, width).astype(F32)
    state_one, *saved_zero, m_zero, m_one, a_one = forward(
        0, state_zero, a_zero, m_block, pick, tables, positions, plane_one
    )
    m_full = (m_zero.reshape(3, D, FS), m_one.reshape(3, D, FS))
    state, *saved_one = forward(1, state_one, a_one, m_full[1], pick, tables, positions, None)
    vectors = (saved_zero[0], saved_one[0])
    kept_layers = [
        ((state_zero,) + tuple(saved_zero[1:8]), saved_zero[8:]),
        ((state_one,) + tuple(saved_one[1:8]), saved_one[8:]),
    ]
    grad_state = cotangent.reshape(local_len, width).astype(F32)
    a_grads = None
    sums = [None, None]
    a_sums = [None, None]
    for l in reversed(range(LAYERS)):
        kept, kept_mlp = kept_layers[l]
        grad_hidden_two, m_grads, *older = mlp_backward(l, grad_state, m_full[l], *kept_mlp, a_grads)
        if older:
            a_sums[l + 1] = older[0]
        grad_state, a_grads, sums[l] = attention_backward(
            l, grad_state, grad_hidden_two, kept, vectors[l], tables, spread, m_grads
        )
    a_sums[0] = last_sum(a_grads)
    stacks = tuple(assemble(a_sums, sums)) + (jnp.stack([sums[0][2].T, sums[1][2].T]),)
    output = state.astype(BF).reshape(sequences, local_len, width)
    input_grad = grad_state.reshape(sequences, local_len, width)
    return (output, input_grad) + stacks


def solution(mesh):
    return jax.shard_map(
        shards,
        mesh=mesh,
        in_specs=(
            P("dp", "ctx", None),
            P("dp", "ctx", None),
            P(),
            P(None, ("dp", "ctx")),
            P(None, ("dp", "ctx"), None),
            P(None, ("dp", "ctx")),
            P(None, ("dp", "ctx"), None),
            P(None, ("dp", "ctx")),
            P(None, "dp", "ctx"),
            P(None, "dp", "ctx"),
            P(None, "ctx", "dp"),
        ),
        out_specs=(
            P("dp", "ctx", None),
            P("dp", "ctx", None),
            P(None, ("dp", "ctx")),
            P(None, ("dp", "ctx"), None),
            P(None, ("dp", "ctx")),
            P(None, ("dp", "ctx")),
            P(None, ("dp", "ctx"), None),
            P(None, ("dp", "ctx")),
            P(None, "dp", "ctx"),
            P(None, "dp", "ctx"),
            P(None, "ctx", "dp"),
        ),
        check_vma=False,
    )
```

```python
import functools

import jax
import jax.numpy as jnp
import numpy as np
from jax import lax
from jax.experimental import pallas as pl
from jax.experimental.pallas import tpu as pltpu
from jax.sharding import PartitionSpec as P

H = 14
KVH = 2
HD = 64
LAYERS = 2
D = 896
QKV = 1152
FS = 608
MESH = pl.DeviceIdType.MESH
BF = jnp.bfloat16
F32 = jnp.float32

eps_norm = 1e-06
rope_base = 1000000.0
neg_fill = -1e30


def place():
    dp = lax.axis_index("dp")
    ctx = lax.axis_index("ctx")
    return lax.div(dp, 4), lax.rem(dp, 4), lax.div(ctx, 2), lax.rem(ctx, 2)


def up1(v):
    return lax.rem(v + 1, 4)


def up2(v):
    return lax.rem(v + 2, 4)


def down1(v):
    return lax.rem(v + 3, 4)


def device(x, z, y, c):
    return (x * 4 + z, y * 2 + c)


def greet(peers):
    barrier = pltpu.get_barrier_semaphore()
    for peer in peers:
        pl.semaphore_signal(barrier, inc=1, device_id=peer, device_id_type=MESH)
    pl.semaphore_wait(barrier, len(peers))


class Mail:
    def __init__(self, send_sem, recv_sem, base=0, sent=None):
        self.send_sem = send_sem
        self.recv_sem = recv_sem
        self.base = base
        self.sent = [] if sent is None else sent

    def shifted(self, base):
        return Mail(self.send_sem, self.recv_sem, self.base + base, self.sent)

    def send(self, slot, src, dst, target):
        copy = pltpu.make_async_remote_copy(
            src_ref=src,
            dst_ref=dst,
            send_sem=self.send_sem.at[self.base + slot],
            recv_sem=self.recv_sem.at[self.base + slot],
            device_id=target,
            device_id_type=MESH,
        )
        copy.start()
        self.sent.append(copy)

    def take(self, slot, dst, source):
        pltpu.make_async_remote_copy(
            src_ref=dst,
            dst_ref=dst,
            send_sem=self.send_sem.at[self.base + slot],
            recv_sem=self.recv_sem.at[self.base + slot],
            device_id=source,
            device_id_type=MESH,
        ).wait_recv()

    def finish(self):
        for copy in self.sent:
            copy.wait_send()


class RowGather:
    slots = 8

    def __init__(self, mail, spot, block, along_x, along_z, local_sem):
        self.mail, self.spot, self.block = mail, spot, block
        self.along_x, self.along_z = along_x, along_z
        self.cut, self.rest = along_x.shape[0], along_z.shape[0]
        x, z = spot[:2]
        self.sa, self.sb = pl.ds(0, self.cut), pl.ds(self.cut, self.rest)
        self.own = [
            pltpu.make_async_copy(block.at[self.sa], along_x.at[:, x], local_sem.at[0]),
            pltpu.make_async_copy(block.at[self.sb], along_z.at[:, z], local_sem.at[1]),
        ]

    def step_one(self):
        x, z = self.spot[:2]
        to_xp, to_xm, to_zp, to_zm = ring_peers(self.spot)
        for copy in self.own:
            copy.start()
        self.mail.send(0, self.block.at[self.sa], self.along_x.at[:, x], to_xp)
        self.mail.send(1, self.block.at[self.sa], self.along_x.at[:, x], to_xm)
        self.mail.send(4, self.block.at[self.sb], self.along_z.at[:, z], to_zp)
        self.mail.send(5, self.block.at[self.sb], self.along_z.at[:, z], to_zm)

    def relays(self):
        x, z = self.spot[:2]
        to_xp, to_xm, to_zp, to_zm = ring_peers(self.spot)
        return (
            (0, self.along_x, self.cut, x, to_xp, to_xm),
            (4, self.along_z, self.rest, z, to_zp, to_zm),
        )

    def step_two(self):
        for base, ref, count, here, plus, minus in self.relays():
            behind, front = down1(here), up1(here)
            half = max(count // 2, 1)
            self.mail.take(base, ref.at[:, behind], minus)
            part = ref.at[pl.ds(0, half), behind]
            self.mail.send(base + 2, part, part, plus)
            self.mail.take(base + 1, ref.at[:, front], plus)
            if count > 1:
                part = ref.at[pl.ds(half, count - half), front]
                self.mail.send(base + 3, part, part, minus)

    def step_three(self):
        for base, ref, count, here, plus, minus in self.relays():
            half = max(count // 2, 1)
            self.mail.take(base + 2, ref.at[pl.ds(0, half), up2(here)], minus)
            if count > 1:
                self.mail.take(base + 3, ref.at[pl.ds(half, count - half), up2(here)], plus)
        for copy in self.own:
            copy.wait()


class PlaneFill:
    slots = 16

    def __init__(self, mail, spot, along_x, along_z, full, local_sem, mirror=None):
        self.mail, self.spot, self.full, self.mirror = mail, spot, full, mirror
        self.along_x, self.along_z = along_x, along_z
        self.cut, self.rest = along_x.shape[0], along_z.shape[0]
        x, z, y, c = spot
        self.other = device(x, z, y, 1 - c)
        self.copies = [
            pltpu.make_async_copy(along_x, full.at[self.first(z)], local_sem.at[0]),
            pltpu.make_async_copy(along_z, full.at[self.second(x)], local_sem.at[1]),
        ]

    def first(self, z, half=None):
        lead = pl.ds(0, self.cut) if half is None else pl.ds(half * (self.cut // 2), self.cut // 2)
        return (lead, pl.ds(0, 4), z)

    def second(self, x, half=None):
        if half is None:
            return (pl.ds(self.cut, self.rest), x, pl.ds(0, 4))
        if self.rest == 1:
            return (pl.ds(self.cut, 1), x, pl.ds(2 * half, 2))
        return (pl.ds(self.cut + half * (self.rest // 2), self.rest // 2), x, pl.ds(0, 4))

    def pass_on(self, slot, where, target):
        self.mail.send(slot, self.full.at[where], self.full.at[where], target)

    def share(self, slot, where, src=None):
        if self.mirror is not None:
            src = self.full.at[where] if src is None else src
            self.mail.send(slot, src, self.full.at[where], self.other)

    def step_one(self):
        x, z = self.spot[:2]
        to_xp, to_xm, to_zp, to_zm = ring_peers(self.spot)
        self.mail.send(0, self.along_x, self.full.at[self.first(z)], to_zp)
        self.mail.send(1, self.along_x, self.full.at[self.first(z)], to_zm)
        self.mail.send(2, self.along_z, self.full.at[self.second(x)], to_xp)
        self.mail.send(3, self.along_z, self.full.at[self.second(x)], to_xm)
        self.share(8, self.first(z), self.along_x)
        self.share(9, self.second(x), self.along_z)
        for copy in self.copies:
            copy.start()

    def step_two(self):
        x, z = self.spot[:2]
        to_xp, to_xm, to_zp, to_zm = ring_peers(self.spot)
        xp, xm, zp, zm = up1(x), down1(x), up1(z), down1(z)
        for slot, where, piece, source, target in (
            (0, self.first(zm), self.first(zm, 0), to_zm, to_zp),
            (2, self.second(xm), self.second(xm, 0), to_xm, to_xp),
            (1, self.first(zp), self.first(zp, 1), to_zp, to_zm),
            (3, self.second(xp), self.second(xp, 1), to_xp, to_xm),
        ):
            self.mail.take(slot, self.full.at[where], source)
            self.pass_on(4 + slot, piece, target)
            self.share(10 + slot, where)

    def step_three(self):
        x, z = self.spot[:2]
        to_xp, to_xm, to_zp, to_zm = ring_peers(self.spot)
        for slot, piece, source in (
            (4, self.first(up2(z), 0), to_zm),
            (6, self.second(up2(x), 0), to_xm),
            (5, self.first(up2(z), 1), to_zp),
            (7, self.second(up2(x), 1), to_xp),
        ):
            self.mail.take(slot, self.full.at[piece], source)
        self.share(14, self.first(up2(z)))
        self.share(15, self.second(up2(x)))
        for copy in self.copies:
            copy.wait()

    def step_four(self):
        x, z = self.spot[:2]
        xp, xm, zp, zm = up1(x), down1(x), up1(z), down1(z)
        for slot, where in (
            (8, self.first(z)),
            (9, self.second(x)),
            (10, self.first(zm)),
            (11, self.first(zp)),
            (12, self.second(xm)),
            (13, self.second(xp)),
            (14, self.first(up2(z))),
            (15, self.second(up2(x))),
        ):
            self.mail.take(slot, self.mirror.at[where], self.other)


def ring_peers(spot):
    x, z, y, c = spot
    return [
        device(up1(x), z, y, c),
        device(down1(x), z, y, c),
        device(x, up1(z), y, c),
        device(x, down1(z), y, c),
    ]


def ctx_peers(spot):
    x, z, y, c = spot
    return [device(x, z, up1(y), c), device(x, z, down1(y), c), device(x, z, y, 1 - c)]


def first_gather_kernel(
    one_ref, qkv_ref, bias_ref, out_ref, two_ref, m_ref,
    full, row_out, m_x, m_z,
    rows, vectors, offsets, line, a_x, a_z, send_sem, recv_sem, local_sem,
):
    spot = place()
    x, z, y, c = spot
    index = (x * 4 + z) * 8 + 2 * y + c
    mail = Mail(send_sem, recv_sem)
    vectors[...] = jnp.zeros_like(vectors)
    offsets[...] = jnp.zeros_like(offsets)
    vectors[0:2, 0:7] = one_ref[...].astype(F32)
    vectors[2:4, 0:7] = two_ref[...].astype(F32)
    offsets[0:2, 0:9] = bias_ref[...].astype(F32)
    gains = pltpu.roll(vectors[...], 7 * index, 1)
    bias = pltpu.roll(offsets[...], 9 * index - 128 * lax.div(index, 16), 1)
    for l in range(LAYERS):
        rows[l, 0:7, :] = qkv_ref[l, :, :1024].astype(F32)
        rows[l, 8:15, 0:128] = qkv_ref[l, :, 1024:].astype(F32)
        rows[l, 8:15, 128:1024] = out_ref[l].astype(F32)
        rows[l, 7:8, 0:D] = gains[l : l + 1, :D]
        rows[l, 15:16, 0:D] = gains[2 + l : 3 + l, :D]
        rows[l, 7:8, D:1024] = bias[l : l + 1, :128]
        rows[l, 15:16, D:1024] = bias[l : l + 1, 128:]
    line[:, y] = rows[...].astype(BF)
    yp, ym, y2 = up1(y), down1(y), up2(y)
    to_yp, to_ym, other = ctx_peers(spot)
    to_y2 = device(x, z, y2, c)
    greet(ring_peers(spot) + [to_yp, to_ym, other, to_y2])
    mail.send(0, line.at[:, y], line.at[:, y], to_yp)
    mail.send(1, line.at[:, y], line.at[:, y], to_ym)
    mail.send(2, line.at[:, y], line.at[:, y], to_y2)
    row = RowGather(mail.shifted(3), spot, line.at[0], a_x, a_z, local_sem.at[pl.ds(0, 2)])
    fill = PlaneFill(
        mail.shifted(11), spot, a_x, a_z, full.at[c], local_sem.at[pl.ds(2, 2)], full.at[1 - c]
    )
    feed = RowGather(mail.shifted(27), spot, m_ref.at[0], m_x, m_z, local_sem.at[pl.ds(4, 2)])
    mail.take(0, line.at[:, ym], to_ym)
    mail.take(1, line.at[:, yp], to_yp)
    mail.take(2, line.at[:, y2], to_y2)
    row.step_one()
    kept = pltpu.make_async_copy(line.at[1], row_out, local_sem.at[6])
    kept.start()
    row.step_two()
    row.step_three()
    fill.step_one()
    feed.step_one()
    fill.step_two()
    feed.step_two()
    fill.step_three()
    feed.step_three()
    fill.step_four()
    kept.wait()
    mail.finish()


def first_gather(gain_one, w_qkv, b_qkv, w_out, gain_two, m_block):
    return pl.pallas_call(
        first_gather_kernel,
        out_shape=(
            jax.ShapeDtypeStruct((2, 4, 4, 4, 16, 1024), BF),
            jax.ShapeDtypeStruct((4, 16, 1024), BF),
            jax.ShapeDtypeStruct((2, 4, 56, FS), BF),
            jax.ShapeDtypeStruct((1, 4, 56, FS), BF),
        ),
        in_specs=[pl.BlockSpec(memory_space=pltpu.VMEM)] * 5 + [pl.BlockSpec(memory_space=pl.ANY)],
        out_specs=[pl.BlockSpec(memory_space=pl.ANY)] * 4,
        scratch_shapes=[
            pltpu.VMEM((2, 16, 1024), F32),
            pltpu.VMEM((8, 1024), F32),
            pltpu.VMEM((8, 256), F32),
            pltpu.VMEM((2, 4, 16, 1024), BF),
            pltpu.VMEM((2, 4, 16, 1024), BF),
            pltpu.VMEM((2, 4, 16, 1024), BF),
            pltpu.SemaphoreType.DMA((35,)),
            pltpu.SemaphoreType.DMA((35,)),
            pltpu.SemaphoreType.DMA((7,)),
        ],
        compiler_params=pltpu.CompilerParams(
            collective_id=1, has_side_effects=True, vmem_limit_bytes=16 * 1024 * 1024
        ),
        name="first_gather",
    )(gain_one, w_qkv, b_qkv, w_out, gain_two, m_block)


class PlaneSum:
    def __init__(self, mail, base, spot, g, cut, buffers):
        self.mail, self.base, self.spot, self.g, self.cut = mail, base, spot, g, cut
        self.count = g.shape[0]
        self.buffers = buffers

    @staticmethod
    def scratch(slabs, cut, rows, columns):
        rest = slabs - cut
        out = [
            pltpu.VMEM((2, cut, 2, rows, columns), BF),
            pltpu.VMEM((2, cut, 4, rows, columns), BF),
            pltpu.VMEM((2, rest, 2, rows, columns), BF),
            pltpu.VMEM((2, rest, 4, rows, columns), BF),
            pltpu.VMEM((2, cut // 2, rows, columns), BF),
            pltpu.VMEM((2, cut, rows, columns), BF),
            pltpu.VMEM((2, max(rest // 2, 1), rows, columns), BF),
            pltpu.VMEM((2, rest, rows, columns), BF),
        ]
        return out

    @staticmethod
    def peers(spot, slabs, cut):
        x, z, y, c = spot
        near = [device(up1(x), z, y, c), device(down1(x), z, y, c), device(x, up1(z), y, c), device(x, down1(z), y, c)]
        return near + ([device(x, up2(z), y, c)] if slabs - cut == 1 else [])

    def names(self):
        x, z, y, c = self.spot
        xp, xm, zp, zm = up1(x), down1(x), up1(z), down1(z)
        to = (device(xp, z, y, c), device(xm, z, y, c), device(x, zp, y, c), device(x, zm, y, c))
        return x, z, xp, xm, zp, zm, up2(x), up2(z), to

    def send(self, slot, src, dst, target):
        self.mail.send(self.base + slot, src, dst, target)

    def take(self, slot, dst, source):
        self.mail.take(self.base + slot, dst, source)

    def add(self, where, extra):
        self.g[where] = (self.g[where].astype(F32) + extra.astype(F32)).astype(BF)

    def step_one(self):
        x, z, xp, xm, zp, zm, x2, z2, (to_xp, to_xm, to_zp, to_zm) = self.names()
        fa, ga, fb, gb, pa, qa, pb, qb = self.buffers
        sa, sb = pl.ds(0, self.cut), pl.ds(self.cut, self.count - self.cut)
        lo, hi = pl.ds(0, 2), pl.ds(2, 2)
        self.send(0, self.g.at[sa, lo, z2], fa.at[0], to_zp)
        self.send(1, self.g.at[sa, hi, z2], fa.at[1], to_zm)
        self.send(2, self.g.at[sb, x2, lo], fb.at[0], to_xp)
        self.send(3, self.g.at[sb, x2, hi], fb.at[1], to_xm)

    def step_two(self):
        x, z, xp, xm, zp, zm, x2, z2, (to_xp, to_xm, to_zp, to_zm) = self.names()
        fa, ga, fb, gb, pa, qa, pb, qb = self.buffers
        sa, sb = pl.ds(0, self.cut), pl.ds(self.cut, self.count - self.cut)
        lo, hi, every = pl.ds(0, 2), pl.ds(2, 2), pl.ds(0, 4)
        self.take(0, fa.at[0], to_zm)
        self.add((sa, lo, zp), fa[0])
        self.send(4, self.g.at[sa, every, zp], ga.at[0], to_zp)
        self.take(2, fb.at[0], to_xm)
        self.add((sb, xp, lo), fb[0])
        self.send(6, self.g.at[sb, xp, every], gb.at[0], to_xp)
        self.take(1, fa.at[1], to_zp)
        self.add((sa, hi, zm), fa[1])
        self.send(5, self.g.at[sa, every, zm], ga.at[1], to_zm)
        self.take(3, fb.at[1], to_xp)
        self.add((sb, xm, hi), fb[1])
        self.send(7, self.g.at[sb, xm, every], gb.at[1], to_xm)

    def step_three(self):
        x, z, xp, xm, zp, zm, x2, z2, (to_xp, to_xm, to_zp, to_zm) = self.names()
        fa, ga, fb, gb, pa, qa, pb, qb = self.buffers
        y, c = self.spot[2:]
        cut, rest = self.cut, self.count - self.cut
        sa, sb = pl.ds(0, cut), pl.ds(cut, rest)
        every = pl.ds(0, 4)
        self.take(4, ga.at[0], to_zm)
        self.take(5, ga.at[1], to_zp)
        self.add((sa, every, z), ga[0].astype(F32) + ga[1].astype(F32))
        self.send(8, self.g.at[pl.ds(0, cut // 2), x2, z], pa.at[0], to_xp)
        self.send(9, self.g.at[pl.ds(cut // 2, cut // 2), x2, z], pa.at[1], to_xm)
        self.take(6, gb.at[0], to_xm)
        self.take(7, gb.at[1], to_xp)
        self.add((sb, x, every), gb[0].astype(F32) + gb[1].astype(F32))
        if rest == 1:
            self.send(10, self.g.at[sb, x, z2], pb.at[0], device(x, z2, y, c))
            self.send(14, self.g.at[sb, x, zp], qb.at[0], to_zp)
            self.send(15, self.g.at[sb, x, zm], qb.at[1], to_zm)
        else:
            self.send(10, self.g.at[pl.ds(cut, rest // 2), x, z2], pb.at[0], to_zp)
            self.send(11, self.g.at[pl.ds(cut + rest // 2, rest // 2), x, z2], pb.at[1], to_zm)

    def step_four(self):
        x, z, xp, xm, zp, zm, x2, z2, (to_xp, to_xm, to_zp, to_zm) = self.names()
        fa, ga, fb, gb, pa, qa, pb, qb = self.buffers
        cut, rest = self.cut, self.count - self.cut
        sa, sb = pl.ds(0, cut), pl.ds(cut, rest)
        self.take(8, pa.at[0], to_xm)
        self.add((pl.ds(0, cut // 2), xp, z), pa[0])
        self.send(12, self.g.at[sa, xp, z], qa.at[0], to_xp)
        self.take(9, pa.at[1], to_xp)
        self.add((pl.ds(cut // 2, cut // 2), xm, z), pa[1])
        self.send(13, self.g.at[sa, xm, z], qa.at[1], to_xm)
        if rest > 1:
            self.take(10, pb.at[0], to_zm)
            self.add((pl.ds(cut, rest // 2), x, zp), pb[0])
            self.send(14, self.g.at[sb, x, zp], qb.at[0], to_zp)
            self.take(11, pb.at[1], to_zp)
            self.add((pl.ds(cut + rest // 2, rest // 2), x, zm), pb[1])
            self.send(15, self.g.at[sb, x, zm], qb.at[1], to_zm)

    def step_five(self, out):
        x, z, xp, xm, zp, zm, x2, z2, (to_xp, to_xm, to_zp, to_zm) = self.names()
        fa, ga, fb, gb, pa, qa, pb, qb = self.buffers
        y, c = self.spot[2:]
        cut, rest = self.cut, self.count - self.cut
        sa, sb = pl.ds(0, cut), pl.ds(cut, rest)
        self.take(12, qa.at[0], to_xm)
        self.take(13, qa.at[1], to_xp)
        out[sa] = (
            self.g[sa, x, z].astype(F32) + qa[0].astype(F32) + qa[1].astype(F32)
        ).astype(out.dtype)
        self.take(14, qb.at[0], to_zm)
        self.take(15, qb.at[1], to_zp)
        total = self.g[sb, x, z].astype(F32) + qb[0].astype(F32) + qb[1].astype(F32)
        if rest == 1:
            self.take(10, pb.at[0], device(x, z2, y, c))
            total = total + pb[0].astype(F32)
        out[sb] = total.astype(out.dtype)


class AttentionSum:
    def __init__(self, mail, base, spot, a_ref, refs, load_sem):
        self.mail, self.base, self.spot, self.a_ref = mail, base, spot, a_ref
        self.mine, self.near, self.block, self.got = refs[:4]
        self.plane = PlaneSum(mail, base + 4, spot, self.mine, 2, refs[4:])
        self.load = pltpu.make_async_copy(a_ref.at[spot[3]], self.mine, load_sem)

    @staticmethod
    def scratch():
        return [
            pltpu.VMEM((4, 4, 4, 16, 1024), BF),
            pltpu.VMEM((4, 4, 4, 16, 1024), BF),
            pltpu.VMEM((4, 16, 1024), BF),
            pltpu.VMEM((3, 16, 1024), BF),
        ] + PlaneSum.scratch(4, 2, 16, 1024)

    slots = 20

    @staticmethod
    def peers(spot):
        x, z, y, c = spot
        return PlaneSum.peers(spot, 4, 2) + [
            device(x, z, up1(y), c),
            device(x, z, up2(y), c),
            device(x, z, down1(y), c),
            device(x, z, y, 1 - c),
        ]

    def start(self):
        x, z, y, c = self.spot
        self.mail.send(self.base, self.a_ref.at[1 - c], self.near, device(x, z, y, 1 - c))

    def cores(self):
        x, z, y, c = self.spot
        self.load.wait()
        self.mail.take(self.base, self.near, device(x, z, y, 1 - c))

        def body(i, carry):
            self.mine[i] = (self.mine[i].astype(F32) + self.near[i].astype(F32)).astype(BF)
            return carry

        lax.fori_loop(0, 4, body, 0)
        self.plane.step_one()

    def rows(self):
        x, z, y, c = self.spot
        self.plane.step_five(self.block)
        for k, step in enumerate((up1, up2, down1)):
            to = device(x, z, step(y), c)
            self.mail.send(self.base + 1 + k, self.block.at[step(y)], self.got.at[k], to)

    def last(self, out):
        x, z, y, c = self.spot
        total = self.block[y].astype(F32)
        for k, step in enumerate((down1, up2, up1)):
            self.mail.take(self.base + 1 + k, self.got.at[k], device(x, z, step(y), c))
            total = total + self.got[k].astype(F32)
        out[...] = total


def nn(left, right):
    return jnp.dot(left, right, preferred_element_type=F32)


def nt(left, right):
    return lax.dot_general(left, right, (((1,), (1,)), ((), ())), preferred_element_type=F32)


def tn(left, right):
    return lax.dot_general(left, right, (((0,), (0,)), ((), ())), preferred_element_type=F32)


def mlp_scratch():
    return [
        pltpu.VMEM((4, 2, 128, D), BF),
        pltpu.VMEM((4, 2, 128, D), BF),
        pltpu.VMEM((4, 128, D), BF),
        pltpu.VMEM((3, 128, D), BF),
        pltpu.VMEM((2, 64, D), BF),
        pltpu.VMEM((2, 64, D), BF),
        pltpu.VMEM((2, 128, D), BF),
    ]


def mlp_exchange(mail, spot, src, buffers, chunk, fillers, hook):
    rows, part, near, own, far, fin, got = buffers
    x, z, y, c = spot
    yp, ym, y2 = up1(y), down1(y), up2(y)
    to_yp, to_ym, other = device(x, z, yp, c), device(x, z, ym, c), device(x, z, y, 1 - c)
    begin, end = pl.ds(0, 32), pl.ds(32, 32)
    first, second = pl.ds(0, 64), pl.ds(64, 64)
    mail.send(0, src.at[first], rows.at[y, c, first], to_yp)
    mail.send(1, src.at[second], rows.at[y, c, second], to_ym)
    mail.send(2, src, rows.at[y, c], other)
    mail.send(19, src.at[second], rows.at[y, c, second], to_yp)
    mail.send(20, src.at[first], rows.at[y, c, first], to_ym)
    rows[y, c] = src[...]
    mail.take(2, rows.at[y, 1 - c], other)
    chunk(y)
    mail.send(12, part.at[y, 1 - c], near.at[3], other)
    mail.take(0, rows.at[ym, c, first], to_ym)
    mail.send(3, rows.at[ym, c, first], rows.at[ym, c, first], to_yp)
    mail.take(1, rows.at[yp, c, second], to_yp)
    mail.send(5, rows.at[yp, c, second], rows.at[yp, c, second], to_ym)
    mail.take(19, rows.at[ym, c, second], to_ym)
    mail.send(4, rows.at[ym, c], rows.at[ym, c], other)
    mail.take(20, rows.at[yp, c, first], to_yp)
    mail.send(6, rows.at[yp, c], rows.at[yp, c], other)
    mail.take(4, rows.at[ym, 1 - c], other)
    chunk(ym)
    mail.send(11, part.at[ym, 1 - c], near.at[2], other)
    hook()
    mail.take(6, rows.at[yp, 1 - c], other)
    chunk(yp)
    mail.send(10, part.at[yp, 1 - c], near.at[1], other)
    mail.take(3, rows.at[y2, c, first], to_ym)
    mail.send(7, rows.at[y2, c, first], rows.at[y2, c, first], other)
    mail.take(5, rows.at[y2, c, second], to_yp)
    mail.send(8, rows.at[y2, c, second], rows.at[y2, c, second], other)
    mail.take(11, near.at[2], other)
    own[2] = (part[ym, c].astype(F32) + near[2].astype(F32)).astype(BF)
    mail.send(16, own.at[2], got.at[1], to_ym)
    mail.take(10, near.at[1], other)
    own[1] = (part[yp, c].astype(F32) + near[1].astype(F32)).astype(BF)
    mail.send(15, own.at[1], got.at[0], to_yp)
    mail.take(7, rows.at[y2, 1 - c, first], other)
    mail.take(8, rows.at[y2, 1 - c, second], other)
    chunk(y2)
    mail.send(9, part.at[y2, 1 - c], near.at[0], other)
    fillers[0]()
    mail.take(9, near.at[0], other)
    own[0] = (part[y2, c].astype(F32) + near[0].astype(F32)).astype(BF)
    mail.send(13, own.at[0, pl.ds(0, 32)], far.at[0, begin], to_yp)
    mail.send(14, own.at[0, pl.ds(64, 32)], far.at[1, begin], to_ym)
    mail.send(21, own.at[0, pl.ds(32, 32)], far.at[0, end], to_yp)
    mail.send(22, own.at[0, pl.ds(96, 32)], far.at[1, end], to_ym)
    fillers[1]()
    mail.take(13, far.at[0, begin], to_ym)
    mail.send(17, far.at[0, begin], fin.at[0, begin], to_yp)
    mail.take(14, far.at[1, begin], to_yp)
    mail.send(18, far.at[1, begin], fin.at[1, begin], to_ym)
    mail.take(21, far.at[0, end], to_ym)
    mail.send(23, far.at[0, end], fin.at[0, end], to_yp)
    mail.take(22, far.at[1, end], to_yp)
    mail.send(24, far.at[1, end], fin.at[1, end], to_ym)
    fillers[2]()
    mail.take(12, near.at[3], other)
    mail.take(15, got.at[0], to_ym)
    mail.take(16, got.at[1], to_yp)
    mail.take(17, fin.at[0, begin], to_ym)
    mail.take(18, fin.at[1, begin], to_yp)
    mail.take(23, fin.at[0, end], to_ym)
    mail.take(24, fin.at[1, end], to_yp)
    total = (
        part[y, c].astype(F32)
        + near[3].astype(F32)
        + got[0].astype(F32)
        + got[1].astype(F32)
    )
    return total + fin[...].reshape(128, D).astype(F32)


def nothing():
    return None


def mlp_backward_kernel(layer, carries, *refs):
    g_ref, w_ref, hr_ref, gate_ref, up_ref = refs[:5]
    refs = refs[5:]
    if carries:
        before, refs = refs[0], refs[1:]
    out_ref, grads = refs[:2]
    refs = refs[2:]
    if carries:
        summed, refs = refs[0], refs[1:]
    buffers, refs = refs[:7], refs[7:]
    w, hr, gate, up, act, src, send_sem, recv_sem, local_sem = refs[:9]
    rows, part = buffers[0], buffers[1]
    spot = place()
    x, z, y, c = spot
    mail = Mail(send_sem, recv_sem)
    loads = [
        pltpu.make_async_copy(a, b, local_sem.at[i])
        for i, (a, b) in enumerate(
            ((w_ref, w), (gate_ref, gate), (up_ref, up), (hr_ref, hr))
        )
    ]
    if carries:
        older = AttentionSum(mail, 25, spot, before, refs[9:], local_sem.at[4])
        loads.append(older.load)
    for load in loads:
        load.start()
    src[...] = g_ref[...].astype(BF)
    greet(AttentionSum.peers(spot) if carries else ctx_peers(spot))
    loaded = []

    def chunk(row):
        if not loaded:
            for load in loads[:3]:
                load.wait()
            loaded.append(True)
        gz = rows[row].reshape(256, D)
        gact = nn(gz, w[2])
        g = gate[row].astype(F32)
        u = up[row].astype(F32)
        s = 1.0 / (1.0 + jnp.exp(-g))
        silu = g * s
        act[row] = (silu * u).astype(BF)
        gg = (gact * u * (s + silu * (1.0 - s))).astype(BF)
        gu = (gact * silu).astype(BF)
        gate[row] = gg
        up[row] = gu
        part[row] = (nt(gg, w[0]) + nt(gu, w[1])).astype(BF).reshape(2, 128, D)

    def weight_grad(member, left, right):
        def run():
            r = right[...].reshape(1024, FS)
            for i in range(7):
                l = left[:, :, :, 128 * i : 128 * (i + 1)].reshape(1024, 128)
                grads[member, 128 * i : 128 * (i + 1)] = tn(l, r).astype(BF)

        return run

    def gates():
        loads[3].wait()
        weight_grad(0, hr, gate)()

    fillers = [weight_grad(2, rows, act), gates, weight_grad(1, hr, up)]
    hook = nothing
    if carries:
        older.start()
        hook = older.cores
        steps = [older.plane.step_two, older.plane.step_three, older.plane.step_four]

        def joined(step, filler):
            def run():
                step()
                filler()

            return run

        fillers = [joined(step, filler) for step, filler in zip(steps, fillers)]
    out_ref[...] = mlp_exchange(mail, spot, src, buffers, chunk, fillers, hook)
    if carries:
        older.rows()
        older.last(summed)
    mail.finish()


def mlp_backward(layer, grad_output, m_full, hidden_rows, gate, up, before):
    anywhere = pl.BlockSpec(memory_space=pl.ANY)
    vmem = pl.BlockSpec(memory_space=pltpu.VMEM)
    carries = before is not None
    out_shape = [jax.ShapeDtypeStruct((128, D), F32), jax.ShapeDtypeStruct((3, D, FS), BF)]
    scratch = mlp_scratch() + [
        pltpu.VMEM((3, D, FS), BF),
        pltpu.VMEM((4, 2, 128, D), BF),
        pltpu.VMEM((4, 256, FS), BF),
        pltpu.VMEM((4, 256, FS), BF),
        pltpu.VMEM((4, 256, FS), BF),
        pltpu.VMEM((128, D), BF),
        pltpu.SemaphoreType.DMA((45,)),
        pltpu.SemaphoreType.DMA((45,)),
        pltpu.SemaphoreType.DMA((5,)),
    ]
    operands = [grad_output, m_full, hidden_rows, gate, up]
    if carries:
        out_shape.append(jax.ShapeDtypeStruct((16, 1024), F32))
        scratch += AttentionSum.scratch()
        operands.append(before)
    return pl.pallas_call(
        functools.partial(mlp_backward_kernel, layer, carries),
        out_shape=tuple(out_shape),
        in_specs=[vmem] + [anywhere] * (len(operands) - 1),
        out_specs=[vmem] * len(out_shape),
        scratch_shapes=scratch,
        compiler_params=pltpu.CompilerParams(
            collective_id=10 + layer, has_side_effects=True, vmem_limit_bytes=52 * 1024 * 1024
        ),
        name="mlp_backward_%d" % layer,
    )(*operands)


def last_sum_kernel(a_ref, out_ref, *refs):
    send_sem, recv_sem, local_sem = refs[-3:]
    spot = place()
    mail = Mail(send_sem, recv_sem)
    older = AttentionSum(mail, 0, spot, a_ref, refs[:-3], local_sem.at[0])
    older.load.start()
    greet(AttentionSum.peers(spot))
    older.start()
    older.cores()
    older.plane.step_two()
    older.plane.step_three()
    older.plane.step_four()
    older.rows()
    older.last(out_ref)
    mail.finish()


def last_sum(a_grads):
    return pl.pallas_call(
        last_sum_kernel,
        out_shape=jax.ShapeDtypeStruct((16, 1024), F32),
        in_specs=[pl.BlockSpec(memory_space=pl.ANY)],
        out_specs=pl.BlockSpec(memory_space=pltpu.VMEM),
        scratch_shapes=AttentionSum.scratch()
        + [
            pltpu.SemaphoreType.DMA((20,)),
            pltpu.SemaphoreType.DMA((20,)),
            pltpu.SemaphoreType.DMA((1,)),
        ],
        compiler_params=pltpu.CompilerParams(
            collective_id=2, has_side_effects=True, vmem_limit_bytes=32 * 1024 * 1024
        ),
        name="last_sum",
    )(a_grads)


def swap_halves(u):
    width = u.shape[1]
    lane = lax.broadcasted_iota(jnp.int32, u.shape, 1)
    return jnp.where(
        lax.rem(lane, 64) < 32, pltpu.roll(u, width - 32, 1), pltpu.roll(u, 32, 1)
    )


def normal(v):
    r = lax.rsqrt(jnp.mean(v * v, axis=-1, keepdims=True) + eps_norm)
    return v * r, r


def forward_kernel(layer, *refs):
    x_ref, a_ref, m_ref, pick_ref, cos_ref, sin_ref, qpos_ref, kpos_ref = refs[:8]
    refs = refs[8:]
    if layer == 0:
        row_ref, shard_ref, m_z_ref = refs[:3]
        refs = refs[3:]
    out_ref, vec_ref, mid_ref, att_ref, qs_ref, kvs_ref, probs_ref, low_ref, high_ref = refs[:9]
    hr_ref, gate_ref, up_ref = refs[9:12]
    refs = refs[12:]
    if layer == 0:
        m_zero, m_one, a_one = refs[:3]
        refs = refs[3:]
    blocks, low, high, kv, kvs, probs, heads, mask, att, qs, mid, h2 = refs[:12]
    buffers, refs = refs[12:19], refs[19:]
    w, gate, up, send_sem, recv_sem, local_sem = refs[:6]
    rows, part = buffers[0], buffers[1]
    spot = place()
    x, z, y, c = spot
    mail = Mail(send_sem, recv_sem)
    load = pltpu.make_async_copy(a_ref, blocks, local_sem.at[0])
    load.start()
    if layer == 0:
        a_x, a_z, m_x, m_z, slabs = refs[6:]

        def sems(k):
            return local_sem.at[pl.ds(21 + 2 * k, 2)]

        fill = PlaneFill(mail.shifted(34), spot, m_ref, m_z_ref, m_zero, sems(0))
        a_row = RowGather(mail.shifted(50), spot, row_ref, a_x, a_z, sems(1))
        m_row = RowGather(mail.shifted(58), spot, shard_ref.at[1], m_x, m_z, sems(2))
        a_fill = PlaneFill(
            mail.shifted(66), spot, a_x, a_z, a_one.at[c], sems(3), a_one.at[1 - c]
        )
        m_fill = PlaneFill(mail.shifted(82), spot, m_x, m_z, m_one, sems(4))
        load_w = pltpu.make_async_copy(m_zero, slabs, local_sem.at[1])
        greet(ctx_peers(spot) + ring_peers(spot))
        fill.step_one()
        a_row.step_one()
        m_row.step_one()
    else:
        load_w = pltpu.make_async_copy(m_ref, w, local_sem.at[1])
        load_w.start()
        greet(ctx_peers(spot))
    inputs = x_ref[...]
    n, r = normal(inputs)
    load.wait()
    spare = []
    for g in range(8):
        group = jnp.concatenate(
            [blocks[k % 2, k % 8 // 2, g // 2, 2 * (g % 2) + k // 8] for k in range(16)], axis=0
        )
        low[112 * g : 112 * (g + 1)] = nn(pick_ref[0:112, :], group).astype(BF)
        high[112 * g : 112 * (g + 1)] = nn(pick_ref[112:224, :], group).astype(BF)
        spare.append(nn(pick_ref[224:240, :], group))
    gains = functools.reduce(lambda u, v: u + v, [block[0:2, :D] for block in spare])
    vec_ref[0:2, 0:D] = gains
    for j in range(9):
        piece = jnp.zeros((1, 128), F32)
        if j < 8:
            piece = piece + spare[j][0:1, D:]
        if j > 0:
            piece = piece + spare[j - 1][1:2, D:]
        vec_ref[2:3, 128 * j : 128 * (j + 1)] = piece
    stores = [
        pltpu.make_async_copy(low, low_ref, local_sem.at[2]),
        pltpu.make_async_copy(high, high_ref, local_sem.at[3]),
    ]
    hidden = (n * gains[0:1]).astype(BF)
    packed = nn(hidden, low[...]) + vec_ref[2:3, :1024]
    values = nn(hidden, high[:, :128]) + vec_ref[2:3, 1024:]
    turned = packed * cos_ref[...] + swap_halves(packed) * sin_ref[...]
    kv[y, c, :, 0:128] = turned[:, D:].astype(BF)
    kv[y, c, :, 128:256] = values.astype(BF)
    yp, ym, y2 = up1(y), down1(y), up2(y)
    to_yp, to_ym, other = ctx_peers(spot)
    first, second = pl.ds(0, 64), pl.ds(64, 64)
    mail.send(0, kv.at[y, c], kv.at[y, c], to_yp)
    mail.send(1, kv.at[y, c], kv.at[y, c], to_ym)
    mail.send(2, kv.at[y, c], kv.at[y, c], other)
    for store in stores:
        store.start()
    if layer == 0:
        a_row.step_two()
        m_row.step_two()
    for h in range(H):
        qs[h] = (turned[:, HD * h : HD * (h + 1)] * HD ** (-0.5)).astype(BF)
    mask[...] = jnp.where(kpos_ref[...] <= qpos_ref[...], 0.0, 1.0)
    mail.take(0, kv.at[ym, c], to_ym)
    mail.send(3, kv.at[ym, c, first], kv.at[ym, c, first], to_yp)
    mail.send(4, kv.at[ym, c], kv.at[ym, c], other)
    mail.take(1, kv.at[yp, c], to_yp)
    mail.send(5, kv.at[yp, c, second], kv.at[yp, c, second], to_ym)
    mail.send(6, kv.at[yp, c], kv.at[yp, c], other)
    mail.take(3, kv.at[y2, c, first], to_ym)
    mail.send(7, kv.at[y2, c, first], kv.at[y2, c, first], other)
    mail.take(5, kv.at[y2, c, second], to_yp)
    mail.send(8, kv.at[y2, c, second], kv.at[y2, c, second], other)
    if layer == 0:
        fill.step_two()
        a_row.step_three()
        m_row.step_three()
    mail.take(2, kv.at[y, 1 - c], other)
    mail.take(4, kv.at[ym, 1 - c], other)
    mail.take(6, kv.at[yp, 1 - c], other)
    mail.take(7, kv.at[y2, 1 - c, first], other)
    mail.take(8, kv.at[y2, 1 - c, second], other)
    for i in range(4):
        kvs[i] = kv[:, :, :, HD * i : HD * (i + 1)].reshape(1024, HD)

    def body(i, carry):
        for k in range(KVH):
            h = i + 7 * k
            scores = nt(qs[h], kvs[k])
            scores = jnp.where(mask[...] > 0.5, neg_fill, scores)
            e = jnp.exp(scores - jnp.max(scores, axis=-1, keepdims=True))
            p = (e * (1.0 / jnp.sum(e, axis=-1, keepdims=True))).astype(BF)
            probs[h] = p
            heads[h] = nn(p, kvs[2 + k]).astype(BF)
        return carry

    lax.fori_loop(0, 4, body, 0)
    if layer == 0:
        a_fill.step_one()
    lax.fori_loop(4, 7, body, 0)
    att[...] = jnp.concatenate([heads[h] for h in range(H)], axis=1)
    mid[...] = inputs + nn(att[...], high[:, 128:])
    h2[...] = (normal(mid[...])[0] * gains[1:2]).astype(BF)
    for i, (src, dst) in enumerate(
        ((kvs, kvs_ref), (probs, probs_ref), (att, att_ref), (qs, qs_ref), (mid, mid_ref))
    ):
        stores.append(pltpu.make_async_copy(src, dst, local_sem.at[4 + i]))
        stores[-1].start()
    if layer == 0:
        fill.step_three()
        load_w.start()
        m_fill.step_one()

    loaded = []

    def chunk(row):
        if not loaded:
            load_w.wait()
            if layer == 0:
                for member in range(3):
                    for i in range(16):
                        w[member, 56 * i : 56 * (i + 1)] = slabs[member, i // 4, i % 4]
            loaded.append(True)
        h = rows[row].reshape(256, D)
        g = nn(h, w[0])
        u = nn(h, w[1])
        gate[row] = g.astype(BF)
        up[row] = u.astype(BF)
        act = (g / (1.0 + jnp.exp(-g)) * u).astype(BF)
        part[row] = nt(act, w[2]).astype(BF).reshape(2, 128, D)
        k = 9 + 3 * (len(loaded) - 1)
        loaded.append(True)
        for i, (src, dst) in enumerate(((rows, hr_ref), (gate, gate_ref), (up, up_ref))):
            stores.append(pltpu.make_async_copy(src.at[row], dst.at[row], local_sem.at[k + i]))
            stores[-1].start()

    steps = [nothing] * 4
    if layer == 0:
        steps = [a_fill.step_two, a_fill.step_three, m_fill.step_two, m_fill.step_three]
    total = mlp_exchange(mail.shifted(9), spot, h2, buffers, chunk, steps[1:], steps[0])
    out_ref[...] = mid[...] + total
    if layer == 0:
        a_fill.step_four()
    for store in stores:
        store.wait()
    mail.finish()


def forward(layer, state, a_full, m_full, pick, tables, positions, *shards):
    anywhere = pl.BlockSpec(memory_space=pl.ANY)
    vmem = pl.BlockSpec(memory_space=pltpu.VMEM)
    out_shape = [
        jax.ShapeDtypeStruct((128, D), F32),
        jax.ShapeDtypeStruct((8, QKV), F32),
        jax.ShapeDtypeStruct((128, D), F32),
        jax.ShapeDtypeStruct((128, D), BF),
        jax.ShapeDtypeStruct((H, 128, HD), BF),
        jax.ShapeDtypeStruct((4, 1024, HD), BF),
        jax.ShapeDtypeStruct((H, 128, 1024), BF),
        jax.ShapeDtypeStruct((D, 1024), BF),
        jax.ShapeDtypeStruct((D, 1024), BF),
        jax.ShapeDtypeStruct((4, 2, 128, D), BF),
        jax.ShapeDtypeStruct((4, 256, FS), BF),
        jax.ShapeDtypeStruct((4, 256, FS), BF),
    ]
    operands = [state, a_full, m_full, pick, *tables, *positions]
    in_specs = [vmem, anywhere, anywhere] + [vmem] * 5
    slots = 34
    extra = []
    if layer == 0:
        out_shape += [
            jax.ShapeDtypeStruct((3, 4, 4, 56, FS), BF),
            jax.ShapeDtypeStruct((3, 4, 4, 56, FS), BF),
            jax.ShapeDtypeStruct((2, 4, 4, 4, 16, 1024), BF),
        ]
        operands += shards
        in_specs += [anywhere] * 3
        slots = 98
        extra = [
            pltpu.VMEM((2, 4, 16, 1024), BF),
            pltpu.VMEM((2, 4, 16, 1024), BF),
            pltpu.VMEM((2, 4, 56, FS), BF),
            pltpu.VMEM((1, 4, 56, FS), BF),
            pltpu.VMEM((3, 4, 4, 56, FS), BF),
        ]
    return pl.pallas_call(
        functools.partial(forward_kernel, layer),
        out_shape=tuple(out_shape),
        in_specs=in_specs,
        out_specs=[vmem] * 2 + [anywhere] * (len(out_shape) - 2),
        scratch_shapes=[
            pltpu.VMEM((2, 4, 4, 4, 16, 1024), BF),
            pltpu.VMEM((D, 1024), BF),
            pltpu.VMEM((D, 1024), BF),
            pltpu.VMEM((4, 2, 128, 256), BF),
            pltpu.VMEM((4, 1024, HD), BF),
            pltpu.VMEM((H, 128, 1024), BF),
            pltpu.VMEM((H, 128, HD), BF),
            pltpu.VMEM((128, 1024), F32),
            pltpu.VMEM((128, D), BF),
            pltpu.VMEM((H, 128, HD), BF),
            pltpu.VMEM((128, D), F32),
            pltpu.VMEM((128, D), BF),
        ]
        + mlp_scratch()
        + [
            pltpu.VMEM((3, D, FS), BF),
            pltpu.VMEM((4, 256, FS), BF),
            pltpu.VMEM((4, 256, FS), BF),
            pltpu.SemaphoreType.DMA((slots,)),
            pltpu.SemaphoreType.DMA((slots,)),
            pltpu.SemaphoreType.DMA((31,)),
        ]
        + extra,
        compiler_params=pltpu.CompilerParams(
            collective_id=12 + layer, has_side_effects=True, vmem_limit_bytes=56 * 1024 * 1024
        ),
        name="forward_layer_%d" % layer,
    )(*operands)


def attention_backward_kernel(
    g_ref, ghid2_ref, mid_ref, x_ref, vec_ref, cos_ref, sin_ref, place_ref, att_ref, qs_ref,
    kvs_ref, probs_ref, low_ref, high_ref, m_ref,
    gin_ref, a_out, m_out,
    low, high, kvs, probs, m, gs, gatt, gqs, part, near, own, got, glow, ghigh, special,
    *refs,
):
    send_sem, recv_sem, local_sem = refs[-3:]
    spot = place()
    x, z, y, c = spot
    mail = Mail(send_sem, recv_sem)
    loads = [
        pltpu.make_async_copy(src, dst, local_sem.at[i])
        for i, (src, dst) in enumerate(
            ((m_ref, m), (high_ref, high), (probs_ref, probs), (kvs_ref, kvs), (low_ref, low))
        )
    ]
    for load in loads:
        load.start()
    plane = PlaneSum(mail, 7, spot, m, 2, refs[:-3])
    yp, ym, y2 = up1(y), down1(y), up2(y)
    to_yp, to_ym, other = ctx_peers(spot)
    to_y2 = device(x, z, y2, c)
    greet([to_yp, to_ym, other, to_y2] + PlaneSum.peers(spot, 3, 2))
    loads[0].wait()
    plane.step_one()
    mid = mid_ref[...]
    n, r = normal(mid)
    ghid2 = ghid2_ref[...]
    t = ghid2 * vec_ref[1:2, :D]
    gmid = g_ref[...] + r * (t - n * jnp.mean(t * n, axis=-1, keepdims=True))
    ggain_two = jnp.sum(ghid2 * n, axis=0, keepdims=True)
    gy = gmid.astype(BF)
    loads[1].wait()
    ga = nt(gy, high[:, 128:]).astype(BF)
    for h in range(H):
        gatt[h] = ga[:, HD * h : HD * (h + 1)]
    ghigh[:, 128:] = tn(att_ref[...], gy).astype(BF)
    loads[2].wait()
    loads[3].wait()

    def body(i, carry):
        for k in range(KVH):
            h = i + 7 * k
            p = probs[h].astype(F32)
            gp = nt(gatt[h], kvs[2 + k])
            s = (p * (gp - jnp.sum(gp * p, axis=-1, keepdims=True))).astype(BF)
            gs[h] = s
            gqs[h] = nn(s, kvs[k])
        return carry

    lax.fori_loop(0, 7, body, 0)
    plane.step_two()
    for k in range(KVH):
        heads = pl.ds(7 * k, 7)
        gk = tn(qs_ref[heads].reshape(D, HD), gs[heads].reshape(D, 1024)).astype(BF)
        gv = tn(gatt[heads].reshape(D, HD), probs[heads].reshape(D, 1024)).astype(BF)
        for j in range(8):
            part[j // 2, j % 2, HD * k : HD * (k + 1)] = gk[:, 128 * j : 128 * (j + 1)]
            part[j // 2, j % 2, 128 + HD * k : 128 + HD * (k + 1)] = gv[:, 128 * j : 128 * (j + 1)]
    mail.send(0, part.at[:, 1 - c], near, other)
    gq = jnp.concatenate([gqs[h] for h in range(H)], axis=1) * HD ** (-0.5)
    gq = (gq * cos_ref[:, :D] - swap_halves(gq) * sin_ref[:, :D]).astype(BF)
    inputs = x_ref[...]
    n, r = normal(inputs)
    hidden = (n * vec_ref[0:1, :D]).astype(BF)
    mail.take(0, near, other)
    own[...] = (part[:, c].astype(F32) + near[...].astype(F32)).astype(BF)
    mail.send(1, own.at[yp], got.at[0], to_yp)
    mail.send(2, own.at[ym], got.at[1], to_ym)
    mail.send(3, own.at[y2], got.at[2], to_y2)
    glow[:, :D] = tn(hidden, gq).astype(BF)
    loads[4].wait()
    ghid = nt(gq, low[:, :D])
    plane.step_three()
    mail.take(1, got.at[0], to_ym)
    mail.take(2, got.at[1], to_yp)
    mail.take(3, got.at[2], to_y2)
    total = own[y].astype(F32) + got[0].astype(F32) + got[1].astype(F32) + got[2].astype(F32)
    total = total.T
    gk = total[:, :128]
    gk = (gk * cos_ref[:, D:] - swap_halves(gk) * sin_ref[:, D:]).astype(BF)
    gv = total[:, 128:].astype(BF)
    ghid = ghid + nt(gk, low[:, D:]) + nt(gv, high[:, :128])
    glow[:, D:] = tn(hidden, gk).astype(BF)
    ghigh[:, :128] = tn(hidden, gv).astype(BF)
    t = ghid * vec_ref[0:1, :D]
    gin_ref[...] = gmid + r * (t - n * jnp.mean(t * n, axis=-1, keepdims=True))
    ggain_one = jnp.sum(ghid * n, axis=0, keepdims=True)
    plane.step_four()
    bias_q = jnp.sum(gq.astype(F32), axis=0, keepdims=True)
    bias_k = jnp.sum(gk.astype(F32), axis=0, keepdims=True)
    bias_v = jnp.sum(gv.astype(F32), axis=0, keepdims=True)
    bias = jnp.concatenate([bias_q, bias_k], axis=1)
    row = lax.broadcasted_iota(jnp.int32, (16, 1024), 0)
    row_last = jnp.concatenate([ggain_two, bias_v], axis=1)
    for g in range(8):
        row_seven = jnp.concatenate([ggain_one, bias[:, 128 * g : 128 * (g + 1)]], axis=1)
        extra = jnp.where(row == 0, row_seven, jnp.where(row == 1, row_last, 0.0))
        special[...] = extra.astype(BF)
        block = (
            nn(place_ref[0], glow[112 * g : 112 * (g + 1)])
            + nn(place_ref[1], ghigh[112 * g : 112 * (g + 1)])
            + nn(place_ref[2, :, 0:16], special[...])
        ).astype(BF)
        for k in range(16):
            ctx = k % 8
            a_out[ctx % 2, ctx // 2, g // 2, 2 * (g % 2) + k // 8] = block[16 * k : 16 * (k + 1)]
    plane.step_five(m_out)
    mail.finish()


def attention_backward(layer, grad_output, grad_hidden_two, kept, vectors, tables, place_rows, m_grads):
    x, mid, att, qs, kvs, probs, low, high = kept
    anywhere = pl.BlockSpec(memory_space=pl.ANY)
    vmem = pl.BlockSpec(memory_space=pltpu.VMEM)
    return pl.pallas_call(
        attention_backward_kernel,
        out_shape=(
            jax.ShapeDtypeStruct((128, D), F32),
            jax.ShapeDtypeStruct((2, 4, 4, 4, 16, 1024), BF),
            jax.ShapeDtypeStruct((3, 56, FS), F32),
        ),
        in_specs=[vmem] * 10 + [anywhere] * 5,
        out_specs=[vmem] * 3,
        scratch_shapes=[
            pltpu.VMEM((D, 1024), BF),
            pltpu.VMEM((D, 1024), BF),
            pltpu.VMEM((4, 1024, HD), BF),
            pltpu.VMEM((H, 128, 1024), BF),
            pltpu.VMEM((3, 4, 4, 56, FS), BF),
            pltpu.VMEM((H, 128, 1024), BF),
            pltpu.VMEM((H, 128, HD), BF),
            pltpu.VMEM((H, 128, HD), F32),
            pltpu.VMEM((4, 2, 256, 128), BF),
            pltpu.VMEM((4, 256, 128), BF),
            pltpu.VMEM((4, 256, 128), BF),
            pltpu.VMEM((3, 256, 128), BF),
            pltpu.VMEM((D, 1024), BF),
            pltpu.VMEM((D, 1024), BF),
            pltpu.VMEM((16, 1024), BF),
        ]
        + PlaneSum.scratch(3, 2, 56, FS)
        + [
            pltpu.SemaphoreType.DMA((23,)),
            pltpu.SemaphoreType.DMA((23,)),
            pltpu.SemaphoreType.DMA((5,)),
        ],
        compiler_params=pltpu.CompilerParams(
            collective_id=14 + layer, has_side_effects=True, vmem_limit_bytes=56 * 1024 * 1024
        ),
        name="attention_backward_%d" % layer,
    )(
        grad_output, grad_hidden_two, mid, x, vectors, *tables, place_rows, att, qs,
        kvs, probs, low, high, m_grads.reshape(3, 4, 4, 56, FS),
    )


def select_matrix():
    pick = np.zeros((226, 256), np.float32)
    for k in range(16):
        for r in range(7):
            pick[7 * k + r, 16 * k + r] = 1
            pick[112 + 7 * k + r, 16 * k + 8 + r] = 1
        pick[224, 16 * k + 7] = 1
        pick[225, 16 * k + 15] = 1
    return pick


def assemble_kernel(a_zero, a_one, m_zero, m_one, g_one, g_qkv, g_qk, g_value, g_out, g_two, g_gate, g_up, rows):
    index = lax.axis_index("dp") * 8 + lax.axis_index("ctx")
    rows[...] = jnp.zeros_like(rows)
    for l, (a_ref, m_ref) in enumerate(((a_zero, m_zero), (a_one, m_one))):
        g_qkv[l, :, 0:1024] = a_ref[0:7, :]
        g_qkv[l, :, 1024:1152] = a_ref[8:15, 0:128]
        g_out[l] = a_ref[8:15, 128:1024]
        g_gate[l] = m_ref[0]
        g_up[l] = m_ref[1]
        rows[l : l + 1] = a_ref[7:8, :]
        rows[2 + l : 3 + l] = a_ref[15:16, :]
    gains = pltpu.roll(rows[...], lax.rem(1024 - 7 * index, 1024), 1)
    g_one[...] = gains[0:2, 0:7]
    g_two[...] = gains[2:4, 0:7]
    g_qk[...] = pltpu.roll(rows[...], 128 - 8 * lax.rem(index, 16), 1)[0:2, 0:8]
    g_value[...] = pltpu.roll(rows[...], 128 - index, 1)[2:4, 0:1]


def assemble(a_sums, m_sums):
    vmem = pl.BlockSpec(memory_space=pltpu.VMEM)
    shapes = ((2, 7), (2, 7, QKV), (2, 8), (2, 1), (2, 7, D), (2, 7), (2, 56, FS), (2, 56, FS))
    return pl.pallas_call(
        assemble_kernel,
        out_shape=tuple(jax.ShapeDtypeStruct(shape, F32) for shape in shapes),
        in_specs=[vmem] * 4,
        out_specs=[vmem] * len(shapes),
        scratch_shapes=[pltpu.VMEM((8, 1024), F32)],
        name="assemble",
    )(*a_sums, *m_sums)


def shards(
    tokens, cotangent, span_order, gain_one, w_qkv, b_qkv, w_out, gain_two, w_gate, w_up, w_down
):
    sequences, local_len, width = tokens.shape
    span_len = local_len // 2
    ctx_place = lax.axis_index("ctx")
    offsets = jnp.arange(span_len, dtype=jnp.int32)
    local_spans = lax.dynamic_slice_in_dim(span_order, 2 * ctx_place, 2)
    local_pos = (local_spans[:, None] * span_len + offsets[None, :]).reshape(local_len)
    all_pos = (span_order[:, None] * span_len + offsets[None, :]).reshape(-1)
    positions = (local_pos[:, None], all_pos[None, :])
    frequency = rope_base ** (-jnp.arange(HD // 2, dtype=F32) * 2.0 / HD)
    angles = local_pos.astype(F32)[:, None] * frequency[None, :]
    cosine, sine = jnp.cos(angles), jnp.sin(angles)
    tables = (jnp.tile(cosine, (1, 32)), jnp.tile(jnp.concatenate([-sine, sine], axis=1), (1, 16)))
    chosen = select_matrix()
    pick = jnp.asarray(np.concatenate([chosen, np.zeros((14, 256), np.float32)]), BF)
    spread = np.zeros((3, 256, 112), np.float32)
    spread[0], spread[1], spread[2, :, :2] = chosen[:112].T, chosen[112:224].T, chosen[224:].T
    spread = jnp.asarray(spread, BF)

    m_block = jnp.stack([w_gate, w_up, w_down.transpose(0, 2, 1)], axis=1)
    a_zero, row_one, m_x, m_z = first_gather(gain_one, w_qkv, b_qkv, w_out, gain_two, m_block)
    state_zero = tokens.reshape(local_len, width).astype(F32)
    state_one, *saved_zero, m_zero, m_one, a_one = forward(
        0, state_zero, a_zero, m_x, pick, tables, positions, row_one, m_block, m_z
    )
    m_full = (m_zero.reshape(3, D, FS), m_one.reshape(3, D, FS))
    state, *saved_one = forward(1, state_one, a_one, m_full[1], pick, tables, positions)
    vectors = (saved_zero[0], saved_one[0])
    kept_layers = [
        ((state_zero,) + tuple(saved_zero[1:8]), saved_zero[8:]),
        ((state_one,) + tuple(saved_one[1:8]), saved_one[8:]),
    ]
    grad_state = cotangent.reshape(local_len, width).astype(F32)
    a_grads = None
    sums = [None, None]
    a_sums = [None, None]
    for l in reversed(range(LAYERS)):
        kept, kept_mlp = kept_layers[l]
        grad_hidden_two, m_grads, *older = mlp_backward(l, grad_state, m_full[l], *kept_mlp, a_grads)
        if older:
            a_sums[l + 1] = older[0]
        grad_state, a_grads, sums[l] = attention_backward(
            l, grad_state, grad_hidden_two, kept, vectors[l], tables, spread, m_grads
        )
    a_sums[0] = last_sum(a_grads)
    stacks = tuple(assemble(a_sums, sums)) + (jnp.stack([sums[0][2].T, sums[1][2].T]),)
    output = state.astype(BF).reshape(sequences, local_len, width)
    input_grad = grad_state.reshape(sequences, local_len, width)
    return (output, input_grad) + stacks


def solution(mesh):
    return jax.shard_map(
        shards,
        mesh=mesh,
        in_specs=(
            P("dp", "ctx", None),
            P("dp", "ctx", None),
            P(),
            P(None, ("dp", "ctx")),
            P(None, ("dp", "ctx"), None),
            P(None, ("dp", "ctx")),
            P(None, ("dp", "ctx"), None),
            P(None, ("dp", "ctx")),
            P(None, "dp", "ctx"),
            P(None, "dp", "ctx"),
            P(None, "ctx", "dp"),
        ),
        out_specs=(
            P("dp", "ctx", None),
            P("dp", "ctx", None),
            P(None, ("dp", "ctx")),
            P(None, ("dp", "ctx"), None),
            P(None, ("dp", "ctx")),
            P(None, ("dp", "ctx")),
            P(None, ("dp", "ctx"), None),
            P(None, ("dp", "ctx")),
            P(None, "dp", "ctx"),
            P(None, "dp", "ctx"),
            P(None, "ctx", "dp"),
        ),
        check_vma=False,
    )
```

```python
import functools

import jax
import jax.numpy as jnp
import numpy as np
from jax import lax
from jax.experimental import pallas as pl
from jax.experimental.pallas import tpu as pltpu
from jax.sharding import PartitionSpec as P

H = 14
KVH = 2
HD = 64
LAYERS = 2
D = 896
QKV = 1152
FS = 608
MESH = pl.DeviceIdType.MESH
BF = jnp.bfloat16
F32 = jnp.float32

eps_norm = 1e-06
rope_base = 1000000.0
neg_fill = -1e30


def place():
    dp = lax.axis_index("dp")
    ctx = lax.axis_index("ctx")
    return lax.div(dp, 4), lax.rem(dp, 4), lax.div(ctx, 2), lax.rem(ctx, 2)


def up1(v):
    return lax.rem(v + 1, 4)


def up2(v):
    return lax.rem(v + 2, 4)


def down1(v):
    return lax.rem(v + 3, 4)


def device(x, z, y, c):
    return (x * 4 + z, y * 2 + c)


def greet(peers):
    barrier = pltpu.get_barrier_semaphore()
    for peer in peers:
        pl.semaphore_signal(barrier, inc=1, device_id=peer, device_id_type=MESH)
    pl.semaphore_wait(barrier, len(peers))


class Mail:
    def __init__(self, send_sem, recv_sem, base=0, sent=None):
        self.send_sem = send_sem
        self.recv_sem = recv_sem
        self.base = base
        self.sent = [] if sent is None else sent

    def shifted(self, base):
        return Mail(self.send_sem, self.recv_sem, self.base + base, self.sent)

    def send(self, slot, src, dst, target):
        copy = pltpu.make_async_remote_copy(
            src_ref=src,
            dst_ref=dst,
            send_sem=self.send_sem.at[self.base + slot],
            recv_sem=self.recv_sem.at[self.base + slot],
            device_id=target,
            device_id_type=MESH,
        )
        copy.start()
        self.sent.append(copy)

    def take(self, slot, dst, source):
        pltpu.make_async_remote_copy(
            src_ref=dst,
            dst_ref=dst,
            send_sem=self.send_sem.at[self.base + slot],
            recv_sem=self.recv_sem.at[self.base + slot],
            device_id=source,
            device_id_type=MESH,
        ).wait_recv()

    def finish(self):
        for copy in self.sent:
            copy.wait_send()


class RowGather:
    slots = 8

    def __init__(self, mail, spot, block, along_x, along_z, local_sem):
        self.mail, self.spot, self.block = mail, spot, block
        self.along_x, self.along_z = along_x, along_z
        self.cut, self.rest = along_x.shape[0], along_z.shape[0]
        x, z = spot[:2]
        self.sa, self.sb = pl.ds(0, self.cut), pl.ds(self.cut, self.rest)
        self.own = [
            pltpu.make_async_copy(block.at[self.sa], along_x.at[:, x], local_sem.at[0]),
            pltpu.make_async_copy(block.at[self.sb], along_z.at[:, z], local_sem.at[1]),
        ]

    def step_one(self):
        x, z = self.spot[:2]
        to_xp, to_xm, to_zp, to_zm = ring_peers(self.spot)
        for copy in self.own:
            copy.start()
        self.mail.send(0, self.block.at[self.sa], self.along_x.at[:, x], to_xp)
        self.mail.send(1, self.block.at[self.sa], self.along_x.at[:, x], to_xm)
        self.mail.send(4, self.block.at[self.sb], self.along_z.at[:, z], to_zp)
        self.mail.send(5, self.block.at[self.sb], self.along_z.at[:, z], to_zm)

    def relays(self):
        x, z = self.spot[:2]
        to_xp, to_xm, to_zp, to_zm = ring_peers(self.spot)
        return (
            (0, self.along_x, self.cut, x, to_xp, to_xm),
            (4, self.along_z, self.rest, z, to_zp, to_zm),
        )

    def step_two(self):
        for base, ref, count, here, plus, minus in self.relays():
            behind, front = down1(here), up1(here)
            half = max(count // 2, 1)
            self.mail.take(base, ref.at[:, behind], minus)
            part = ref.at[pl.ds(0, half), behind]
            self.mail.send(base + 2, part, part, plus)
            self.mail.take(base + 1, ref.at[:, front], plus)
            if count > 1:
                part = ref.at[pl.ds(half, count - half), front]
                self.mail.send(base + 3, part, part, minus)

    def step_three(self):
        for base, ref, count, here, plus, minus in self.relays():
            half = max(count // 2, 1)
            self.mail.take(base + 2, ref.at[pl.ds(0, half), up2(here)], minus)
            if count > 1:
                self.mail.take(base + 3, ref.at[pl.ds(half, count - half), up2(here)], plus)
        for copy in self.own:
            copy.wait()


class PlaneFill:
    slots = 16

    def __init__(self, mail, spot, along_x, along_z, full, local_sem, mirror=None):
        self.mail, self.spot, self.full, self.mirror = mail, spot, full, mirror
        self.along_x, self.along_z = along_x, along_z
        self.cut, self.rest = along_x.shape[0], along_z.shape[0]
        x, z, y, c = spot
        self.other = device(x, z, y, 1 - c)
        self.copies = [
            pltpu.make_async_copy(along_x, full.at[self.first(z)], local_sem.at[0]),
            pltpu.make_async_copy(along_z, full.at[self.second(x)], local_sem.at[1]),
        ]

    def first(self, z, half=None):
        lead = pl.ds(0, self.cut) if half is None else pl.ds(half * (self.cut // 2), self.cut // 2)
        return (lead, pl.ds(0, 4), z)

    def second(self, x, half=None):
        if half is None:
            return (pl.ds(self.cut, self.rest), x, pl.ds(0, 4))
        if self.rest == 1:
            return (pl.ds(self.cut, 1), x, pl.ds(2 * half, 2))
        return (pl.ds(self.cut + half * (self.rest // 2), self.rest // 2), x, pl.ds(0, 4))

    def pass_on(self, slot, where, target):
        self.mail.send(slot, self.full.at[where], self.full.at[where], target)

    def share(self, slot, where, src=None):
        if self.mirror is not None:
            src = self.full.at[where] if src is None else src
            self.mail.send(slot, src, self.full.at[where], self.other)

    def step_one(self):
        x, z = self.spot[:2]
        to_xp, to_xm, to_zp, to_zm = ring_peers(self.spot)
        self.mail.send(0, self.along_x, self.full.at[self.first(z)], to_zp)
        self.mail.send(1, self.along_x, self.full.at[self.first(z)], to_zm)
        self.mail.send(2, self.along_z, self.full.at[self.second(x)], to_xp)
        self.mail.send(3, self.along_z, self.full.at[self.second(x)], to_xm)
        self.share(8, self.first(z), self.along_x)
        self.share(9, self.second(x), self.along_z)
        for copy in self.copies:
            copy.start()

    def step_two(self):
        x, z = self.spot[:2]
        to_xp, to_xm, to_zp, to_zm = ring_peers(self.spot)
        xp, xm, zp, zm = up1(x), down1(x), up1(z), down1(z)
        for slot, where, piece, source, target in (
            (0, self.first(zm), self.first(zm, 0), to_zm, to_zp),
            (2, self.second(xm), self.second(xm, 0), to_xm, to_xp),
            (1, self.first(zp), self.first(zp, 1), to_zp, to_zm),
            (3, self.second(xp), self.second(xp, 1), to_xp, to_xm),
        ):
            self.mail.take(slot, self.full.at[where], source)
            self.pass_on(4 + slot, piece, target)
            self.share(10 + slot, where)

    def step_three(self):
        x, z = self.spot[:2]
        to_xp, to_xm, to_zp, to_zm = ring_peers(self.spot)
        for slot, piece, source in (
            (4, self.first(up2(z), 0), to_zm),
            (6, self.second(up2(x), 0), to_xm),
            (5, self.first(up2(z), 1), to_zp),
            (7, self.second(up2(x), 1), to_xp),
        ):
            self.mail.take(slot, self.full.at[piece], source)
        self.share(14, self.first(up2(z)))
        self.share(15, self.second(up2(x)))
        for copy in self.copies:
            copy.wait()

    def step_four(self):
        x, z = self.spot[:2]
        xp, xm, zp, zm = up1(x), down1(x), up1(z), down1(z)
        for slot, where in (
            (8, self.first(z)),
            (9, self.second(x)),
            (10, self.first(zm)),
            (11, self.first(zp)),
            (12, self.second(xm)),
            (13, self.second(xp)),
            (14, self.first(up2(z))),
            (15, self.second(up2(x))),
        ):
            self.mail.take(slot, self.mirror.at[where], self.other)


def ring_peers(spot):
    x, z, y, c = spot
    return [
        device(up1(x), z, y, c),
        device(down1(x), z, y, c),
        device(x, up1(z), y, c),
        device(x, down1(z), y, c),
    ]


def ctx_peers(spot):
    x, z, y, c = spot
    return [device(x, z, up1(y), c), device(x, z, down1(y), c), device(x, z, y, 1 - c)]


def first_gather_kernel(
    one_ref, qkv_ref, bias_ref, out_ref, two_ref, m_ref,
    full, row_out, m_x, m_z,
    rows, vectors, offsets, line, a_x, a_z, send_sem, recv_sem, local_sem,
):
    spot = place()
    x, z, y, c = spot
    index = (x * 4 + z) * 8 + 2 * y + c
    mail = Mail(send_sem, recv_sem)
    vectors[...] = jnp.zeros_like(vectors)
    offsets[...] = jnp.zeros_like(offsets)
    vectors[0:2, 0:7] = one_ref[...].astype(F32)
    vectors[2:4, 0:7] = two_ref[...].astype(F32)
    offsets[0:2, 0:9] = bias_ref[...].astype(F32)
    gains = pltpu.roll(vectors[...], 7 * index, 1)
    bias = pltpu.roll(offsets[...], 9 * index - 128 * lax.div(index, 16), 1)
    for l in range(LAYERS):
        rows[l, 0:7, :] = qkv_ref[l, :, :1024].astype(F32)
        rows[l, 8:15, 0:128] = qkv_ref[l, :, 1024:].astype(F32)
        rows[l, 8:15, 128:1024] = out_ref[l].astype(F32)
        rows[l, 7:8, 0:D] = gains[l : l + 1, :D]
        rows[l, 15:16, 0:D] = gains[2 + l : 3 + l, :D]
        rows[l, 7:8, D:1024] = bias[l : l + 1, :128]
        rows[l, 15:16, D:1024] = bias[l : l + 1, 128:]
    line[:, y] = rows[...].astype(BF)
    yp, ym, y2 = up1(y), down1(y), up2(y)
    to_yp, to_ym, other = ctx_peers(spot)
    to_y2 = device(x, z, y2, c)
    greet(ring_peers(spot) + [to_yp, to_ym, other, to_y2])
    mail.send(0, line.at[:, y], line.at[:, y], to_yp)
    mail.send(1, line.at[:, y], line.at[:, y], to_ym)
    mail.send(2, line.at[:, y], line.at[:, y], to_y2)
    row = RowGather(mail.shifted(3), spot, line.at[0], a_x, a_z, local_sem.at[pl.ds(0, 2)])
    fill = PlaneFill(
        mail.shifted(11), spot, a_x, a_z, full.at[c], local_sem.at[pl.ds(2, 2)], full.at[1 - c]
    )
    feed = RowGather(mail.shifted(27), spot, m_ref.at[0], m_x, m_z, local_sem.at[pl.ds(4, 2)])
    mail.take(0, line.at[:, ym], to_ym)
    mail.take(1, line.at[:, yp], to_yp)
    mail.take(2, line.at[:, y2], to_y2)
    row.step_one()
    kept = pltpu.make_async_copy(line.at[1], row_out, local_sem.at[6])
    kept.start()
    row.step_two()
    row.step_three()
    fill.step_one()
    feed.step_one()
    fill.step_two()
    feed.step_two()
    fill.step_three()
    feed.step_three()
    fill.step_four()
    kept.wait()
    mail.finish()


def first_gather(gain_one, w_qkv, b_qkv, w_out, gain_two, m_block):
    return pl.pallas_call(
        first_gather_kernel,
        out_shape=(
            jax.ShapeDtypeStruct((2, 4, 4, 4, 16, 1024), BF),
            jax.ShapeDtypeStruct((4, 16, 1024), BF),
            jax.ShapeDtypeStruct((2, 4, 56, FS), BF),
            jax.ShapeDtypeStruct((1, 4, 56, FS), BF),
        ),
        in_specs=[pl.BlockSpec(memory_space=pltpu.VMEM)] * 5 + [pl.BlockSpec(memory_space=pl.ANY)],
        out_specs=[pl.BlockSpec(memory_space=pl.ANY)] * 4,
        scratch_shapes=[
            pltpu.VMEM((2, 16, 1024), F32),
            pltpu.VMEM((8, 1024), F32),
            pltpu.VMEM((8, 256), F32),
            pltpu.VMEM((2, 4, 16, 1024), BF),
            pltpu.VMEM((2, 4, 16, 1024), BF),
            pltpu.VMEM((2, 4, 16, 1024), BF),
            pltpu.SemaphoreType.DMA((35,)),
            pltpu.SemaphoreType.DMA((35,)),
            pltpu.SemaphoreType.DMA((7,)),
        ],
        compiler_params=pltpu.CompilerParams(
            collective_id=1, has_side_effects=True, vmem_limit_bytes=16 * 1024 * 1024
        ),
        name="first_gather",
    )(gain_one, w_qkv, b_qkv, w_out, gain_two, m_block)


class PlaneSum:
    def __init__(self, mail, base, spot, g, cut, buffers):
        self.mail, self.base, self.spot, self.g, self.cut = mail, base, spot, g, cut
        self.count = g.shape[0]
        self.buffers = buffers

    @staticmethod
    def scratch(slabs, cut, rows, columns):
        rest = slabs - cut
        out = [
            pltpu.VMEM((2, cut, 2, rows, columns), BF),
            pltpu.VMEM((2, cut, 4, rows, columns), BF),
            pltpu.VMEM((2, rest, 2, rows, columns), BF),
            pltpu.VMEM((2, rest, 4, rows, columns), BF),
            pltpu.VMEM((2, cut // 2, rows, columns), BF),
            pltpu.VMEM((2, cut, rows, columns), BF),
            pltpu.VMEM((2, max(rest // 2, 1), rows, columns), BF),
            pltpu.VMEM((2, rest, rows, columns), BF),
        ]
        return out

    @staticmethod
    def peers(spot, slabs, cut):
        x, z, y, c = spot
        near = [device(up1(x), z, y, c), device(down1(x), z, y, c), device(x, up1(z), y, c), device(x, down1(z), y, c)]
        return near + ([device(x, up2(z), y, c)] if slabs - cut == 1 else [])

    def names(self):
        x, z, y, c = self.spot
        xp, xm, zp, zm = up1(x), down1(x), up1(z), down1(z)
        to = (device(xp, z, y, c), device(xm, z, y, c), device(x, zp, y, c), device(x, zm, y, c))
        return x, z, xp, xm, zp, zm, up2(x), up2(z), to

    def send(self, slot, src, dst, target):
        self.mail.send(self.base + slot, src, dst, target)

    def take(self, slot, dst, source):
        self.mail.take(self.base + slot, dst, source)

    def add(self, where, extra):
        part = self.g.at[where]
        part[...] = (part[...].astype(F32) + extra.astype(F32)).astype(BF)

    def step_one(self):
        x, z, xp, xm, zp, zm, x2, z2, (to_xp, to_xm, to_zp, to_zm) = self.names()
        fa, ga, fb, gb, pa, qa, pb, qb = self.buffers
        sa, sb = pl.ds(0, self.cut), pl.ds(self.cut, self.count - self.cut)
        lo, hi = pl.ds(0, 2), pl.ds(2, 2)
        self.send(0, self.g.at[sa, lo, z2], fa.at[0], to_zp)
        self.send(1, self.g.at[sa, hi, z2], fa.at[1], to_zm)
        self.send(2, self.g.at[sb, x2, lo], fb.at[0], to_xp)
        self.send(3, self.g.at[sb, x2, hi], fb.at[1], to_xm)

    def step_two(self):
        x, z, xp, xm, zp, zm, x2, z2, (to_xp, to_xm, to_zp, to_zm) = self.names()
        fa, ga, fb, gb, pa, qa, pb, qb = self.buffers
        sa, sb = pl.ds(0, self.cut), pl.ds(self.cut, self.count - self.cut)
        lo, hi, every = pl.ds(0, 2), pl.ds(2, 2), pl.ds(0, 4)
        self.take(0, fa.at[0], to_zm)
        self.add((sa, lo, zp), fa[0])
        self.send(4, self.g.at[sa, every, zp], ga.at[0], to_zp)
        self.take(2, fb.at[0], to_xm)
        self.add((sb, xp, lo), fb[0])
        self.send(6, self.g.at[sb, xp, every], gb.at[0], to_xp)
        self.take(1, fa.at[1], to_zp)
        self.add((sa, hi, zm), fa[1])
        self.send(5, self.g.at[sa, every, zm], ga.at[1], to_zm)
        self.take(3, fb.at[1], to_xp)
        self.add((sb, xm, hi), fb[1])
        self.send(7, self.g.at[sb, xm, every], gb.at[1], to_xm)

    def step_three(self):
        x, z, xp, xm, zp, zm, x2, z2, (to_xp, to_xm, to_zp, to_zm) = self.names()
        fa, ga, fb, gb, pa, qa, pb, qb = self.buffers
        y, c = self.spot[2:]
        cut, rest = self.cut, self.count - self.cut
        sa, sb = pl.ds(0, cut), pl.ds(cut, rest)
        every = pl.ds(0, 4)
        self.take(4, ga.at[0], to_zm)
        self.take(5, ga.at[1], to_zp)
        self.add((sa, every, z), ga[0].astype(F32) + ga[1].astype(F32))
        self.send(8, self.g.at[pl.ds(0, cut // 2), x2, z], pa.at[0], to_xp)
        self.send(9, self.g.at[pl.ds(cut // 2, cut // 2), x2, z], pa.at[1], to_xm)
        self.take(6, gb.at[0], to_xm)
        self.take(7, gb.at[1], to_xp)
        self.add((sb, x, every), gb[0].astype(F32) + gb[1].astype(F32))
        if rest == 1:
            self.send(10, self.g.at[sb, x, z2], pb.at[0], device(x, z2, y, c))
            self.send(14, self.g.at[sb, x, zp], qb.at[0], to_zp)
            self.send(15, self.g.at[sb, x, zm], qb.at[1], to_zm)
        else:
            self.send(10, self.g.at[pl.ds(cut, rest // 2), x, z2], pb.at[0], to_zp)
            self.send(11, self.g.at[pl.ds(cut + rest // 2, rest // 2), x, z2], pb.at[1], to_zm)

    def step_four(self):
        x, z, xp, xm, zp, zm, x2, z2, (to_xp, to_xm, to_zp, to_zm) = self.names()
        fa, ga, fb, gb, pa, qa, pb, qb = self.buffers
        cut, rest = self.cut, self.count - self.cut
        sa, sb = pl.ds(0, cut), pl.ds(cut, rest)
        self.take(8, pa.at[0], to_xm)
        self.add((pl.ds(0, cut // 2), xp, z), pa[0])
        self.send(12, self.g.at[sa, xp, z], qa.at[0], to_xp)
        self.take(9, pa.at[1], to_xp)
        self.add((pl.ds(cut // 2, cut // 2), xm, z), pa[1])
        self.send(13, self.g.at[sa, xm, z], qa.at[1], to_xm)
        if rest > 1:
            self.take(10, pb.at[0], to_zm)
            self.add((pl.ds(cut, rest // 2), x, zp), pb[0])
            self.send(14, self.g.at[sb, x, zp], qb.at[0], to_zp)
            self.take(11, pb.at[1], to_zp)
            self.add((pl.ds(cut + rest // 2, rest // 2), x, zm), pb[1])
            self.send(15, self.g.at[sb, x, zm], qb.at[1], to_zm)

    def step_five(self, out):
        x, z, xp, xm, zp, zm, x2, z2, (to_xp, to_xm, to_zp, to_zm) = self.names()
        fa, ga, fb, gb, pa, qa, pb, qb = self.buffers
        y, c = self.spot[2:]
        cut, rest = self.cut, self.count - self.cut
        sa, sb = pl.ds(0, cut), pl.ds(cut, rest)
        self.take(12, qa.at[0], to_xm)
        self.take(13, qa.at[1], to_xp)
        out[sa] = (
            self.g.at[sa, x, z][...].astype(F32) + qa[0].astype(F32) + qa[1].astype(F32)
        ).astype(out.dtype)
        self.take(14, qb.at[0], to_zm)
        self.take(15, qb.at[1], to_zp)
        total = self.g.at[sb, x, z][...].astype(F32) + qb[0].astype(F32) + qb[1].astype(F32)
        if rest == 1:
            self.take(10, pb.at[0], device(x, z2, y, c))
            total = total + pb[0].astype(F32)
        out[sb] = total.astype(out.dtype)


class AttentionSum:
    slots = 23

    def __init__(self, mail, spot, mine, theirs, refs):
        self.mail, self.spot, self.mine, self.theirs = mail, spot, mine, theirs
        self.near, self.block, self.got = refs[:3]
        self.plane = PlaneSum(mail, 7, spot, mine, 2, refs[3:])

    @staticmethod
    def scratch():
        return [
            pltpu.VMEM((4, 4, 4, 16, 1024), BF),
            pltpu.VMEM((4, 16, 1024), BF),
            pltpu.VMEM((3, 16, 1024), BF),
        ] + PlaneSum.scratch(4, 2, 16, 1024)

    def start(self, i):
        x, z, y, c = self.spot
        self.mail.send(i, self.theirs.at[:, i], self.near.at[:, i], device(x, z, y, 1 - c))

    def cores(self):
        x, z, y, c = self.spot
        for i in range(4):
            self.mail.take(i, self.near.at[:, i], device(x, z, y, 1 - c))
            part = self.mine.at[:, i]
            part[...] = (part[...].astype(F32) + self.near[:, i].astype(F32)).astype(BF)
        self.plane.step_one()

    def rows(self):
        x, z, y, c = self.spot
        self.plane.step_five(self.block)
        for k, step in enumerate((up1, up2, down1)):
            to = device(x, z, step(y), c)
            self.mail.send(4 + k, self.block.at[step(y)], self.got.at[k], to)

    def last(self, out):
        x, z, y, c = self.spot
        total = self.block[y].astype(F32)
        for k, step in enumerate((down1, up2, up1)):
            self.mail.take(4 + k, self.got.at[k], device(x, z, step(y), c))
            total = total + self.got[k].astype(F32)
        out[...] = total


def nn(left, right):
    return jnp.dot(left, right, preferred_element_type=F32)


def nt(left, right):
    return lax.dot_general(left, right, (((1,), (1,)), ((), ())), preferred_element_type=F32)


def tn(left, right):
    return lax.dot_general(left, right, (((0,), (0,)), ((), ())), preferred_element_type=F32)


def mlp_scratch():
    return [
        pltpu.VMEM((4, 2, 128, D), BF),
        pltpu.VMEM((4, 2, 128, D), BF),
        pltpu.VMEM((4, 128, D), BF),
        pltpu.VMEM((3, 128, D), BF),
        pltpu.VMEM((2, 64, D), BF),
        pltpu.VMEM((2, 64, D), BF),
        pltpu.VMEM((2, 128, D), BF),
    ]


def mlp_exchange(mail, spot, src, buffers, chunk, fillers, hook):
    rows, part, near, own, far, fin, got = buffers
    x, z, y, c = spot
    yp, ym, y2 = up1(y), down1(y), up2(y)
    to_yp, to_ym, other = device(x, z, yp, c), device(x, z, ym, c), device(x, z, y, 1 - c)
    begin, end = pl.ds(0, 32), pl.ds(32, 32)
    first, second = pl.ds(0, 64), pl.ds(64, 64)
    mail.send(0, src.at[first], rows.at[y, c, first], to_yp)
    mail.send(1, src.at[second], rows.at[y, c, second], to_ym)
    mail.send(2, src, rows.at[y, c], other)
    mail.send(19, src.at[second], rows.at[y, c, second], to_yp)
    mail.send(20, src.at[first], rows.at[y, c, first], to_ym)
    rows[y, c] = src[...]
    mail.take(2, rows.at[y, 1 - c], other)
    chunk(y)
    mail.send(12, part.at[y, 1 - c], near.at[3], other)
    mail.take(0, rows.at[ym, c, first], to_ym)
    mail.send(3, rows.at[ym, c, first], rows.at[ym, c, first], to_yp)
    mail.take(1, rows.at[yp, c, second], to_yp)
    mail.send(5, rows.at[yp, c, second], rows.at[yp, c, second], to_ym)
    mail.take(19, rows.at[ym, c, second], to_ym)
    mail.send(4, rows.at[ym, c], rows.at[ym, c], other)
    mail.take(20, rows.at[yp, c, first], to_yp)
    mail.send(6, rows.at[yp, c], rows.at[yp, c], other)
    mail.take(4, rows.at[ym, 1 - c], other)
    chunk(ym)
    mail.send(11, part.at[ym, 1 - c], near.at[2], other)
    hook()
    mail.take(6, rows.at[yp, 1 - c], other)
    chunk(yp)
    mail.send(10, part.at[yp, 1 - c], near.at[1], other)
    mail.take(3, rows.at[y2, c, first], to_ym)
    mail.send(7, rows.at[y2, c, first], rows.at[y2, c, first], other)
    mail.take(5, rows.at[y2, c, second], to_yp)
    mail.send(8, rows.at[y2, c, second], rows.at[y2, c, second], other)
    mail.take(11, near.at[2], other)
    own[2] = (part[ym, c].astype(F32) + near[2].astype(F32)).astype(BF)
    mail.send(16, own.at[2], got.at[1], to_ym)
    mail.take(10, near.at[1], other)
    own[1] = (part[yp, c].astype(F32) + near[1].astype(F32)).astype(BF)
    mail.send(15, own.at[1], got.at[0], to_yp)
    mail.take(7, rows.at[y2, 1 - c, first], other)
    mail.take(8, rows.at[y2, 1 - c, second], other)
    chunk(y2)
    mail.send(9, part.at[y2, 1 - c], near.at[0], other)
    fillers[0]()
    mail.take(9, near.at[0], other)
    own[0] = (part[y2, c].astype(F32) + near[0].astype(F32)).astype(BF)
    mail.send(13, own.at[0, pl.ds(0, 32)], far.at[0, begin], to_yp)
    mail.send(14, own.at[0, pl.ds(64, 32)], far.at[1, begin], to_ym)
    mail.send(21, own.at[0, pl.ds(32, 32)], far.at[0, end], to_yp)
    mail.send(22, own.at[0, pl.ds(96, 32)], far.at[1, end], to_ym)
    fillers[1]()
    mail.take(13, far.at[0, begin], to_ym)
    mail.send(17, far.at[0, begin], fin.at[0, begin], to_yp)
    mail.take(14, far.at[1, begin], to_yp)
    mail.send(18, far.at[1, begin], fin.at[1, begin], to_ym)
    mail.take(21, far.at[0, end], to_ym)
    mail.send(23, far.at[0, end], fin.at[0, end], to_yp)
    mail.take(22, far.at[1, end], to_yp)
    mail.send(24, far.at[1, end], fin.at[1, end], to_ym)
    fillers[2]()
    mail.take(12, near.at[3], other)
    mail.take(15, got.at[0], to_ym)
    mail.take(16, got.at[1], to_yp)
    mail.take(17, fin.at[0, begin], to_ym)
    mail.take(18, fin.at[1, begin], to_yp)
    mail.take(23, fin.at[0, end], to_ym)
    mail.take(24, fin.at[1, end], to_yp)
    total = (
        part[y, c].astype(F32)
        + near[3].astype(F32)
        + got[0].astype(F32)
        + got[1].astype(F32)
    )
    return total + fin[...].reshape(128, D).astype(F32)


def nothing():
    return None


def swap_halves(u):
    width = u.shape[1]
    lane = lax.broadcasted_iota(jnp.int32, u.shape, 1)
    return jnp.where(
        lax.rem(lane, 64) < 32, pltpu.roll(u, width - 32, 1), pltpu.roll(u, 32, 1)
    )


def normal(v):
    r = lax.rsqrt(jnp.mean(v * v, axis=-1, keepdims=True) + eps_norm)
    return v * r, r


def forward_kernel(layer, *refs):
    x_ref, a_ref, m_ref, pick_ref, cos_ref, sin_ref, qpos_ref, kpos_ref = refs[:8]
    refs = refs[8:]
    if layer == 0:
        row_ref, shard_ref, m_z_ref = refs[:3]
        refs = refs[3:]
    out_ref, vec_ref, mid_ref, att_ref, qs_ref, kvs_ref, probs_ref, low_ref, high_ref = refs[:9]
    hr_ref, gate_ref, up_ref = refs[9:12]
    refs = refs[12:]
    if layer == 0:
        m_zero, m_one, a_one = refs[:3]
        refs = refs[3:]
    blocks, low, high, kv, kvs, probs, heads, mask, att, qs, mid, h2 = refs[:12]
    buffers, refs = refs[12:19], refs[19:]
    w, gate, up, send_sem, recv_sem, local_sem = refs[:6]
    rows, part = buffers[0], buffers[1]
    spot = place()
    x, z, y, c = spot
    mail = Mail(send_sem, recv_sem)
    load = pltpu.make_async_copy(a_ref, blocks, local_sem.at[0])
    load.start()
    if layer == 0:
        a_x, a_z, m_x, m_z, slabs = refs[6:]

        def sems(k):
            return local_sem.at[pl.ds(21 + 2 * k, 2)]

        fill = PlaneFill(mail.shifted(34), spot, m_ref, m_z_ref, m_zero, sems(0))
        a_row = RowGather(mail.shifted(50), spot, row_ref, a_x, a_z, sems(1))
        m_row = RowGather(mail.shifted(58), spot, shard_ref.at[1], m_x, m_z, sems(2))
        a_fill = PlaneFill(
            mail.shifted(66), spot, a_x, a_z, a_one.at[c], sems(3), a_one.at[1 - c]
        )
        m_fill = PlaneFill(mail.shifted(82), spot, m_x, m_z, m_one, sems(4))
        load_w = pltpu.make_async_copy(m_zero, slabs, local_sem.at[1])
        greet(ctx_peers(spot) + ring_peers(spot))
        fill.step_one()
        a_row.step_one()
        m_row.step_one()
    else:
        load_w = pltpu.make_async_copy(m_ref, w, local_sem.at[1])
        load_w.start()
        greet(ctx_peers(spot))
    inputs = x_ref[...].astype(F32)
    n, r = normal(inputs)
    load.wait()
    spare = []
    for g in range(8):
        group = jnp.concatenate(
            [blocks[k % 2, k % 8 // 2, g // 2, 2 * (g % 2) + k // 8] for k in range(16)], axis=0
        )
        low[112 * g : 112 * (g + 1)] = nn(pick_ref[0:112, :], group).astype(BF)
        high[112 * g : 112 * (g + 1)] = nn(pick_ref[112:224, :], group).astype(BF)
        spare.append(nn(pick_ref[224:240, :], group))
    gains = functools.reduce(lambda u, v: u + v, [block[0:2, :D] for block in spare])
    vec_ref[0:2, 0:D] = gains
    for j in range(9):
        piece = jnp.zeros((1, 128), F32)
        if j < 8:
            piece = piece + spare[j][0:1, D:]
        if j > 0:
            piece = piece + spare[j - 1][1:2, D:]
        vec_ref[2:3, 128 * j : 128 * (j + 1)] = piece
    stores = [
        pltpu.make_async_copy(low, low_ref, local_sem.at[2]),
        pltpu.make_async_copy(high, high_ref, local_sem.at[3]),
    ]
    hidden = (n * gains[0:1]).astype(BF)
    packed = nn(hidden, low[...]) + vec_ref[2:3, :1024]
    values = nn(hidden, high[:, :128]) + vec_ref[2:3, 1024:]
    cos = jnp.concatenate([cos_ref[...]] * 8, axis=1)
    sin = jnp.concatenate([sin_ref[...]] * 8, axis=1)
    turned = packed * cos + swap_halves(packed) * sin
    kv[y, c, :, 0:128] = turned[:, D:].astype(BF)
    kv[y, c, :, 128:256] = values.astype(BF)
    yp, ym, y2 = up1(y), down1(y), up2(y)
    to_yp, to_ym, other = ctx_peers(spot)
    first, second = pl.ds(0, 64), pl.ds(64, 64)
    mail.send(0, kv.at[y, c], kv.at[y, c], to_yp)
    mail.send(1, kv.at[y, c], kv.at[y, c], to_ym)
    mail.send(2, kv.at[y, c], kv.at[y, c], other)
    for store in stores:
        store.start()
    if layer == 0:
        a_row.step_two()
        m_row.step_two()
    for h in range(H):
        qs[h] = (turned[:, HD * h : HD * (h + 1)] * HD ** (-0.5)).astype(BF)
    mask[...] = jnp.where(kpos_ref[...] <= qpos_ref[...], 0.0, 1.0)
    mail.take(0, kv.at[ym, c], to_ym)
    mail.send(3, kv.at[ym, c, first], kv.at[ym, c, first], to_yp)
    mail.send(4, kv.at[ym, c], kv.at[ym, c], other)
    mail.take(1, kv.at[yp, c], to_yp)
    mail.send(5, kv.at[yp, c, second], kv.at[yp, c, second], to_ym)
    mail.send(6, kv.at[yp, c], kv.at[yp, c], other)
    mail.take(3, kv.at[y2, c, first], to_ym)
    mail.send(7, kv.at[y2, c, first], kv.at[y2, c, first], other)
    mail.take(5, kv.at[y2, c, second], to_yp)
    mail.send(8, kv.at[y2, c, second], kv.at[y2, c, second], other)
    if layer == 0:
        fill.step_two()
        a_row.step_three()
        m_row.step_three()
    mail.take(2, kv.at[y, 1 - c], other)
    mail.take(4, kv.at[ym, 1 - c], other)
    mail.take(6, kv.at[yp, 1 - c], other)
    mail.take(7, kv.at[y2, 1 - c, first], other)
    mail.take(8, kv.at[y2, 1 - c, second], other)
    for i in range(4):
        kvs[i] = kv[:, :, :, HD * i : HD * (i + 1)].reshape(1024, HD)

    def body(i, carry):
        for k in range(KVH):
            h = i + 7 * k
            scores = nt(qs[h], kvs[k])
            scores = jnp.where(mask[...] > 0.5, neg_fill, scores)
            e = jnp.exp(scores - jnp.max(scores, axis=-1, keepdims=True))
            p = (e * (1.0 / jnp.sum(e, axis=-1, keepdims=True))).astype(BF)
            probs[h] = p
            heads[h] = nn(p, kvs[2 + k]).astype(BF)
        return carry

    lax.fori_loop(0, 4, body, 0)
    if layer == 0:
        a_fill.step_one()
    lax.fori_loop(4, 7, body, 0)
    att[...] = jnp.concatenate([heads[h] for h in range(H)], axis=1)
    mid[...] = inputs + nn(att[...], high[:, 128:])
    h2[...] = (normal(mid[...])[0] * gains[1:2]).astype(BF)
    for i, (src, dst) in enumerate(
        ((kvs, kvs_ref), (probs, probs_ref), (att, att_ref), (qs, qs_ref), (mid, mid_ref))
    ):
        stores.append(pltpu.make_async_copy(src, dst, local_sem.at[4 + i]))
        stores[-1].start()
    if layer == 0:
        fill.step_three()
        load_w.start()
        m_fill.step_one()

    loaded = []

    def chunk(row):
        if not loaded:
            load_w.wait()
            if layer == 0:
                for member in range(3):
                    for i in range(16):
                        w[member, 56 * i : 56 * (i + 1)] = slabs[member, i // 4, i % 4]
            loaded.append(True)
        h = rows[row].reshape(256, D)
        g = nn(h, w[0])
        u = nn(h, w[1])
        gate[row] = g.astype(BF)
        up[row] = u.astype(BF)
        act = (g / (1.0 + jnp.exp(-g)) * u).astype(BF)
        part[row] = nt(act, w[2]).astype(BF).reshape(2, 128, D)
        k = 9 + 3 * (len(loaded) - 1)
        loaded.append(True)
        for i, (src, dst) in enumerate(((rows, hr_ref), (gate, gate_ref), (up, up_ref))):
            stores.append(pltpu.make_async_copy(src.at[row], dst.at[row], local_sem.at[k + i]))
            stores[-1].start()

    steps = [nothing] * 4
    if layer == 0:
        steps = [a_fill.step_two, a_fill.step_three, m_fill.step_two, m_fill.step_three]
    total = mlp_exchange(mail.shifted(9), spot, h2, buffers, chunk, steps[1:], steps[0])
    out_ref[...] = mid[...] + total
    if layer == 0:
        a_fill.step_four()
    for store in stores:
        store.wait()
    mail.finish()


def forward(layer, state, a_full, m_full, pick, tables, positions, *shards):
    anywhere = pl.BlockSpec(memory_space=pl.ANY)
    vmem = pl.BlockSpec(memory_space=pltpu.VMEM)
    out_shape = [
        jax.ShapeDtypeStruct((128, D), F32),
        jax.ShapeDtypeStruct((8, QKV), F32),
        jax.ShapeDtypeStruct((128, D), F32),
        jax.ShapeDtypeStruct((128, D), BF),
        jax.ShapeDtypeStruct((H, 128, HD), BF),
        jax.ShapeDtypeStruct((4, 1024, HD), BF),
        jax.ShapeDtypeStruct((H, 128, 1024), BF),
        jax.ShapeDtypeStruct((D, 1024), BF),
        jax.ShapeDtypeStruct((D, 1024), BF),
        jax.ShapeDtypeStruct((4, 2, 128, D), BF),
        jax.ShapeDtypeStruct((4, 256, FS), BF),
        jax.ShapeDtypeStruct((4, 256, FS), BF),
    ]
    operands = [state, a_full, m_full, pick, *tables, *positions]
    in_specs = [vmem, anywhere, anywhere] + [vmem] * 5
    slots = 34
    extra = []
    if layer == 0:
        out_shape += [
            jax.ShapeDtypeStruct((3, 4, 4, 56, FS), BF),
            jax.ShapeDtypeStruct((3, 4, 4, 56, FS), BF),
            jax.ShapeDtypeStruct((2, 4, 4, 4, 16, 1024), BF),
        ]
        operands += shards
        in_specs += [anywhere] * 3
        slots = 98
        extra = [
            pltpu.VMEM((2, 4, 16, 1024), BF),
            pltpu.VMEM((2, 4, 16, 1024), BF),
            pltpu.VMEM((2, 4, 56, FS), BF),
            pltpu.VMEM((1, 4, 56, FS), BF),
            pltpu.VMEM((3, 4, 4, 56, FS), BF),
        ]
    return pl.pallas_call(
        functools.partial(forward_kernel, layer),
        out_shape=tuple(out_shape),
        in_specs=in_specs,
        out_specs=[vmem] * 2 + [anywhere] * (len(out_shape) - 2),
        scratch_shapes=[
            pltpu.VMEM((2, 4, 4, 4, 16, 1024), BF),
            pltpu.VMEM((D, 1024), BF),
            pltpu.VMEM((D, 1024), BF),
            pltpu.VMEM((4, 2, 128, 256), BF),
            pltpu.VMEM((4, 1024, HD), BF),
            pltpu.VMEM((H, 128, 1024), BF),
            pltpu.VMEM((H, 128, HD), BF),
            pltpu.VMEM((128, 1024), F32),
            pltpu.VMEM((128, D), BF),
            pltpu.VMEM((H, 128, HD), BF),
            pltpu.VMEM((128, D), F32),
            pltpu.VMEM((128, D), BF),
        ]
        + mlp_scratch()
        + [
            pltpu.VMEM((3, D, FS), BF),
            pltpu.VMEM((4, 256, FS), BF),
            pltpu.VMEM((4, 256, FS), BF),
            pltpu.SemaphoreType.DMA((slots,)),
            pltpu.SemaphoreType.DMA((slots,)),
            pltpu.SemaphoreType.DMA((31,)),
        ]
        + extra,
        compiler_params=pltpu.CompilerParams(
            collective_id=12 + layer, has_side_effects=True, vmem_limit_bytes=56 * 1024 * 1024
        ),
        name="forward_layer_%d" % layer,
    )(*operands)


BACK_SLOTS = {1: 45, 0: 91}


def backward_kernel(layer, *refs):
    g_ref, x_ref, vec_ref, cos_ref, sin_ref, place_ref = refs[:6]
    w_ref, hr_ref, gate_ref, up_ref, mid_ref, att_ref, qs_ref = refs[6:13]
    kvs_ref, probs_ref, low_ref, high_ref = refs[13:17]
    refs = refs[17:]
    if layer == 0:
        before, gin_ref, m_out, a_zero, a_one = refs[:5]
        refs = refs[5:]
    else:
        gin_ref, m_out, a_out = refs[:3]
        refs = refs[3:]
    buffers, refs = refs[:7], refs[7:]
    w, hr, gate, up, act, src, mid, att, qs = refs[:9]
    low, high, kvs, probs, m, gatt, gqs, part, near, own, got, glow, ghigh, special = refs[9:23]
    plane_refs, refs = refs[23:31], refs[31:]
    send_sem, recv_sem, local_sem = refs[-3:]
    rows, back = buffers[0], buffers[1]
    spot = place()
    x, z, y, c = spot
    mail = Mail(send_sem, recv_sem)
    pairs = (
        (w_ref, w), (gate_ref, gate), (up_ref, up), (hr_ref, hr), (high_ref, high), (mid_ref, mid),
        (att_ref, att), (probs_ref, probs), (kvs_ref, kvs), (qs_ref, qs), (low_ref, low),
    )
    loads = [pltpu.make_async_copy(u, v, local_sem.at[i]) for i, (u, v) in enumerate(pairs)]
    for load in loads[:4]:
        load.start()
    src[...] = g_ref[...].astype(BF)
    yp, ym, y2 = up1(y), down1(y), up2(y)
    to_yp, to_ym, other = ctx_peers(spot)
    to_y2 = device(x, z, y2, c)
    greet([to_yp, to_ym, other, to_y2] + PlaneSum.peers(spot, 3, 2))
    plane = PlaneSum(mail, 29, spot, m, 2, plane_refs)
    older = final = None
    if layer == 0:
        older_mine, older_refs = refs[0], refs[1:12]
        pair, final_refs = refs[12], refs[13:24]
        older = AttentionSum(mail.shifted(45), spot, older_mine, before.at[1 - c], older_refs)
        final = AttentionSum(mail.shifted(68), spot, pair.at[0], pair.at[1], final_refs)
        older_load = pltpu.make_async_copy(before.at[c], older_mine, local_sem.at[11])
        older_load.start()

    loaded = []

    def chunk(row):
        if not loaded:
            for load in loads[:3]:
                load.wait()
            loaded.append(True)
            for load in loads[4:]:
                load.start()
        gz = rows[row].reshape(256, D)
        gact = nn(gz, w[2])
        g = gate[row].astype(F32)
        u = up[row].astype(F32)
        s = 1.0 / (1.0 + jnp.exp(-g))
        silu = g * s
        act[row] = (silu * u).astype(BF)
        gg = (gact * u * (s + silu * (1.0 - s))).astype(BF)
        gu = (gact * silu).astype(BF)
        gate[row] = gg
        up[row] = gu
        back[row] = (nt(gg, w[0]) + nt(gu, w[1])).astype(BF).reshape(2, 128, D)

    def weight_grad(member, left, right):
        r = right[...].reshape(1024, FS)
        for i in range(7):
            l = left[:, :, :, 128 * i : 128 * (i + 1)].reshape(1024, 128)
            tile = tn(l, r).astype(BF)
            for b in range(16):
                lo, hi = max(56 * b, 128 * i), min(56 * (b + 1), 128 * (i + 1))
                if lo < hi:
                    m[member, b // 4, b % 4, lo - 56 * b : hi - 56 * b] = tile[
                        lo - 128 * i : hi - 128 * i
                    ]

    def first_filler():
        weight_grad(2, rows, act)

    def second_filler():
        loads[3].wait()
        weight_grad(0, hr, gate)

    def third_filler():
        weight_grad(1, hr, up)
        plane.step_one()

    def hook():
        if older:
            for i in range(4):
                older.start(i)

    ghid2 = mlp_exchange(
        mail, spot, src, buffers, chunk, [first_filler, second_filler, third_filler], hook
    )
    if older:
        older_load.wait()
        older.cores()
    for load in loads[4:7]:
        load.wait()
    n, r = normal(mid[...])
    t = ghid2 * vec_ref[1:2, :D]
    gmid = g_ref[...].astype(F32) + r * (t - n * jnp.mean(t * n, axis=-1, keepdims=True))
    ggain_two = jnp.sum(ghid2 * n, axis=0, keepdims=True)
    gin_ref[...] = gmid
    gy = gmid.astype(BF)
    ga = nt(gy, high[:, 128:]).astype(BF)
    for h in range(H):
        gatt[h] = ga[:, HD * h : HD * (h + 1)]
    ghigh[:, 128:] = tn(att[...], gy).astype(BF)
    for load in loads[7:]:
        load.wait()
    plane.step_two()
    for k in range(KVH):
        heads = pl.ds(7 * k, 7)
        gv = tn(gatt[heads].reshape(D, HD), probs[heads].reshape(D, 1024)).astype(BF)
        for j in range(8):
            part[j // 2, j % 2, 128 + HD * k : 128 + HD * (k + 1)] = gv[:, 128 * j : 128 * (j + 1)]
    if older:
        older.plane.step_two()

    def body(i, carry):
        for k in range(KVH):
            h = i + 7 * k
            p = probs[h].astype(F32)
            gp = nt(gatt[h], kvs[2 + k])
            s = (p * (gp - jnp.sum(gp * p, axis=-1, keepdims=True))).astype(BF)
            probs[h] = s
            gqs[h] = nn(s, kvs[k])
        return carry

    lax.fori_loop(0, 7, body, 0)
    for k in range(KVH):
        heads = pl.ds(7 * k, 7)
        gk = tn(qs[heads].reshape(D, HD), probs[heads].reshape(D, 1024)).astype(BF)
        for j in range(8):
            part[j // 2, j % 2, HD * k : HD * (k + 1)] = gk[:, 128 * j : 128 * (j + 1)]
    mail.send(25, part.at[:, 1 - c], near, other)
    plane.step_three()
    cos = jnp.concatenate([cos_ref[...]] * 7, axis=1)
    sin = jnp.concatenate([sin_ref[...]] * 7, axis=1)
    gq = jnp.concatenate([gqs[h] for h in range(H)], axis=1) * HD ** (-0.5)
    gq = (gq * cos - swap_halves(gq) * sin).astype(BF)
    inputs = x_ref[...].astype(F32)
    n, r = normal(inputs)
    hidden = (n * vec_ref[0:1, :D]).astype(BF)
    mail.take(25, near, other)
    own[...] = (part[:, c].astype(F32) + near[...].astype(F32)).astype(BF)
    mail.send(26, own.at[yp], got.at[0], to_yp)
    mail.send(27, own.at[ym], got.at[1], to_ym)
    mail.send(28, own.at[y2], got.at[2], to_y2)
    if older:
        older.plane.step_three()
    glow[:, :D] = tn(hidden, gq).astype(BF)
    ghid = nt(gq, low[:, :D])
    bias_q = jnp.sum(gq.astype(F32), axis=0, keepdims=True)
    plane.step_four()
    mail.take(26, got.at[0], to_ym)
    mail.take(27, got.at[1], to_yp)
    mail.take(28, got.at[2], to_y2)
    total = own[y].astype(F32) + got[0].astype(F32) + got[1].astype(F32) + got[2].astype(F32)
    total = total.T
    gk = total[:, :128]
    gk = (gk * cos_ref[...] - swap_halves(gk) * sin_ref[...]).astype(BF)
    gv = total[:, 128:].astype(BF)
    ghid = ghid + nt(gk, low[:, D:]) + nt(gv, high[:, :128])
    glow[:, D:] = tn(hidden, gk).astype(BF)
    ghigh[:, :128] = tn(hidden, gv).astype(BF)
    t = ghid * vec_ref[0:1, :D]
    gin_ref[...] += r * (t - n * jnp.mean(t * n, axis=-1, keepdims=True))
    ggain_one = jnp.sum(ghid * n, axis=0, keepdims=True)
    if older:
        older.plane.step_four()
    bias_k = jnp.sum(gk.astype(F32), axis=0, keepdims=True)
    bias_v = jnp.sum(gv.astype(F32), axis=0, keepdims=True)
    bias = jnp.concatenate([bias_q, bias_k], axis=1)
    row = lax.broadcasted_iota(jnp.int32, (16, 1024), 0)
    row_last = jnp.concatenate([ggain_two, bias_v], axis=1)
    for g in range(8):
        row_seven = jnp.concatenate([ggain_one, bias[:, 128 * g : 128 * (g + 1)]], axis=1)
        extra = jnp.where(row == 0, row_seven, jnp.where(row == 1, row_last, 0.0))
        special[...] = extra.astype(BF)
        block = (
            nn(place_ref[0], glow[112 * g : 112 * (g + 1)])
            + nn(place_ref[1], ghigh[112 * g : 112 * (g + 1)])
            + nn(place_ref[2, :, 0:16], special[...])
        ).astype(BF)
        for k in range(16):
            core, line, column = k % 2, k % 8 // 2, 2 * (g % 2) + k // 8
            piece = block[16 * k : 16 * (k + 1)]
            if layer == 0:
                pair[lax.rem(c + core, 2), line, g // 2, column] = piece
            else:
                a_out[core, line, g // 2, column] = piece
        if layer == 0 and g % 2 == 1:
            final.start(g // 2)
    if layer == 0:
        older.rows()
        plane.step_five(m_out)
        final.cores()
        older.last(a_one)
        final.plane.step_two()
        final.plane.step_three()
        final.plane.step_four()
        final.rows()
        final.last(a_zero)
    else:
        plane.step_five(m_out)
    mail.finish()


def backward(layer, grad_output, x, vectors, tables, place_rows, w, kept_mlp, kept, before):
    anywhere = pl.BlockSpec(memory_space=pl.ANY)
    vmem = pl.BlockSpec(memory_space=pltpu.VMEM)
    operands = [grad_output, x, vectors, *tables, place_rows, w, *kept_mlp, *kept]
    out_shape = [jax.ShapeDtypeStruct((128, D), F32), jax.ShapeDtypeStruct((3, 56, FS), F32)]
    extra = []
    if layer == 0:
        operands.append(before)
        out_shape += [jax.ShapeDtypeStruct((16, 1024), F32)] * 2
        extra = [pltpu.VMEM((4, 4, 4, 16, 1024), BF)] + AttentionSum.scratch()
        extra += [pltpu.VMEM((2, 4, 4, 4, 16, 1024), BF)] + AttentionSum.scratch()
    else:
        out_shape.append(jax.ShapeDtypeStruct((2, 4, 4, 4, 16, 1024), BF))
    return pl.pallas_call(
        functools.partial(backward_kernel, layer),
        out_shape=tuple(out_shape),
        in_specs=[vmem] * 6 + [anywhere] * (len(operands) - 6),
        out_specs=[vmem] * len(out_shape),
        scratch_shapes=mlp_scratch()
        + [
            pltpu.VMEM((3, D, FS), BF),
            pltpu.VMEM((4, 2, 128, D), BF),
            pltpu.VMEM((4, 256, FS), BF),
            pltpu.VMEM((4, 256, FS), BF),
            pltpu.VMEM((4, 256, FS), BF),
            pltpu.VMEM((128, D), BF),
            pltpu.VMEM((128, D), F32),
            pltpu.VMEM((128, D), BF),
            pltpu.VMEM((H, 128, HD), BF),
            pltpu.VMEM((D, 1024), BF),
            pltpu.VMEM((D, 1024), BF),
            pltpu.VMEM((4, 1024, HD), BF),
            pltpu.VMEM((H, 128, 1024), BF),
            pltpu.VMEM((3, 4, 4, 56, FS), BF),
            pltpu.VMEM((H, 128, HD), BF),
            pltpu.VMEM((H, 128, HD), F32),
            pltpu.VMEM((4, 2, 256, 128), BF),
            pltpu.VMEM((4, 256, 128), BF),
            pltpu.VMEM((4, 256, 128), BF),
            pltpu.VMEM((3, 256, 128), BF),
            pltpu.VMEM((D, 1024), BF),
            pltpu.VMEM((D, 1024), BF),
            pltpu.VMEM((16, 1024), BF),
        ]
        + PlaneSum.scratch(3, 2, 56, FS)
        + extra
        + [
            pltpu.SemaphoreType.DMA((BACK_SLOTS[layer],)),
            pltpu.SemaphoreType.DMA((BACK_SLOTS[layer],)),
            pltpu.SemaphoreType.DMA((12,)),
        ],
        compiler_params=pltpu.CompilerParams(
            collective_id=14 + layer, has_side_effects=True, vmem_limit_bytes=60 * 1024 * 1024
        ),
        name="backward_layer_%d" % layer,
    )(*operands)


def select_matrix():
    pick = np.zeros((226, 256), np.float32)
    for k in range(16):
        for r in range(7):
            pick[7 * k + r, 16 * k + r] = 1
            pick[112 + 7 * k + r, 16 * k + 8 + r] = 1
        pick[224, 16 * k + 7] = 1
        pick[225, 16 * k + 15] = 1
    return pick


def assemble_kernel(a_zero, a_one, m_zero, m_one, g_one, g_qkv, g_qk, g_value, g_out, g_two, g_gate, g_up, rows):
    index = lax.axis_index("dp") * 8 + lax.axis_index("ctx")
    rows[...] = jnp.zeros_like(rows)
    for l, (a_ref, m_ref) in enumerate(((a_zero, m_zero), (a_one, m_one))):
        g_qkv[l, :, 0:1024] = a_ref[0:7, :]
        g_qkv[l, :, 1024:1152] = a_ref[8:15, 0:128]
        g_out[l] = a_ref[8:15, 128:1024]
        g_gate[l] = m_ref[0]
        g_up[l] = m_ref[1]
        rows[l : l + 1] = a_ref[7:8, :]
        rows[2 + l : 3 + l] = a_ref[15:16, :]
    gains = pltpu.roll(rows[...], lax.rem(1024 - 7 * index, 1024), 1)
    g_one[...] = gains[0:2, 0:7]
    g_two[...] = gains[2:4, 0:7]
    g_qk[...] = pltpu.roll(rows[...], 128 - 8 * lax.rem(index, 16), 1)[0:2, 0:8]
    g_value[...] = pltpu.roll(rows[...], 128 - index, 1)[2:4, 0:1]


def assemble(a_sums, m_sums):
    vmem = pl.BlockSpec(memory_space=pltpu.VMEM)
    shapes = ((2, 7), (2, 7, QKV), (2, 8), (2, 1), (2, 7, D), (2, 7), (2, 56, FS), (2, 56, FS))
    return pl.pallas_call(
        assemble_kernel,
        out_shape=tuple(jax.ShapeDtypeStruct(shape, F32) for shape in shapes),
        in_specs=[vmem] * 4,
        out_specs=[vmem] * len(shapes),
        scratch_shapes=[pltpu.VMEM((8, 1024), F32)],
        name="assemble",
    )(*a_sums, *m_sums)


def shards(
    tokens, cotangent, span_order, gain_one, w_qkv, b_qkv, w_out, gain_two, w_gate, w_up, w_down
):
    sequences, local_len, width = tokens.shape
    span_len = local_len // 2
    ctx_place = lax.axis_index("ctx")
    offsets = jnp.arange(span_len, dtype=jnp.int32)
    local_spans = lax.dynamic_slice_in_dim(span_order, 2 * ctx_place, 2)
    local_pos = (local_spans[:, None] * span_len + offsets[None, :]).reshape(local_len)
    all_pos = (span_order[:, None] * span_len + offsets[None, :]).reshape(-1)
    positions = (local_pos[:, None], all_pos[None, :])
    frequency = rope_base ** (-jnp.arange(HD // 2, dtype=F32) * 2.0 / HD)
    angles = local_pos.astype(F32)[:, None] * jnp.tile(frequency, 4)[None, :]
    sign = jnp.tile(jnp.concatenate([-jnp.ones(32, F32), jnp.ones(32, F32)]), 2)
    tables = (jnp.cos(angles), jnp.sin(angles) * sign[None, :])
    chosen = select_matrix()
    pick = jnp.asarray(np.concatenate([chosen, np.zeros((14, 256), np.float32)]), BF)
    spread = np.zeros((3, 256, 112), np.float32)
    spread[0], spread[1], spread[2, :, :2] = chosen[:112].T, chosen[112:224].T, chosen[224:].T
    spread = jnp.asarray(spread, BF)

    m_block = jnp.stack([w_gate, w_up, w_down.transpose(0, 2, 1)], axis=1)
    a_zero, row_one, m_x, m_z = first_gather(gain_one, w_qkv, b_qkv, w_out, gain_two, m_block)
    state_zero = tokens.reshape(local_len, width)
    state_one, *saved_zero, m_zero, m_one, a_one = forward(
        0, state_zero, a_zero, m_x, pick, tables, positions, row_one, m_block, m_z
    )
    m_full = (m_zero.reshape(3, D, FS), m_one.reshape(3, D, FS))
    state, *saved_one = forward(1, state_one, a_one, m_full[1], pick, tables, positions)
    vectors = (saved_zero[0], saved_one[0])
    kept_layers = [
        (saved_zero[1:8], saved_zero[8:]),
        (saved_one[1:8], saved_one[8:]),
    ]
    grad_one = cotangent.reshape(local_len, width)
    (state_in, kept, kept_mlp) = (state_one,) + kept_layers[1]
    grad_zero, m_sum_one, a_grads = backward(
        1, grad_one, state_in, vectors[1], tables, spread, m_full[1], kept_mlp, kept, None
    )
    kept, kept_mlp = kept_layers[0]
    grad_state, m_sum_zero, a_sum_zero, a_sum_one = backward(
        0, grad_zero, state_zero, vectors[0], tables, spread, m_full[0], kept_mlp, kept, a_grads
    )
    a_sums = (a_sum_zero, a_sum_one)
    sums = (m_sum_zero, m_sum_one)
    stacks = tuple(assemble(a_sums, sums)) + (jnp.stack([sums[0][2].T, sums[1][2].T]),)
    output = state.astype(BF).reshape(sequences, local_len, width)
    input_grad = grad_state.reshape(sequences, local_len, width)
    return (output, input_grad) + stacks


def solution(mesh):
    return jax.shard_map(
        shards,
        mesh=mesh,
        in_specs=(
            P("dp", "ctx", None),
            P("dp", "ctx", None),
            P(),
            P(None, ("dp", "ctx")),
            P(None, ("dp", "ctx"), None),
            P(None, ("dp", "ctx")),
            P(None, ("dp", "ctx"), None),
            P(None, ("dp", "ctx")),
            P(None, "dp", "ctx"),
            P(None, "dp", "ctx"),
            P(None, "ctx", "dp"),
        ),
        out_specs=(
            P("dp", "ctx", None),
            P("dp", "ctx", None),
            P(None, ("dp", "ctx")),
            P(None, ("dp", "ctx"), None),
            P(None, ("dp", "ctx")),
            P(None, ("dp", "ctx")),
            P(None, ("dp", "ctx"), None),
            P(None, ("dp", "ctx")),
            P(None, "dp", "ctx"),
            P(None, "dp", "ctx"),
            P(None, "ctx", "dp"),
        ),
        check_vma=False,
    )
```

```python
import functools

import jax
import jax.numpy as jnp
import numpy as np
from jax import lax
from jax.experimental import pallas as pl
from jax.experimental.pallas import tpu as pltpu
from jax.sharding import PartitionSpec as P

H = 14
KVH = 2
HD = 64
LAYERS = 2
D = 896
QKV = 1152
FS = 608
MESH = pl.DeviceIdType.MESH
BF = jnp.bfloat16
F32 = jnp.float32

eps_norm = 1e-06
rope_base = 1000000.0
neg_fill = -1e30


def place():
    dp = lax.axis_index("dp")
    ctx = lax.axis_index("ctx")
    return lax.div(dp, 4), lax.rem(dp, 4), lax.div(ctx, 2), lax.rem(ctx, 2)


def up1(v):
    return lax.rem(v + 1, 4)


def up2(v):
    return lax.rem(v + 2, 4)


def down1(v):
    return lax.rem(v + 3, 4)


def device(x, z, y, c):
    return (x * 4 + z, y * 2 + c)


def greet(peers):
    barrier = pltpu.get_barrier_semaphore()
    for peer in peers:
        pl.semaphore_signal(barrier, inc=1, device_id=peer, device_id_type=MESH)
    pl.semaphore_wait(barrier, len(peers))


class Mail:
    def __init__(self, send_sem, recv_sem, base=0, sent=None):
        self.send_sem = send_sem
        self.recv_sem = recv_sem
        self.base = base
        self.sent = [] if sent is None else sent

    def shifted(self, base):
        return Mail(self.send_sem, self.recv_sem, self.base + base, self.sent)

    def send(self, slot, src, dst, target):
        copy = pltpu.make_async_remote_copy(
            src_ref=src,
            dst_ref=dst,
            send_sem=self.send_sem.at[self.base + slot],
            recv_sem=self.recv_sem.at[self.base + slot],
            device_id=target,
            device_id_type=MESH,
        )
        copy.start()
        self.sent.append(copy)

    def take(self, slot, dst, source):
        pltpu.make_async_remote_copy(
            src_ref=dst,
            dst_ref=dst,
            send_sem=self.send_sem.at[self.base + slot],
            recv_sem=self.recv_sem.at[self.base + slot],
            device_id=source,
            device_id_type=MESH,
        ).wait_recv()

    def finish(self):
        for copy in self.sent:
            copy.wait_send()


class RowGather:
    slots = 8

    def __init__(self, mail, spot, block, along_x, along_z, local_sem):
        self.mail, self.spot, self.block = mail, spot, block
        self.along_x, self.along_z = along_x, along_z
        self.cut, self.rest = along_x.shape[0], along_z.shape[0]
        x, z = spot[:2]
        self.sa, self.sb = pl.ds(0, self.cut), pl.ds(self.cut, self.rest)
        self.own = [
            pltpu.make_async_copy(block.at[self.sa], along_x.at[:, x], local_sem.at[0]),
            pltpu.make_async_copy(block.at[self.sb], along_z.at[:, z], local_sem.at[1]),
        ]

    def step_one(self):
        x, z = self.spot[:2]
        to_xp, to_xm, to_zp, to_zm = ring_peers(self.spot)
        for copy in self.own:
            copy.start()
        self.mail.send(0, self.block.at[self.sa], self.along_x.at[:, x], to_xp)
        self.mail.send(1, self.block.at[self.sa], self.along_x.at[:, x], to_xm)
        self.mail.send(4, self.block.at[self.sb], self.along_z.at[:, z], to_zp)
        self.mail.send(5, self.block.at[self.sb], self.along_z.at[:, z], to_zm)

    def relays(self):
        x, z = self.spot[:2]
        to_xp, to_xm, to_zp, to_zm = ring_peers(self.spot)
        return (
            (0, self.along_x, self.cut, x, to_xp, to_xm),
            (4, self.along_z, self.rest, z, to_zp, to_zm),
        )

    def step_two(self):
        for base, ref, count, here, plus, minus in self.relays():
            behind, front = down1(here), up1(here)
            half = max(count // 2, 1)
            self.mail.take(base, ref.at[:, behind], minus)
            part = ref.at[pl.ds(0, half), behind]
            self.mail.send(base + 2, part, part, plus)
            self.mail.take(base + 1, ref.at[:, front], plus)
            if count > 1:
                part = ref.at[pl.ds(half, count - half), front]
                self.mail.send(base + 3, part, part, minus)

    def step_three(self):
        for base, ref, count, here, plus, minus in self.relays():
            half = max(count // 2, 1)
            self.mail.take(base + 2, ref.at[pl.ds(0, half), up2(here)], minus)
            if count > 1:
                self.mail.take(base + 3, ref.at[pl.ds(half, count - half), up2(here)], plus)
        for copy in self.own:
            copy.wait()


class PlaneFill:
    slots = 16

    def __init__(self, mail, spot, along_x, along_z, full, local_sem, mirror=None):
        self.mail, self.spot, self.full, self.mirror = mail, spot, full, mirror
        self.along_x, self.along_z = along_x, along_z
        self.cut, self.rest = along_x.shape[0], along_z.shape[0]
        x, z, y, c = spot
        self.other = device(x, z, y, 1 - c)
        self.copies = [
            pltpu.make_async_copy(along_x, full.at[self.first(z)], local_sem.at[0]),
            pltpu.make_async_copy(along_z, full.at[self.second(x)], local_sem.at[1]),
        ]

    def first(self, z, half=None):
        lead = pl.ds(0, self.cut) if half is None else pl.ds(half * (self.cut // 2), self.cut // 2)
        return (lead, pl.ds(0, 4), z)

    def second(self, x, half=None):
        if half is None:
            return (pl.ds(self.cut, self.rest), x, pl.ds(0, 4))
        if self.rest == 1:
            return (pl.ds(self.cut, 1), x, pl.ds(2 * half, 2))
        return (pl.ds(self.cut + half * (self.rest // 2), self.rest // 2), x, pl.ds(0, 4))

    def pass_on(self, slot, where, target):
        self.mail.send(slot, self.full.at[where], self.full.at[where], target)

    def share(self, slot, where, src=None):
        if self.mirror is not None:
            src = self.full.at[where] if src is None else src
            self.mail.send(slot, src, self.full.at[where], self.other)

    def step_one(self):
        x, z = self.spot[:2]
        to_xp, to_xm, to_zp, to_zm = ring_peers(self.spot)
        self.mail.send(0, self.along_x, self.full.at[self.first(z)], to_zp)
        self.mail.send(1, self.along_x, self.full.at[self.first(z)], to_zm)
        self.mail.send(2, self.along_z, self.full.at[self.second(x)], to_xp)
        self.mail.send(3, self.along_z, self.full.at[self.second(x)], to_xm)
        self.share(8, self.first(z), self.along_x)
        self.share(9, self.second(x), self.along_z)
        for copy in self.copies:
            copy.start()

    def step_two(self):
        x, z = self.spot[:2]
        to_xp, to_xm, to_zp, to_zm = ring_peers(self.spot)
        xp, xm, zp, zm = up1(x), down1(x), up1(z), down1(z)
        for slot, where, piece, source, target in (
            (0, self.first(zm), self.first(zm, 0), to_zm, to_zp),
            (2, self.second(xm), self.second(xm, 0), to_xm, to_xp),
            (1, self.first(zp), self.first(zp, 1), to_zp, to_zm),
            (3, self.second(xp), self.second(xp, 1), to_xp, to_xm),
        ):
            self.mail.take(slot, self.full.at[where], source)
            self.pass_on(4 + slot, piece, target)
            self.share(10 + slot, where)

    def step_three(self):
        x, z = self.spot[:2]
        to_xp, to_xm, to_zp, to_zm = ring_peers(self.spot)
        for slot, piece, source in (
            (4, self.first(up2(z), 0), to_zm),
            (6, self.second(up2(x), 0), to_xm),
            (5, self.first(up2(z), 1), to_zp),
            (7, self.second(up2(x), 1), to_xp),
        ):
            self.mail.take(slot, self.full.at[piece], source)
        self.share(14, self.first(up2(z)))
        self.share(15, self.second(up2(x)))
        for copy in self.copies:
            copy.wait()

    def step_four(self):
        x, z = self.spot[:2]
        xp, xm, zp, zm = up1(x), down1(x), up1(z), down1(z)
        for slot, where in (
            (8, self.first(z)),
            (9, self.second(x)),
            (10, self.first(zm)),
            (11, self.first(zp)),
            (12, self.second(xm)),
            (13, self.second(xp)),
            (14, self.first(up2(z))),
            (15, self.second(up2(x))),
        ):
            self.mail.take(slot, self.mirror.at[where], self.other)


def ring_peers(spot):
    x, z, y, c = spot
    return [
        device(up1(x), z, y, c),
        device(down1(x), z, y, c),
        device(x, up1(z), y, c),
        device(x, down1(z), y, c),
    ]


def ctx_peers(spot):
    x, z, y, c = spot
    return [device(x, z, up1(y), c), device(x, z, down1(y), c), device(x, z, y, 1 - c)]


def first_gather_kernel(
    one_ref, qkv_ref, bias_ref, out_ref, two_ref, m_ref,
    full, row_out, m_x, m_z,
    rows, vectors, offsets, line, a_x, a_z, send_sem, recv_sem, local_sem,
):
    spot = place()
    x, z, y, c = spot
    index = (x * 4 + z) * 8 + 2 * y + c
    mail = Mail(send_sem, recv_sem)
    vectors[...] = jnp.zeros_like(vectors)
    offsets[...] = jnp.zeros_like(offsets)
    vectors[0:2, 0:7] = one_ref[...].astype(F32)
    vectors[2:4, 0:7] = two_ref[...].astype(F32)
    offsets[0:2, 0:9] = bias_ref[...].astype(F32)
    gains = pltpu.roll(vectors[...], 7 * index, 1)
    bias = pltpu.roll(offsets[...], 9 * index - 128 * lax.div(index, 16), 1)
    qkv, out = qkv_ref[...].astype(F32), out_ref[...].astype(F32)
    for l in range(LAYERS):
        for r in range(7):
            rows[l, r : r + 1, :] = qkv[r, l : l + 1, :1024]
            rows[l, 8 + r : 9 + r, 0:128] = qkv[r, l : l + 1, 1024:]
            rows[l, 8 + r : 9 + r, 128:1024] = out[r, l : l + 1]
        rows[l, 7:8, 0:D] = gains[l : l + 1, :D]
        rows[l, 15:16, 0:D] = gains[2 + l : 3 + l, :D]
        rows[l, 7:8, D:1024] = bias[l : l + 1, :128]
        rows[l, 15:16, D:1024] = bias[l : l + 1, 128:]
    line[:, y] = rows[...].astype(BF)
    yp, ym, y2 = up1(y), down1(y), up2(y)
    to_yp, to_ym, other = ctx_peers(spot)
    to_y2 = device(x, z, y2, c)
    greet(ring_peers(spot) + [to_yp, to_ym, other, to_y2])
    mail.send(0, line.at[:, y], line.at[:, y], to_yp)
    mail.send(1, line.at[:, y], line.at[:, y], to_ym)
    mail.send(2, line.at[:, y], line.at[:, y], to_y2)
    row = RowGather(mail.shifted(3), spot, line.at[0], a_x, a_z, local_sem.at[pl.ds(0, 2)])
    fill = PlaneFill(
        mail.shifted(11), spot, a_x, a_z, full.at[c], local_sem.at[pl.ds(2, 2)], full.at[1 - c]
    )
    feed = RowGather(mail.shifted(27), spot, m_ref.at[0], m_x, m_z, local_sem.at[pl.ds(4, 2)])
    mail.take(0, line.at[:, ym], to_ym)
    mail.take(1, line.at[:, yp], to_yp)
    mail.take(2, line.at[:, y2], to_y2)
    row.step_one()
    kept = pltpu.make_async_copy(line.at[1], row_out, local_sem.at[6])
    kept.start()
    row.step_two()
    row.step_three()
    fill.step_one()
    feed.step_one()
    fill.step_two()
    feed.step_two()
    fill.step_three()
    feed.step_three()
    fill.step_four()
    kept.wait()
    mail.finish()


def first_gather(gain_one, w_qkv, b_qkv, w_out, gain_two, m_block):
    return pl.pallas_call(
        first_gather_kernel,
        out_shape=(
            jax.ShapeDtypeStruct((2, 4, 4, 4, 16, 1024), BF),
            jax.ShapeDtypeStruct((4, 16, 1024), BF),
            jax.ShapeDtypeStruct((2, 4, 56, FS), BF),
            jax.ShapeDtypeStruct((1, 4, 56, FS), BF),
        ),
        in_specs=[pl.BlockSpec(memory_space=pltpu.VMEM)] * 5 + [pl.BlockSpec(memory_space=pl.ANY)],
        out_specs=[pl.BlockSpec(memory_space=pl.ANY)] * 4,
        scratch_shapes=[
            pltpu.VMEM((2, 16, 1024), F32),
            pltpu.VMEM((8, 1024), F32),
            pltpu.VMEM((8, 256), F32),
            pltpu.VMEM((2, 4, 16, 1024), BF),
            pltpu.VMEM((2, 4, 16, 1024), BF),
            pltpu.VMEM((2, 4, 16, 1024), BF),
            pltpu.SemaphoreType.DMA((35,)),
            pltpu.SemaphoreType.DMA((35,)),
            pltpu.SemaphoreType.DMA((7,)),
        ],
        compiler_params=pltpu.CompilerParams(
            collective_id=1, has_side_effects=True, vmem_limit_bytes=60 * 1024 * 1024
        ),
        name="first_gather",
    )(gain_one, w_qkv, b_qkv, w_out, gain_two, m_block)


class PlaneSum:
    def __init__(self, mail, base, spot, g, cut, buffers):
        self.mail, self.base, self.spot, self.g, self.cut = mail, base, spot, g, cut
        self.count = g.shape[0]
        self.buffers = buffers

    @staticmethod
    def scratch(slabs, cut, rows, columns):
        rest = slabs - cut
        out = [
            pltpu.VMEM((2, cut, 2, rows, columns), BF),
            pltpu.VMEM((2, cut, 4, rows, columns), BF),
            pltpu.VMEM((2, rest, 2, rows, columns), BF),
            pltpu.VMEM((2, rest, 4, rows, columns), BF),
            pltpu.VMEM((2, cut // 2, rows, columns), BF),
            pltpu.VMEM((2, cut, rows, columns), BF),
            pltpu.VMEM((2, max(rest // 2, 1), rows, columns), BF),
            pltpu.VMEM((2, rest, rows, columns), BF),
        ]
        return out

    @staticmethod
    def peers(spot, slabs, cut):
        x, z, y, c = spot
        near = [device(up1(x), z, y, c), device(down1(x), z, y, c), device(x, up1(z), y, c), device(x, down1(z), y, c)]
        return near + ([device(x, up2(z), y, c)] if slabs - cut == 1 else [])

    def names(self):
        x, z, y, c = self.spot
        xp, xm, zp, zm = up1(x), down1(x), up1(z), down1(z)
        to = (device(xp, z, y, c), device(xm, z, y, c), device(x, zp, y, c), device(x, zm, y, c))
        return x, z, xp, xm, zp, zm, up2(x), up2(z), to

    def send(self, slot, src, dst, target):
        self.mail.send(self.base + slot, src, dst, target)

    def take(self, slot, dst, source):
        self.mail.take(self.base + slot, dst, source)

    def add(self, where, extra):
        part = self.g.at[where]
        part[...] = (part[...].astype(F32) + extra.astype(F32)).astype(BF)

    def step_one(self):
        x, z, xp, xm, zp, zm, x2, z2, (to_xp, to_xm, to_zp, to_zm) = self.names()
        fa, ga, fb, gb, pa, qa, pb, qb = self.buffers
        sa, sb = pl.ds(0, self.cut), pl.ds(self.cut, self.count - self.cut)
        lo, hi = pl.ds(0, 2), pl.ds(2, 2)
        self.send(0, self.g.at[sa, lo, z2], fa.at[0], to_zp)
        self.send(1, self.g.at[sa, hi, z2], fa.at[1], to_zm)
        self.send(2, self.g.at[sb, x2, lo], fb.at[0], to_xp)
        self.send(3, self.g.at[sb, x2, hi], fb.at[1], to_xm)

    def step_two(self):
        x, z, xp, xm, zp, zm, x2, z2, (to_xp, to_xm, to_zp, to_zm) = self.names()
        fa, ga, fb, gb, pa, qa, pb, qb = self.buffers
        sa, sb = pl.ds(0, self.cut), pl.ds(self.cut, self.count - self.cut)
        lo, hi, every = pl.ds(0, 2), pl.ds(2, 2), pl.ds(0, 4)
        self.take(0, fa.at[0], to_zm)
        self.add((sa, lo, zp), fa[0])
        self.send(4, self.g.at[sa, every, zp], ga.at[0], to_zp)
        self.take(2, fb.at[0], to_xm)
        self.add((sb, xp, lo), fb[0])
        self.send(6, self.g.at[sb, xp, every], gb.at[0], to_xp)
        self.take(1, fa.at[1], to_zp)
        self.add((sa, hi, zm), fa[1])
        self.send(5, self.g.at[sa, every, zm], ga.at[1], to_zm)
        self.take(3, fb.at[1], to_xp)
        self.add((sb, xm, hi), fb[1])
        self.send(7, self.g.at[sb, xm, every], gb.at[1], to_xm)

    def step_three(self):
        x, z, xp, xm, zp, zm, x2, z2, (to_xp, to_xm, to_zp, to_zm) = self.names()
        fa, ga, fb, gb, pa, qa, pb, qb = self.buffers
        y, c = self.spot[2:]
        cut, rest = self.cut, self.count - self.cut
        sa, sb = pl.ds(0, cut), pl.ds(cut, rest)
        every = pl.ds(0, 4)
        self.take(4, ga.at[0], to_zm)
        self.take(5, ga.at[1], to_zp)
        self.add((sa, every, z), ga[0].astype(F32) + ga[1].astype(F32))
        self.send(8, self.g.at[pl.ds(0, cut // 2), x2, z], pa.at[0], to_xp)
        self.send(9, self.g.at[pl.ds(cut // 2, cut // 2), x2, z], pa.at[1], to_xm)
        self.take(6, gb.at[0], to_xm)
        self.take(7, gb.at[1], to_xp)
        self.add((sb, x, every), gb[0].astype(F32) + gb[1].astype(F32))
        if rest == 1:
            self.send(10, self.g.at[sb, x, z2], pb.at[0], device(x, z2, y, c))
            self.send(14, self.g.at[sb, x, zp], qb.at[0], to_zp)
            self.send(15, self.g.at[sb, x, zm], qb.at[1], to_zm)
        else:
            self.send(10, self.g.at[pl.ds(cut, rest // 2), x, z2], pb.at[0], to_zp)
            self.send(11, self.g.at[pl.ds(cut + rest // 2, rest // 2), x, z2], pb.at[1], to_zm)

    def step_four(self):
        x, z, xp, xm, zp, zm, x2, z2, (to_xp, to_xm, to_zp, to_zm) = self.names()
        fa, ga, fb, gb, pa, qa, pb, qb = self.buffers
        cut, rest = self.cut, self.count - self.cut
        sa, sb = pl.ds(0, cut), pl.ds(cut, rest)
        self.take(8, pa.at[0], to_xm)
        self.add((pl.ds(0, cut // 2), xp, z), pa[0])
        self.send(12, self.g.at[sa, xp, z], qa.at[0], to_xp)
        self.take(9, pa.at[1], to_xp)
        self.add((pl.ds(cut // 2, cut // 2), xm, z), pa[1])
        self.send(13, self.g.at[sa, xm, z], qa.at[1], to_xm)
        if rest > 1:
            self.take(10, pb.at[0], to_zm)
            self.add((pl.ds(cut, rest // 2), x, zp), pb[0])
            self.send(14, self.g.at[sb, x, zp], qb.at[0], to_zp)
            self.take(11, pb.at[1], to_zp)
            self.add((pl.ds(cut + rest // 2, rest // 2), x, zm), pb[1])
            self.send(15, self.g.at[sb, x, zm], qb.at[1], to_zm)

    def step_five(self, out):
        x, z, xp, xm, zp, zm, x2, z2, (to_xp, to_xm, to_zp, to_zm) = self.names()
        fa, ga, fb, gb, pa, qa, pb, qb = self.buffers
        y, c = self.spot[2:]
        cut, rest = self.cut, self.count - self.cut
        sa, sb = pl.ds(0, cut), pl.ds(cut, rest)
        self.take(12, qa.at[0], to_xm)
        self.take(13, qa.at[1], to_xp)
        out[sa] = (
            self.g.at[sa, x, z][...].astype(F32) + qa[0].astype(F32) + qa[1].astype(F32)
        ).astype(out.dtype)
        self.take(14, qb.at[0], to_zm)
        self.take(15, qb.at[1], to_zp)
        total = self.g.at[sb, x, z][...].astype(F32) + qb[0].astype(F32) + qb[1].astype(F32)
        if rest == 1:
            self.take(10, pb.at[0], device(x, z2, y, c))
            total = total + pb[0].astype(F32)
        out[sb] = total.astype(out.dtype)


class AttentionSum:
    slots = 23

    def __init__(self, mail, spot, mine, theirs, refs):
        self.mail, self.spot, self.mine, self.theirs = mail, spot, mine, theirs
        self.near, self.block, self.got = refs[:3]
        self.plane = PlaneSum(mail, 7, spot, mine, 2, refs[3:])

    @staticmethod
    def scratch():
        return [
            pltpu.VMEM((4, 4, 4, 16, 1024), BF),
            pltpu.VMEM((4, 16, 1024), BF),
            pltpu.VMEM((3, 16, 1024), BF),
        ] + PlaneSum.scratch(4, 2, 16, 1024)

    def start(self, i):
        x, z, y, c = self.spot
        self.mail.send(i, self.theirs.at[:, i], self.near.at[:, i], device(x, z, y, 1 - c))

    def cores(self):
        x, z, y, c = self.spot
        for i in range(4):
            self.mail.take(i, self.near.at[:, i], device(x, z, y, 1 - c))
            part = self.mine.at[:, i]
            part[...] = (part[...].astype(F32) + self.near[:, i].astype(F32)).astype(BF)
        self.plane.step_one()

    def rows(self):
        x, z, y, c = self.spot
        self.plane.step_five(self.block)
        for k, step in enumerate((up1, up2, down1)):
            to = device(x, z, step(y), c)
            self.mail.send(4 + k, self.block.at[step(y)], self.got.at[k], to)

    def last(self, out):
        x, z, y, c = self.spot
        total = self.block[y].astype(F32)
        for k, step in enumerate((down1, up2, up1)):
            self.mail.take(4 + k, self.got.at[k], device(x, z, step(y), c))
            total = total + self.got[k].astype(F32)
        out[...] = total


def nn(left, right):
    return jnp.dot(left, right, preferred_element_type=F32)


def nt(left, right):
    return lax.dot_general(left, right, (((1,), (1,)), ((), ())), preferred_element_type=F32)


def tn(left, right):
    return lax.dot_general(left, right, (((0,), (0,)), ((), ())), preferred_element_type=F32)


def mlp_scratch():
    return [
        pltpu.VMEM((4, 2, 128, D), BF),
        pltpu.VMEM((4, 2, 128, D), BF),
        pltpu.VMEM((4, 128, D), BF),
        pltpu.VMEM((3, 128, D), BF),
        pltpu.VMEM((2, 64, D), BF),
        pltpu.VMEM((2, 64, D), BF),
        pltpu.VMEM((2, 128, D), BF),
    ]


def mlp_exchange(mail, spot, src, buffers, chunk, fillers, hook):
    rows, part, near, own, far, fin, got = buffers
    x, z, y, c = spot
    yp, ym, y2 = up1(y), down1(y), up2(y)
    to_yp, to_ym, other = device(x, z, yp, c), device(x, z, ym, c), device(x, z, y, 1 - c)
    begin, end = pl.ds(0, 32), pl.ds(32, 32)
    first, second = pl.ds(0, 64), pl.ds(64, 64)
    mail.send(0, src.at[first], rows.at[y, c, first], to_yp)
    mail.send(1, src.at[second], rows.at[y, c, second], to_ym)
    mail.send(2, src, rows.at[y, c], other)
    mail.send(19, src.at[second], rows.at[y, c, second], to_yp)
    mail.send(20, src.at[first], rows.at[y, c, first], to_ym)
    rows[y, c] = src[...]
    mail.take(2, rows.at[y, 1 - c], other)
    chunk(y)
    mail.send(12, part.at[y, 1 - c], near.at[3], other)
    mail.take(0, rows.at[ym, c, first], to_ym)
    mail.send(3, rows.at[ym, c, first], rows.at[ym, c, first], to_yp)
    mail.take(1, rows.at[yp, c, second], to_yp)
    mail.send(5, rows.at[yp, c, second], rows.at[yp, c, second], to_ym)
    mail.take(19, rows.at[ym, c, second], to_ym)
    mail.send(4, rows.at[ym, c], rows.at[ym, c], other)
    mail.take(20, rows.at[yp, c, first], to_yp)
    mail.send(6, rows.at[yp, c], rows.at[yp, c], other)
    mail.take(4, rows.at[ym, 1 - c], other)
    chunk(ym)
    mail.send(11, part.at[ym, 1 - c], near.at[2], other)
    hook()
    mail.take(6, rows.at[yp, 1 - c], other)
    chunk(yp)
    mail.send(10, part.at[yp, 1 - c], near.at[1], other)
    mail.take(3, rows.at[y2, c, first], to_ym)
    mail.send(7, rows.at[y2, c, first], rows.at[y2, c, first], other)
    mail.take(5, rows.at[y2, c, second], to_yp)
    mail.send(8, rows.at[y2, c, second], rows.at[y2, c, second], other)
    mail.take(11, near.at[2], other)
    own[2] = (part[ym, c].astype(F32) + near[2].astype(F32)).astype(BF)
    mail.send(16, own.at[2], got.at[1], to_ym)
    mail.take(10, near.at[1], other)
    own[1] = (part[yp, c].astype(F32) + near[1].astype(F32)).astype(BF)
    mail.send(15, own.at[1], got.at[0], to_yp)
    mail.take(7, rows.at[y2, 1 - c, first], other)
    mail.take(8, rows.at[y2, 1 - c, second], other)
    chunk(y2)
    mail.send(9, part.at[y2, 1 - c], near.at[0], other)
    fillers[0]()
    mail.take(9, near.at[0], other)
    own[0] = (part[y2, c].astype(F32) + near[0].astype(F32)).astype(BF)
    mail.send(13, own.at[0, pl.ds(0, 32)], far.at[0, begin], to_yp)
    mail.send(14, own.at[0, pl.ds(64, 32)], far.at[1, begin], to_ym)
    mail.send(21, own.at[0, pl.ds(32, 32)], far.at[0, end], to_yp)
    mail.send(22, own.at[0, pl.ds(96, 32)], far.at[1, end], to_ym)
    fillers[1]()
    mail.take(13, far.at[0, begin], to_ym)
    mail.send(17, far.at[0, begin], fin.at[0, begin], to_yp)
    mail.take(14, far.at[1, begin], to_yp)
    mail.send(18, far.at[1, begin], fin.at[1, begin], to_ym)
    mail.take(21, far.at[0, end], to_ym)
    mail.send(23, far.at[0, end], fin.at[0, end], to_yp)
    mail.take(22, far.at[1, end], to_yp)
    mail.send(24, far.at[1, end], fin.at[1, end], to_ym)
    fillers[2]()
    mail.take(12, near.at[3], other)
    mail.take(15, got.at[0], to_ym)
    mail.take(16, got.at[1], to_yp)
    mail.take(17, fin.at[0, begin], to_ym)
    mail.take(18, fin.at[1, begin], to_yp)
    mail.take(23, fin.at[0, end], to_ym)
    mail.take(24, fin.at[1, end], to_yp)
    total = (
        part[y, c].astype(F32)
        + near[3].astype(F32)
        + got[0].astype(F32)
        + got[1].astype(F32)
    )
    return total + fin[...].reshape(128, D).astype(F32)


def nothing():
    return None


def swap_halves(u):
    width = u.shape[1]
    lane = lax.broadcasted_iota(jnp.int32, u.shape, 1)
    return jnp.where(
        lax.rem(lane, 64) < 32, pltpu.roll(u, width - 32, 1), pltpu.roll(u, 32, 1)
    )


def normal(v):
    r = lax.rsqrt(jnp.mean(v * v, axis=-1, keepdims=True) + eps_norm)
    return v * r, r


def forward_kernel(layer, *refs):
    x_ref, a_ref, m_ref, pick_ref, cos_ref, sin_ref, span_ref = refs[:7]
    refs = refs[7:]
    if layer == 0:
        row_ref, shard_ref, m_z_ref = refs[:3]
        refs = refs[3:]
    out_ref, vec_ref, mid_ref, att_ref, qs_ref, kv_ref, probs_ref, low_ref, high_ref = refs[:9]
    hr_ref, gate_ref, up_ref = refs[9:12]
    refs = refs[12:]
    if layer == 0:
        m_zero, m_one, a_one = refs[:3]
        refs = refs[3:]
    blocks, low, high, kv, probs, weights, mask, att, qs, mid, h2 = refs[:11]
    buffers, refs = refs[11:18], refs[18:]
    w, gate, up, send_sem, recv_sem, local_sem = refs[:6]
    rows, part = buffers[0], buffers[1]
    spot = place()
    x, z, y, c = spot
    mail = Mail(send_sem, recv_sem)
    load = pltpu.make_async_copy(a_ref, blocks, local_sem.at[0])
    load.start()
    if layer == 0:
        a_x, a_z, m_x, m_z, slabs = refs[6:]

        def sems(k):
            return local_sem.at[pl.ds(21 + 2 * k, 2)]

        fill = PlaneFill(mail.shifted(34), spot, m_ref, m_z_ref, m_zero, sems(0))
        a_row = RowGather(mail.shifted(50), spot, row_ref, a_x, a_z, sems(1))
        m_row = RowGather(mail.shifted(58), spot, shard_ref.at[1], m_x, m_z, sems(2))
        a_fill = PlaneFill(
            mail.shifted(66), spot, a_x, a_z, a_one.at[c], sems(3), a_one.at[1 - c]
        )
        m_fill = PlaneFill(mail.shifted(82), spot, m_x, m_z, m_one, sems(4))
        load_w = pltpu.make_async_copy(m_zero, slabs, local_sem.at[1])
        greet(ctx_peers(spot) + ring_peers(spot))
        fill.step_one()
        a_row.step_one()
        m_row.step_one()
    else:
        load_w = pltpu.make_async_copy(m_ref, w, local_sem.at[1])
        load_w.start()
        greet(ctx_peers(spot))
    inputs = x_ref[...].astype(F32)
    n, r = normal(inputs)
    load.wait()
    spare = []
    for g in range(8):
        group = jnp.concatenate(
            [blocks[k % 2, k % 8 // 2, g // 2, 2 * (g % 2) + k // 8] for k in range(16)], axis=0
        )
        low[112 * g : 112 * (g + 1)] = nn(pick_ref[0:112, :], group).astype(BF)
        high[112 * g : 112 * (g + 1)] = nn(pick_ref[112:224, :], group).astype(BF)
        spare.append(nn(pick_ref[224:240, :], group))
    gains = functools.reduce(lambda u, v: u + v, [block[0:2, :D] for block in spare])
    vec_ref[0:2, 0:D] = gains
    for j in range(9):
        piece = jnp.zeros((1, 128), F32)
        if j < 8:
            piece = piece + spare[j][0:1, D:]
        if j > 0:
            piece = piece + spare[j - 1][1:2, D:]
        vec_ref[2:3, 128 * j : 128 * (j + 1)] = piece
    stores = [
        pltpu.make_async_copy(low, low_ref, local_sem.at[2]),
        pltpu.make_async_copy(high, high_ref, local_sem.at[3]),
    ]
    hidden = (n * gains[0:1]).astype(BF)
    packed = nn(hidden, low[...]) + vec_ref[2:3, :1024]
    values = nn(hidden, high[:, :128]) + vec_ref[2:3, 1024:]
    cos = jnp.concatenate([cos_ref[...]] * 8, axis=1)
    sin = jnp.concatenate([sin_ref[...]] * 8, axis=1)
    turned = packed * cos + swap_halves(packed) * sin
    kv[y, c, :, 0:128] = turned[:, D:].astype(BF)
    kv[y, c, :, 128:256] = values.astype(BF)
    yp, ym, y2 = up1(y), down1(y), up2(y)
    to_yp, to_ym, other = ctx_peers(spot)
    first, second = pl.ds(0, 64), pl.ds(64, 64)
    mail.send(0, kv.at[y, c], kv.at[y, c], to_yp)
    mail.send(1, kv.at[y, c], kv.at[y, c], to_ym)
    mail.send(2, kv.at[y, c], kv.at[y, c], other)
    for store in stores:
        store.start()
    if layer == 0:
        a_row.step_two()
        m_row.step_two()
    for h in range(H):
        head = (turned[:, HD * h : HD * (h + 1)] * HD ** (-0.5)).astype(BF)
        qs[h // 7, 128 * (h % 7) : 128 * (h % 7 + 1)] = head
    token = lax.broadcasted_iota(jnp.int32, (128, 256), 0)
    key = lax.broadcasted_iota(jnp.int32, (128, 256), 1)
    begin, end = span_ref[4 * y + 2 * c], span_ref[4 * y + 2 * c + 1]
    query_at = lax.rem(token, 64) + 64 * jnp.where(token < 64, begin, end)
    for j in range(4):
        spans = [span_ref[4 * j + i] for i in range(4)]
        upper = jnp.where(key < 192, spans[2], spans[3])
        span = jnp.where(key < 64, spans[0], jnp.where(key < 128, spans[1], upper))
        mask[j] = jnp.where(lax.rem(key, 64) + 64 * span <= query_at, 0.0, neg_fill)
    tops, sums = [], []

    def score(row):
        for k in range(KVH):
            keys = kv[row, :, :, HD * k : HD * (k + 1)].reshape(256, HD)
            s = nt(qs[k], keys) + jnp.concatenate([mask[row]] * 7, axis=0)
            top = jnp.max(s, axis=-1, keepdims=True)
            e = jnp.exp(s - top)
            weights[k, row] = e
            tops.append(top)
            sums.append(jnp.sum(e, axis=-1, keepdims=True))

    mail.take(2, kv.at[y, 1 - c], other)
    score(y)
    mail.take(0, kv.at[ym, c], to_ym)
    mail.send(3, kv.at[ym, c, first], kv.at[ym, c, first], to_yp)
    mail.send(4, kv.at[ym, c], kv.at[ym, c], other)
    mail.take(1, kv.at[yp, c], to_yp)
    mail.send(5, kv.at[yp, c, second], kv.at[yp, c, second], to_ym)
    mail.send(6, kv.at[yp, c], kv.at[yp, c], other)
    if layer == 0:
        fill.step_two()
        a_row.step_three()
        m_row.step_three()
    mail.take(4, kv.at[ym, 1 - c], other)
    score(ym)
    mail.take(3, kv.at[y2, c, first], to_ym)
    mail.send(7, kv.at[y2, c, first], kv.at[y2, c, first], other)
    mail.take(5, kv.at[y2, c, second], to_yp)
    mail.send(8, kv.at[y2, c, second], kv.at[y2, c, second], other)
    mail.take(6, kv.at[yp, 1 - c], other)
    score(yp)
    if layer == 0:
        a_fill.step_one()
    mail.take(7, kv.at[y2, 1 - c, first], other)
    mail.take(8, kv.at[y2, 1 - c, second], other)
    score(y2)
    heads = []
    for k in range(KVH):
        top = functools.reduce(jnp.maximum, tops[k::2])
        scales = [jnp.exp(t - top) for t in tops[k::2]]
        whole = functools.reduce(
            lambda u, v: u + v, [f * t for f, t in zip(scales, sums[k::2])]
        )
        inverse = 1.0 / whole
        total = jnp.zeros((D, HD), F32)
        for f, row in zip(scales, (y, ym, yp, y2)):
            p = (weights[k, row] * (f * inverse)).astype(BF)
            probs[k, row] = p
            total = total + nn(p, kv[row, :, :, 128 + HD * k : 128 + HD * (k + 1)].reshape(256, HD))
        heads += [total[128 * i : 128 * (i + 1)] for i in range(7)]
    att[...] = jnp.concatenate(heads, axis=1)
    mid[...] = inputs + nn(att[...].astype(BF), high[:, 128:])
    h2[...] = (normal(mid[...])[0] * gains[1:2]).astype(BF)
    for i, (src, dst) in enumerate(
        ((kv, kv_ref), (probs, probs_ref), (att, att_ref), (qs, qs_ref), (mid, mid_ref))
    ):
        stores.append(pltpu.make_async_copy(src, dst, local_sem.at[4 + i]))
        stores[-1].start()
    if layer == 0:
        fill.step_three()
        load_w.start()
        m_fill.step_one()

    loaded = []

    def chunk(row):
        if not loaded:
            load_w.wait()
            if layer == 0:
                for member in range(3):
                    for i in range(16):
                        w[member, 56 * i : 56 * (i + 1)] = slabs[member, i // 4, i % 4]
            loaded.append(True)
        h = rows[row].reshape(256, D)
        g = nn(h, w[0])
        u = nn(h, w[1])
        gate[row] = g.astype(BF)
        up[row] = u.astype(BF)
        act = (g / (1.0 + jnp.exp(-g)) * u).astype(BF)
        part[row] = nt(act, w[2]).astype(BF).reshape(2, 128, D)
        k = 9 + 3 * (len(loaded) - 1)
        loaded.append(True)
        for i, (src, dst) in enumerate(((rows, hr_ref), (gate, gate_ref), (up, up_ref))):
            stores.append(pltpu.make_async_copy(src.at[row], dst.at[row], local_sem.at[k + i]))
            stores[-1].start()

    steps = [nothing] * 4
    if layer == 0:
        steps = [nothing, a_fill.step_two, a_fill.step_three, m_fill.step_two]
    total = mlp_exchange(mail.shifted(9), spot, h2, buffers, chunk, steps[1:], steps[0])
    out_ref[...] = mid[...] + total
    if layer == 0:
        m_fill.step_three()
        a_fill.step_four()
    for store in stores:
        store.wait()
    mail.finish()


def forward(layer, state, a_full, m_full, pick, tables, span_order, *shards):
    anywhere = pl.BlockSpec(memory_space=pl.ANY)
    vmem = pl.BlockSpec(memory_space=pltpu.VMEM)
    out_shape = [
        jax.ShapeDtypeStruct((128, D), F32),
        jax.ShapeDtypeStruct((8, QKV), F32),
        jax.ShapeDtypeStruct((128, D), F32),
        jax.ShapeDtypeStruct((128, D), F32),
        jax.ShapeDtypeStruct((KVH, D, HD), BF),
        jax.ShapeDtypeStruct((4, 2, 128, 256), BF),
        jax.ShapeDtypeStruct((KVH, 4, D, 256), BF),
        jax.ShapeDtypeStruct((D, 1024), BF),
        jax.ShapeDtypeStruct((D, 1024), BF),
        jax.ShapeDtypeStruct((4, 2, 128, D), BF),
        jax.ShapeDtypeStruct((4, 256, FS), BF),
        jax.ShapeDtypeStruct((4, 256, FS), BF),
    ]
    operands = [state, a_full, m_full, pick, *tables, span_order]
    smem = pl.BlockSpec(memory_space=pltpu.SMEM)
    in_specs = [vmem, anywhere, anywhere] + [vmem] * 3 + [smem]
    slots = 34
    extra = []
    if layer == 0:
        out_shape += [
            jax.ShapeDtypeStruct((3, 4, 4, 56, FS), BF),
            jax.ShapeDtypeStruct((3, 4, 4, 56, FS), BF),
            jax.ShapeDtypeStruct((2, 4, 4, 4, 16, 1024), BF),
        ]
        operands += shards
        in_specs += [anywhere] * 3
        slots = 98
        extra = [
            pltpu.VMEM((2, 4, 16, 1024), BF),
            pltpu.VMEM((2, 4, 16, 1024), BF),
            pltpu.VMEM((2, 4, 56, FS), BF),
            pltpu.VMEM((1, 4, 56, FS), BF),
            pltpu.VMEM((3, 4, 4, 56, FS), BF),
        ]
    return pl.pallas_call(
        functools.partial(forward_kernel, layer),
        out_shape=tuple(out_shape),
        in_specs=in_specs,
        out_specs=[vmem] * 2 + [anywhere] * (len(out_shape) - 2),
        scratch_shapes=[
            pltpu.VMEM((2, 4, 4, 4, 16, 1024), BF),
            pltpu.VMEM((D, 1024), BF),
            pltpu.VMEM((D, 1024), BF),
            pltpu.VMEM((4, 2, 128, 256), BF),
            pltpu.VMEM((KVH, 4, D, 256), BF),
            pltpu.VMEM((KVH, 4, D, 256), F32),
            pltpu.VMEM((4, 128, 256), F32),
            pltpu.VMEM((128, D), F32),
            pltpu.VMEM((KVH, D, HD), BF),
            pltpu.VMEM((128, D), F32),
            pltpu.VMEM((128, D), BF),
        ]
        + mlp_scratch()
        + [
            pltpu.VMEM((3, D, FS), BF),
            pltpu.VMEM((4, 256, FS), BF),
            pltpu.VMEM((4, 256, FS), BF),
            pltpu.SemaphoreType.DMA((slots,)),
            pltpu.SemaphoreType.DMA((slots,)),
            pltpu.SemaphoreType.DMA((31,)),
        ]
        + extra,
        compiler_params=pltpu.CompilerParams(
            collective_id=12 + layer, has_side_effects=True, vmem_limit_bytes=56 * 1024 * 1024
        ),
        name="forward_layer_%d" % layer,
    )(*operands)


BACK_SLOTS = {1: 48, 0: 94}


def backward_kernel(layer, *refs):
    g_ref, x_ref, vec_ref, cos_ref, sin_ref, place_ref = refs[:6]
    w_ref, hr_ref, gate_ref, up_ref, mid_ref, att_ref, qs_ref = refs[6:13]
    kv_ref, probs_ref, low_ref, high_ref = refs[13:17]
    refs = refs[17:]
    if layer == 0:
        before, gin_ref, m_out, a_zero, a_one = refs[:5]
        refs = refs[5:]
    else:
        gin_ref, m_out, a_out = refs[:3]
        refs = refs[3:]
    buffers, refs = refs[:7], refs[7:]
    w, hr, gate, up, act, src, mid, att, qs = refs[:9]
    low, high, kv, probs, m, gatt, part, near, own, got, glow, ghigh, special = refs[9:22]
    plane_refs, refs = refs[22:30], refs[30:]
    send_sem, recv_sem, local_sem = refs[-3:]
    rows, back = buffers[0], buffers[1]
    spot = place()
    x, z, y, c = spot
    mail = Mail(send_sem, recv_sem)
    pairs = (
        (w_ref, w), (gate_ref, gate), (up_ref, up), (hr_ref, hr), (high_ref, high), (mid_ref, mid),
        (att_ref, att), (probs_ref, probs), (kv_ref, kv), (qs_ref, qs), (low_ref, low),
    )
    loads = [pltpu.make_async_copy(u, v, local_sem.at[i]) for i, (u, v) in enumerate(pairs)]
    for load in loads[:4]:
        load.start()
    src[...] = g_ref[...].astype(BF)
    yp, ym, y2 = up1(y), down1(y), up2(y)
    to_yp, to_ym, other = ctx_peers(spot)
    to_y2 = device(x, z, y2, c)
    greet([to_yp, to_ym, other, to_y2] + PlaneSum.peers(spot, 3, 2))
    plane = PlaneSum(mail, 32, spot, m, 2, plane_refs)
    older = final = None
    if layer == 0:
        older_mine, older_refs = refs[0], refs[1:12]
        pair, final_refs = refs[12], refs[13:24]
        older = AttentionSum(mail.shifted(48), spot, older_mine, before.at[1 - c], older_refs)
        final = AttentionSum(mail.shifted(71), spot, pair.at[0], pair.at[1], final_refs)
        older_load = pltpu.make_async_copy(before.at[c], older_mine, local_sem.at[11])
        older_load.start()

    loaded = []

    def chunk(row):
        if not loaded:
            for load in loads[:3]:
                load.wait()
            loaded.append(True)
            for load in loads[4:]:
                load.start()
        gz = rows[row].reshape(256, D)
        gact = nn(gz, w[2])
        g = gate[row].astype(F32)
        u = up[row].astype(F32)
        s = 1.0 / (1.0 + jnp.exp(-g))
        silu = g * s
        act[row] = (silu * u).astype(BF)
        gg = (gact * u * (s + silu * (1.0 - s))).astype(BF)
        gu = (gact * silu).astype(BF)
        gate[row] = gg
        up[row] = gu
        back[row] = (nt(gg, w[0]) + nt(gu, w[1])).astype(BF).reshape(2, 128, D)

    def weight_grad(member, left, right):
        r = right[...].reshape(1024, FS)
        for i in range(7):
            l = left[:, :, :, 128 * i : 128 * (i + 1)].reshape(1024, 128)
            tile = tn(l, r).astype(BF)
            for b in range(16):
                lo, hi = max(56 * b, 128 * i), min(56 * (b + 1), 128 * (i + 1))
                if lo < hi:
                    m[member, b // 4, b % 4, lo - 56 * b : hi - 56 * b] = tile[
                        lo - 128 * i : hi - 128 * i
                    ]

    def first_filler():
        weight_grad(2, rows, act)

    def second_filler():
        loads[3].wait()
        weight_grad(0, hr, gate)

    def third_filler():
        weight_grad(1, hr, up)
        plane.step_one()

    def hook():
        if older:
            for i in range(4):
                older.start(i)

    ghid2 = mlp_exchange(
        mail, spot, src, buffers, chunk, [first_filler, second_filler, third_filler], hook
    )
    if older:
        older_load.wait()
        older.cores()
    for load in loads[4:7]:
        load.wait()
    n, r = normal(mid[...])
    t = ghid2 * vec_ref[1:2, :D]
    gmid = g_ref[...].astype(F32) + r * (t - n * jnp.mean(t * n, axis=-1, keepdims=True))
    ggain_two = jnp.sum(ghid2 * n, axis=0, keepdims=True)
    gin_ref[...] = gmid
    gy = gmid.astype(BF)
    ga = nt(gy, high[:, 128:]).astype(BF)
    product = ga.astype(F32) * att[...]
    deltas = [[], []]
    for h in range(H):
        gatt[h // 7, 128 * (h % 7) : 128 * (h % 7 + 1)] = ga[:, HD * h : HD * (h + 1)]
        deltas[h // 7].append(
            jnp.sum(product[:, HD * h : HD * (h + 1)], axis=-1, keepdims=True)
        )
    ghigh[:, 128:] = tn(att[...].astype(BF), gy).astype(BF)
    for load in loads[7:]:
        load.wait()
    plane.step_two()
    deltas = [jnp.concatenate(group, axis=0) for group in deltas]
    gqs = [jnp.zeros((D, HD), F32) for k in range(KVH)]
    for row in range(4):
        for k in range(KVH):
            keys = kv[row, :, :, HD * k : HD * (k + 1)].reshape(256, HD)
            values = kv[row, :, :, 128 + HD * k : 128 + HD * (k + 1)].reshape(256, HD)
            p = probs[k, row]
            s = (p.astype(F32) * (nt(gatt[k], values) - deltas[k])).astype(BF)
            gqs[k] = gqs[k] + nn(s, keys)
            gk = tn(qs[k], s).astype(BF)
            gv = tn(gatt[k], p).astype(BF)
            for j in range(2):
                part[row, j, HD * k : HD * (k + 1)] = gk[:, 128 * j : 128 * (j + 1)]
                part[row, j, 128 + HD * k : 128 + HD * (k + 1)] = gv[:, 128 * j : 128 * (j + 1)]
        mail.send(25 + row, part.at[row, 1 - c], near.at[row], other)
        if older and row == 1:
            older.plane.step_two()
    plane.step_three()
    cos = jnp.concatenate([cos_ref[...]] * 7, axis=1)
    sin = jnp.concatenate([sin_ref[...]] * 7, axis=1)
    gq = [gqs[h // 7][128 * (h % 7) : 128 * (h % 7 + 1)] for h in range(H)]
    gq = jnp.concatenate(gq, axis=1) * HD ** (-0.5)
    gq = (gq * cos - swap_halves(gq) * sin).astype(BF)
    inputs = x_ref[...].astype(F32)
    n, r = normal(inputs)
    hidden = (n * vec_ref[0:1, :D]).astype(BF)
    for i in range(4):
        mail.take(25 + i, near.at[i], other)
    own[...] = (part[:, c].astype(F32) + near[...].astype(F32)).astype(BF)
    mail.send(29, own.at[yp], got.at[0], to_yp)
    mail.send(30, own.at[ym], got.at[1], to_ym)
    mail.send(31, own.at[y2], got.at[2], to_y2)
    if older:
        older.plane.step_three()
    glow[:, :D] = tn(hidden, gq).astype(BF)
    ghid = nt(gq, low[:, :D])
    bias_q = jnp.sum(gq.astype(F32), axis=0, keepdims=True)
    plane.step_four()
    mail.take(29, got.at[0], to_ym)
    mail.take(30, got.at[1], to_yp)
    mail.take(31, got.at[2], to_y2)
    total = own[y].astype(F32) + got[0].astype(F32) + got[1].astype(F32) + got[2].astype(F32)
    total = total.T
    gk = total[:, :128]
    gk = (gk * cos_ref[...] - swap_halves(gk) * sin_ref[...]).astype(BF)
    gv = total[:, 128:].astype(BF)
    ghid = ghid + nt(gk, low[:, D:]) + nt(gv, high[:, :128])
    glow[:, D:] = tn(hidden, gk).astype(BF)
    ghigh[:, :128] = tn(hidden, gv).astype(BF)
    t = ghid * vec_ref[0:1, :D]
    gin_ref[...] += r * (t - n * jnp.mean(t * n, axis=-1, keepdims=True))
    ggain_one = jnp.sum(ghid * n, axis=0, keepdims=True)
    if older:
        older.plane.step_four()
    bias_k = jnp.sum(gk.astype(F32), axis=0, keepdims=True)
    bias_v = jnp.sum(gv.astype(F32), axis=0, keepdims=True)
    bias = jnp.concatenate([bias_q, bias_k], axis=1)
    row = lax.broadcasted_iota(jnp.int32, (16, 1024), 0)
    row_last = jnp.concatenate([ggain_two, bias_v], axis=1)
    for g in range(8):
        row_seven = jnp.concatenate([ggain_one, bias[:, 128 * g : 128 * (g + 1)]], axis=1)
        extra = jnp.where(row == 0, row_seven, jnp.where(row == 1, row_last, 0.0))
        special[...] = extra.astype(BF)
        block = (
            nn(place_ref[0], glow[112 * g : 112 * (g + 1)])
            + nn(place_ref[1], ghigh[112 * g : 112 * (g + 1)])
            + nn(place_ref[2, :, 0:16], special[...])
        ).astype(BF)
        for k in range(16):
            core, line, column = k % 2, k % 8 // 2, 2 * (g % 2) + k // 8
            piece = block[16 * k : 16 * (k + 1)]
            if layer == 0:
                pair[lax.rem(c + core, 2), line, g // 2, column] = piece
            else:
                a_out[core, line, g // 2, column] = piece
        if layer == 0 and g % 2 == 1:
            final.start(g // 2)
    if layer == 0:
        older.rows()
        plane.step_five(m_out)
        final.cores()
        older.last(a_one)
        final.plane.step_two()
        final.plane.step_three()
        final.plane.step_four()
        final.rows()
        final.last(a_zero)
    else:
        plane.step_five(m_out)
    mail.finish()


def backward(layer, grad_output, x, vectors, tables, place_rows, w, kept_mlp, kept, before):
    anywhere = pl.BlockSpec(memory_space=pl.ANY)
    vmem = pl.BlockSpec(memory_space=pltpu.VMEM)
    operands = [grad_output, x, vectors, *tables, place_rows, w, *kept_mlp, *kept]
    out_shape = [jax.ShapeDtypeStruct((128, D), F32), jax.ShapeDtypeStruct((3, 56, FS), F32)]
    extra = []
    if layer == 0:
        operands.append(before)
        out_shape += [jax.ShapeDtypeStruct((16, 1024), F32)] * 2
        extra = [pltpu.VMEM((4, 4, 4, 16, 1024), BF)] + AttentionSum.scratch()
        extra += [pltpu.VMEM((2, 4, 4, 4, 16, 1024), BF)] + AttentionSum.scratch()
    else:
        out_shape.append(jax.ShapeDtypeStruct((2, 4, 4, 4, 16, 1024), BF))
    return pl.pallas_call(
        functools.partial(backward_kernel, layer),
        out_shape=tuple(out_shape),
        in_specs=[vmem] * 6 + [anywhere] * (len(operands) - 6),
        out_specs=[vmem] * len(out_shape),
        scratch_shapes=mlp_scratch()
        + [
            pltpu.VMEM((3, D, FS), BF),
            pltpu.VMEM((4, 2, 128, D), BF),
            pltpu.VMEM((4, 256, FS), BF),
            pltpu.VMEM((4, 256, FS), BF),
            pltpu.VMEM((4, 256, FS), BF),
            pltpu.VMEM((128, D), BF),
            pltpu.VMEM((128, D), F32),
            pltpu.VMEM((128, D), F32),
            pltpu.VMEM((KVH, D, HD), BF),
            pltpu.VMEM((D, 1024), BF),
            pltpu.VMEM((D, 1024), BF),
            pltpu.VMEM((4, 2, 128, 256), BF),
            pltpu.VMEM((KVH, 4, D, 256), BF),
            pltpu.VMEM((3, 4, 4, 56, FS), BF),
            pltpu.VMEM((KVH, D, HD), BF),
            pltpu.VMEM((4, 2, 256, 128), BF),
            pltpu.VMEM((4, 256, 128), BF),
            pltpu.VMEM((4, 256, 128), BF),
            pltpu.VMEM((3, 256, 128), BF),
            pltpu.VMEM((D, 1024), BF),
            pltpu.VMEM((D, 1024), BF),
            pltpu.VMEM((16, 1024), BF),
        ]
        + PlaneSum.scratch(3, 2, 56, FS)
        + extra
        + [
            pltpu.SemaphoreType.DMA((BACK_SLOTS[layer],)),
            pltpu.SemaphoreType.DMA((BACK_SLOTS[layer],)),
            pltpu.SemaphoreType.DMA((12,)),
        ],
        compiler_params=pltpu.CompilerParams(
            collective_id=14 + layer, has_side_effects=True, vmem_limit_bytes=60 * 1024 * 1024
        ),
        name="backward_layer_%d" % layer,
    )(*operands)


def select_matrix():
    pick = np.zeros((226, 256), np.float32)
    for k in range(16):
        for r in range(7):
            pick[7 * k + r, 16 * k + r] = 1
            pick[112 + 7 * k + r, 16 * k + 8 + r] = 1
        pick[224, 16 * k + 7] = 1
        pick[225, 16 * k + 15] = 1
    return pick


def assemble_kernel(
    a_zero, a_one, m_zero, m_one, g_one, g_qkv, g_qk, g_value, g_out, g_two, g_gate, g_up, g_down, rows
):
    index = lax.axis_index("dp") * 8 + lax.axis_index("ctx")
    rows[...] = jnp.zeros_like(rows)
    for l, (a_ref, m_ref) in enumerate(((a_zero, m_zero), (a_one, m_one))):
        for r in range(7):
            g_qkv[r, l : l + 1, 0:1024] = a_ref[r : r + 1, :]
            g_qkv[r, l : l + 1, 1024:1152] = a_ref[8 + r : 9 + r, 0:128]
            g_out[r, l : l + 1] = a_ref[8 + r : 9 + r, 128:1024]
        g_gate[l] = m_ref[0]
        g_up[l] = m_ref[1]
        g_down[l] = m_ref[2]
        rows[l : l + 1] = a_ref[7:8, :]
        rows[2 + l : 3 + l] = a_ref[15:16, :]
    gains = pltpu.roll(rows[...], lax.rem(1024 - 7 * index, 1024), 1)
    g_one[...] = gains[0:2, 0:7]
    g_two[...] = gains[2:4, 0:7]
    g_qk[...] = pltpu.roll(rows[...], 128 - 8 * lax.rem(index, 16), 1)[0:2, 0:8]
    g_value[...] = pltpu.roll(rows[...], 128 - index, 1)[2:4, 0:1]


def assemble(a_sums, m_sums):
    vmem = pl.BlockSpec(memory_space=pltpu.VMEM)
    shapes = ((2, 7), (7, 2, QKV), (2, 8), (2, 1), (7, 2, D), (2, 7)) + ((2, 56, FS),) * 3
    out = pl.pallas_call(
        assemble_kernel,
        out_shape=tuple(jax.ShapeDtypeStruct(shape, F32) for shape in shapes),
        in_specs=[vmem] * 4,
        out_specs=[vmem] * len(shapes),
        scratch_shapes=[pltpu.VMEM((8, 1024), F32)],
        name="assemble",
    )(*a_sums, *m_sums)
    one, qkv, qk, value, outs, two, gate, up, down = out
    qkv, outs = qkv.transpose(1, 0, 2), outs.transpose(1, 0, 2)
    return one, qkv, qk, value, outs, two, gate, up, down.transpose(0, 2, 1)


def shards(
    tokens, cotangent, span_order, gain_one, w_qkv, b_qkv, w_out, gain_two, w_gate, w_up, w_down
):
    sequences, local_len, width = tokens.shape
    span_len = local_len // 2
    local_spans = lax.dynamic_slice_in_dim(span_order, 2 * lax.axis_index("ctx"), 2)
    local_pos = jnp.repeat(local_spans * span_len, span_len) + np.tile(np.arange(span_len), 2)
    half = np.arange(HD // 2, dtype=np.float32)
    frequency = np.tile(np.float32(rope_base) ** (-half * np.float32(2.0 / HD)), 4)
    sign = np.tile(np.repeat(np.float32([-1, 1]), HD // 2), 2)
    angles = local_pos.astype(F32)[:, None] * frequency[None, :].astype(np.float32)
    tables = (jnp.cos(angles), jnp.sin(angles) * sign[None, :])
    chosen = select_matrix()
    pick = jnp.asarray(np.concatenate([chosen, np.zeros((14, 256), np.float32)]), BF)
    spread = np.zeros((3, 256, 112), np.float32)
    spread[0], spread[1], spread[2, :, :2] = chosen[:112].T, chosen[112:224].T, chosen[224:].T
    spread = jnp.asarray(spread, BF)

    m_block = jnp.stack([w_gate, w_up, w_down.transpose(0, 2, 1)], axis=1)
    a_zero, row_one, m_x, m_z = first_gather(
        gain_one, w_qkv.transpose(1, 0, 2), b_qkv, w_out.transpose(1, 0, 2), gain_two, m_block
    )
    state_zero = tokens.reshape(local_len, width)
    state_one, *saved_zero, m_zero, m_one, a_one = forward(
        0, state_zero, a_zero, m_x, pick, tables, span_order, row_one, m_block, m_z
    )
    m_full = (m_zero.reshape(3, D, FS), m_one.reshape(3, D, FS))
    state, *saved_one = forward(1, state_one, a_one, m_full[1], pick, tables, span_order)
    vectors = (saved_zero[0], saved_one[0])
    kept_layers = [
        (saved_zero[1:8], saved_zero[8:]),
        (saved_one[1:8], saved_one[8:]),
    ]
    grad_one = cotangent.reshape(local_len, width)
    (state_in, kept, kept_mlp) = (state_one,) + kept_layers[1]
    grad_zero, m_sum_one, a_grads = backward(
        1, grad_one, state_in, vectors[1], tables, spread, m_full[1], kept_mlp, kept, None
    )
    kept, kept_mlp = kept_layers[0]
    grad_state, m_sum_zero, a_sum_zero, a_sum_one = backward(
        0, grad_zero, state_zero, vectors[0], tables, spread, m_full[0], kept_mlp, kept, a_grads
    )
    a_sums = (a_sum_zero, a_sum_one)
    sums = (m_sum_zero, m_sum_one)
    stacks = assemble(a_sums, sums)
    output = state.astype(BF).reshape(sequences, local_len, width)
    input_grad = grad_state.reshape(sequences, local_len, width)
    return (output, input_grad) + stacks


def solution(mesh):
    return jax.shard_map(
        shards,
        mesh=mesh,
        in_specs=(
            P("dp", "ctx", None),
            P("dp", "ctx", None),
            P(),
            P(None, ("dp", "ctx")),
            P(None, ("dp", "ctx"), None),
            P(None, ("dp", "ctx")),
            P(None, ("dp", "ctx"), None),
            P(None, ("dp", "ctx")),
            P(None, "dp", "ctx"),
            P(None, "dp", "ctx"),
            P(None, "ctx", "dp"),
        ),
        out_specs=(
            P("dp", "ctx", None),
            P("dp", "ctx", None),
            P(None, ("dp", "ctx")),
            P(None, ("dp", "ctx"), None),
            P(None, ("dp", "ctx")),
            P(None, ("dp", "ctx")),
            P(None, ("dp", "ctx"), None),
            P(None, ("dp", "ctx")),
            P(None, "dp", "ctx"),
            P(None, "dp", "ctx"),
            P(None, "ctx", "dp"),
        ),
        check_vma=False,
    )
```

```python
import functools

import jax
import jax.numpy as jnp
import numpy as np
from jax import lax
from jax.experimental import pallas as pl
from jax.experimental.pallas import tpu as pltpu
from jax.sharding import PartitionSpec as P

H = 14
KVH = 2
HD = 64
LAYERS = 2
D = 896
QKV = 1152
FS = 608
MESH = pl.DeviceIdType.MESH
BF = jnp.bfloat16
F32 = jnp.float32

eps_norm = 1e-06
rope_base = 1000000.0
neg_fill = -1e30


def place():
    dp = lax.axis_index("dp")
    ctx = lax.axis_index("ctx")
    return lax.div(dp, 4), lax.rem(dp, 4), lax.div(ctx, 2), lax.rem(ctx, 2)


def up1(v):
    return lax.rem(v + 1, 4)


def up2(v):
    return lax.rem(v + 2, 4)


def down1(v):
    return lax.rem(v + 3, 4)


def device(x, z, y, c):
    return (x * 4 + z, y * 2 + c)


def greet(peers):
    barrier = pltpu.get_barrier_semaphore()
    for peer in peers:
        pl.semaphore_signal(barrier, inc=1, device_id=peer, device_id_type=MESH)
    pl.semaphore_wait(barrier, len(peers))


class Mail:
    def __init__(self, send_sem, recv_sem, base=0, sent=None):
        self.send_sem = send_sem
        self.recv_sem = recv_sem
        self.base = base
        self.sent = [] if sent is None else sent

    def shifted(self, base):
        return Mail(self.send_sem, self.recv_sem, self.base + base, self.sent)

    def send(self, slot, src, dst, target):
        copy = pltpu.make_async_remote_copy(
            src_ref=src,
            dst_ref=dst,
            send_sem=self.send_sem.at[self.base + slot],
            recv_sem=self.recv_sem.at[self.base + slot],
            device_id=target,
            device_id_type=MESH,
        )
        copy.start()
        self.sent.append(copy)

    def take(self, slot, dst, source):
        pltpu.make_async_remote_copy(
            src_ref=dst,
            dst_ref=dst,
            send_sem=self.send_sem.at[self.base + slot],
            recv_sem=self.recv_sem.at[self.base + slot],
            device_id=source,
            device_id_type=MESH,
        ).wait_recv()

    def finish(self):
        for copy in self.sent:
            copy.wait_send()


class RowGather:
    slots = 8

    def __init__(self, mail, spot, block, along_x, along_z, local_sem):
        self.mail, self.spot, self.block = mail, spot, block
        self.along_x, self.along_z = along_x, along_z
        self.cut, self.rest = along_x.shape[0], along_z.shape[0]
        x, z = spot[:2]
        self.sa, self.sb = pl.ds(0, self.cut), pl.ds(self.cut, self.rest)
        self.own = [
            pltpu.make_async_copy(block.at[self.sa], along_x.at[:, x], local_sem.at[0]),
            pltpu.make_async_copy(block.at[self.sb], along_z.at[:, z], local_sem.at[1]),
        ]

    def step_one(self):
        x, z = self.spot[:2]
        to_xp, to_xm, to_zp, to_zm = ring_peers(self.spot)
        for copy in self.own:
            copy.start()
        self.mail.send(0, self.block.at[self.sa], self.along_x.at[:, x], to_xp)
        self.mail.send(1, self.block.at[self.sa], self.along_x.at[:, x], to_xm)
        self.mail.send(4, self.block.at[self.sb], self.along_z.at[:, z], to_zp)
        self.mail.send(5, self.block.at[self.sb], self.along_z.at[:, z], to_zm)

    def relays(self):
        x, z = self.spot[:2]
        to_xp, to_xm, to_zp, to_zm = ring_peers(self.spot)
        return (
            (0, self.along_x, self.cut, x, to_xp, to_xm),
            (4, self.along_z, self.rest, z, to_zp, to_zm),
        )

    def step_two(self):
        for base, ref, count, here, plus, minus in self.relays():
            behind, front = down1(here), up1(here)
            half = max(count // 2, 1)
            self.mail.take(base, ref.at[:, behind], minus)
            part = ref.at[pl.ds(0, half), behind]
            self.mail.send(base + 2, part, part, plus)
            self.mail.take(base + 1, ref.at[:, front], plus)
            if count > 1:
                part = ref.at[pl.ds(half, count - half), front]
                self.mail.send(base + 3, part, part, minus)

    def step_three(self):
        for base, ref, count, here, plus, minus in self.relays():
            half = max(count // 2, 1)
            self.mail.take(base + 2, ref.at[pl.ds(0, half), up2(here)], minus)
            if count > 1:
                self.mail.take(base + 3, ref.at[pl.ds(half, count - half), up2(here)], plus)
        for copy in self.own:
            copy.wait()


class PlaneFill:
    slots = 16

    def __init__(self, mail, spot, along_x, along_z, full, local_sem, mirror=None):
        self.mail, self.spot, self.full, self.mirror = mail, spot, full, mirror
        self.along_x, self.along_z = along_x, along_z
        self.cut, self.rest = along_x.shape[0], along_z.shape[0]
        x, z, y, c = spot
        self.other = device(x, z, y, 1 - c)
        self.copies = [
            pltpu.make_async_copy(along_x, full.at[self.first(z)], local_sem.at[0]),
            pltpu.make_async_copy(along_z, full.at[self.second(x)], local_sem.at[1]),
        ]

    def first(self, z, half=None):
        if half is None:
            return (pl.ds(0, self.cut), pl.ds(0, 4), z)
        if self.cut == 1:
            return (pl.ds(0, 1), pl.ds(2 * half, 2), z)
        return (pl.ds(half * (self.cut // 2), self.cut // 2), pl.ds(0, 4), z)

    def second(self, x, half=None):
        if half is None:
            return (pl.ds(self.cut, self.rest), x, pl.ds(0, 4))
        if self.rest == 1:
            return (pl.ds(self.cut, 1), x, pl.ds(2 * half, 2))
        return (pl.ds(self.cut + half * (self.rest // 2), self.rest // 2), x, pl.ds(0, 4))

    def pass_on(self, slot, where, target):
        self.mail.send(slot, self.full.at[where], self.full.at[where], target)

    def share(self, slot, where, src=None):
        if self.mirror is not None:
            src = self.full.at[where] if src is None else src
            self.mail.send(slot, src, self.full.at[where], self.other)

    def step_one(self):
        x, z = self.spot[:2]
        to_xp, to_xm, to_zp, to_zm = ring_peers(self.spot)
        self.mail.send(0, self.along_x, self.full.at[self.first(z)], to_zp)
        self.mail.send(1, self.along_x, self.full.at[self.first(z)], to_zm)
        self.mail.send(2, self.along_z, self.full.at[self.second(x)], to_xp)
        self.mail.send(3, self.along_z, self.full.at[self.second(x)], to_xm)
        self.share(8, self.first(z), self.along_x)
        self.share(9, self.second(x), self.along_z)
        for copy in self.copies:
            copy.start()

    def step_two(self):
        x, z = self.spot[:2]
        to_xp, to_xm, to_zp, to_zm = ring_peers(self.spot)
        xp, xm, zp, zm = up1(x), down1(x), up1(z), down1(z)
        for slot, where, piece, source, target in (
            (0, self.first(zm), self.first(zm, 0), to_zm, to_zp),
            (2, self.second(xm), self.second(xm, 0), to_xm, to_xp),
            (1, self.first(zp), self.first(zp, 1), to_zp, to_zm),
            (3, self.second(xp), self.second(xp, 1), to_xp, to_xm),
        ):
            self.mail.take(slot, self.full.at[where], source)
            self.pass_on(4 + slot, piece, target)
            self.share(10 + slot, where)

    def step_three(self):
        x, z = self.spot[:2]
        to_xp, to_xm, to_zp, to_zm = ring_peers(self.spot)
        for slot, piece, source in (
            (4, self.first(up2(z), 0), to_zm),
            (6, self.second(up2(x), 0), to_xm),
            (5, self.first(up2(z), 1), to_zp),
            (7, self.second(up2(x), 1), to_xp),
        ):
            self.mail.take(slot, self.full.at[piece], source)
        self.share(14, self.first(up2(z)))
        self.share(15, self.second(up2(x)))
        for copy in self.copies:
            copy.wait()

    def step_four(self):
        x, z = self.spot[:2]
        xp, xm, zp, zm = up1(x), down1(x), up1(z), down1(z)
        for slot, where in (
            (8, self.first(z)),
            (9, self.second(x)),
            (10, self.first(zm)),
            (11, self.first(zp)),
            (12, self.second(xm)),
            (13, self.second(xp)),
            (14, self.first(up2(z))),
            (15, self.second(up2(x))),
        ):
            self.mail.take(slot, self.mirror.at[where], self.other)


def ring_peers(spot):
    x, z, y, c = spot
    return [
        device(up1(x), z, y, c),
        device(down1(x), z, y, c),
        device(x, up1(z), y, c),
        device(x, down1(z), y, c),
    ]


def ctx_peers(spot):
    x, z, y, c = spot
    return [device(x, z, up1(y), c), device(x, z, down1(y), c), device(x, z, y, 1 - c)]


def first_gather_kernel(
    one_ref, qkv_ref, bias_ref, out_ref, two_ref, m_ref,
    full, row_out, m_x, m_z,
    rows, vectors, offsets, line, a_x, a_z, send_sem, recv_sem, local_sem,
):
    spot = place()
    x, z, y, c = spot
    index = (x * 4 + z) * 8 + 2 * y + c
    mail = Mail(send_sem, recv_sem)
    vectors[...] = jnp.zeros_like(vectors)
    offsets[...] = jnp.zeros_like(offsets)
    vectors[0:2, 0:7] = one_ref[...].astype(F32)
    vectors[2:4, 0:7] = two_ref[...].astype(F32)
    offsets[0:2, 0:9] = bias_ref[...].astype(F32)
    gains = pltpu.roll(vectors[...], 7 * index, 1)
    bias = pltpu.roll(offsets[...], 9 * index - 128 * lax.div(index, 16), 1)
    qkv, out = qkv_ref[...].astype(F32), out_ref[...].astype(F32)
    for l in range(LAYERS):
        for r in range(7):
            rows[l, r : r + 1, :] = qkv[r, l : l + 1, :1024]
            rows[l, 8 + r : 9 + r, 0:128] = qkv[r, l : l + 1, 1024:]
            rows[l, 8 + r : 9 + r, 128:1024] = out[r, l : l + 1]
        rows[l, 7:8, 0:D] = gains[l : l + 1, :D]
        rows[l, 15:16, 0:D] = gains[2 + l : 3 + l, :D]
        rows[l, 7:8, D:1024] = bias[l : l + 1, :128]
        rows[l, 15:16, D:1024] = bias[l : l + 1, 128:]
    line[:, y] = rows[...].astype(BF)
    yp, ym, y2 = up1(y), down1(y), up2(y)
    to_yp, to_ym, other = ctx_peers(spot)
    to_y2 = device(x, z, y2, c)
    greet(ring_peers(spot) + [to_yp, to_ym, other, to_y2])
    mail.send(0, line.at[:, y], line.at[:, y], to_yp)
    mail.send(1, line.at[:, y], line.at[:, y], to_ym)
    mail.send(2, line.at[:, y], line.at[:, y], to_y2)
    row = RowGather(mail.shifted(3), spot, line.at[0], a_x, a_z, local_sem.at[pl.ds(0, 2)])
    fill = PlaneFill(
        mail.shifted(11), spot, a_x, a_z, full.at[c], local_sem.at[pl.ds(2, 2)], full.at[1 - c]
    )
    feed = RowGather(mail.shifted(27), spot, m_ref.at[0], m_x, m_z, local_sem.at[pl.ds(4, 2)])
    mail.take(0, line.at[:, ym], to_ym)
    mail.take(1, line.at[:, yp], to_yp)
    mail.take(2, line.at[:, y2], to_y2)
    row.step_one()
    kept = pltpu.make_async_copy(line.at[1], row_out, local_sem.at[6])
    kept.start()
    row.step_two()
    row.step_three()
    fill.step_one()
    feed.step_one()
    fill.step_two()
    feed.step_two()
    fill.step_three()
    feed.step_three()
    fill.step_four()
    kept.wait()
    mail.finish()


def first_gather(gain_one, w_qkv, b_qkv, w_out, gain_two, m_block):
    return pl.pallas_call(
        first_gather_kernel,
        out_shape=(
            jax.ShapeDtypeStruct((2, 4, 4, 4, 16, 1024), BF),
            jax.ShapeDtypeStruct((4, 16, 1024), BF),
            jax.ShapeDtypeStruct((2, 4, 56, FS), BF),
            jax.ShapeDtypeStruct((1, 4, 56, FS), BF),
        ),
        in_specs=[pl.BlockSpec(memory_space=pltpu.VMEM)] * 5 + [pl.BlockSpec(memory_space=pl.ANY)],
        out_specs=[pl.BlockSpec(memory_space=pl.ANY)] * 4,
        scratch_shapes=[
            pltpu.VMEM((2, 16, 1024), F32),
            pltpu.VMEM((8, 1024), F32),
            pltpu.VMEM((8, 256), F32),
            pltpu.VMEM((2, 4, 16, 1024), BF),
            pltpu.VMEM((2, 4, 16, 1024), BF),
            pltpu.VMEM((2, 4, 16, 1024), BF),
            pltpu.SemaphoreType.DMA((35,)),
            pltpu.SemaphoreType.DMA((35,)),
            pltpu.SemaphoreType.DMA((7,)),
        ],
        compiler_params=pltpu.CompilerParams(
            collective_id=1, has_side_effects=True, vmem_limit_bytes=60 * 1024 * 1024
        ),
        name="first_gather",
    )(gain_one, w_qkv, b_qkv, w_out, gain_two, m_block)


class PlaneSum:
    def __init__(self, mail, base, spot, g, cut, buffers):
        self.mail, self.base, self.spot, self.g, self.cut = mail, base, spot, g, cut
        self.count = g.shape[0]
        self.buffers = buffers

    @staticmethod
    def scratch(slabs, cut, rows, columns):
        rest = slabs - cut
        out = [
            pltpu.VMEM((2, cut, 2, rows, columns), BF),
            pltpu.VMEM((2, cut, 4, rows, columns), BF),
            pltpu.VMEM((2, rest, 2, rows, columns), BF),
            pltpu.VMEM((2, rest, 4, rows, columns), BF),
            pltpu.VMEM((2, cut // 2, rows, columns), BF),
            pltpu.VMEM((2, cut, rows, columns), BF),
            pltpu.VMEM((2, max(rest // 2, 1), rows, columns), BF),
            pltpu.VMEM((2, rest, rows, columns), BF),
        ]
        return out

    @staticmethod
    def peers(spot, slabs, cut):
        x, z, y, c = spot
        near = [device(up1(x), z, y, c), device(down1(x), z, y, c), device(x, up1(z), y, c), device(x, down1(z), y, c)]
        return near + ([device(x, up2(z), y, c)] if slabs - cut == 1 else [])

    def names(self):
        x, z, y, c = self.spot
        xp, xm, zp, zm = up1(x), down1(x), up1(z), down1(z)
        to = (device(xp, z, y, c), device(xm, z, y, c), device(x, zp, y, c), device(x, zm, y, c))
        return x, z, xp, xm, zp, zm, up2(x), up2(z), to

    def send(self, slot, src, dst, target):
        self.mail.send(self.base + slot, src, dst, target)

    def take(self, slot, dst, source):
        self.mail.take(self.base + slot, dst, source)

    def add(self, where, extra):
        part = self.g.at[where]
        part[...] = (part[...].astype(F32) + extra.astype(F32)).astype(BF)

    def step_one(self):
        x, z, xp, xm, zp, zm, x2, z2, (to_xp, to_xm, to_zp, to_zm) = self.names()
        fa, ga, fb, gb, pa, qa, pb, qb = self.buffers
        sa, sb = pl.ds(0, self.cut), pl.ds(self.cut, self.count - self.cut)
        lo, hi = pl.ds(0, 2), pl.ds(2, 2)
        self.send(0, self.g.at[sa, lo, z2], fa.at[0], to_zp)
        self.send(1, self.g.at[sa, hi, z2], fa.at[1], to_zm)
        self.send(2, self.g.at[sb, x2, lo], fb.at[0], to_xp)
        self.send(3, self.g.at[sb, x2, hi], fb.at[1], to_xm)

    def step_two(self):
        x, z, xp, xm, zp, zm, x2, z2, (to_xp, to_xm, to_zp, to_zm) = self.names()
        fa, ga, fb, gb, pa, qa, pb, qb = self.buffers
        sa, sb = pl.ds(0, self.cut), pl.ds(self.cut, self.count - self.cut)
        lo, hi, every = pl.ds(0, 2), pl.ds(2, 2), pl.ds(0, 4)
        self.take(0, fa.at[0], to_zm)
        self.add((sa, lo, zp), fa[0])
        self.send(4, self.g.at[sa, every, zp], ga.at[0], to_zp)
        self.take(2, fb.at[0], to_xm)
        self.add((sb, xp, lo), fb[0])
        self.send(6, self.g.at[sb, xp, every], gb.at[0], to_xp)
        self.take(1, fa.at[1], to_zp)
        self.add((sa, hi, zm), fa[1])
        self.send(5, self.g.at[sa, every, zm], ga.at[1], to_zm)
        self.take(3, fb.at[1], to_xp)
        self.add((sb, xm, hi), fb[1])
        self.send(7, self.g.at[sb, xm, every], gb.at[1], to_xm)

    def step_three(self):
        x, z, xp, xm, zp, zm, x2, z2, (to_xp, to_xm, to_zp, to_zm) = self.names()
        fa, ga, fb, gb, pa, qa, pb, qb = self.buffers
        y, c = self.spot[2:]
        cut, rest = self.cut, self.count - self.cut
        sa, sb = pl.ds(0, cut), pl.ds(cut, rest)
        every = pl.ds(0, 4)
        self.take(4, ga.at[0], to_zm)
        self.take(5, ga.at[1], to_zp)
        self.add((sa, every, z), ga[0].astype(F32) + ga[1].astype(F32))
        self.send(8, self.g.at[pl.ds(0, cut // 2), x2, z], pa.at[0], to_xp)
        self.send(9, self.g.at[pl.ds(cut // 2, cut // 2), x2, z], pa.at[1], to_xm)
        self.take(6, gb.at[0], to_xm)
        self.take(7, gb.at[1], to_xp)
        self.add((sb, x, every), gb[0].astype(F32) + gb[1].astype(F32))
        if rest == 1:
            self.send(10, self.g.at[sb, x, z2], pb.at[0], device(x, z2, y, c))
            self.send(14, self.g.at[sb, x, zp], qb.at[0], to_zp)
            self.send(15, self.g.at[sb, x, zm], qb.at[1], to_zm)
        else:
            self.send(10, self.g.at[pl.ds(cut, rest // 2), x, z2], pb.at[0], to_zp)
            self.send(11, self.g.at[pl.ds(cut + rest // 2, rest // 2), x, z2], pb.at[1], to_zm)

    def step_four(self):
        x, z, xp, xm, zp, zm, x2, z2, (to_xp, to_xm, to_zp, to_zm) = self.names()
        fa, ga, fb, gb, pa, qa, pb, qb = self.buffers
        cut, rest = self.cut, self.count - self.cut
        sa, sb = pl.ds(0, cut), pl.ds(cut, rest)
        self.take(8, pa.at[0], to_xm)
        self.add((pl.ds(0, cut // 2), xp, z), pa[0])
        self.send(12, self.g.at[sa, xp, z], qa.at[0], to_xp)
        self.take(9, pa.at[1], to_xp)
        self.add((pl.ds(cut // 2, cut // 2), xm, z), pa[1])
        self.send(13, self.g.at[sa, xm, z], qa.at[1], to_xm)
        if rest > 1:
            self.take(10, pb.at[0], to_zm)
            self.add((pl.ds(cut, rest // 2), x, zp), pb[0])
            self.send(14, self.g.at[sb, x, zp], qb.at[0], to_zp)
            self.take(11, pb.at[1], to_zp)
            self.add((pl.ds(cut + rest // 2, rest // 2), x, zm), pb[1])
            self.send(15, self.g.at[sb, x, zm], qb.at[1], to_zm)

    def step_five(self, out):
        x, z, xp, xm, zp, zm, x2, z2, (to_xp, to_xm, to_zp, to_zm) = self.names()
        fa, ga, fb, gb, pa, qa, pb, qb = self.buffers
        y, c = self.spot[2:]
        cut, rest = self.cut, self.count - self.cut
        sa, sb = pl.ds(0, cut), pl.ds(cut, rest)
        self.take(12, qa.at[0], to_xm)
        self.take(13, qa.at[1], to_xp)
        out[sa] = (
            self.g.at[sa, x, z][...].astype(F32) + qa[0].astype(F32) + qa[1].astype(F32)
        ).astype(out.dtype)
        self.take(14, qb.at[0], to_zm)
        self.take(15, qb.at[1], to_zp)
        total = self.g.at[sb, x, z][...].astype(F32) + qb[0].astype(F32) + qb[1].astype(F32)
        if rest == 1:
            self.take(10, pb.at[0], device(x, z2, y, c))
            total = total + pb[0].astype(F32)
        out[sb] = total.astype(out.dtype)


class AttentionSum:
    slots = 23

    def __init__(self, mail, spot, mine, theirs, refs):
        self.mail, self.spot, self.mine, self.theirs = mail, spot, mine, theirs
        self.near, self.block, self.got = refs[:3]
        self.plane = PlaneSum(mail, 7, spot, mine, 2, refs[3:])

    @staticmethod
    def scratch():
        return [
            pltpu.VMEM((4, 4, 4, 16, 1024), BF),
            pltpu.VMEM((4, 16, 1024), BF),
            pltpu.VMEM((3, 16, 1024), BF),
        ] + PlaneSum.scratch(4, 2, 16, 1024)

    def start(self, i):
        x, z, y, c = self.spot
        self.mail.send(i, self.theirs.at[:, i], self.near.at[:, i], device(x, z, y, 1 - c))

    def core(self, i):
        x, z, y, c = self.spot
        self.mail.take(i, self.near.at[:, i], device(x, z, y, 1 - c))
        part = self.mine.at[:, i]
        part[...] = (part[...].astype(F32) + self.near[:, i].astype(F32)).astype(BF)

    def cores(self):
        for i in range(4):
            self.core(i)
        self.plane.step_one()

    def rows(self):
        x, z, y, c = self.spot
        self.plane.step_five(self.block)
        for k, step in enumerate((up1, up2, down1)):
            to = device(x, z, step(y), c)
            self.mail.send(4 + k, self.block.at[step(y)], self.got.at[k], to)

    def last(self, out):
        x, z, y, c = self.spot
        total = self.block[y].astype(F32)
        for k, step in enumerate((down1, up2, up1)):
            self.mail.take(4 + k, self.got.at[k], device(x, z, step(y), c))
            total = total + self.got[k].astype(F32)
        out[...] = total


def nn(left, right):
    return jnp.dot(left, right, preferred_element_type=F32)


def nt(left, right):
    return lax.dot_general(left, right, (((1,), (1,)), ((), ())), preferred_element_type=F32)


def tn(left, right):
    return lax.dot_general(left, right, (((0,), (0,)), ((), ())), preferred_element_type=F32)


def mlp_scratch():
    return [
        pltpu.VMEM((4, 2, 128, D), BF),
        pltpu.VMEM((4, 2, 128, D), BF),
        pltpu.VMEM((4, 128, D), BF),
        pltpu.VMEM((3, 128, D), BF),
        pltpu.VMEM((2, 64, D), BF),
        pltpu.VMEM((2, 64, D), BF),
        pltpu.VMEM((2, 128, D), BF),
    ]


def mlp_exchange(mail, spot, src, buffers, chunk, fillers, hook):
    rows, part, near, own, far, fin, got = buffers
    x, z, y, c = spot
    yp, ym, y2 = up1(y), down1(y), up2(y)
    to_yp, to_ym, other = device(x, z, yp, c), device(x, z, ym, c), device(x, z, y, 1 - c)
    begin, end = pl.ds(0, 32), pl.ds(32, 32)
    first, second = pl.ds(0, 64), pl.ds(64, 64)
    mail.send(0, src.at[first], rows.at[y, c, first], to_yp)
    mail.send(1, src.at[second], rows.at[y, c, second], to_ym)
    mail.send(2, src, rows.at[y, c], other)
    mail.send(19, src.at[second], rows.at[y, c, second], to_yp)
    mail.send(20, src.at[first], rows.at[y, c, first], to_ym)
    rows[y, c] = src[...]
    mail.take(2, rows.at[y, 1 - c], other)
    chunk(y)
    mail.send(12, part.at[y, 1 - c], near.at[3], other)
    mail.take(0, rows.at[ym, c, first], to_ym)
    mail.send(3, rows.at[ym, c, first], rows.at[ym, c, first], to_yp)
    mail.take(1, rows.at[yp, c, second], to_yp)
    mail.send(5, rows.at[yp, c, second], rows.at[yp, c, second], to_ym)
    mail.take(19, rows.at[ym, c, second], to_ym)
    mail.send(4, rows.at[ym, c], rows.at[ym, c], other)
    mail.take(20, rows.at[yp, c, first], to_yp)
    mail.send(6, rows.at[yp, c], rows.at[yp, c], other)
    mail.take(4, rows.at[ym, 1 - c], other)
    chunk(ym)
    mail.send(11, part.at[ym, 1 - c], near.at[2], other)
    hook()
    mail.take(6, rows.at[yp, 1 - c], other)
    chunk(yp)
    mail.send(10, part.at[yp, 1 - c], near.at[1], other)
    mail.take(3, rows.at[y2, c, first], to_ym)
    mail.send(7, rows.at[y2, c, first], rows.at[y2, c, first], other)
    mail.take(5, rows.at[y2, c, second], to_yp)
    mail.send(8, rows.at[y2, c, second], rows.at[y2, c, second], other)
    mail.take(11, near.at[2], other)
    own[2] = (part[ym, c].astype(F32) + near[2].astype(F32)).astype(BF)
    mail.send(16, own.at[2], got.at[1], to_ym)
    mail.take(10, near.at[1], other)
    own[1] = (part[yp, c].astype(F32) + near[1].astype(F32)).astype(BF)
    mail.send(15, own.at[1], got.at[0], to_yp)
    mail.take(7, rows.at[y2, 1 - c, first], other)
    mail.take(8, rows.at[y2, 1 - c, second], other)
    chunk(y2)
    mail.send(9, part.at[y2, 1 - c], near.at[0], other)
    fillers[0]()
    mail.take(9, near.at[0], other)
    own[0] = (part[y2, c].astype(F32) + near[0].astype(F32)).astype(BF)
    mail.send(13, own.at[0, pl.ds(0, 32)], far.at[0, begin], to_yp)
    mail.send(14, own.at[0, pl.ds(64, 32)], far.at[1, begin], to_ym)
    mail.send(21, own.at[0, pl.ds(32, 32)], far.at[0, end], to_yp)
    mail.send(22, own.at[0, pl.ds(96, 32)], far.at[1, end], to_ym)
    fillers[1]()
    mail.take(13, far.at[0, begin], to_ym)
    mail.send(17, far.at[0, begin], fin.at[0, begin], to_yp)
    mail.take(14, far.at[1, begin], to_yp)
    mail.send(18, far.at[1, begin], fin.at[1, begin], to_ym)
    mail.take(21, far.at[0, end], to_ym)
    mail.send(23, far.at[0, end], fin.at[0, end], to_yp)
    mail.take(22, far.at[1, end], to_yp)
    mail.send(24, far.at[1, end], fin.at[1, end], to_ym)
    fillers[2]()
    mail.take(12, near.at[3], other)
    mail.take(15, got.at[0], to_ym)
    mail.take(16, got.at[1], to_yp)
    mail.take(17, fin.at[0, begin], to_ym)
    mail.take(18, fin.at[1, begin], to_yp)
    mail.take(23, fin.at[0, end], to_ym)
    mail.take(24, fin.at[1, end], to_yp)
    total = (
        part[y, c].astype(F32)
        + near[3].astype(F32)
        + got[0].astype(F32)
        + got[1].astype(F32)
    )
    return total + fin[...].reshape(128, D).astype(F32)


def nothing():
    return None


def swap_halves(u):
    width = u.shape[1]
    lane = lax.broadcasted_iota(jnp.int32, u.shape, 1)
    return jnp.where(
        lax.rem(lane, 64) < 32, pltpu.roll(u, width - 32, 1), pltpu.roll(u, 32, 1)
    )


def normal(v):
    r = lax.rsqrt(jnp.mean(v * v, axis=-1, keepdims=True) + eps_norm)
    return v * r, r


def forward_kernel(layer, *refs):
    x_ref, a_ref, m_ref, pick_ref, cos_ref, sin_ref, span_ref = refs[:7]
    refs = refs[7:]
    if layer == 0:
        row_ref, shard_ref, m_z_ref = refs[:3]
        refs = refs[3:]
    out_ref, vec_ref, mid_ref, att_ref, qs_ref, kv_ref, probs_ref, low_ref, high_ref = refs[:9]
    hr_ref, gate_ref, up_ref = refs[9:12]
    refs = refs[12:]
    if layer == 0:
        m_zero, m_one, a_one = refs[:3]
        refs = refs[3:]
    blocks, low, high, kv, probs, weights, mask, att, qs, mid, h2 = refs[:11]
    buffers, refs = refs[11:18], refs[18:]
    w, gate, up, send_sem, recv_sem, local_sem = refs[:6]
    rows, part = buffers[0], buffers[1]
    spot = place()
    x, z, y, c = spot
    mail = Mail(send_sem, recv_sem)
    load = pltpu.make_async_copy(a_ref, blocks, local_sem.at[0])
    load.start()
    if layer == 0:
        a_x, a_z, m_x, m_z, slabs = refs[6:]

        def sems(k):
            return local_sem.at[pl.ds(21 + 2 * k, 2)]

        fill = PlaneFill(mail.shifted(34), spot, m_ref, m_z_ref, m_zero, sems(0))
        a_row = RowGather(mail.shifted(50), spot, row_ref, a_x, a_z, sems(1))
        m_row = RowGather(mail.shifted(58), spot, shard_ref.at[1], m_x, m_z, sems(2))
        a_fill = PlaneFill(
            mail.shifted(66), spot, a_x, a_z, a_one.at[c], sems(3), a_one.at[1 - c]
        )
        m_fill = PlaneFill(mail.shifted(82), spot, m_x, m_z, m_one, sems(4))
        load_w = pltpu.make_async_copy(m_zero, slabs, local_sem.at[1])
        greet(ctx_peers(spot) + ring_peers(spot))
        fill.step_one()
        a_row.step_one()
        m_row.step_one()
    else:
        load_w = pltpu.make_async_copy(m_ref, w, local_sem.at[1])
        load_w.start()
        greet(ctx_peers(spot))
    inputs = x_ref[...].astype(F32)
    n, r = normal(inputs)
    load.wait()
    spare = []
    for g in range(8):
        group = jnp.concatenate(
            [blocks[k % 2, k % 8 // 2, g // 2, 2 * (g % 2) + k // 8] for k in range(16)], axis=0
        )
        low[112 * g : 112 * (g + 1)] = nn(pick_ref[0:112, :], group).astype(BF)
        high[112 * g : 112 * (g + 1)] = nn(pick_ref[112:224, :], group).astype(BF)
        spare.append(nn(pick_ref[224:240, :], group))
    gains = functools.reduce(lambda u, v: u + v, [block[0:2, :D] for block in spare])
    vec_ref[0:2, 0:D] = gains
    for j in range(9):
        piece = jnp.zeros((1, 128), F32)
        if j < 8:
            piece = piece + spare[j][0:1, D:]
        if j > 0:
            piece = piece + spare[j - 1][1:2, D:]
        vec_ref[2:3, 128 * j : 128 * (j + 1)] = piece
    stores = [
        pltpu.make_async_copy(low, low_ref, local_sem.at[2]),
        pltpu.make_async_copy(high, high_ref, local_sem.at[3]),
    ]
    hidden = (n * gains[0:1]).astype(BF)
    packed = nn(hidden, low[...]) + vec_ref[2:3, :1024]
    values = nn(hidden, high[:, :128]) + vec_ref[2:3, 1024:]
    cos = jnp.concatenate([cos_ref[...]] * 8, axis=1)
    sin = jnp.concatenate([sin_ref[...]] * 8, axis=1)
    turned = packed * cos + swap_halves(packed) * sin
    kv[y, c, :, 0:128] = turned[:, D:].astype(BF)
    kv[y, c, :, 128:256] = values.astype(BF)
    yp, ym, y2 = up1(y), down1(y), up2(y)
    to_yp, to_ym, other = ctx_peers(spot)
    first, second = pl.ds(0, 64), pl.ds(64, 64)
    mail.send(0, kv.at[y, c], kv.at[y, c], to_yp)
    mail.send(1, kv.at[y, c], kv.at[y, c], to_ym)
    mail.send(2, kv.at[y, c], kv.at[y, c], other)
    for store in stores:
        store.start()
    if layer == 0:
        a_row.step_two()
        m_row.step_two()
    for h in range(H):
        head = (turned[:, HD * h : HD * (h + 1)] * HD ** (-0.5)).astype(BF)
        qs[h // 7, 128 * (h % 7) : 128 * (h % 7 + 1)] = head
    token = lax.broadcasted_iota(jnp.int32, (128, 256), 0)
    key = lax.broadcasted_iota(jnp.int32, (128, 256), 1)
    begin, end = span_ref[4 * y + 2 * c], span_ref[4 * y + 2 * c + 1]
    query_at = lax.rem(token, 64) + 64 * jnp.where(token < 64, begin, end)
    for j in range(4):
        spans = [span_ref[4 * j + i] for i in range(4)]
        upper = jnp.where(key < 192, spans[2], spans[3])
        span = jnp.where(key < 64, spans[0], jnp.where(key < 128, spans[1], upper))
        mask[j] = jnp.where(lax.rem(key, 64) + 64 * span <= query_at, 0.0, neg_fill)
    tops, sums = [], []

    def score(row):
        for k in range(KVH):
            keys = kv[row, :, :, HD * k : HD * (k + 1)].reshape(256, HD)
            s = nt(qs[k], keys) + jnp.concatenate([mask[row]] * 7, axis=0)
            top = jnp.max(s, axis=-1, keepdims=True)
            e = jnp.exp(s - top)
            weights[k, row] = e
            tops.append(top)
            sums.append(jnp.sum(e, axis=-1, keepdims=True))

    mail.take(2, kv.at[y, 1 - c], other)
    score(y)
    mail.take(0, kv.at[ym, c], to_ym)
    mail.send(3, kv.at[ym, c, first], kv.at[ym, c, first], to_yp)
    mail.send(4, kv.at[ym, c], kv.at[ym, c], other)
    mail.take(1, kv.at[yp, c], to_yp)
    mail.send(5, kv.at[yp, c, second], kv.at[yp, c, second], to_ym)
    mail.send(6, kv.at[yp, c], kv.at[yp, c], other)
    if layer == 0:
        fill.step_two()
        a_row.step_three()
        m_row.step_three()
    mail.take(4, kv.at[ym, 1 - c], other)
    score(ym)
    mail.take(3, kv.at[y2, c, first], to_ym)
    mail.send(7, kv.at[y2, c, first], kv.at[y2, c, first], other)
    mail.take(5, kv.at[y2, c, second], to_yp)
    mail.send(8, kv.at[y2, c, second], kv.at[y2, c, second], other)
    mail.take(6, kv.at[yp, 1 - c], other)
    score(yp)
    if layer == 0:
        a_fill.step_one()
        m_fill.step_one()
    mail.take(7, kv.at[y2, 1 - c, first], other)
    mail.take(8, kv.at[y2, 1 - c, second], other)
    score(y2)
    heads = []
    for k in range(KVH):
        top = functools.reduce(jnp.maximum, tops[k::2])
        scales = [jnp.exp(t - top) for t in tops[k::2]]
        whole = functools.reduce(
            lambda u, v: u + v, [f * t for f, t in zip(scales, sums[k::2])]
        )
        inverse = 1.0 / whole
        total = jnp.zeros((D, HD), F32)
        for f, row in zip(scales, (y, ym, yp, y2)):
            p = (weights[k, row] * (f * inverse)).astype(BF)
            probs[k, row] = p
            total = total + nn(p, kv[row, :, :, 128 + HD * k : 128 + HD * (k + 1)].reshape(256, HD))
        heads += [total[128 * i : 128 * (i + 1)] for i in range(7)]
    att[...] = jnp.concatenate(heads, axis=1)
    mid[...] = inputs + nn(att[...].astype(BF), high[:, 128:])
    h2[...] = (normal(mid[...])[0] * gains[1:2]).astype(BF)
    for i, (src, dst) in enumerate(
        ((kv, kv_ref), (probs, probs_ref), (att, att_ref), (qs, qs_ref), (mid, mid_ref))
    ):
        stores.append(pltpu.make_async_copy(src, dst, local_sem.at[4 + i]))
        stores[-1].start()
    if layer == 0:
        fill.step_three()
        load_w.start()

    loaded = []

    def chunk(row):
        if not loaded:
            load_w.wait()
            if layer == 0:
                for member in range(3):
                    for i in range(16):
                        w[member, 56 * i : 56 * (i + 1)] = slabs[member, i // 4, i % 4]
            loaded.append(True)
        h = rows[row].reshape(256, D)
        g = nn(h, w[0])
        u = nn(h, w[1])
        gate[row] = g.astype(BF)
        up[row] = u.astype(BF)
        act = (g / (1.0 + jnp.exp(-g)) * u).astype(BF)
        part[row] = nt(act, w[2]).astype(BF).reshape(2, 128, D)
        k = 9 + 3 * (len(loaded) - 1)
        loaded.append(True)
        for i, (src, dst) in enumerate(((rows, hr_ref), (gate, gate_ref), (up, up_ref))):
            stores.append(pltpu.make_async_copy(src.at[row], dst.at[row], local_sem.at[k + i]))
            stores[-1].start()

    steps = [nothing] * 4
    if layer == 0:
        steps = [nothing, a_fill.step_two, m_fill.step_two, a_fill.step_three]
    total = mlp_exchange(mail.shifted(9), spot, h2, buffers, chunk, steps[1:], steps[0])
    out_ref[...] = mid[...] + total
    if layer == 0:
        m_fill.step_three()
        a_fill.step_four()
    for store in stores:
        store.wait()
    mail.finish()


def forward(layer, state, a_full, m_full, pick, tables, span_order, *shards):
    anywhere = pl.BlockSpec(memory_space=pl.ANY)
    vmem = pl.BlockSpec(memory_space=pltpu.VMEM)
    out_shape = [
        jax.ShapeDtypeStruct((128, D), F32),
        jax.ShapeDtypeStruct((8, QKV), F32),
        jax.ShapeDtypeStruct((128, D), F32),
        jax.ShapeDtypeStruct((128, D), F32),
        jax.ShapeDtypeStruct((KVH, D, HD), BF),
        jax.ShapeDtypeStruct((4, 2, 128, 256), BF),
        jax.ShapeDtypeStruct((KVH, 4, D, 256), BF),
        jax.ShapeDtypeStruct((D, 1024), BF),
        jax.ShapeDtypeStruct((D, 1024), BF),
        jax.ShapeDtypeStruct((4, 2, 128, D), BF),
        jax.ShapeDtypeStruct((4, 256, FS), BF),
        jax.ShapeDtypeStruct((4, 256, FS), BF),
    ]
    operands = [state, a_full, m_full, pick, *tables, span_order]
    smem = pl.BlockSpec(memory_space=pltpu.SMEM)
    in_specs = [vmem, anywhere, anywhere] + [vmem] * 3 + [smem]
    slots = 34
    extra = []
    if layer == 0:
        out_shape += [
            jax.ShapeDtypeStruct((3, 4, 4, 56, FS), BF),
            jax.ShapeDtypeStruct((3, 4, 4, 56, FS), BF),
            jax.ShapeDtypeStruct((2, 4, 4, 4, 16, 1024), BF),
        ]
        operands += shards
        in_specs += [anywhere] * 3
        slots = 98
        extra = [
            pltpu.VMEM((2, 4, 16, 1024), BF),
            pltpu.VMEM((2, 4, 16, 1024), BF),
            pltpu.VMEM((1, 4, 56, FS), BF),
            pltpu.VMEM((2, 4, 56, FS), BF),
            pltpu.VMEM((3, 4, 4, 56, FS), BF),
        ]
    return pl.pallas_call(
        functools.partial(forward_kernel, layer),
        out_shape=tuple(out_shape),
        in_specs=in_specs,
        out_specs=[vmem] * 2 + [anywhere] * (len(out_shape) - 2),
        scratch_shapes=[
            pltpu.VMEM((2, 4, 4, 4, 16, 1024), BF),
            pltpu.VMEM((D, 1024), BF),
            pltpu.VMEM((D, 1024), BF),
            pltpu.VMEM((4, 2, 128, 256), BF),
            pltpu.VMEM((KVH, 4, D, 256), BF),
            pltpu.VMEM((KVH, 4, D, 256), F32),
            pltpu.VMEM((4, 128, 256), F32),
            pltpu.VMEM((128, D), F32),
            pltpu.VMEM((KVH, D, HD), BF),
            pltpu.VMEM((128, D), F32),
            pltpu.VMEM((128, D), BF),
        ]
        + mlp_scratch()
        + [
            pltpu.VMEM((3, D, FS), BF),
            pltpu.VMEM((4, 256, FS), BF),
            pltpu.VMEM((4, 256, FS), BF),
            pltpu.SemaphoreType.DMA((slots,)),
            pltpu.SemaphoreType.DMA((slots,)),
            pltpu.SemaphoreType.DMA((31,)),
        ]
        + extra,
        compiler_params=pltpu.CompilerParams(
            collective_id=12 + layer, has_side_effects=True, vmem_limit_bytes=56 * 1024 * 1024
        ),
        name="forward_layer_%d" % layer,
    )(*operands)


BACK_SLOTS = {1: 48, 0: 94}


def backward_kernel(layer, *refs):
    g_ref, x_ref, vec_ref, cos_ref, sin_ref, place_ref = refs[:6]
    w_ref, hr_ref, gate_ref, up_ref, mid_ref, att_ref, qs_ref = refs[6:13]
    kv_ref, probs_ref, low_ref, high_ref = refs[13:17]
    refs = refs[17:]
    if layer == 0:
        before, gin_ref, m_out, a_zero, a_one = refs[:5]
        refs = refs[5:]
    else:
        gin_ref, m_out, a_out = refs[:3]
        refs = refs[3:]
    buffers, refs = refs[:7], refs[7:]
    w, hr, gate, up, act, src, mid, att, qs = refs[:9]
    low, high, kv, probs, m, gatt, part, near, own, got, glow, ghigh, special = refs[9:22]
    plane_refs, refs = refs[22:30], refs[30:]
    send_sem, recv_sem, local_sem = refs[-3:]
    rows, back = buffers[0], buffers[1]
    spot = place()
    x, z, y, c = spot
    mail = Mail(send_sem, recv_sem)
    pairs = (
        (w_ref, w), (gate_ref, gate), (up_ref, up), (hr_ref, hr), (high_ref, high), (mid_ref, mid),
        (att_ref, att), (probs_ref, probs), (kv_ref, kv), (qs_ref, qs), (low_ref, low),
    )
    loads = [pltpu.make_async_copy(u, v, local_sem.at[i]) for i, (u, v) in enumerate(pairs)]
    for load in loads[:4]:
        load.start()
    src[...] = g_ref[...].astype(BF)
    yp, ym, y2 = up1(y), down1(y), up2(y)
    to_yp, to_ym, other = ctx_peers(spot)
    to_y2 = device(x, z, y2, c)
    greet([to_yp, to_ym, other, to_y2] + PlaneSum.peers(spot, 3, 2))
    plane = PlaneSum(mail, 32, spot, m, 2, plane_refs)
    older = final = None
    if layer == 0:
        older_mine, older_refs = refs[0], refs[1:12]
        pair, final_refs = refs[12], refs[13:24]
        older = AttentionSum(mail.shifted(48), spot, older_mine, before.at[1 - c], older_refs)
        final = AttentionSum(mail.shifted(71), spot, pair.at[0], pair.at[1], final_refs)
        older_load = pltpu.make_async_copy(before.at[c], older_mine, local_sem.at[11])
        older_load.start()

    loaded = []

    def chunk(row):
        if not loaded:
            for load in loads[:3]:
                load.wait()
            loaded.append(True)
            for load in loads[4:]:
                load.start()
        gz = rows[row].reshape(256, D)
        gact = nn(gz, w[2])
        g = gate[row].astype(F32)
        u = up[row].astype(F32)
        s = 1.0 / (1.0 + jnp.exp(-g))
        silu = g * s
        act[row] = (silu * u).astype(BF)
        gg = (gact * u * (s + silu * (1.0 - s))).astype(BF)
        gu = (gact * silu).astype(BF)
        gate[row] = gg
        up[row] = gu
        back[row] = (nt(gg, w[0]) + nt(gu, w[1])).astype(BF).reshape(2, 128, D)

    def weight_grad(member, left, right):
        r = right[...].reshape(1024, FS)
        for i in range(7):
            l = left[:, :, :, 128 * i : 128 * (i + 1)].reshape(1024, 128)
            tile = tn(l, r).astype(BF)
            for b in range(16):
                lo, hi = max(56 * b, 128 * i), min(56 * (b + 1), 128 * (i + 1))
                if lo < hi:
                    m[member, b // 4, b % 4, lo - 56 * b : hi - 56 * b] = tile[
                        lo - 128 * i : hi - 128 * i
                    ]

    def first_filler():
        weight_grad(2, rows, act)

    def second_filler():
        loads[3].wait()
        weight_grad(0, hr, gate)

    def third_filler():
        weight_grad(1, hr, up)
        plane.step_one()

    def hook():
        if older:
            for i in range(4):
                older.start(i)

    ghid2 = mlp_exchange(
        mail, spot, src, buffers, chunk, [first_filler, second_filler, third_filler], hook
    )
    if older:
        older_load.wait()
        older.cores()
    for load in loads[4:7]:
        load.wait()
    n, r = normal(mid[...])
    t = ghid2 * vec_ref[1:2, :D]
    gmid = g_ref[...].astype(F32) + r * (t - n * jnp.mean(t * n, axis=-1, keepdims=True))
    ggain_two = jnp.sum(ghid2 * n, axis=0, keepdims=True)
    gin_ref[...] = gmid
    gy = gmid.astype(BF)
    ga = nt(gy, high[:, 128:]).astype(BF)
    product = ga.astype(F32) * att[...]
    deltas = [[], []]
    for h in range(H):
        gatt[h // 7, 128 * (h % 7) : 128 * (h % 7 + 1)] = ga[:, HD * h : HD * (h + 1)]
        deltas[h // 7].append(
            jnp.sum(product[:, HD * h : HD * (h + 1)], axis=-1, keepdims=True)
        )
    ghigh[:, 128:] = tn(att[...].astype(BF), gy).astype(BF)
    for load in loads[7:]:
        load.wait()
    plane.step_two()
    deltas = [jnp.concatenate(group, axis=0) for group in deltas]
    gqs = [jnp.zeros((D, HD), F32) for k in range(KVH)]
    for row in range(4):
        for k in range(KVH):
            keys = kv[row, :, :, HD * k : HD * (k + 1)].reshape(256, HD)
            values = kv[row, :, :, 128 + HD * k : 128 + HD * (k + 1)].reshape(256, HD)
            p = probs[k, row]
            s = (p.astype(F32) * (nt(gatt[k], values) - deltas[k])).astype(BF)
            gqs[k] = gqs[k] + nn(s, keys)
            gk = tn(qs[k], s).astype(BF)
            gv = tn(gatt[k], p).astype(BF)
            for j in range(2):
                part[row, j, HD * k : HD * (k + 1)] = gk[:, 128 * j : 128 * (j + 1)]
                part[row, j, 128 + HD * k : 128 + HD * (k + 1)] = gv[:, 128 * j : 128 * (j + 1)]
        mail.send(25 + row, part.at[row, 1 - c], near.at[row], other)
        if older and row == 1:
            older.plane.step_two()
    plane.step_three()
    cos = jnp.concatenate([cos_ref[...]] * 7, axis=1)
    sin = jnp.concatenate([sin_ref[...]] * 7, axis=1)
    gq = [gqs[h // 7][128 * (h % 7) : 128 * (h % 7 + 1)] for h in range(H)]
    gq = jnp.concatenate(gq, axis=1) * HD ** (-0.5)
    gq = (gq * cos - swap_halves(gq) * sin).astype(BF)
    inputs = x_ref[...].astype(F32)
    n, r = normal(inputs)
    hidden = (n * vec_ref[0:1, :D]).astype(BF)
    for i in range(4):
        mail.take(25 + i, near.at[i], other)
    own[...] = (part[:, c].astype(F32) + near[...].astype(F32)).astype(BF)
    mail.send(29, own.at[yp], got.at[0], to_yp)
    mail.send(30, own.at[ym], got.at[1], to_ym)
    mail.send(31, own.at[y2], got.at[2], to_y2)
    if older:
        older.plane.step_three()
    glow[:, :D] = tn(hidden, gq).astype(BF)
    ghid = nt(gq, low[:, :D])
    bias_q = jnp.sum(gq.astype(F32), axis=0, keepdims=True)
    plane.step_four()
    mail.take(29, got.at[0], to_ym)
    mail.take(30, got.at[1], to_yp)
    mail.take(31, got.at[2], to_y2)
    total = own[y].astype(F32) + got[0].astype(F32) + got[1].astype(F32) + got[2].astype(F32)
    total = total.T
    gk = total[:, :128]
    gk = (gk * cos_ref[...] - swap_halves(gk) * sin_ref[...]).astype(BF)
    gv = total[:, 128:].astype(BF)
    ghid = ghid + nt(gk, low[:, D:]) + nt(gv, high[:, :128])
    glow[:, D:] = tn(hidden, gk).astype(BF)
    ghigh[:, :128] = tn(hidden, gv).astype(BF)
    t = ghid * vec_ref[0:1, :D]
    gin_ref[...] += r * (t - n * jnp.mean(t * n, axis=-1, keepdims=True))
    ggain_one = jnp.sum(ghid * n, axis=0, keepdims=True)
    if older:
        older.plane.step_four()
    bias_k = jnp.sum(gk.astype(F32), axis=0, keepdims=True)
    bias_v = jnp.sum(gv.astype(F32), axis=0, keepdims=True)
    bias = jnp.concatenate([bias_q, bias_k], axis=1)
    row = lax.broadcasted_iota(jnp.int32, (16, 1024), 0)
    row_last = jnp.concatenate([ggain_two, bias_v], axis=1)
    for g in range(8):
        row_seven = jnp.concatenate([ggain_one, bias[:, 128 * g : 128 * (g + 1)]], axis=1)
        extra = jnp.where(row == 0, row_seven, jnp.where(row == 1, row_last, 0.0))
        special[...] = extra.astype(BF)
        block = (
            nn(place_ref[0], glow[112 * g : 112 * (g + 1)])
            + nn(place_ref[1], ghigh[112 * g : 112 * (g + 1)])
            + nn(place_ref[2, :, 0:16], special[...])
        ).astype(BF)
        for k in range(16):
            core, line, column = k % 2, k % 8 // 2, 2 * (g % 2) + k // 8
            piece = block[16 * k : 16 * (k + 1)]
            if layer == 0:
                pair[lax.rem(c + core, 2), line, g // 2, column] = piece
            else:
                a_out[core, line, g // 2, column] = piece
        if layer == 0 and g % 2 == 1:
            final.start(g // 2)
            if g > 1:
                final.core(g // 2 - 1)
    if layer == 0:
        final.core(3)
        final.plane.step_one()
        older.rows()
        plane.step_five(m_out)
        final.plane.step_two()
        older.last(a_one)
        final.plane.step_three()
        final.plane.step_four()
        final.rows()
        final.last(a_zero)
    else:
        plane.step_five(m_out)
    mail.finish()


def backward(layer, grad_output, x, vectors, tables, place_rows, w, kept_mlp, kept, before):
    anywhere = pl.BlockSpec(memory_space=pl.ANY)
    vmem = pl.BlockSpec(memory_space=pltpu.VMEM)
    operands = [grad_output, x, vectors, *tables, place_rows, w, *kept_mlp, *kept]
    out_shape = [jax.ShapeDtypeStruct((128, D), F32), jax.ShapeDtypeStruct((3, 56, FS), F32)]
    extra = []
    if layer == 0:
        operands.append(before)
        out_shape += [jax.ShapeDtypeStruct((16, 1024), F32)] * 2
        extra = [pltpu.VMEM((4, 4, 4, 16, 1024), BF)] + AttentionSum.scratch()
        extra += [pltpu.VMEM((2, 4, 4, 4, 16, 1024), BF)] + AttentionSum.scratch()
    else:
        out_shape.append(jax.ShapeDtypeStruct((2, 4, 4, 4, 16, 1024), BF))
    return pl.pallas_call(
        functools.partial(backward_kernel, layer),
        out_shape=tuple(out_shape),
        in_specs=[vmem] * 6 + [anywhere] * (len(operands) - 6),
        out_specs=[vmem] * len(out_shape),
        scratch_shapes=mlp_scratch()
        + [
            pltpu.VMEM((3, D, FS), BF),
            pltpu.VMEM((4, 2, 128, D), BF),
            pltpu.VMEM((4, 256, FS), BF),
            pltpu.VMEM((4, 256, FS), BF),
            pltpu.VMEM((4, 256, FS), BF),
            pltpu.VMEM((128, D), BF),
            pltpu.VMEM((128, D), F32),
            pltpu.VMEM((128, D), F32),
            pltpu.VMEM((KVH, D, HD), BF),
            pltpu.VMEM((D, 1024), BF),
            pltpu.VMEM((D, 1024), BF),
            pltpu.VMEM((4, 2, 128, 256), BF),
            pltpu.VMEM((KVH, 4, D, 256), BF),
            pltpu.VMEM((3, 4, 4, 56, FS), BF),
            pltpu.VMEM((KVH, D, HD), BF),
            pltpu.VMEM((4, 2, 256, 128), BF),
            pltpu.VMEM((4, 256, 128), BF),
            pltpu.VMEM((4, 256, 128), BF),
            pltpu.VMEM((3, 256, 128), BF),
            pltpu.VMEM((D, 1024), BF),
            pltpu.VMEM((D, 1024), BF),
            pltpu.VMEM((16, 1024), BF),
        ]
        + PlaneSum.scratch(3, 2, 56, FS)
        + extra
        + [
            pltpu.SemaphoreType.DMA((BACK_SLOTS[layer],)),
            pltpu.SemaphoreType.DMA((BACK_SLOTS[layer],)),
            pltpu.SemaphoreType.DMA((12,)),
        ],
        compiler_params=pltpu.CompilerParams(
            collective_id=14 + layer, has_side_effects=True, vmem_limit_bytes=60 * 1024 * 1024
        ),
        name="backward_layer_%d" % layer,
    )(*operands)


def select_matrix():
    pick = np.zeros((226, 256), np.float32)
    for k in range(16):
        for r in range(7):
            pick[7 * k + r, 16 * k + r] = 1
            pick[112 + 7 * k + r, 16 * k + 8 + r] = 1
        pick[224, 16 * k + 7] = 1
        pick[225, 16 * k + 15] = 1
    return pick


def assemble_kernel(
    a_zero, a_one, m_zero, m_one, g_one, g_qkv, g_qk, g_value, g_out, g_two, g_gate, g_up, g_down, rows
):
    index = lax.axis_index("dp") * 8 + lax.axis_index("ctx")
    rows[...] = jnp.zeros_like(rows)
    for l, (a_ref, m_ref) in enumerate(((a_zero, m_zero), (a_one, m_one))):
        for r in range(7):
            g_qkv[r, l : l + 1, 0:1024] = a_ref[r : r + 1, :]
            g_qkv[r, l : l + 1, 1024:1152] = a_ref[8 + r : 9 + r, 0:128]
            g_out[r, l : l + 1] = a_ref[8 + r : 9 + r, 128:1024]
        g_gate[l] = m_ref[0]
        g_up[l] = m_ref[1]
        g_down[l] = m_ref[2]
        rows[l : l + 1] = a_ref[7:8, :]
        rows[2 + l : 3 + l] = a_ref[15:16, :]
    gains = pltpu.roll(rows[...], lax.rem(1024 - 7 * index, 1024), 1)
    g_one[...] = gains[0:2, 0:7]
    g_two[...] = gains[2:4, 0:7]
    g_qk[...] = pltpu.roll(rows[...], 128 - 8 * lax.rem(index, 16), 1)[0:2, 0:8]
    g_value[...] = pltpu.roll(rows[...], 128 - index, 1)[2:4, 0:1]


def assemble(a_sums, m_sums):
    vmem = pl.BlockSpec(memory_space=pltpu.VMEM)
    shapes = ((2, 7), (7, 2, QKV), (2, 8), (2, 1), (7, 2, D), (2, 7)) + ((2, 56, FS),) * 3
    out = pl.pallas_call(
        assemble_kernel,
        out_shape=tuple(jax.ShapeDtypeStruct(shape, F32) for shape in shapes),
        in_specs=[vmem] * 4,
        out_specs=[vmem] * len(shapes),
        scratch_shapes=[pltpu.VMEM((8, 1024), F32)],
        name="assemble",
    )(*a_sums, *m_sums)
    one, qkv, qk, value, outs, two, gate, up, down = out
    qkv, outs = qkv.transpose(1, 0, 2), outs.transpose(1, 0, 2)
    return one, qkv, qk, value, outs, two, gate, up, down.transpose(0, 2, 1)


def shards(
    tokens, cotangent, span_order, gain_one, w_qkv, b_qkv, w_out, gain_two, w_gate, w_up, w_down
):
    sequences, local_len, width = tokens.shape
    span_len = local_len // 2
    local_spans = lax.dynamic_slice_in_dim(span_order, 2 * lax.axis_index("ctx"), 2)
    local_pos = jnp.repeat(local_spans * span_len, span_len) + np.tile(np.arange(span_len), 2)
    half = np.arange(HD // 2, dtype=np.float32)
    frequency = np.tile(np.float32(rope_base) ** (-half * np.float32(2.0 / HD)), 4)
    sign = np.tile(np.repeat(np.float32([-1, 1]), HD // 2), 2)
    angles = local_pos.astype(F32)[:, None] * frequency[None, :].astype(np.float32)
    tables = (jnp.cos(angles), jnp.sin(angles) * sign[None, :])
    chosen = select_matrix()
    pick = jnp.asarray(np.concatenate([chosen, np.zeros((14, 256), np.float32)]), BF)
    spread = np.zeros((3, 256, 112), np.float32)
    spread[0], spread[1], spread[2, :, :2] = chosen[:112].T, chosen[112:224].T, chosen[224:].T
    spread = jnp.asarray(spread, BF)

    m_block = jnp.stack([w_gate, w_up, w_down.transpose(0, 2, 1)], axis=1)
    a_zero, row_one, m_x, m_z = first_gather(
        gain_one, w_qkv.transpose(1, 0, 2), b_qkv, w_out.transpose(1, 0, 2), gain_two, m_block
    )
    state_zero = tokens.reshape(local_len, width)
    state_one, *saved_zero, m_zero, m_one, a_one = forward(
        0, state_zero, a_zero, m_x, pick, tables, span_order, row_one, m_block, m_z
    )
    m_full = (m_zero.reshape(3, D, FS), m_one.reshape(3, D, FS))
    state, *saved_one = forward(1, state_one, a_one, m_full[1], pick, tables, span_order)
    vectors = (saved_zero[0], saved_one[0])
    kept_layers = [
        (saved_zero[1:8], saved_zero[8:]),
        (saved_one[1:8], saved_one[8:]),
    ]
    grad_one = cotangent.reshape(local_len, width)
    (state_in, kept, kept_mlp) = (state_one,) + kept_layers[1]
    grad_zero, m_sum_one, a_grads = backward(
        1, grad_one, state_in, vectors[1], tables, spread, m_full[1], kept_mlp, kept, None
    )
    kept, kept_mlp = kept_layers[0]
    grad_state, m_sum_zero, a_sum_zero, a_sum_one = backward(
        0, grad_zero, state_zero, vectors[0], tables, spread, m_full[0], kept_mlp, kept, a_grads
    )
    a_sums = (a_sum_zero, a_sum_one)
    sums = (m_sum_zero, m_sum_one)
    stacks = assemble(a_sums, sums)
    output = state.astype(BF).reshape(sequences, local_len, width)
    input_grad = grad_state.reshape(sequences, local_len, width)
    return (output, input_grad) + stacks


def solution(mesh):
    return jax.shard_map(
        shards,
        mesh=mesh,
        in_specs=(
            P("dp", "ctx", None),
            P("dp", "ctx", None),
            P(),
            P(None, ("dp", "ctx")),
            P(None, ("dp", "ctx"), None),
            P(None, ("dp", "ctx")),
            P(None, ("dp", "ctx"), None),
            P(None, ("dp", "ctx")),
            P(None, "dp", "ctx"),
            P(None, "dp", "ctx"),
            P(None, "ctx", "dp"),
        ),
        out_specs=(
            P("dp", "ctx", None),
            P("dp", "ctx", None),
            P(None, ("dp", "ctx")),
            P(None, ("dp", "ctx"), None),
            P(None, ("dp", "ctx")),
            P(None, ("dp", "ctx")),
            P(None, ("dp", "ctx"), None),
            P(None, ("dp", "ctx")),
            P(None, "dp", "ctx"),
            P(None, "dp", "ctx"),
            P(None, "ctx", "dp"),
        ),
        check_vma=False,
    )
```
